32 devices in a mesh: head: 4 (over y, x), seq: 8 (over z, core).
Axes of the slice: x: 2, y: 2, z: 4, core: 2. Of those that a mesh axis runs over, the one named last changes fastest.
Arguments:
- layer_input: bfloat16 [8192, 768], P('seq'), may hold values from -6 to 6
- cotangent: bfloat16 [8192, 768], P('seq'), may hold values from -6 to 6
- norm1_gain: float32 [768], replicated, may hold values from 0.25 to 1.75
- w_query: bfloat16 [768, 768], P(None, 'head'), may hold values from -0.21875 to 0.21875
- w_key: bfloat16 [768, 768], P(None, 'head'), may hold values from -0.21875 to 0.21875
- w_value: bfloat16 [768, 768], P(None, 'head'), may hold values from -0.21875 to 0.21875
- w_attn_out: bfloat16 [768, 768], P('head'), may hold values from -3 to 3
- bias_table: float32 [32, 12], P(None, 'head'), may hold values from -6 to 6
- norm2_gain: float32 [768], replicated, may hold values from 0.25 to 1.75
- w_router: float32 [768, 8], replicated, may hold values from -0.109375 to 0.109375
- w_expert_in: bfloat16 [8, 768, 3072], P('seq', None, 'head'), may hold values from -0.21875 to 0.21875
- w_expert_out: bfloat16 [8, 3072, 768], P('seq', 'head'), may hold values from -6 to 6
- expert_ids: int32 [8192], P('seq'), may hold values from 0 to 7, as said below
- slot_ids: int32 [8192], P('seq'), may hold values from 0 to 20, as said below
- buckets: int32 [2047], replicated, may hold values from 0 to 31
Outputs:
- layer_output: float32 [8192, 768], P('seq')
- input_grad: float32 [8192, 768], P('seq')
- norm1_gain_grad: float32 [768], replicated
- w_query_grad: float32 [768, 768], P(None, 'head')
- w_key_grad: float32 [768, 768], P(None, 'head')
- w_value_grad: float32 [768, 768], P(None, 'head')
- w_attn_out_grad: float32 [768, 768], P('head')
- bias_table_grad: float32 [32, 12], P(None, 'head')
- norm2_gain_grad: float32 [768], replicated
- w_router_grad: float32 [768, 8], replicated
- w_expert_in_grad: float32 [8, 768, 3072], P('seq', None, 'head')
- w_expert_out_grad: float32 [8, 3072, 768], P('seq', 'head')
The draws below stay inside these ranges and needn't reach their ends.
Inputs may be any that keep to these rules, and one draw needn't show every extreme that they name: `expert_ids`: in the 1024 tokens of each index of seq one expert, the same for every index, is named by 20 + 1 tokens or more. `slot_ids`: the token's rank, counted from 0 in token order, among the tokens of its index of seq that name the same expert; 20 where that rank is 20 or more (the token is dropped).
All inputs are finite; a program needn't handle non-finite values.
Results may differ from the reference program's by a relative error of at most 0.024.
Values may be sent and summed in bfloat16 or wider, within the bound.
No kernel may reach another device: no remote copies, remote signals or barrier semaphores. Data moves between devices by JAX's collectives and lax.ppermute only.
A program may use at most 192 MiB of HBM per device.

```python
import jax
import jax.numpy as jnp
from jax import lax

D = 768
HEADS = 12
HEAD_DIM = 64
FF = 3072
BUCKETS = 32
SEQ_LEN = 1024
CAP = 20
TOK_DEV = 1024
TOKENS = 8192
EXPERTS = 8
INNER = 768
OFFSETS = 2047
N_SEQ = 8


def route_table(key):
    pick_key, hot_key, coin_key, order_key, star_key = jax.random.split(key, 5)
    base_ids = jax.random.randint(pick_key, (TOKENS,), 0, EXPERTS)
    popular = jax.random.permutation(hot_key, EXPERTS)
    hot_ids = popular[jax.random.randint(jax.random.fold_in(hot_key, 1), (TOKENS,), 0, max(EXPERTS // 8, 1))]
    coin_flip = jax.random.randint(coin_key, (TOKENS,), 0, 4)
    chosen_ids = jnp.where(coin_flip == 0, hot_ids, base_ids)
    star_id = jax.random.randint(star_key, (), 0, EXPERTS)
    scores_int = jax.random.randint(order_key, (N_SEQ, TOK_DEV), 0, 2 ** 20) * TOK_DEV + jnp.arange(TOK_DEV, dtype=jnp.int32)[None, :]
    ranking = jnp.argsort(jnp.argsort(scores_int, axis=1), axis=1)
    forced = (ranking <= CAP).reshape(TOKENS)
    chosen_ids = jnp.where(forced, star_id, chosen_ids).astype(jnp.int32)
    one_hot = (chosen_ids.reshape(N_SEQ, TOK_DEV, 1) == jnp.arange(EXPERTS, dtype=jnp.int32)[None, None, :]).astype(jnp.int32)
    running = jnp.cumsum(one_hot, axis=1)
    ranks = jnp.sum(running * one_hot, axis=-1).reshape(TOKENS) - 1
    return (chosen_ids, jnp.minimum(ranks, CAP).astype(jnp.int32))


def draw_expert_ids(key, part):
    return route_table(key)[0]


def draw_slot_ids(key, part):
    return route_table(key)[1]


def place_ends(array, own_key, low, high):
    dims = array.shape
    index_at = [jax.random.randint(jax.random.fold_in(own_key, axis), (), 0, dims[axis]) for axis in range(len(dims))]
    array = array.at[tuple(index_at)].set(low)
    longest = dims.index(max(dims))
    index_at[longest] = (index_at[longest] + 1) % dims[longest]
    return array.at[tuple(index_at)].set(high)


def level_of(rng, shape, cuts, low, top_value):
    loudness = 1.0
    for dim, parts in cuts:
        draws = jax.random.uniform(jax.random.fold_in(jax.random.fold_in(rng, 6), dim), (parts,), jnp.float32, low / len(cuts), top_value / len(cuts))
        loudness = loudness * jnp.repeat(jnp.exp(draws), shape[dim] // parts).reshape((-1,) + (1,) * (len(shape) - 1 - dim))
    return loudness


def scatter_about(rng, dims, scale, most, pieces=(), kind=jnp.bfloat16):
    result = jax.random.normal(rng, dims, jnp.float32) * scale
    if len(pieces) > 0:
        result = level_of(rng, dims, pieces, -0.22, 0.18) * result
    return jnp.clip(result, min=-most, max=most).astype(kind)


def setup_inputs(seed: int = 0) -> dict:
    arg_keys = jax.random.split(jax.random.key(seed), 16)
    layer_input = scatter_about(arg_keys[0], (TOKENS, D), 1.0, 6.0, ((0, 8),))
    cotangent = scatter_about(arg_keys[1], (TOKENS, D), 1.0, 6.0, ((0, 8),))
    norm1_gain = jnp.clip(1.0 + 0.15 * jax.random.normal(arg_keys[2], (D,), jnp.float32), 0.25, 1.75)
    w_query = scatter_about(arg_keys[3], (D, INNER), D ** -0.5, 0.21875, ((1, 4),))
    w_key = scatter_about(arg_keys[4], (D, INNER), D ** -0.5, 0.21875, ((1, 4),))
    w_value = scatter_about(arg_keys[5], (D, INNER), D ** -0.5, 0.21875, ((1, 4),))
    w_attn_out = scatter_about(arg_keys[6], (INNER, D), 0.5, 3.0, ((0, 4),))
    bias_table = scatter_about(arg_keys[7], (BUCKETS, HEADS), 1.0, 6.0, ((1, 4),), jnp.float32)
    norm2_gain = jnp.clip(1.0 + 0.15 * jax.random.normal(arg_keys[8], (D,), jnp.float32), 0.25, 1.75)
    w_router = scatter_about(arg_keys[9], (D, EXPERTS), (4 * D) ** -0.5, 0.109375, (), jnp.float32)
    w_expert_in = scatter_about(arg_keys[10], (EXPERTS, D, FF), D ** -0.5, 0.21875, ((0, 8), (2, 4)))
    w_expert_out = scatter_about(arg_keys[11], (EXPERTS, FF, D), ((EXPERTS * EXPERTS // FF + 1) ** 0.5), 6.0, ((0, 8), (1, 4)))
    expert_ids = draw_expert_ids(jax.random.fold_in(arg_keys[15], 71), 0)
    slot_ids = draw_slot_ids(jax.random.fold_in(arg_keys[15], 71), 0)
    buckets = place_ends(jax.random.randint(arg_keys[14], (OFFSETS,), 0, BUCKETS), jax.random.fold_in(arg_keys[14], 1), 0, BUCKETS - 1).astype(jnp.int32)
    return {"layer_input": layer_input, "cotangent": cotangent, "norm1_gain": norm1_gain, "w_query": w_query, "w_key": w_key, "w_value": w_value, "w_attn_out": w_attn_out, "bias_table": bias_table, "norm2_gain": norm2_gain, "w_router": w_router, "w_expert_in": w_expert_in, "w_expert_out": w_expert_out, "expert_ids": expert_ids, "slot_ids": slot_ids, "buckets": buckets}


highest = lax.Precision.HIGHEST

@jax.custom_vjp
def low(v):
    return lax.optimization_barrier(v.astype(jnp.bfloat16)).astype(jnp.float32)

@jax.custom_vjp
def low_back(v):
    return v

def low_keep(v):
    return (low(v), None)

def low_pass(kept, grad):
    return (grad,)

def back_keep(v):
    return (v, None)

def back_low(kept, grad):
    return (low(grad),)
low.defvjp(low_keep, low_pass)
low_back.defvjp(back_keep, back_low)

def rms_norm(values, gain_vec):
    return values * lax.rsqrt(lax.optimization_barrier(jnp.mean(values * values, axis=-1, keepdims=True)) + 1e-06) * gain_vec

def matmul(left_side, right_side):
    return jnp.dot(left_side, right_side, precision=highest, preferred_element_type=jnp.float32)

def reference(layer_input, cotangent, norm1_gain, w_query, w_key, w_value, w_attn_out, bias_table, norm2_gain, w_router, w_expert_in, w_expert_out, expert_ids, slot_ids, buckets):
    score_scale = HEAD_DIM ** (-0.5)
    positions = jnp.arange(TOKENS, dtype=jnp.int32)
    seq_pos = jnp.arange(SEQ_LEN, dtype=jnp.int32)
    bucket_ids = buckets[seq_pos[None, :] - seq_pos[:, None] + SEQ_LEN - 1]
    cell_row = jnp.where(slot_ids < CAP, positions // TOK_DEV * CAP + slot_ids, N_SEQ * CAP).astype(jnp.int32)
    chosen = (expert_ids[:, None] == jnp.arange(EXPERTS, dtype=jnp.int32)[None, :]).astype(jnp.float32)

    def block_layer(input_full, gain_first, query_w, key_w, value_w, mix_w, table_w, gain_second, router_w, inner_w, outer_w):
        normed_first = low(rms_norm(input_full, gain_first))
        queries = low_back(low(matmul(normed_first, query_w))).reshape(TOKENS, HEADS, HEAD_DIM)
        key_rows = low_back(low(matmul(normed_first, key_w))).reshape(TOKENS, HEADS, HEAD_DIM)
        value_rows = low_back(low(matmul(normed_first, value_w))).reshape(TOKENS, HEADS, HEAD_DIM)
        bias_vals = jnp.transpose(table_w[bucket_ids], (2, 0, 1))

        def attend(seq_index):
            first_row = seq_index * SEQ_LEN
            seq_query = lax.dynamic_slice_in_dim(queries, first_row, SEQ_LEN, 0)
            seq_key = lax.dynamic_slice_in_dim(key_rows, first_row, SEQ_LEN, 0)
            seq_value = lax.dynamic_slice_in_dim(value_rows, first_row, SEQ_LEN, 0)
            raw_score = jnp.einsum('qhd,khd->hqk', seq_query, seq_key, precision=highest) * score_scale
            score = low_back(raw_score + bias_vals)
            weights = low(jax.nn.softmax(score, axis=-1))
            return jnp.einsum('hqk,khd->qhd', weights, seq_value, precision=highest).reshape(SEQ_LEN, INNER)
        attended = lax.map(jax.checkpoint(attend), jnp.arange(TOKENS // SEQ_LEN, dtype=jnp.int32)).reshape(TOKENS, INNER)
        attended = low_back(low(attended))
        hidden = input_full + low_back(matmul(attended, mix_w))
        normed_second = rms_norm(hidden, gain_second)
        router_probs = jax.nn.softmax(matmul(normed_second, router_w), axis=-1)
        gate_prob = lax.optimization_barrier(jnp.sum(router_probs * chosen, axis=-1))
        routed = low_back(low(normed_second))
        buffer = jnp.zeros((EXPERTS, N_SEQ * CAP, D), jnp.float32).at[expert_ids, cell_row].set(routed, mode='drop')
        pre_act = low_back(jnp.einsum('erd,edf->erf', buffer, inner_w, precision=highest))
        activated = low(jax.nn.gelu(pre_act, approximate=False))
        expert_out = low_back(low(jnp.einsum('erf,efd->erd', activated, outer_w, precision=highest)))
        combined = expert_out.at[expert_ids, cell_row].get(mode='fill', fill_value=0.0)
        return hidden + gate_prob[:, None] * combined
    floats = (layer_input.astype(jnp.float32), norm1_gain.astype(jnp.float32), w_query.astype(jnp.float32), w_key.astype(jnp.float32), w_value.astype(jnp.float32), w_attn_out.astype(jnp.float32), bias_table.astype(jnp.float32), norm2_gain.astype(jnp.float32), w_router.astype(jnp.float32), w_expert_in.astype(jnp.float32), w_expert_out.astype(jnp.float32))
    layer_output, pullback = jax.vjp(block_layer, *floats)
    grads = pullback(cotangent.astype(jnp.float32))
    return (layer_output, grads[0], grads[1], grads[2], grads[3], grads[4], grads[5], grads[6], grads[7], grads[8], grads[9], grads[10])
```

```python
from functools import partial

import jax
import jax.numpy as jnp
import numpy as np
from jax import lax
from jax.experimental import pallas as pl
from jax.experimental.pallas import tpu as pltpu
from jax.sharding import PartitionSpec as P

CAP = 20
SLOT = 24
EPS = 1e-06
BLOCK = 128
MIB = 1024 * 1024

f32 = jnp.float32
bf16 = jnp.bfloat16
highest = lax.Precision.HIGHEST


def dot(a, b):
    return jnp.dot(a, b, preferred_element_type=f32)


def dot_nt(a, b, precision=None):
    return lax.dot_general(
        a, b, (((1,), (1,)), ((), ())), precision=precision, preferred_element_type=f32
    )


def dot_tn(a, b, precision=None):
    return lax.dot_general(
        a, b, (((0,), (0,)), ((), ())), precision=precision, preferred_element_type=f32
    )


def iota(shape, dim):
    return lax.broadcasted_iota(jnp.int32, shape, dim)


def split_two(v):
    high = v.astype(bf16)
    return high, (v - high.astype(f32)).astype(bf16)


def shape_of(rows, cols, dtype):
    return jax.ShapeDtypeStruct((rows, cols), dtype)


def call(kernel, outs, args, scratch=(), name=None, flops=0, vmem=48, smem=()):
    outs = tuple(outs)
    moved = sum(int(np.prod(a.shape)) * a.dtype.itemsize for a in tuple(args) + outs)
    specs = [
        pl.BlockSpec(memory_space=pltpu.SMEM if i in smem else pltpu.VMEM)
        for i in range(len(args))
    ]
    return pl.pallas_call(
        kernel,
        out_shape=outs,
        in_specs=specs,
        out_specs=tuple(pl.BlockSpec(memory_space=pltpu.VMEM) for _ in outs),
        scratch_shapes=list(scratch),
        compiler_params=pltpu.CompilerParams(vmem_limit_bytes=vmem * MIB),
        cost_estimate=pl.CostEstimate(flops=flops, bytes_accessed=moved, transcendentals=0),
        name=name,
    )(*args)


def slot_rows(ids, slots, rows):
    cell = jnp.where(slots < CAP, ids * SLOT + slots, -1)
    return (iota((rows, cell.shape[1]), 0) == cell).astype(f32)


def select_kernel(where_ref, x_ref, cot_ref, ids_ref, slots_ref, *refs, shards, heads):
    sel_in, sel_up, place, place_c, x_c, cot_c = refs[:6]
    pieces = refs[6 : 6 + shards]
    up_s, place_s = refs[6 + shards :]
    head, shard = where_ref[0], where_ref[1]
    rows = sel_in.shape[0]
    tokens = x_ref.shape[0]
    part = tokens // heads
    slot_hot = slot_rows(ids_ref[...], slots_ref[...], rows)
    place_s[...] = jnp.transpose(slot_hot)
    place[...] = place_s[...].astype(bf16)
    slot_low = slot_hot.astype(bf16)
    sel_in[...] = dot(slot_low, x_ref[...]).astype(bf16)
    up_s[...] = dot(slot_low, cot_ref[...])
    sel_up[...] = up_s[...].astype(bf16)
    for j in range(shards):
        first = pl.multiple_of((shard ^ j) * SLOT, SLOT)
        pieces[j][...] = up_s[pl.ds(first, SLOT), :].astype(bf16)
    mine = pl.ds(pl.multiple_of(head * part, part), part)
    place_c[...] = place_s[mine, :].astype(bf16)
    x_c[...] = x_ref[mine, :]
    cot_c[...] = cot_ref[mine, :]


def attend_kernel(
    x_ref, gain_ref, wq_ref, wk_ref, wv_ref, table_ref, buckets_ref, ids_ref, slots_ref,
    low_ref, k_ref, qt_ref, vt_ref, prob_ref, att_ref, attt_ref, sel_ref, gcat_ref,
    q_s, kt_s, v_s, bias_s, skew_s, low_att,
):
    step = pl.program_id(0)
    heads = pl.num_programs(0)
    tokens = x_ref.shape[0]
    inner = wq_ref.shape[1]
    count = q_s.shape[0]
    width = inner // count

    @pl.when(step == 0)
    def _():
        for i in range(0, tokens, 256):
            rows = pl.ds(i, 256)
            x = x_ref[rows, :].astype(f32)
            inverse = lax.rsqrt(jnp.mean(x * x, axis=-1, keepdims=True) + EPS)
            low_ref[rows, :] = (x * inverse * gain_ref[...]).astype(bf16)
            low = low_ref[rows, :]
            q = dot(low, wq_ref[...]).astype(bf16).astype(f32) * (width ** (-0.5))
            k = dot(low, wk_ref[...])
            v = dot(low, wv_ref[...])
            qt_ref[:, rows] = jnp.transpose(q).astype(bf16)
            kt = jnp.transpose(k).astype(bf16)
            vt_ref[:, rows] = jnp.transpose(v).astype(bf16)
            for h in range(count):
                cols = slice(h * width, (h + 1) * width)
                q_s[h, rows, :] = q[:, cols].astype(bf16)
                k_ref[h, rows, :] = k[:, cols].astype(bf16)
                kt_s[h, :, rows] = kt[cols, :]
                v_s[h, rows, :] = v[:, cols].astype(bf16)
        offsets = buckets_ref.shape[1]
        bucket_hot = (iota((table_ref.shape[0], offsets), 0) == buckets_ref[...]).astype(f32)
        bias_s[...] = jnp.zeros_like(bias_s)
        bias_s[:count, :offsets] = dot_tn(table_ref[...], bucket_hot, highest)
        gcat_ref[0:inner, :] = jnp.transpose(wq_ref[...].astype(f32)).astype(bf16)
        gcat_ref[inner : 2 * inner, :] = jnp.transpose(wk_ref[...].astype(f32)).astype(bf16)
        gcat_ref[2 * inner :, :] = jnp.transpose(wv_ref[...].astype(f32)).astype(bf16)

    span = skew_s.shape[1]
    row = bias_s[pl.ds(step, 1), :]
    skew_s[...] = pltpu.roll(
        jnp.broadcast_to(row, skew_s.shape), span - (BLOCK - 1), 1, stride=1, stride_axis=0
    )
    for i in range(0, tokens, BLOCK):
        rows = pl.ds(i, BLOCK)
        first = tokens - BLOCK - i
        score = dot(q_s[step, rows, :], kt_s[step]) + skew_s[:, first : first + tokens]
        top = jnp.max(score, axis=-1, keepdims=True)
        weight = jnp.exp(score - top)
        total = jnp.sum(weight, axis=-1, keepdims=True)
        prob = (weight * (1.0 / total)).astype(bf16)
        prob_ref[0, rows, :] = prob
        att = dot(prob, v_s[step])
        att_ref[0, rows, :] = att
        low_att[step, rows, :] = att.astype(bf16)
        attt_ref[pl.ds(pl.multiple_of(step * width, width), width), rows] = jnp.transpose(
            att
        ).astype(bf16)

    @pl.when(step == heads - 1)
    def _():
        slot_low = slot_rows(ids_ref[...], slots_ref[...], 2 * sel_ref.shape[0]).astype(bf16)
        half = sel_ref.shape[0]
        for h in range(count):
            picked = dot(slot_low, low_att[h])
            for part in range(2):
                start = part * inner + h * width
                sel_ref[:, start : start + width] = picked[
                    part * half : (part + 1) * half
                ].astype(bf16)


def route_kernel(where_ref, *refs, shards, heads):
    att_parts = refs[:heads]
    w_parts = refs[heads : 2 * heads]
    sel_in, gain_ref, router_ref, hidden_ref, normed_ref, probs_ref = refs[2 * heads : 2 * heads + 6]
    pieces = refs[2 * heads + 6 : 2 * heads + 6 + shards]
    att_s, w_s, pay_s = refs[2 * heads + 6 + shards :]
    head, shard = where_ref[0], where_ref[1]
    inner = w_parts[0].shape[0]
    half = att_parts[0].shape[0]
    width = sel_in.shape[1]
    for d in range(heads):
        att_s[d, 0:half, :] = att_parts[d][:, 0:inner]
        att_s[d, half : 2 * half, :] = att_parts[d][:, inner : 2 * inner]
        w_s[d] = w_parts[d][...]
    mixed = None
    for k in range(heads):
        term = dot(att_s[head ^ k], w_s[head ^ k])
        mixed = term if mixed is None else mixed + term
    hidden = sel_in[...].astype(f32) + mixed
    hidden_ref[...] = hidden
    inverse = lax.rsqrt(jnp.mean(hidden * hidden, axis=-1, keepdims=True) + EPS)
    normed = hidden * inverse * gain_ref[...]
    normed_ref[...] = normed
    logits = jnp.dot(normed, router_ref[...], precision=highest, preferred_element_type=f32)
    logits = logits - jnp.max(logits, axis=-1, keepdims=True)
    powers = jnp.exp(logits)
    probs = powers / jnp.sum(powers, axis=-1, keepdims=True)
    probs_ref[...] = probs
    gate = jnp.sum(jnp.where(chosen_of(probs.shape), probs, 0.0), axis=-1, keepdims=True)
    high = gate.astype(bf16).astype(f32)
    lane = iota((gate.shape[0], 128), 1)
    pay_s[:, :width] = normed
    pay_s[:, width:] = jnp.where(lane == 0, high, jnp.where(lane == 1, gate - high, 0.0))
    for j in range(shards):
        first = pl.multiple_of((shard ^ j) * SLOT, SLOT)
        pieces[j][...] = pay_s[pl.ds(first, SLOT), :].astype(bf16)


def chosen_of(shape):
    expert = iota(shape, 1) * SLOT
    slot_row = iota(shape, 0)
    return (slot_row >= expert) & (slot_row < expert + SLOT)


def upstream_kernel(*refs, shards):
    parts = refs[:shards]
    w_out, up_ref, grad_ref, up_s = refs[shards:]
    for j in range(shards):
        up_s[j * SLOT : (j + 1) * SLOT, :] = parts[j][...].astype(f32)
    up_ref[...] = up_s[...].astype(bf16)
    grad_ref[...] = dot_nt(up_ref[...], w_out[...])


def expert_kernel(where_ref, *refs, shards, heads):
    parts = refs[:shards]
    up_ref, grad_ref, w_in, w_out, base_ref = refs[shards : shards + 5]
    chunks = refs[shards + 5 : shards + 5 + heads]
    xt_ref, act_t_ref, pre_ref, out_ref = refs[shards + 5 + heads : shards + 9 + heads]
    pay_s, both_s = refs[shards + 9 + heads :]
    head = where_ref[0]
    width = w_in.shape[0]
    for j in range(shards):
        pay_s[j * SLOT : (j + 1) * SLOT, :] = parts[j][...].astype(f32)
    rows = pay_s.shape[0]
    x = pay_s[:, :width]
    gate = pay_s[:, width : width + 1] + pay_s[:, width + 1 : width + 2]
    pre = dot(x.astype(bf16), w_in[...])
    cdf = 0.5 * (1.0 + lax.erf(pre * (0.5**0.5)))
    act = pre * cdf
    slope = cdf + pre * jnp.exp(-0.5 * pre * pre) * ((2.0 * np.pi) ** (-0.5))
    both_s[0:rows, :] = dot(act.astype(bf16), w_out[...]).astype(bf16)
    pre_low = (gate * grad_ref[...] * slope).astype(bf16)
    both_s[rows : 2 * rows, :] = dot_nt(pre_low, w_in[...]).astype(bf16)
    pre_ref[...] = pre_low
    out_ref[...] = (gate * up_ref[...].astype(f32)).astype(bf16)
    xt_ref[...] = jnp.transpose(x).astype(bf16)
    act_t_ref[...] = jnp.transpose(act).astype(bf16)
    quarter = CAP // heads
    base = base_ref[...]
    lanes = iota((base.shape[0], 2 * rows), 1)
    for d in range(heads):
        hot = (lanes == base + quarter * (head ^ d)).astype(f32).astype(bf16)
        chunks[d][...] = dot(hot, both_s[...]).astype(bf16)


def expert_grad_kernel(xt_ref, pre_ref, act_t_ref, out_ref, in_grad, out_grad):
    in_grad[0] = dot(xt_ref[...], pre_ref[...])
    out_grad[0] = dot(act_t_ref[...], out_ref[...])


def sum_kernel(*refs, shards, heads):
    parts = refs[:heads]
    pieces = refs[heads : heads + shards]
    sum_s = refs[heads + shards]
    total = parts[0][...].astype(f32)
    for d in range(1, heads):
        total = total + parts[d][...].astype(f32)
    sum_s[...] = total
    rows = pieces[0].shape[0]
    for j in range(shards):
        pieces[j][...] = sum_s[j * rows : (j + 1) * rows, :].astype(bf16)


def join_kernel(*refs, shards):
    parts = refs[:shards]
    out_ref, sum_s = refs[shards:]
    rows = parts[0].shape[0]
    for j in range(shards):
        sum_s[j * rows : (j + 1) * rows, :] = parts[j][...].astype(f32)
    out_ref[...] = sum_s[...].astype(bf16)


def masked_back_kernel(
    cot_ref, w_ref, place_ref, att_ref, prob_ref, k_ref, qt_ref, vt_ref, attt_ref,
    dq_ref, dkt_ref, dvt_ref, offs_ref, wout_ref, psel_ref, qsel_ref,
    gh_s, ght_s, mcot_s, acc_s,
):
    step = pl.program_id(0)
    count, tokens, width = gh_s.shape

    @pl.when(step == 0)
    def _():
        for i in range(0, tokens, 256):
            rows = pl.ds(i, 256)
            free = 1.0 - jnp.sum(place_ref[rows, :].astype(f32), axis=-1, keepdims=True)
            mcot_s[rows, :] = (cot_ref[rows, :].astype(f32) * free).astype(bf16)
            grad = dot_nt(mcot_s[rows, :], w_ref[...])
            ght_s[:, rows] = jnp.transpose(grad).astype(bf16)
            for h in range(count):
                gh_s[h, rows, :] = grad[:, h * width : (h + 1) * width].astype(bf16)
        wout_ref[...] = dot(attt_ref[...], mcot_s[...])
        qsel_ref[...] = dot(qt_ref[...], place_ref[...]).astype(bf16)

    acc_s[...] = jnp.zeros_like(acc_s)
    head_rows = pl.ds(pl.multiple_of(step * width, width), width)
    for i in range(0, tokens, BLOCK):
        rows = pl.ds(i, BLOCK)
        first = tokens - BLOCK - i
        gh = gh_s[step, rows, :]
        delta = jnp.sum(gh.astype(f32) * att_ref[0, rows, :], axis=-1, keepdims=True)
        grad = dot(gh, vt_ref[head_rows, :])
        prob = prob_ref[0, rows, :]
        score = (prob.astype(f32) * (grad - delta)).astype(bf16)
        acc_s[:, first : first + tokens] += score.astype(f32)
        dq_ref[0, rows, :] = dot(score, k_ref[0]) * (width ** (-0.5))
        dk = dot(qt_ref[head_rows, rows], score)
        dv = dot(ght_s[head_rows, rows], prob)
        if i == 0:
            dkt_ref[...] = dk
            dvt_ref[...] = dv
        else:
            dkt_ref[...] += dk
            dvt_ref[...] += dv
    offs_ref[0] = diagonals(acc_s[...])
    psel_ref[0] = lax.dot_general(
        place_ref[...], prob_ref[0], (((0,), (0,)), ((), ())), preferred_element_type=f32
    ).astype(bf16)


def diagonals(acc):
    span = acc.shape[1]
    rows = acc.shape[0] // 2
    while rows >= 8:
        acc = acc[:rows] + pltpu.roll(acc[rows:], span - rows, 1)
        rows //= 2
    total = acc[0:1]
    for r in range(1, 8):
        total = total + pltpu.roll(acc[r : r + 1], span - r, 1)
    return jnp.broadcast_to(pltpu.roll(total, BLOCK - 1, 1), (8, span))


def slot_back_kernel(where_ref, *refs, heads):
    parts = refs[:heads]
    (tags_ref, up_ref, normed_ref, hidden_ref, probs_ref, router_ref, gain_ref, w_ref, att_ref,
     wout0_ref) = refs[heads : heads + 10]
    dv_ref, comb_ref, small_ref, wout_ref, gh_ref, ght_ref, delta_ref = refs[heads + 10 : heads + 17]
    head, shard = where_ref[0], where_ref[1]
    rows, width = up_ref.shape
    chunk = parts[0].shape[0]
    quarter = CAP // heads
    tags = tags_ref[...]
    peer, slot, is_grad = tags[0:1], tags[1:2], tags[2:3]
    base = (peer ^ shard) * SLOT + slot
    slot_row = iota((rows, chunk), 0)
    combined = jnp.zeros((rows, width), f32)
    grad_buf = jnp.zeros((rows, width), f32)
    for d in range(heads):
        here = slot_row == base + quarter * (head ^ d)
        part = parts[d][...]
        combined = combined + dot((here & (is_grad == 0)).astype(f32).astype(bf16), part)
        grad_buf = grad_buf + dot((here & (is_grad == 1)).astype(f32).astype(bf16), part)
    up = up_ref[...].astype(f32)
    hidden, normed, probs, gain = hidden_ref[...], normed_ref[...], probs_ref[...], gain_ref[...]
    chosen = chosen_of(probs.shape)
    gate = jnp.sum(jnp.where(chosen, probs, 0.0), axis=-1, keepdims=True)
    comb_ref[...] = gate * combined
    gate_grad = jnp.sum(up * combined, axis=-1, keepdims=True)
    marked = jnp.where(chosen, gate_grad, 0.0)
    logit_grad = probs * (marked - jnp.sum(marked * probs, axis=-1, keepdims=True))
    experts = probs.shape[1]
    grad = grad_buf + dot_nt(logit_grad, router_ref[...], highest)
    inverse = lax.rsqrt(jnp.mean(hidden * hidden, axis=-1, keepdims=True) + EPS)
    scaled = grad * gain
    inner_sum = jnp.mean(scaled * hidden, axis=-1, keepdims=True)
    dv = inverse * scaled - hidden * (inverse * inverse * inverse * inner_sum)
    dv_ref[...] = dv
    small_ref[...] = jnp.zeros_like(small_ref)
    small_ref[0:1, :] = jnp.sum(grad * hidden * inverse, axis=0, keepdims=True)
    small_ref[8 : 8 + experts, :] = dot_tn(logit_grad, normed, highest)
    grad_low = (up + dv).astype(bf16)
    half = att_ref.shape[0]
    inner = w_ref.shape[0]
    att = jnp.concatenate(
        [att_ref[:, 0:inner].astype(f32), att_ref[:, inner : 2 * inner].astype(f32)], axis=0
    )
    wout_ref[...] = wout0_ref[...] + dot(jnp.transpose(att).astype(bf16), grad_low)
    gh = dot_nt(grad_low, w_ref[...])
    gh_low = gh.astype(bf16)
    count = gh_ref.shape[0]
    each = inner // count
    ght_ref[...] = jnp.transpose(gh).astype(bf16)
    for h in range(count):
        cols = slice(h * each, (h + 1) * each)
        gh_ref[h] = gh_low[:, cols]
        delta_ref[h] = jnp.sum(
            gh_low[:, cols].astype(f32) * att[:, cols], axis=-1, keepdims=True
        )


def sparse_back_kernel(
    where_ref, gh_ref, ght_ref, delta_ref, vt_ref, k_ref, qsel_ref, psel_ref, dq0_ref, dkt0_ref,
    dvt0_ref, place_ref, wcat_ref, *refs, heads,
):
    chunks = refs[:heads]
    gt_ref, score_ref = refs[heads : heads + 2]
    g_s, gt_s, dq_s, g_low = refs[heads + 2 :]
    head = where_ref[0]
    count, rows, width = gh_ref.shape
    tokens = vt_ref.shape[1]
    inner = count * width
    for h in range(count):
        cols = slice(h * width, (h + 1) * width)
        grad = dot(gh_ref[h], vt_ref[cols, :])
        prob = psel_ref[h]
        score = (prob.astype(f32) * (grad - delta_ref[h])).astype(bf16)
        score_ref[h] = score
        dq_s[:, cols] = dot(score, k_ref[h]) * (width ** (-0.5))
        gt_s[inner + h * width : inner + (h + 1) * width, :] = dkt0_ref[cols, :] + dot(
            qsel_ref[cols, :], score
        )
        gt_s[2 * inner + h * width : 2 * inner + (h + 1) * width, :] = dvt0_ref[cols, :] + dot(
            ght_ref[cols, :], prob
        )
    spread = dot(place_ref[...], dq_s[...].astype(bf16))
    for h in range(count):
        cols = slice(h * width, (h + 1) * width)
        g_s[:, cols] = spread[:, cols] + dq0_ref[h]
    gt_s[0:inner, :] = jnp.transpose(g_s[...])
    gt_ref[...] = gt_s[...].astype(bf16)
    g_low[...] = jnp.transpose(gt_s[...]).astype(bf16)
    part = tokens // heads
    for d in list(range(1, heads)) + [0]:
        mine = pl.ds(pl.multiple_of((head ^ d) * part, part), part)
        chunks[d][...] = dot(g_low[mine, :], wcat_ref[...]).astype(bf16)


def weight_grad_kernel(gt_ref, low_ref, out_ref):
    out_ref[...] = dot(gt_ref[...], low_ref[...])


def bias_grad_kernel(score_ref, place_ref, offs_ref, buckets_ref, out_ref, acc_s):
    count = score_ref.shape[0]
    tokens = place_ref.shape[0]
    offsets = buckets_ref.shape[1]
    bucket_count = out_ref.shape[1]
    bucket_hot = (iota((bucket_count, offsets), 0) == buckets_ref[...]).astype(f32)
    for h in range(count):
        acc_s[...] = jnp.zeros_like(acc_s)
        for i in range(0, tokens, BLOCK):
            first = tokens - BLOCK - i
            acc_s[:, first : first + tokens] += dot(place_ref[i : i + BLOCK, :], score_ref[h])
        sums = diagonals(acc_s[...]) + offs_ref[h]
        out_ref[h : h + 1, :] = dot_nt(sums[:, :offsets], bucket_hot, highest)[0:1]


def output_kernel(where_ref, *refs, heads):
    att_parts = refs[:heads]
    w_parts = refs[heads : 2 * heads]
    x_ref, place_ref, comb_ref, out_ref, att_s, w_s = refs[2 * heads :]
    head = where_ref[0]
    tokens = x_ref.shape[0]
    for d in range(heads):
        att_s[d] = jnp.transpose(att_parts[d][...].astype(f32)).astype(bf16)
        w_s[d] = w_parts[d][...]
    high, rest = split_two(comb_ref[...])
    for i in range(0, tokens, 256):
        rows = pl.ds(i, 256)
        mixed = None
        for k in range(heads):
            term = dot(att_s[head ^ k, rows, :], w_s[head ^ k])
            mixed = term if mixed is None else mixed + term
        hidden = x_ref[rows, :].astype(f32) + mixed
        where = place_ref[rows, :]
        out_ref[rows, :] = hidden + (dot(where, high) + dot(where, rest))


def first_norm_kernel(*refs, heads):
    parts = refs[:heads]
    x_ref, cot_ref, place_ref, dv_ref, gain_ref, out_ref, small_ref = refs[heads:]
    grad = parts[0][...].astype(f32)
    for d in range(1, heads):
        grad = grad + parts[d][...].astype(f32)
    x = x_ref[...].astype(f32)
    inverse = lax.rsqrt(jnp.mean(x * x, axis=-1, keepdims=True) + EPS)
    scaled = grad * gain_ref[...]
    inner_sum = jnp.mean(scaled * x, axis=-1, keepdims=True)
    high, rest = split_two(dv_ref[...])
    hidden_grad = cot_ref[...].astype(f32) + (dot(place_ref[...], high) + dot(place_ref[...], rest))
    out_ref[...] = (
        hidden_grad + inverse * scaled - x * (inverse * inverse * inverse * inner_sum)
    ).astype(bf16)
    small_ref[...] = jnp.broadcast_to(
        jnp.sum(grad * x * inverse, axis=0, keepdims=True), small_ref.shape
    )


def spread_kernel(where_ref, *refs, heads):
    parts = refs[:heads]
    out_ref = refs[heads]
    head = where_ref[0]
    part = parts[0].shape[0]
    for d in range(heads):
        mine = pl.ds(pl.multiple_of((head ^ d) * part, part), part)
        out_ref[mine, :] = parts[d][...].astype(f32)


def swap(x, axis, d):
    size = lax.axis_size(axis)
    return lax.ppermute(x, axis, [(i, i ^ d) for i in range(size)])


def share(x, axis):
    return [x] + [swap(x, axis, d) for d in range(1, lax.axis_size(axis))]


def trade(pieces, axis):
    return [pieces[0]] + [swap(pieces[d], axis, d) for d in range(1, len(pieces))]


def sum_over(x, axis):
    size = lax.axis_size(axis)
    me = lax.axis_index(axis)
    bits = [b for b in (1 << i for i in range(16)) if b < size]
    now = x
    for b in bits:
        half = now.shape[0] // 2
        upper = (me & b) != 0
        low, high = now[:half], now[half:]
        sent = jnp.where(upper, low, high).astype(bf16)
        kept = jnp.where(upper, high, low).astype(f32)
        now = kept + swap(sent, axis, b).astype(f32)
    now = now.astype(bf16)
    for b in reversed(bits):
        upper = (me & b) != 0
        other = swap(now, axis, b)
        now = jnp.where(
            upper, jnp.concatenate([other, now], axis=0), jnp.concatenate([now, other], axis=0)
        )
    return now.astype(f32)


def sum_small(x, axes):
    for axis in axes:
        d = 1
        while d < lax.axis_size(axis):
            x = x + swap(x, axis, d)
            d *= 2
    return x


def on_device(
    layer_input, cotangent, norm1_gain, w_query, w_key, w_value, w_attn_out, bias_table,
    norm2_gain, w_router, w_expert_in, w_expert_out, expert_ids, slot_ids, buckets,
):
    tokens, width = layer_input.shape
    shards = lax.axis_size("seq")
    heads = lax.axis_size("head")
    bucket_count, count = bias_table.shape
    inner = w_query.shape[1]
    each = inner // count
    experts = w_router.shape[1]
    rows = experts * SLOT
    hidden_units = w_expert_in.shape[2]
    part = tokens // heads
    chunk = 2 * CAP // heads * shards
    piece_rows = chunk // shards
    span = 2 * tokens

    where = jnp.stack([lax.axis_index("head"), lax.axis_index("seq")]).astype(jnp.int32)
    ids = expert_ids.reshape(1, tokens)
    slots = slot_ids.reshape(1, tokens)
    bucket_row = buckets.reshape(1, -1)
    gain1 = norm1_gain.reshape(1, width)
    gain2 = norm2_gain.reshape(1, width)
    w_in = w_expert_in.reshape(width, hidden_units)
    w_out = w_expert_out.reshape(hidden_units, width)

    quarter = CAP // heads
    place_in = np.arange(chunk)
    peer, turn = place_in // piece_rows, place_in % piece_rows
    is_grad = (turn >= quarter).astype(np.int32)
    base = (is_grad * rows + peer * SLOT + turn % quarter).astype(np.int32).reshape(chunk, 1)
    tags = np.zeros((8, chunk), np.int32)
    tags[0], tags[1], tags[2] = peer, turn % quarter, is_grad

    w_mix = share(w_attn_out, "head")

    picked = call(
        partial(select_kernel, shards=shards, heads=heads),
        [shape_of(rows, width, bf16)] * 2
        + [shape_of(tokens, rows, bf16), shape_of(part, rows, bf16)]
        + [shape_of(part, width, bf16)] * 2
        + [shape_of(SLOT, width, bf16)] * shards,
        (where, layer_input, cotangent, ids, slots),
        scratch=[pltpu.VMEM((rows, width), f32), pltpu.VMEM((tokens, rows), f32)],
        name="select",
        flops=4 * rows * tokens * width,
        smem=(0,),
    )
    sel_in, sel_up, place, place_c, x_c, cot_c = picked[:6]
    up_parts = trade(list(picked[6:]), "seq")

    whole = lambda shape: pl.BlockSpec(shape, lambda h: (0,) * len(shape))
    by_head = lambda shape: pl.BlockSpec(shape, lambda h: (h,) + (0,) * (len(shape) - 1))
    low, k_rows, q_t, v_t, prob, att, att_t, att_sel, w_cat = pl.pallas_call(
        attend_kernel,
        grid=(count,),
        out_shape=(
            shape_of(tokens, width, bf16),
            jax.ShapeDtypeStruct((count, tokens, each), bf16),
            shape_of(inner, tokens, bf16),
            shape_of(inner, tokens, bf16),
            jax.ShapeDtypeStruct((count, tokens, tokens), bf16),
            jax.ShapeDtypeStruct((count, tokens, each), f32),
            shape_of(inner, tokens, bf16),
            shape_of(rows // 2, 2 * inner, bf16),
            shape_of(3 * inner, width, bf16),
        ),
        in_specs=[
            whole((tokens, width)), whole((1, width)), whole((width, inner)),
            whole((width, inner)), whole((width, inner)), whole((bucket_count, count)),
            whole((1, span - 1)), whole((1, tokens)), whole((1, tokens)),
        ],
        out_specs=(
            whole((tokens, width)), whole((count, tokens, each)), whole((inner, tokens)),
            whole((inner, tokens)), by_head((1, tokens, tokens)), by_head((1, tokens, each)),
            whole((inner, tokens)), whole((rows // 2, 2 * inner)), whole((3 * inner, width)),
        ),
        scratch_shapes=[
            pltpu.VMEM((count, tokens, each), bf16),
            pltpu.VMEM((count, each, tokens), bf16),
            pltpu.VMEM((count, tokens, each), bf16),
            pltpu.VMEM((8, span), f32),
            pltpu.VMEM((BLOCK, span), f32),
            pltpu.VMEM((count, tokens, each), bf16),
        ],
        compiler_params=pltpu.CompilerParams(vmem_limit_bytes=50 * MIB),
        cost_estimate=pl.CostEstimate(
            flops=2 * tokens * width * inner * 3 + 4 * count * tokens * tokens * each,
            bytes_accessed=14 * MIB,
            transcendentals=count * tokens * tokens,
        ),
        name="attend",
    )(layer_input, gain1, w_query, w_key, w_value, bias_table, bucket_row, ids, slots)

    sel_parts = share(att_sel, "head")
    routed = call(
        partial(route_kernel, shards=shards, heads=heads),
        [shape_of(rows, width, f32)] * 2
        + [shape_of(rows, experts, f32)]
        + [shape_of(SLOT, width + 128, bf16)] * shards,
        (where,) + tuple(sel_parts) + tuple(w_mix) + (sel_in, gain2, w_router),
        scratch=[
            pltpu.VMEM((heads, rows, inner), bf16),
            pltpu.VMEM((heads, inner, width), bf16),
            pltpu.VMEM((rows, width + 128), f32),
        ],
        name="route",
        flops=2 * rows * width * width,
        smem=(0,),
    )
    hidden_sel, normed_sel, probs = routed[:3]
    pay_parts = trade(list(routed[3:]), "seq")

    att_t_later, _ = lax.optimization_barrier((att_t, tuple(sel_parts)))
    att_parts = share(att_t_later, "head")

    up_rows, up_grad = call(
        partial(upstream_kernel, shards=shards),
        [shape_of(rows, width, bf16), shape_of(rows, hidden_units, f32)],
        tuple(up_parts) + (w_out,),
        scratch=[pltpu.VMEM((rows, width), f32)],
        name="upstream",
        flops=2 * rows * width * hidden_units,
    )

    dq0, dk0, dv0, offs, wout0, prob_sel, q_sel = pl.pallas_call(
        masked_back_kernel,
        grid=(count,),
        out_shape=(
            jax.ShapeDtypeStruct((count, tokens, each), f32),
            shape_of(inner, tokens, f32),
            shape_of(inner, tokens, f32),
            jax.ShapeDtypeStruct((count, 8, span), f32),
            shape_of(inner, width, f32),
            jax.ShapeDtypeStruct((count, rows, tokens), bf16),
            shape_of(inner, rows, bf16),
        ),
        in_specs=[
            whole((tokens, width)), whole((inner, width)), whole((tokens, rows)),
            by_head((1, tokens, each)), by_head((1, tokens, tokens)), by_head((1, tokens, each)),
            whole((inner, tokens)), whole((inner, tokens)), whole((inner, tokens)),
        ],
        out_specs=(
            by_head((1, tokens, each)), by_head((each, tokens)), by_head((each, tokens)),
            by_head((1, 8, span)), whole((inner, width)), by_head((1, rows, tokens)),
            whole((inner, rows)),
        ),
        scratch_shapes=[
            pltpu.VMEM((count, tokens, each), bf16),
            pltpu.VMEM((inner, tokens), bf16),
            pltpu.VMEM((tokens, width), bf16),
            pltpu.VMEM((BLOCK, span), f32),
        ],
        compiler_params=pltpu.CompilerParams(vmem_limit_bytes=50 * MIB),
        cost_estimate=pl.CostEstimate(
            flops=2 * tokens * width * inner * 2 + 8 * count * tokens * tokens * each,
            bytes_accessed=16 * MIB,
            transcendentals=count * tokens * tokens,
        ),
        name="masked_back",
    )(cotangent, w_attn_out, place, att, prob, k_rows, q_t, v_t, att_t)

    done = call(
        partial(expert_kernel, shards=shards, heads=heads),
        [shape_of(chunk, width, bf16)] * heads
        + [
            shape_of(width, rows, bf16),
            shape_of(hidden_units, rows, bf16),
            shape_of(rows, hidden_units, bf16),
            shape_of(rows, width, bf16),
        ],
        (where,) + tuple(pay_parts) + (up_rows, up_grad, w_in, w_out, jnp.asarray(base)),
        scratch=[pltpu.VMEM((rows, width + 128), f32), pltpu.VMEM((2 * rows, width), bf16)],
        name="expert",
        flops=6 * rows * width * hidden_units,
        smem=(0,),
    )
    x_t, act_t, pre_low, out_low = done[heads:]
    summed_parts = trade(list(done[:heads]), "head")
    returned = call(
        partial(sum_kernel, shards=shards, heads=heads),
        [shape_of(piece_rows, width, bf16)] * shards,
        tuple(summed_parts),
        scratch=[pltpu.VMEM((chunk, width), f32)],
        name="sum",
    )
    back_parts = trade(list(returned), "seq")
    (joined,) = call(
        partial(join_kernel, shards=shards),
        [shape_of(chunk, width, bf16)],
        tuple(back_parts),
        scratch=[pltpu.VMEM((chunk, width), f32)],
        name="join",
    )
    full_parts = share(joined, "head")

    w_in_grad, w_out_grad = call(
        expert_grad_kernel,
        [
            jax.ShapeDtypeStruct(w_expert_in.shape, f32),
            jax.ShapeDtypeStruct(w_expert_out.shape, f32),
        ],
        (x_t, pre_low, act_t, out_low),
        name="expert_grad",
        flops=4 * rows * width * hidden_units,
    )

    small_rows = 8 + -(-experts // 8) * 8
    dv_sel, comb_sel, small, wout_part, gh_sel, ght_sel, delta_sel = call(
        partial(slot_back_kernel, heads=heads),
        [
            shape_of(rows, width, f32),
            shape_of(rows, width, f32),
            shape_of(small_rows, width, f32),
            shape_of(inner, width, f32),
            jax.ShapeDtypeStruct((count, rows, each), bf16),
            shape_of(inner, rows, bf16),
            jax.ShapeDtypeStruct((count, rows, 1), f32),
        ],
        (where,)
        + tuple(full_parts)
        + (jnp.asarray(tags), sel_up, normed_sel, hidden_sel, probs, w_router, gain2, w_attn_out)
        + (att_sel, wout0),
        name="slot_back",
        flops=4 * rows * width * inner,
        smem=(0,),
    )

    back = call(
        partial(sparse_back_kernel, heads=heads),
        [shape_of(part, width, bf16)] * heads
        + [
            shape_of(3 * inner, tokens, bf16),
            jax.ShapeDtypeStruct((count, rows, tokens), bf16),
        ],
        (where, gh_sel, ght_sel, delta_sel, v_t, k_rows, q_sel, prob_sel, dq0, dk0, dv0, place)
        + (w_cat,),
        scratch=[
            pltpu.VMEM((tokens, inner), f32),
            pltpu.VMEM((3 * inner, tokens), f32),
            pltpu.VMEM((rows, inner), f32),
            pltpu.VMEM((tokens, 3 * inner), bf16),
        ],
        name="sparse_back",
        flops=8 * rows * tokens * inner + 6 * tokens * inner * width,
        smem=(0,),
        vmem=50,
    )
    g_t, score_sel = back[heads:]
    first_parts = trade(list(back[:heads]), "head")

    (qkv_grad,) = call(
        weight_grad_kernel,
        [shape_of(3 * inner, width, f32)],
        (g_t, low),
        name="weight_grad",
        flops=6 * tokens * inner * width,
    )
    wout_grad = sum_over(wout_part, "seq")
    qkv_sum = sum_over(qkv_grad, "seq")

    (table_part,) = call(
        bias_grad_kernel,
        [shape_of(8, bucket_count, f32)],
        (score_sel, place, offs, bucket_row),
        scratch=[pltpu.VMEM((BLOCK, span), f32)],
        name="bias_grad",
        flops=2 * count * rows * tokens * tokens,
    )
    small_sum = sum_small(small, ("seq",))
    table_sum = sum_small(table_part, ("seq",))

    (layer_output,) = call(
        partial(output_kernel, heads=heads),
        [shape_of(tokens, width, f32)],
        (where,) + tuple(att_parts) + tuple(w_mix) + (layer_input, place, comb_sel),
        scratch=[
            pltpu.VMEM((heads, tokens, inner), bf16),
            pltpu.VMEM((heads, inner, width), bf16),
        ],
        name="output",
        flops=2 * tokens * width * width,
        smem=(0,),
    )

    grad_part, gain1_part = call(
        partial(first_norm_kernel, heads=heads),
        [shape_of(part, width, bf16), shape_of(8, width, f32)],
        tuple(first_parts) + (x_c, cot_c, place_c, dv_sel, gain1),
        name="first_norm",
        flops=4 * part * rows * width,
    )
    grad_parts = share(grad_part, "head")
    gain1_sum = sum_small(gain1_part, ("head", "seq"))
    (input_grad,) = call(
        partial(spread_kernel, heads=heads),
        [shape_of(tokens, width, f32)],
        (where,) + tuple(grad_parts),
        name="spread",
        smem=(0,),
    )

    return (
        layer_output,
        input_grad,
        gain1_sum[0],
        jnp.transpose(qkv_sum[:inner]),
        jnp.transpose(qkv_sum[inner : 2 * inner]),
        jnp.transpose(qkv_sum[2 * inner :]),
        wout_grad,
        jnp.transpose(table_sum[:count]),
        small_sum[0],
        jnp.transpose(small_sum[8 : 8 + experts]),
        w_in_grad,
        w_out_grad,
    )


def solution(mesh):
    return jax.shard_map(
        on_device,
        mesh=mesh,
        in_specs=(
            P("seq", None),
            P("seq", None),
            P(),
            P(None, "head"),
            P(None, "head"),
            P(None, "head"),
            P("head", None),
            P(None, "head"),
            P(),
            P(),
            P("seq", None, "head"),
            P("seq", "head", None),
            P("seq"),
            P("seq"),
            P(),
        ),
        out_specs=(
            P("seq", None),
            P("seq", None),
            P(),
            P(None, "head"),
            P(None, "head"),
            P(None, "head"),
            P("head", None),
            P(None, "head"),
            P(),
            P(),
            P("seq", None, "head"),
            P("seq", "head", None),
        ),
        check_vma=False,
    )
```

```python
from functools import partial

import jax
import jax.numpy as jnp
import numpy as np
from jax import lax
from jax.experimental import pallas as pl
from jax.experimental.pallas import tpu as pltpu
from jax.sharding import PartitionSpec as P

CAP = 20
SLOT = 24
EPS = 1e-06
BLOCK = 128
VMEM_LIMIT = 64 * 1024 * 1024

f32 = jnp.float32
bf16 = jnp.bfloat16
highest = lax.Precision.HIGHEST


def dot(a, b):
    return jnp.dot(a, b, preferred_element_type=f32)


def dot_nt(a, b, precision=None):
    return lax.dot_general(
        a, b, (((1,), (1,)), ((), ())), precision=precision, preferred_element_type=f32
    )


def dot_tn(a, b, precision=None):
    return lax.dot_general(
        a, b, (((0,), (0,)), ((), ())), precision=precision, preferred_element_type=f32
    )


def iota(shape, dim):
    return lax.broadcasted_iota(jnp.int32, shape, dim)


def split_two(v):
    high = v.astype(bf16)
    return high, (v - high.astype(f32)).astype(bf16)


def shape_of(rows, cols, dtype):
    return jax.ShapeDtypeStruct((rows, cols), dtype)


def spec(memory):
    return pl.BlockSpec(memory_space=memory)


def call(kernel, outs, args, scratch=(), name=None, flops=0, after=()):
    outs, args = tuple(outs), tuple(args)
    moved = sum(int(np.prod(a.shape)) * a.dtype.itemsize for a in args + outs)

    def body(*refs):
        kernel(*refs[: len(args)], *refs[len(args) + len(after) :])

    return pl.pallas_call(
        body,
        out_shape=outs,
        in_specs=[spec(pltpu.VMEM)] * len(args) + [spec(pl.ANY)] * len(after),
        out_specs=tuple(spec(pltpu.VMEM) for _ in outs),
        scratch_shapes=list(scratch),
        compiler_params=pltpu.CompilerParams(vmem_limit_bytes=VMEM_LIMIT),
        cost_estimate=pl.CostEstimate(flops=flops, bytes_accessed=moved, transcendentals=0),
        name=name,
    )(*args, *after)


def whole(shape):
    return pl.BlockSpec(shape, lambda h: (0,) * len(shape))


def by_head(shape):
    return pl.BlockSpec(shape, lambda h: (h,) + (0,) * (len(shape) - 1))


def slot_rows(ids, slots, rows):
    cell = jnp.where(slots < CAP, ids * SLOT + slots, -1)
    return (iota((rows, cell.shape[1]), 0) == cell).astype(f32)


def select_kernel(cot_ref, ids_ref, slots_ref, sel_up, pieces, place_t):
    slot_hot = slot_rows(ids_ref[...], slots_ref[...], sel_up.shape[0]).astype(bf16)
    place_t[...] = slot_hot
    up = dot(slot_hot, cot_ref[...])
    sel_up[...] = up.astype(bf16)
    pieces[...] = up.reshape(pieces.shape).astype(bf16)


def place_kernel(x_ref, cot_ref, place_t, sel_in, place, place_c, x_c, cot_c, place_s):
    head = lax.axis_index("head")
    part = x_c.shape[0]
    sel_in[...] = dot(place_t[...], x_ref[...]).astype(bf16)
    place_s[...] = jnp.transpose(place_t[...].astype(f32))
    place[...] = place_s[...].astype(bf16)
    mine = pl.ds(pl.multiple_of(head * part, part), part)
    place_c[...] = place_s[mine, :].astype(bf16)
    x_c[...] = x_ref[mine, :]
    cot_c[...] = cot_ref[mine, :]


def attend_kernel(
    x_ref, gain_ref, wq_ref, wk_ref, wv_ref, table_ref, buckets_ref, place_ref,
    low_ref, prob_ref, att_ref, attt_ref, sel_ref,
    q_s, kt_s, v_s, bias_s, skew_s,
):
    step = pl.program_id(0)
    tokens = x_ref.shape[0]
    inner = wq_ref.shape[0]
    count = q_s.shape[0]
    width = inner // count

    @pl.when(step == 0)
    def _():
        for i in range(0, tokens, 256):
            rows = pl.ds(i, 256)
            x = x_ref[rows, :].astype(f32)
            inverse = lax.rsqrt(jnp.mean(x * x, axis=-1, keepdims=True) + EPS)
            low_ref[rows, :] = (x * inverse * gain_ref[...]).astype(bf16)
        low = low_ref[...]
        q = dot_nt(low, wq_ref[...]).astype(bf16) * bf16(width ** (-0.5))
        kt_s[...] = dot_nt(wk_ref[...], low).astype(bf16)
        v = dot_nt(low, wv_ref[...]).astype(bf16)
        for h in range(count):
            cols = slice(h * width, (h + 1) * width)
            q_s[h] = q[:, cols]
            v_s[h] = v[:, cols]
        offsets = buckets_ref.shape[1]
        bucket_hot = (iota((table_ref.shape[1], offsets), 0) == buckets_ref[...]).astype(f32)
        bias_s[...] = jnp.zeros_like(bias_s)
        bias_s[:count, :offsets] = jnp.dot(
            table_ref[...], bucket_hot, precision=highest, preferred_element_type=f32
        )

    span = skew_s.shape[1]
    row = bias_s[pl.ds(step, 1), :]
    skew_s[...] = pltpu.roll(
        jnp.broadcast_to(row, skew_s.shape), span - (BLOCK - 1), 1, stride=1, stride_axis=0
    )
    head_rows = pl.ds(pl.multiple_of(step * width, width), width)
    for i in range(0, tokens, 2 * BLOCK):
        scores = dot(q_s[step, pl.ds(i, 2 * BLOCK), :], kt_s[head_rows, :])
        for j in range(2):
            start = i + j * BLOCK
            first = tokens - BLOCK - start
            score = scores[j * BLOCK : (j + 1) * BLOCK] + skew_s[:, first : first + tokens]
            top = jnp.max(score, axis=-1, keepdims=True)
            weight = jnp.exp(score - top)
            total = jnp.sum(weight, axis=-1, keepdims=True)
            prob_ref[0, pl.ds(start, BLOCK), :] = (weight * (1.0 / total)).astype(bf16)
    att = dot(prob_ref[0], v_s[step])
    att_low = att.astype(bf16)
    att_ref[0] = att_low
    attt_ref[head_rows, :] = jnp.transpose(att).astype(bf16)
    picked = dot(place_ref[...], att_low).astype(bf16)
    half = sel_ref.shape[0]
    for h in range(count):

        @pl.when(step == h)
        def _():
            for part in range(2):
                start = part * inner + h * width
                sel_ref[:, start : start + width] = picked[part * half : (part + 1) * half]


def route_kernel(*refs, shards, heads):
    att_parts = refs[:heads]
    w_parts = refs[heads : 2 * heads]
    sel_in, gain_ref, router_ref, hidden_ref, normed_ref, probs_ref, pieces = refs[
        2 * heads : 2 * heads + 7
    ]
    att_s, w_s = refs[2 * heads + 7 :]
    head = lax.axis_index("head")
    inner = w_parts[0].shape[0]
    half = att_parts[0].shape[0]
    for d in range(heads):
        att_s[d, 0:half, :] = att_parts[d][:, 0:inner]
        att_s[d, half : 2 * half, :] = att_parts[d][:, inner : 2 * inner]
        w_s[d] = w_parts[d][...]
    mixed = None
    for k in range(heads):
        term = dot(att_s[head ^ k], w_s[head ^ k])
        mixed = term if mixed is None else mixed + term
    hidden = sel_in[...].astype(f32) + mixed
    hidden_ref[...] = hidden
    inverse = lax.rsqrt(jnp.mean(hidden * hidden, axis=-1, keepdims=True) + EPS)
    normed = hidden * inverse * gain_ref[...]
    normed_ref[...] = normed
    logits = dot_nt(normed, router_ref[...], highest)
    logits = logits - jnp.max(logits, axis=-1, keepdims=True)
    powers = jnp.exp(logits)
    probs = powers / jnp.sum(powers, axis=-1, keepdims=True)
    probs_ref[...] = probs
    gate = jnp.sum(jnp.where(chosen_of(probs.shape), probs, 0.0), axis=-1, keepdims=True)
    high = gate.astype(bf16).astype(f32)
    lane = iota((gate.shape[0], 128), 1)
    width = normed.shape[1]
    extra = jnp.where(lane == 0, high, jnp.where(lane == 1, gate - high, 0.0))
    pieces[:, :, :width] = normed.reshape(shards, SLOT, width).astype(bf16)
    pieces[:, :, width:] = extra.reshape(shards, SLOT, 128).astype(bf16)


def chosen_of(shape):
    expert = iota(shape, 1) * SLOT
    slot_row = iota(shape, 0)
    return (slot_row >= expert) & (slot_row < expert + SLOT)


def upstream_kernel(pieces, w_out, up_ref, grad_ref):
    up = pieces[...].astype(f32).reshape(up_ref.shape).astype(bf16)
    up_ref[...] = up
    grad_ref[...] = dot_nt(up, w_out[...])


def expert_kernel(
    pieces, up_ref, grad_ref, w_in, w_out, base_ref,
    chunks, x_ref, act_ref, pre_ref, out_ref, both_s, *, heads,
):
    width = w_in.shape[0]
    rows = up_ref.shape[0]
    pay = pieces[...].astype(f32).reshape(rows, pieces.shape[2])
    x = pay[:, :width].astype(bf16)
    gate = pay[:, width : width + 1] + pay[:, width + 1 : width + 2]
    pre = dot(x, w_in[...])
    cdf = 0.5 * (1.0 + lax.erf(pre * (0.5**0.5)))
    act = (pre * cdf).astype(bf16)
    slope = cdf + pre * jnp.exp(-0.5 * pre * pre) * ((2.0 * np.pi) ** (-0.5))
    both_s[0:rows, :] = dot(act, w_out[...]).astype(bf16)
    pre_low = (gate * grad_ref[...] * slope).astype(bf16)
    both_s[rows : 2 * rows, :] = dot_nt(pre_low, w_in[...]).astype(bf16)
    pre_ref[...] = pre_low
    out_ref[...] = (gate * up_ref[...].astype(f32)).astype(bf16)
    x_ref[...] = x
    act_ref[...] = act
    base = base_ref[...]
    lanes = iota((base.shape[0], 2 * rows), 1)
    for k in range(heads):
        hot = (lanes == base + CAP // heads * k).astype(f32).astype(bf16)
        chunks[k] = dot(hot, both_s[...]).astype(bf16)


def expert_grad_kernel(x_ref, pre_ref, act_ref, out_ref, in_grad, out_grad):
    in_grad[0] = dot_tn(x_ref[...], pre_ref[...])
    out_grad[0] = dot_tn(act_ref[...], out_ref[...])


def sum_kernel(parts, pieces, sum_s):
    total = parts[0].astype(f32)
    for d in range(1, parts.shape[0]):
        total = total + parts[d].astype(f32)
    sum_s[...] = total
    shards, rows = pieces.shape[:2]
    for j in range(shards):
        pieces[j] = sum_s[j * rows : (j + 1) * rows, :].astype(bf16)


def join_kernel(pieces, out_ref, sum_s):
    shards, rows = pieces.shape[:2]
    for j in range(shards):
        sum_s[j * rows : (j + 1) * rows, :] = pieces[j].astype(f32)
    out_ref[...] = sum_s[...].astype(bf16)


def masked_back_kernel(
    cot_ref, w_ref, wq_ref, wk_ref, wv_ref, low_ref, place_ref, att_ref, prob_ref, attt_ref, _,
    dq_ref, dkt_ref, dvt_ref, offs_ref, wout_ref, psel_ref, qsel_ref, k_ref, vt_ref,
    gh_s, ght_s, qt_s, mcot_s, acc_s, score_s, stack_s,
):
    step = pl.program_id(0)
    count, tokens, width = gh_s.shape
    rows_all = place_ref.shape[1]

    @pl.when(step == 0)
    def _():
        for i in range(0, tokens, 256):
            rows = pl.ds(i, 256)
            where = place_ref[rows, :].astype(f32)
            free = 1.0 - jnp.sum(where, axis=-1, keepdims=True)
            mcot_s[rows, :] = (cot_ref[rows, :].astype(f32) * free).astype(bf16)
            stack_s[width:, rows] = jnp.transpose(where).astype(bf16)
        gh = dot_nt(mcot_s[...], w_ref[...]).astype(bf16)
        ght_s[...] = dot_nt(w_ref[...], mcot_s[...]).astype(bf16)
        k = dot_nt(low_ref[...], wk_ref[...]).astype(bf16)
        qt_s[...] = dot_nt(wq_ref[...], low_ref[...]).astype(bf16) * bf16(width ** (-0.5))
        vt_ref[...] = dot_nt(wv_ref[...], low_ref[...]).astype(bf16)
        for h in range(count):
            cols = slice(h * width, (h + 1) * width)
            gh_s[h] = gh[:, cols]
            k_ref[h] = k[:, cols]
        wout_ref[...] = dot(attt_ref[...], mcot_s[...])
        qsel_ref[...] = dot(qt_s[...], place_ref[...]).astype(bf16)

    acc_s[...] = jnp.zeros_like(acc_s)
    head_rows = pl.ds(pl.multiple_of(step * width, width), width)
    stack_s[0:width, :] = ght_s[head_rows, :]
    for i in range(0, tokens, 2 * BLOCK):
        rows = pl.ds(i, 2 * BLOCK)
        gh = gh_s[step, rows, :]
        delta = jnp.sum(gh.astype(f32) * att_ref[0, rows, :].astype(f32), axis=-1, keepdims=True)
        grads = dot(gh, vt_ref[head_rows, :]) - delta
        for j in range(2):
            start = i + j * BLOCK
            first = tokens - BLOCK - start
            here = pl.ds(start, BLOCK)
            score = prob_ref[0, here, :].astype(f32) * grads[j * BLOCK : (j + 1) * BLOCK]
            acc_s[:, first : first + tokens] += score
            score_s[here, :] = score.astype(bf16)
    dq_ref[0] = dot(score_s[...], k_ref[step]) * (width ** (-0.5))
    dkt_ref[...] = dot(qt_s[head_rows, :], score_s[...])
    both = dot(stack_s[...], prob_ref[0])
    dvt_ref[...] = both[:width]
    psel_ref[0] = both[width:].astype(bf16)
    offs_ref[0] = diagonals(acc_s[...])


def diagonals(acc):
    span = acc.shape[1]
    rows = acc.shape[0] // 2
    while rows >= 8:
        acc = acc[:rows] + pltpu.roll(acc[rows:], span - rows, 1)
        rows //= 2
    total = acc[0:1]
    for r in range(1, 8):
        total = total + pltpu.roll(acc[r : r + 1], span - r, 1)
    return jnp.broadcast_to(pltpu.roll(total, BLOCK - 1, 1), (8, span))


def slot_back_kernel(*refs, heads):
    parts = refs[:heads]
    (tags_ref, up_ref, normed_ref, hidden_ref, probs_ref, router_ref, gain_ref, w_ref, att_ref,
     wout0_ref) = refs[heads : heads + 10]
    dv_ref, comb_ref, small_ref, wout_ref, gh_ref, ght_ref, delta_ref = refs[heads + 10 :]
    head = lax.axis_index("head")
    rows, width = up_ref.shape
    chunk = parts[0].shape[0]
    quarter = CAP // heads
    tags = tags_ref[...]
    peer, slot, is_grad = tags[0:1], tags[1:2], tags[2:3]
    base = peer * SLOT + slot
    slot_row = iota((rows, chunk), 0)
    combined = jnp.zeros((rows, width), f32)
    grad_buf = jnp.zeros((rows, width), f32)
    for d in range(heads):
        here = slot_row == base + quarter * (head ^ d)
        part = parts[d][...]
        combined = combined + dot((here & (is_grad == 0)).astype(f32).astype(bf16), part)
        grad_buf = grad_buf + dot((here & (is_grad == 1)).astype(f32).astype(bf16), part)
    up = up_ref[...].astype(f32)
    hidden, normed, probs, gain = hidden_ref[...], normed_ref[...], probs_ref[...], gain_ref[...]
    chosen = chosen_of(probs.shape)
    gate = jnp.sum(jnp.where(chosen, probs, 0.0), axis=-1, keepdims=True)
    comb_ref[...] = gate * combined
    gate_grad = jnp.sum(up * combined, axis=-1, keepdims=True)
    marked = jnp.where(chosen, gate_grad, 0.0)
    logit_grad = probs * (marked - jnp.sum(marked * probs, axis=-1, keepdims=True))
    experts = probs.shape[1]
    grad = grad_buf + jnp.dot(
        logit_grad, router_ref[...], precision=highest, preferred_element_type=f32
    )
    inverse = lax.rsqrt(jnp.mean(hidden * hidden, axis=-1, keepdims=True) + EPS)
    scaled = grad * gain
    inner_sum = jnp.mean(scaled * hidden, axis=-1, keepdims=True)
    dv = inverse * scaled - hidden * (inverse * inverse * inverse * inner_sum)
    dv_ref[...] = dv
    small_ref[...] = jnp.zeros_like(small_ref)
    small_ref[0:1, :] = jnp.sum(grad * hidden * inverse, axis=0, keepdims=True)
    small_ref[8 : 8 + experts, :] = dot_tn(logit_grad, normed, highest)
    grad_low = (up + dv).astype(bf16)
    half = att_ref.shape[0]
    inner = w_ref.shape[0]
    att = jnp.concatenate(
        [att_ref[:, 0:inner].astype(f32), att_ref[:, inner : 2 * inner].astype(f32)], axis=0
    )
    wout_ref[...] = wout0_ref[...] + dot_tn(att.astype(bf16), grad_low)
    gh = dot_nt(grad_low, w_ref[...])
    gh_low = gh.astype(bf16)
    count = gh_ref.shape[0]
    each = inner // count
    ght_ref[...] = dot_nt(w_ref[...], grad_low).astype(bf16)
    for h in range(count):
        cols = slice(h * each, (h + 1) * each)
        gh_ref[h] = gh_low[:, cols]
        delta_ref[h] = jnp.sum(
            gh_low[:, cols].astype(f32) * att[:, cols], axis=-1, keepdims=True
        )


def sparse_back_kernel(
    gh_ref, ght_ref, delta_ref, vt_ref, k_ref, qsel_ref, psel_ref, dq0_ref, dkt0_ref, dvt0_ref,
    place_ref, wq_ref, wk_ref, wv_ref, first_ref, q_low, kt_ref, vt_low, score_ref,
    dq_s, k_low, v_low,
):
    count, rows, width = gh_ref.shape
    tokens = vt_ref.shape[1]
    for h in range(count):
        cols = slice(h * width, (h + 1) * width)
        grad = dot(gh_ref[h], vt_ref[cols, :])
        prob = psel_ref[h]
        score = (prob.astype(f32) * (grad - delta_ref[h])).astype(bf16)
        score_ref[h] = score
        dq_s[:, cols] = dot(score, k_ref[h]) * (width ** (-0.5))
        dkt = dkt0_ref[cols, :] + dot(qsel_ref[cols, :], score)
        dvt = dvt0_ref[cols, :] + dot(ght_ref[cols, :], prob)
        kt_ref[cols, :] = dkt.astype(bf16)
        vt_low[cols, :] = dvt.astype(bf16)
        k_low[:, cols] = jnp.transpose(dkt).astype(bf16)
        v_low[:, cols] = jnp.transpose(dvt).astype(bf16)
    spread = dot(place_ref[...], dq_s[...].astype(bf16))
    for h in range(count):
        cols = slice(h * width, (h + 1) * width)
        q_low[:, cols] = (spread[:, cols] + dq0_ref[h]).astype(bf16)
    for i in range(0, tokens, 256):
        mine = pl.ds(i, 256)
        first_ref[mine, :] = (
            dot(q_low[mine, :], wq_ref[...])
            + dot(k_low[mine, :], wk_ref[...])
            + dot(v_low[mine, :], wv_ref[...])
        ).astype(bf16)


def weight_grad_kernel(
    q_low, kt_ref, vt_ref, low_ref, wq_ref, wk_ref, wv_ref, gain_ref, small_ref, qkv_ref, out_ref
):
    inner = kt_ref.shape[0]
    low = low_ref[...]
    total = None
    grads = (dot_tn(q_low[...], low), dot(kt_ref[...], low), dot(vt_ref[...], low))
    for i, (grad, w) in enumerate(zip(grads, (wq_ref, wk_ref, wv_ref))):
        qkv_ref[i * inner : (i + 1) * inner, :] = grad
        term = jnp.sum(grad * w[...].astype(f32), axis=0, keepdims=True)
        total = term if total is None else total + term
    out_ref[...] = small_ref[...]
    out_ref[1:2, :] = total / gain_ref[...]


def bias_grad_kernel(score_ref, place_ref, offs_ref, buckets_ref, out_ref, acc_s):
    count = score_ref.shape[0]
    tokens = place_ref.shape[0]
    offsets = buckets_ref.shape[1]
    bucket_count = out_ref.shape[1]
    bucket_hot = (iota((bucket_count, offsets), 0) == buckets_ref[...]).astype(f32)
    for h in range(count):
        acc_s[...] = jnp.zeros_like(acc_s)
        for i in range(0, tokens, BLOCK):
            first = tokens - BLOCK - i
            acc_s[:, first : first + tokens] += dot(place_ref[i : i + BLOCK, :], score_ref[h])
        sums = diagonals(acc_s[...]) + offs_ref[h]
        out_ref[h : h + 1, :] = dot_nt(sums[:, :offsets], bucket_hot, highest)[0:1]


def output_kernel(att_ref, *refs, heads):
    w_parts = refs[:heads]
    x_ref, place_ref, comb_ref, out_ref, w_s = refs[heads:]
    head = lax.axis_index("head")
    tokens = x_ref.shape[0]
    inner = w_parts[0].shape[0]
    for d in range(heads):
        w_s[pl.ds(pl.multiple_of((head ^ d) * inner, inner), inner), :] = w_parts[d][...]
    high, rest = split_two(comb_ref[...])
    for i in range(0, tokens, 256):
        rows = pl.ds(i, 256)
        hidden = x_ref[rows, :].astype(f32) + dot_tn(att_ref[:, rows], w_s[...])
        where = place_ref[rows, :]
        out_ref[rows, :] = hidden + (dot(where, high) + dot(where, rest))


def first_norm_kernel(parts, x_ref, cot_ref, place_ref, dv_ref, gain_ref, out_ref):
    grad = parts[0].astype(f32)
    for d in range(1, parts.shape[0]):
        grad = grad + parts[d].astype(f32)
    x = x_ref[...].astype(f32)
    inverse = lax.rsqrt(jnp.mean(x * x, axis=-1, keepdims=True) + EPS)
    scaled = grad * gain_ref[...]
    inner_sum = jnp.mean(scaled * x, axis=-1, keepdims=True)
    high, rest = split_two(dv_ref[...])
    hidden_grad = cot_ref[...].astype(f32) + (dot(place_ref[...], high) + dot(place_ref[...], rest))
    out_ref[...] = (
        hidden_grad + inverse * scaled - x * (inverse * inverse * inverse * inner_sum)
    ).astype(bf16)


def spread_kernel(*refs):
    parts, out_ref = refs[:-1], refs[-1]
    head = lax.axis_index("head")
    part = parts[0].shape[0]
    for d in range(len(parts)):
        mine = pl.ds(pl.multiple_of((head ^ d) * part, part), part)
        out_ref[mine, :] = parts[d][...].astype(f32)


def swap(x, axis, d):
    size = lax.axis_size(axis)
    return lax.ppermute(x, axis, [(i, i ^ d) for i in range(size)])


def share(x, axis):
    return [x] + [swap(x, axis, d) for d in range(1, lax.axis_size(axis))]


def trade(pieces, axis):
    return lax.all_to_all(pieces, axis, split_axis=0, concat_axis=0, tiled=True)


def sum_over(x, axis):
    size = lax.axis_size(axis)
    me = lax.axis_index(axis)
    bits = [b for b in (1 << i for i in range(16)) if b < size]
    now = x
    for b in bits:
        half = now.shape[0] // 2
        upper = (me & b) != 0
        low, high = now[:half], now[half:]
        sent = jnp.where(upper, low, high).astype(bf16)
        kept = jnp.where(upper, high, low).astype(f32)
        now = kept + swap(sent, axis, b).astype(f32)
    now = now.astype(bf16)
    for b in reversed(bits):
        upper = (me & b) != 0
        other = swap(now, axis, b)
        now = jnp.where(
            upper, jnp.concatenate([other, now], axis=0), jnp.concatenate([now, other], axis=0)
        )
    return now.astype(f32)


def sum_small(x, axes):
    for axis in axes:
        d = 1
        while d < lax.axis_size(axis):
            x = x + swap(x, axis, d)
            d *= 2
    return x


def on_device(
    layer_input, cotangent, norm1_gain, w_query, w_key, w_value, w_attn_out, bias_table,
    norm2_gain, w_router, w_expert_in, w_expert_out, expert_ids, slot_ids, buckets,
):
    tokens, width = layer_input.shape
    shards = lax.axis_size("seq")
    heads = lax.axis_size("head")
    bucket_count, count = bias_table.shape
    inner = w_query.shape[1]
    each = inner // count
    experts = w_router.shape[1]
    rows = experts * SLOT
    hidden_units = w_expert_in.shape[2]
    part = tokens // heads
    chunk = 2 * CAP // heads * shards
    piece_rows = chunk // shards
    span = 2 * tokens
    params = pltpu.CompilerParams(vmem_limit_bytes=VMEM_LIMIT)

    ids = expert_ids.reshape(1, tokens)
    slots = slot_ids.reshape(1, tokens)
    bucket_row = buckets.reshape(1, -1)
    wq_t, wk_t, wv_t = jnp.transpose(w_query), jnp.transpose(w_key), jnp.transpose(w_value)
    router_t, table_t = jnp.transpose(w_router), jnp.transpose(bias_table)
    w_in = w_expert_in.reshape(width, hidden_units)
    w_out = w_expert_out.reshape(hidden_units, width)

    quarter = CAP // heads
    place_in = np.arange(chunk)
    peer, turn = place_in // piece_rows, place_in % piece_rows
    is_grad = (turn >= quarter).astype(np.int32)
    base = (is_grad * rows + peer * SLOT + turn % quarter).astype(np.int32).reshape(chunk, 1)
    tags = np.zeros((8, chunk), np.int32)
    tags[0], tags[1], tags[2] = peer, turn % quarter, is_grad

    sel_up, up_pieces, place_t = call(
        select_kernel,
        [
            shape_of(rows, width, bf16),
            jax.ShapeDtypeStruct((shards, SLOT, width), bf16),
            shape_of(rows, tokens, bf16),
        ],
        (cotangent, ids, slots),
        name="select",
        flops=2 * rows * tokens * width,
    )
    up_parts = trade(up_pieces, "seq")
    w_mix = share(w_attn_out, "head")

    low, prob, att, att_t, att_sel = pl.pallas_call(
        attend_kernel,
        grid=(count,),
        out_shape=(
            shape_of(tokens, width, bf16),
            jax.ShapeDtypeStruct((count, tokens, tokens), bf16),
            jax.ShapeDtypeStruct((count, tokens, each), bf16),
            shape_of(inner, tokens, bf16),
            shape_of(rows // 2, 2 * inner, bf16),
        ),
        in_specs=[
            whole((tokens, width)), whole((width,)), whole((inner, width)), whole((inner, width)),
            whole((inner, width)), whole((count, bucket_count)), whole((1, span - 1)),
            whole((rows, tokens)),
        ],
        out_specs=(
            whole((tokens, width)), by_head((1, tokens, tokens)), by_head((1, tokens, each)),
            whole((inner, tokens)), whole((rows // 2, 2 * inner)),
        ),
        scratch_shapes=[
            pltpu.VMEM((count, tokens, each), bf16),
            pltpu.VMEM((inner, tokens), bf16),
            pltpu.VMEM((count, tokens, each), bf16),
            pltpu.VMEM((8, span), f32),
            pltpu.VMEM((BLOCK, span), f32),
        ],
        compiler_params=params,
        cost_estimate=pl.CostEstimate(
            flops=2 * tokens * width * inner * 3 + 4 * count * tokens * tokens * each,
            bytes_accessed=12 * 2**20,
            transcendentals=count * tokens * tokens,
        ),
        name="attend",
    )(layer_input, norm1_gain, wq_t, wk_t, wv_t, table_t, bucket_row, place_t)

    sel_parts = share(att_sel, "head")
    sel_in, place, place_c, x_c, cot_c = call(
        place_kernel,
        [
            shape_of(rows, width, bf16),
            shape_of(tokens, rows, bf16),
            shape_of(part, rows, bf16),
            shape_of(part, width, bf16),
            shape_of(part, width, bf16),
        ],
        (layer_input, cotangent, place_t),
        scratch=[pltpu.VMEM((tokens, rows), f32)],
        name="place",
        flops=2 * rows * tokens * width,
        after=(att_sel,),
    )
    up_rows, up_grad = call(
        upstream_kernel,
        [shape_of(rows, width, bf16), shape_of(rows, hidden_units, f32)],
        (up_parts, w_out),
        name="upstream",
        flops=2 * rows * width * hidden_units,
        after=(att_sel,),
    )
    hidden_sel, normed_sel, probs, pay_pieces = call(
        partial(route_kernel, shards=shards, heads=heads),
        [
            shape_of(rows, width, f32),
            shape_of(rows, width, f32),
            shape_of(rows, experts, f32),
            jax.ShapeDtypeStruct((shards, SLOT, width + 128), bf16),
        ],
        tuple(sel_parts) + tuple(w_mix) + (sel_in, norm2_gain, router_t),
        scratch=[
            pltpu.VMEM((heads, rows, inner), bf16),
            pltpu.VMEM((heads, inner, width), bf16),
        ],
        name="route",
        flops=2 * rows * width * width,
        after=(up_grad,),
    )
    pay_parts = trade(pay_pieces, "seq")
    att_all = lax.all_gather(att_t, "head", axis=0, tiled=True)

    dq0, dk0, dv0, offs, wout0, prob_sel, q_sel, k_rows, v_t = pl.pallas_call(
        masked_back_kernel,
        grid=(count,),
        out_shape=(
            jax.ShapeDtypeStruct((count, tokens, each), f32),
            shape_of(inner, tokens, f32),
            shape_of(inner, tokens, f32),
            jax.ShapeDtypeStruct((count, 8, span), f32),
            shape_of(inner, width, f32),
            jax.ShapeDtypeStruct((count, rows, tokens), bf16),
            shape_of(inner, rows, bf16),
            jax.ShapeDtypeStruct((count, tokens, each), bf16),
            shape_of(inner, tokens, bf16),
        ),
        in_specs=[
            whole((tokens, width)), whole((inner, width)), whole((inner, width)),
            whole((inner, width)), whole((inner, width)), whole((tokens, width)),
            whole((tokens, rows)), by_head((1, tokens, each)), by_head((1, tokens, tokens)),
            whole((inner, tokens)), spec(pl.ANY),
        ],
        out_specs=(
            by_head((1, tokens, each)), by_head((each, tokens)), by_head((each, tokens)),
            by_head((1, 8, span)), whole((inner, width)), by_head((1, rows, tokens)),
            whole((inner, rows)), whole((count, tokens, each)), whole((inner, tokens)),
        ),
        scratch_shapes=[
            pltpu.VMEM((count, tokens, each), bf16),
            pltpu.VMEM((inner, tokens), bf16),
            pltpu.VMEM((inner, tokens), bf16),
            pltpu.VMEM((tokens, width), bf16),
            pltpu.VMEM((BLOCK, span), f32),
            pltpu.VMEM((tokens, tokens), bf16),
            pltpu.VMEM((each + rows, tokens), bf16),
        ],
        compiler_params=params,
        cost_estimate=pl.CostEstimate(
            flops=2 * tokens * width * inner * 5 + 10 * count * tokens * tokens * each,
            bytes_accessed=16 * 2**20,
            transcendentals=0,
        ),
        name="masked_back",
    )(cotangent, w_attn_out, wq_t, wk_t, wv_t, low, place, att, prob, att_t, pay_pieces)

    chunks, x_rows, act, pre_low, out_low = call(
        partial(expert_kernel, heads=heads),
        [
            jax.ShapeDtypeStruct((heads, chunk, width), bf16),
            shape_of(rows, width, bf16),
            shape_of(rows, hidden_units, bf16),
            shape_of(rows, hidden_units, bf16),
            shape_of(rows, width, bf16),
        ],
        (pay_parts, up_rows, up_grad, w_in, w_out, jnp.asarray(base)),
        scratch=[pltpu.VMEM((2 * rows, width), bf16)],
        name="expert",
        flops=6 * rows * width * hidden_units,
        after=(dq0,),
    )
    (returned,) = call(
        sum_kernel,
        [jax.ShapeDtypeStruct((shards, piece_rows, width), bf16)],
        (trade(chunks, "head"),),
        scratch=[pltpu.VMEM((chunk, width), f32)],
        name="sum",
    )
    (joined,) = call(
        join_kernel,
        [shape_of(chunk, width, bf16)],
        (trade(returned, "seq"),),
        scratch=[pltpu.VMEM((chunk, width), f32)],
        name="join",
    )
    full_parts = share(joined, "head")

    w_in_grad, w_out_grad = call(
        expert_grad_kernel,
        [
            jax.ShapeDtypeStruct(w_expert_in.shape, f32),
            jax.ShapeDtypeStruct(w_expert_out.shape, f32),
        ],
        (x_rows, pre_low, act, out_low),
        name="expert_grad",
        flops=4 * rows * width * hidden_units,
        after=(chunks,),
    )

    small_rows = 8 + -(-experts // 8) * 8
    dv_sel, comb_sel, small, wout_part, gh_sel, ght_sel, delta_sel = call(
        partial(slot_back_kernel, heads=heads),
        [
            shape_of(rows, width, f32),
            shape_of(rows, width, f32),
            shape_of(small_rows, width, f32),
            shape_of(inner, width, f32),
            jax.ShapeDtypeStruct((count, rows, each), bf16),
            shape_of(inner, rows, bf16),
            jax.ShapeDtypeStruct((count, rows, 1), f32),
        ],
        tuple(full_parts)
        + (jnp.asarray(tags), sel_up, normed_sel, hidden_sel, probs, router_t, norm2_gain)
        + (w_attn_out, att_sel, wout0),
        name="slot_back",
        flops=4 * rows * width * inner,
        after=(w_in_grad,),
    )

    first, q_low, dk_t, dv_t, score_sel = call(
        sparse_back_kernel,
        [
            shape_of(tokens, width, bf16),
            shape_of(tokens, inner, bf16),
            shape_of(inner, tokens, bf16),
            shape_of(inner, tokens, bf16),
            jax.ShapeDtypeStruct((count, rows, tokens), bf16),
        ],
        (gh_sel, ght_sel, delta_sel, v_t, k_rows, q_sel, prob_sel, dq0, dk0, dv0, place)
        + (wq_t, wk_t, wv_t),
        scratch=[
            pltpu.VMEM((rows, inner), f32),
            pltpu.VMEM((tokens, inner), bf16),
            pltpu.VMEM((tokens, inner), bf16),
        ],
        name="sparse_back",
        flops=8 * rows * tokens * inner + 6 * tokens * inner * width,
    )
    first_parts = trade(first.reshape(heads, part, width), "head")

    qkv_grad, small = call(
        weight_grad_kernel,
        [shape_of(3 * inner, width, f32), shape_of(small_rows, width, f32)],
        (q_low, dk_t, dv_t, low, wq_t, wk_t, wv_t, norm1_gain, small),
        name="weight_grad",
        flops=6 * tokens * inner * width,
    )
    wout_grad = sum_over(wout_part, "seq")
    qkv_sum = sum_over(qkv_grad, "seq")

    (table_part,) = call(
        bias_grad_kernel,
        [shape_of(8, bucket_count, f32)],
        (score_sel, place, offs, bucket_row),
        scratch=[pltpu.VMEM((BLOCK, span), f32)],
        name="bias_grad",
        flops=2 * count * rows * tokens * tokens,
        after=(qkv_grad,),
    )
    small_sum = sum_small(small, ("seq",))
    gain1_sum = sum_small(small_sum[1:2], ("head",))
    table_sum = sum_small(table_part, ("seq",))

    (layer_output,) = call(
        partial(output_kernel, heads=heads),
        [shape_of(tokens, width, f32)],
        (att_all,) + tuple(w_mix) + (layer_input, place, comb_sel),
        scratch=[pltpu.VMEM((heads * inner, width), bf16)],
        name="output",
        flops=2 * tokens * width * width,
        after=(table_part,),
    )

    (grad_part,) = call(
        first_norm_kernel,
        [shape_of(part, width, bf16)],
        (first_parts, x_c, cot_c, place_c, dv_sel, norm1_gain),
        name="first_norm",
        flops=4 * part * rows * width,
    )
    (input_grad,) = call(
        spread_kernel,
        [shape_of(tokens, width, f32)],
        tuple(share(grad_part, "head")),
        name="spread",
    )

    return (
        layer_output,
        input_grad,
        gain1_sum[0],
        jnp.transpose(qkv_sum[:inner]),
        jnp.transpose(qkv_sum[inner : 2 * inner]),
        jnp.transpose(qkv_sum[2 * inner :]),
        wout_grad,
        jnp.transpose(table_sum[:count]),
        small_sum[0],
        jnp.transpose(small_sum[8 : 8 + experts]),
        w_in_grad,
        w_out_grad,
    )


def solution(mesh):
    return jax.shard_map(
        on_device,
        mesh=mesh,
        in_specs=(
            P("seq", None),
            P("seq", None),
            P(),
            P(None, "head"),
            P(None, "head"),
            P(None, "head"),
            P("head", None),
            P(None, "head"),
            P(),
            P(),
            P("seq", None, "head"),
            P("seq", "head", None),
            P("seq"),
            P("seq"),
            P(),
        ),
        out_specs=(
            P("seq", None),
            P("seq", None),
            P(),
            P(None, "head"),
            P(None, "head"),
            P(None, "head"),
            P("head", None),
            P(None, "head"),
            P(),
            P(),
            P("seq", None, "head"),
            P("seq", "head", None),
        ),
        check_vma=False,
    )
```

```python
from functools import partial

import jax
import jax.numpy as jnp
import numpy as np
from jax import lax
from jax.experimental import pallas as pl
from jax.experimental.pallas import tpu as pltpu
from jax.sharding import PartitionSpec as P

CAP = 20
SLOT = 24
EPS = 1e-06
BLOCK = 128
VMEM_LIMIT = 64 * 1024 * 1024
NO_COST = pl.CostEstimate(flops=1, bytes_accessed=1, transcendentals=0)

f32 = jnp.float32
bf16 = jnp.bfloat16
highest = lax.Precision.HIGHEST


def dot(a, b):
    return jnp.dot(a, b, preferred_element_type=f32)


def dot_nt(a, b, precision=None):
    return lax.dot_general(
        a, b, (((1,), (1,)), ((), ())), precision=precision, preferred_element_type=f32
    )


def dot_tn(a, b, precision=None):
    return lax.dot_general(
        a, b, (((0,), (0,)), ((), ())), precision=precision, preferred_element_type=f32
    )


def iota(shape, dim):
    return lax.broadcasted_iota(jnp.int32, shape, dim)


def split_two(v):
    high = v.astype(bf16)
    return high, (v - high.astype(f32)).astype(bf16)


def shape_of(rows, cols, dtype):
    return jax.ShapeDtypeStruct((rows, cols), dtype)


def spec(memory):
    return pl.BlockSpec(memory_space=memory)


def call(kernel, outs, args, scratch=(), name=None, after=(), moved=1):
    outs, args = tuple(outs), tuple(args)

    def body(*refs):
        kernel(*refs[: len(args)], *refs[len(args) + len(after) :])

    return pl.pallas_call(
        body,
        out_shape=outs,
        in_specs=[spec(pltpu.VMEM)] * len(args) + [spec(pl.ANY)] * len(after),
        out_specs=tuple(spec(pltpu.VMEM) for _ in outs),
        scratch_shapes=list(scratch),
        compiler_params=pltpu.CompilerParams(vmem_limit_bytes=VMEM_LIMIT),
        cost_estimate=pl.CostEstimate(flops=1, bytes_accessed=moved, transcendentals=0),
        name=name,
    )(*args, *after)


def whole(shape):
    return pl.BlockSpec(shape, lambda h: (0,) * len(shape))


def by_head(shape):
    return pl.BlockSpec(shape, lambda h: (h,) + (0,) * (len(shape) - 1))


def slot_rows(ids, slots, rows):
    cell = jnp.where(slots < CAP, ids * SLOT + slots, -1)
    return (iota((rows, cell.shape[1]), 0) == cell).astype(f32)


def place_kernel(
    x_ref, cot_ref, ids_ref, slots_ref, sel_in, sel_up, place, place_c, x_c, cot_c, place_s
):
    head = lax.axis_index("head")
    part = x_c.shape[0]
    slot_hot = slot_rows(ids_ref[...], slots_ref[...], sel_in.shape[0])
    place_s[...] = jnp.transpose(slot_hot)
    slot_low = slot_hot.astype(bf16)
    sel_in[...] = dot(slot_low, x_ref[...]).astype(bf16)
    sel_up[...] = dot(slot_low, cot_ref[...]).astype(bf16)
    place[...] = place_s[...].astype(bf16)
    mine = pl.ds(pl.multiple_of(head * part, part), part)
    place_c[...] = place_s[mine, :].astype(bf16)
    x_c[...] = x_ref[mine, :]
    cot_c[...] = cot_ref[mine, :]


def attend_kernel(
    x_ref, gain_ref, wq_ref, wk_ref, wv_ref, table_ref, buckets_ref, ids_ref, slots_ref,
    low_ref, prob_ref, att_ref, attt_ref, sel_ref,
    q_s, kt_s, v_s, bias_s, skew_s, slot_s,
):
    step = pl.program_id(0)
    tokens = x_ref.shape[0]
    inner = wq_ref.shape[0]
    count = q_s.shape[0]
    width = inner // count

    @pl.when(step == 0)
    def _():
        for i in range(0, tokens, 256):
            rows = pl.ds(i, 256)
            x = x_ref[rows, :].astype(f32)
            inverse = lax.rsqrt(jnp.mean(x * x, axis=-1, keepdims=True) + EPS)
            low_ref[rows, :] = (x * inverse * gain_ref[...]).astype(bf16)
        low = low_ref[...]
        q = dot_nt(low, wq_ref[...]).astype(bf16) * bf16(width ** (-0.5))
        kt_s[...] = dot_nt(wk_ref[...], low).astype(bf16)
        v = dot_nt(low, wv_ref[...]).astype(bf16)
        for h in range(count):
            cols = slice(h * width, (h + 1) * width)
            q_s[h] = q[:, cols]
            v_s[h] = v[:, cols]
        offsets = buckets_ref.shape[1]
        bucket_hot = (iota((table_ref.shape[1], offsets), 0) == buckets_ref[...]).astype(f32)
        slot_s[...] = slot_rows(ids_ref[...], slots_ref[...], slot_s.shape[0]).astype(bf16)
        bias_s[...] = jnp.zeros_like(bias_s)
        bias_s[:count, :offsets] = jnp.dot(
            table_ref[...], bucket_hot, precision=highest, preferred_element_type=f32
        )

    span = skew_s.shape[1]
    row = bias_s[pl.ds(step, 1), :]
    skew_s[...] = pltpu.roll(
        jnp.broadcast_to(row, skew_s.shape), span - (BLOCK - 1), 1, stride=1, stride_axis=0
    )
    head_rows = pl.ds(pl.multiple_of(step * width, width), width)
    for i in range(0, tokens, 2 * BLOCK):
        scores = dot(q_s[step, pl.ds(i, 2 * BLOCK), :], kt_s[head_rows, :])
        for j in range(2):
            start = i + j * BLOCK
            first = tokens - BLOCK - start
            score = scores[j * BLOCK : (j + 1) * BLOCK] + skew_s[:, first : first + tokens]
            top = jnp.max(score, axis=-1, keepdims=True)
            weight = jnp.exp(score - top)
            total = jnp.sum(weight, axis=-1, keepdims=True)
            prob_ref[0, pl.ds(start, BLOCK), :] = (weight * (1.0 / total)).astype(bf16)
    att = dot(prob_ref[0], v_s[step])
    att_low = att.astype(bf16)
    att_ref[0] = att_low
    attt_ref[head_rows, :] = jnp.transpose(att).astype(bf16)
    picked = dot(slot_s[...], att_low).astype(bf16)
    half = sel_ref.shape[0]
    for h in range(count):

        @pl.when(step == h)
        def _():
            for part in range(2):
                start = part * inner + h * width
                sel_ref[:, start : start + width] = picked[part * half : (part + 1) * half]


def route_kernel(*refs, shards, heads):
    att_parts = refs[:heads]
    w_parts = refs[heads : 2 * heads]
    (sel_in, sel_up, gain_ref, router_ref, att_t, hidden_ref, normed_ref, probs_ref, pieces,
     att_on) = refs[2 * heads : 2 * heads + 10]
    att_s, w_s = refs[2 * heads + 10 :]
    head = lax.axis_index("head")
    inner = w_parts[0].shape[0]
    half = att_parts[0].shape[0]
    for d in range(heads):
        att_s[d, 0:half, :] = att_parts[d][:, 0:inner]
        att_s[d, half : 2 * half, :] = att_parts[d][:, inner : 2 * inner]
        w_s[d] = w_parts[d][...]
    mixed = None
    for k in range(heads):
        term = dot(att_s[head ^ k], w_s[head ^ k])
        mixed = term if mixed is None else mixed + term
    hidden = sel_in[...].astype(f32) + mixed
    hidden_ref[...] = hidden
    inverse = lax.rsqrt(jnp.mean(hidden * hidden, axis=-1, keepdims=True) + EPS)
    normed = hidden * inverse * gain_ref[...]
    normed_ref[...] = normed
    logits = dot_nt(normed, router_ref[...], highest)
    logits = logits - jnp.max(logits, axis=-1, keepdims=True)
    powers = jnp.exp(logits)
    probs = powers / jnp.sum(powers, axis=-1, keepdims=True)
    probs_ref[...] = probs
    gate = jnp.sum(jnp.where(chosen_of(probs.shape), probs, 0.0), axis=-1, keepdims=True)
    high = gate.astype(bf16).astype(f32)
    lane = iota((gate.shape[0], 128), 1)
    width = normed.shape[1]
    extra = jnp.where(lane == 0, high, jnp.where(lane == 1, gate - high, 0.0))
    pieces[:, :, :width] = normed.reshape(shards, SLOT, width).astype(bf16)
    pieces[:, :, width : 2 * width] = (
        sel_up[...].astype(f32).reshape(shards, SLOT, width).astype(bf16)
    )
    pieces[:, :, 2 * width :] = extra.reshape(shards, SLOT, 128).astype(bf16)
    att_on[...] = att_t[...]


def chosen_of(shape):
    expert = iota(shape, 1) * SLOT
    slot_row = iota(shape, 0)
    return (slot_row >= expert) & (slot_row < expert + SLOT)


def expert_kernel(pieces, w_in, w_out, base_ref, *refs, heads):
    chunks = refs[:heads]
    x_ref, act_ref, pre_ref, out_ref, both_s = refs[heads:]
    head = lax.axis_index("head")
    rows, width = x_ref.shape
    pay = pieces[...].astype(f32).reshape(rows, pieces.shape[2])
    x = pay[:, :width].astype(bf16)
    up = pay[:, width : 2 * width]
    gate = pay[:, 2 * width : 2 * width + 1] + pay[:, 2 * width + 1 : 2 * width + 2]
    out_low = (gate * up).astype(bf16)
    pre = dot(x, w_in[...])
    cdf = 0.5 * (1.0 + lax.erf(pre * (0.5**0.5)))
    act = (pre * cdf).astype(bf16)
    slope = cdf + pre * jnp.exp(-0.5 * pre * pre) * ((2.0 * np.pi) ** (-0.5))
    both_s[0:rows, :] = dot(act, w_out[...]).astype(bf16)
    pre_low = (dot_nt(out_low, w_out[...]) * slope).astype(bf16)
    both_s[rows : 2 * rows, :] = dot_nt(pre_low, w_in[...]).astype(bf16)
    shard = lax.axis_index("seq")
    peer, place_in = base_ref[:, 0:1], base_ref[:, 1:2]
    base = (peer ^ shard) * SLOT + place_in
    lanes = iota((base.shape[0], 2 * rows), 1)
    for d in range(heads):
        hot = (lanes == base + CAP // heads * (head ^ d)).astype(f32).astype(bf16)
        chunks[d][...] = dot(hot, both_s[...]).astype(bf16)
    pre_ref[...] = pre_low
    out_ref[...] = out_low
    x_ref[...] = x
    act_ref[...] = act


def expert_grad_kernel(x_ref, pre_ref, act_ref, out_ref, in_grad, out_grad):
    in_grad[0] = dot_tn(x_ref[...], pre_ref[...])
    out_grad[0] = dot_tn(act_ref[...], out_ref[...])


def sum_kernel(*refs, heads):
    parts, pieces, sum_s = refs[:heads], refs[heads:-1], refs[-1]
    total = parts[0][...].astype(f32)
    for d in range(1, heads):
        total = total + parts[d][...].astype(f32)
    sum_s[...] = total
    rows = pieces[0].shape[0]
    for j in range(len(pieces)):
        pieces[j][...] = sum_s[j * rows : (j + 1) * rows, :].astype(bf16)


def join_kernel(*refs):
    pieces, out_ref, sum_s = refs[:-2], refs[-2], refs[-1]
    rows = pieces[0].shape[0]
    for j in range(len(pieces)):
        sum_s[j * rows : (j + 1) * rows, :] = pieces[j][...].astype(f32)
    out_ref[...] = sum_s[...].astype(bf16)


def masked_back_kernel(
    cot_ref, w_ref, wq_ref, wk_ref, wv_ref, low_ref, place_ref, att_ref, prob_ref, attt_ref, _,
    dq_ref, dkt_ref, dvt_ref, offs_ref, wout_ref, psel_ref, qsel_ref, k_ref, vt_ref,
    gh_s, ght_s, qt_s, mcot_s, acc_s, score_s, stack_s,
):
    step = pl.program_id(0)
    count, tokens, width = gh_s.shape
    rows_all = place_ref.shape[1]

    @pl.when(step == 0)
    def _():
        for i in range(0, tokens, 256):
            rows = pl.ds(i, 256)
            where = place_ref[rows, :].astype(f32)
            free = 1.0 - jnp.sum(where, axis=-1, keepdims=True)
            mcot_s[rows, :] = (cot_ref[rows, :].astype(f32) * free).astype(bf16)
            stack_s[width:, rows] = jnp.transpose(where).astype(bf16)
        gh = dot_nt(mcot_s[...], w_ref[...]).astype(bf16)
        ght_s[...] = dot_nt(w_ref[...], mcot_s[...]).astype(bf16)
        k = dot_nt(low_ref[...], wk_ref[...]).astype(bf16)
        qt_s[...] = dot_nt(wq_ref[...], low_ref[...]).astype(bf16) * bf16(width ** (-0.5))
        vt_ref[...] = dot_nt(wv_ref[...], low_ref[...]).astype(bf16)
        for h in range(count):
            cols = slice(h * width, (h + 1) * width)
            gh_s[h] = gh[:, cols]
            k_ref[h] = k[:, cols]
        wout_ref[...] = dot(attt_ref[...], mcot_s[...])
        qsel_ref[...] = dot(qt_s[...], place_ref[...]).astype(bf16)

    acc_s[...] = jnp.zeros_like(acc_s)
    head_rows = pl.ds(pl.multiple_of(step * width, width), width)
    stack_s[0:width, :] = ght_s[head_rows, :]
    for i in range(0, tokens, 2 * BLOCK):
        rows = pl.ds(i, 2 * BLOCK)
        gh = gh_s[step, rows, :]
        delta = jnp.sum(gh.astype(f32) * att_ref[0, rows, :].astype(f32), axis=-1, keepdims=True)
        grads = dot(gh, vt_ref[head_rows, :]) - delta
        for j in range(2):
            start = i + j * BLOCK
            first = tokens - BLOCK - start
            here = pl.ds(start, BLOCK)
            score = prob_ref[0, here, :].astype(f32) * grads[j * BLOCK : (j + 1) * BLOCK]
            acc_s[:, first : first + tokens] += score
            score_s[here, :] = score.astype(bf16)
    dq_ref[0] = dot(score_s[...], k_ref[step]) * (width ** (-0.5))
    dkt_ref[...] = dot(qt_s[head_rows, :], score_s[...])
    both = dot(stack_s[...], prob_ref[0])
    dvt_ref[...] = both[:width]
    psel_ref[0] = both[width:].astype(bf16)
    offs_ref[0] = diagonals(acc_s[...])


def diagonals(acc):
    span = acc.shape[1]
    rows = acc.shape[0] // 2
    while rows >= 8:
        acc = acc[:rows] + pltpu.roll(acc[rows:], span - rows, 1)
        rows //= 2
    total = acc[0:1]
    for r in range(1, 8):
        total = total + pltpu.roll(acc[r : r + 1], span - r, 1)
    return jnp.broadcast_to(pltpu.roll(total, BLOCK - 1, 1), (8, span))


def slot_back_kernel(*refs, heads):
    parts = refs[:heads]
    (tags_ref, up_ref, normed_ref, hidden_ref, probs_ref, router_ref, gain_ref, w_ref, att_ref,
     wout0_ref) = refs[heads : heads + 10]
    dv_ref, comb_ref, small_ref, wout_ref, gh_ref, ght_ref, delta_ref = refs[heads + 10 :]
    head, shard = lax.axis_index("head"), lax.axis_index("seq")
    rows, width = up_ref.shape
    chunk = parts[0].shape[0]
    quarter = CAP // heads
    tags = tags_ref[...]
    peer, slot, is_grad = tags[0:1], tags[1:2], tags[2:3]
    base = (peer ^ shard) * SLOT + slot
    slot_row = iota((rows, chunk), 0)
    combined = jnp.zeros((rows, width), f32)
    grad_buf = jnp.zeros((rows, width), f32)
    for d in range(heads):
        here = slot_row == base + quarter * (head ^ d)
        part = parts[d][...]
        combined = combined + dot((here & (is_grad == 0)).astype(f32).astype(bf16), part)
        grad_buf = grad_buf + dot((here & (is_grad == 1)).astype(f32).astype(bf16), part)
    up = up_ref[...].astype(f32)
    hidden, normed, probs, gain = hidden_ref[...], normed_ref[...], probs_ref[...], gain_ref[...]
    chosen = chosen_of(probs.shape)
    gate = jnp.sum(jnp.where(chosen, probs, 0.0), axis=-1, keepdims=True)
    comb_ref[...] = gate * combined
    gate_grad = jnp.sum(up * combined, axis=-1, keepdims=True)
    marked = jnp.where(chosen, gate_grad, 0.0)
    logit_grad = probs * (marked - jnp.sum(marked * probs, axis=-1, keepdims=True))
    experts = probs.shape[1]
    grad = grad_buf + jnp.dot(
        logit_grad, router_ref[...], precision=highest, preferred_element_type=f32
    )
    inverse = lax.rsqrt(jnp.mean(hidden * hidden, axis=-1, keepdims=True) + EPS)
    scaled = grad * gain
    inner_sum = jnp.mean(scaled * hidden, axis=-1, keepdims=True)
    dv = inverse * scaled - hidden * (inverse * inverse * inverse * inner_sum)
    dv_ref[...] = dv
    small_ref[...] = jnp.zeros_like(small_ref)
    small_ref[0:1, :] = jnp.sum(grad * hidden * inverse, axis=0, keepdims=True)
    small_ref[8 : 8 + experts, :] = dot_tn(logit_grad, normed, highest)
    grad_low = (up + dv).astype(bf16)
    half = att_ref.shape[0]
    inner = w_ref.shape[0]
    att = jnp.concatenate(
        [att_ref[:, 0:inner].astype(f32), att_ref[:, inner : 2 * inner].astype(f32)], axis=0
    )
    wout_ref[...] = wout0_ref[...] + dot_tn(att.astype(bf16), grad_low)
    gh = dot_nt(grad_low, w_ref[...])
    gh_low = gh.astype(bf16)
    count = gh_ref.shape[0]
    each = inner // count
    ght_ref[...] = dot_nt(w_ref[...], grad_low).astype(bf16)
    for h in range(count):
        cols = slice(h * each, (h + 1) * each)
        gh_ref[h] = gh_low[:, cols]
        delta_ref[h] = jnp.sum(
            gh_low[:, cols].astype(f32) * att[:, cols], axis=-1, keepdims=True
        )


def sparse_back_kernel(
    gh_ref, ght_ref, delta_ref, vt_ref, k_ref, qsel_ref, psel_ref, dq0_ref, dkt0_ref, dvt0_ref,
    place_ref, wq_ref, wk_ref, wv_ref, low_ref, gain_ref, small_ref, wout_ref, *refs, heads,
):
    chunks = refs[:heads]
    (score_ref, send_ref, keep_ref, out_ref,
     dq_s, q_low, k_low, v_low, kt_s, vt_s, all_s) = refs[heads:]
    head = lax.axis_index("head")
    count, rows, width = gh_ref.shape
    tokens = vt_ref.shape[1]
    inner = count * width
    for h in range(count):
        cols = slice(h * width, (h + 1) * width)
        grad = dot(gh_ref[h], vt_ref[cols, :])
        prob = psel_ref[h]
        score = (prob.astype(f32) * (grad - delta_ref[h])).astype(bf16)
        score_ref[h] = score
        dq_s[:, cols] = dot(score, k_ref[h]) * (width ** (-0.5))
        dkt = dkt0_ref[cols, :] + dot(qsel_ref[cols, :], score)
        dvt = dvt0_ref[cols, :] + dot(ght_ref[cols, :], prob)
        kt_s[cols, :] = dkt.astype(bf16)
        vt_s[cols, :] = dvt.astype(bf16)
        k_low[:, cols] = jnp.transpose(dkt).astype(bf16)
        v_low[:, cols] = jnp.transpose(dvt).astype(bf16)
    spread = dot(place_ref[...], dq_s[...].astype(bf16))
    for h in range(count):
        cols = slice(h * width, (h + 1) * width)
        q_low[:, cols] = (spread[:, cols] + dq0_ref[h]).astype(bf16)
    part = tokens // heads
    for d in range(heads):
        mine = pl.ds(pl.multiple_of((head ^ d) * part, part), part)
        chunks[d][...] = (
            dot(q_low[mine, :], wq_ref[...])
            + dot(k_low[mine, :], wk_ref[...])
            + dot(v_low[mine, :], wv_ref[...])
        ).astype(bf16)
    low = low_ref[...]
    total = None
    grads = (dot_tn(q_low[...], low), dot(kt_s[...], low), dot(vt_s[...], low))
    for i, (grad, w) in enumerate(zip(grads, (wq_ref, wk_ref, wv_ref))):
        all_s[i * inner : (i + 1) * inner, :] = grad
        term = jnp.sum(grad * w[...].astype(f32), axis=0, keepdims=True)
        total = term if total is None else total + term
    all_s[3 * inner :, :] = wout_ref[...]
    out_ref[...] = small_ref[...]
    out_ref[1:2, :] = total / gain_ref[...]
    split_rows(all_s, 1, send_ref, keep_ref)


def is_upper(bit):
    return (lax.axis_index("seq") & bit) != 0


def split_rows(all_s, bit, send_ref, keep_ref):
    half = send_ref.shape[0]
    low, high = all_s[0:half, :], all_s[half : 2 * half, :]
    keep_ref[...] = jnp.where(is_upper(bit), high, low)
    send_ref[...] = jnp.where(is_upper(bit), low, high).astype(bf16)


def halve_kernel(keep_ref, got_ref, send_ref, out_ref, all_s, *, bit):
    all_s[...] = keep_ref[...] + got_ref[...].astype(f32)
    split_rows(all_s, bit, send_ref, out_ref)


def join_rows(mine_ref, got_ref, all_s, bit):
    half = mine_ref.shape[0]
    mine, got = mine_ref[...].astype(f32), got_ref[...].astype(f32)
    all_s[0:half, :] = jnp.where(is_upper(bit), got, mine)
    all_s[half : 2 * half, :] = jnp.where(is_upper(bit), mine, got)


def pair_kernel(mine_ref, got_ref, out_ref, all_s, *, bit):
    join_rows(mine_ref, got_ref, all_s, bit)
    out_ref[...] = all_s[...].astype(bf16)


def final_kernel(mine_ref, got_ref, *refs, bit):
    outs, all_s = refs[:-1], refs[-1]
    join_rows(mine_ref, got_ref, all_s, bit)
    inner = outs[0].shape[0]
    for i, out in enumerate(outs):
        out[...] = all_s[i * inner : (i + 1) * inner, :]


def bias_grad_kernel(
    score_ref, place_ref, offs_ref, buckets_ref, small_ref, out_ref, acc_s, *, bucket_count
):
    count = score_ref.shape[0]
    tokens = place_ref.shape[0]
    offsets = buckets_ref.shape[1]
    out_ref[...] = small_ref[...]
    bucket_hot = (iota((bucket_count, offsets), 0) == buckets_ref[...]).astype(f32)
    for h in range(count):
        acc_s[...] = jnp.zeros_like(acc_s)
        for i in range(0, tokens, BLOCK):
            first = tokens - BLOCK - i
            acc_s[:, first : first + tokens] += dot(place_ref[i : i + BLOCK, :], score_ref[h])
        sums = diagonals(acc_s[...]) + offs_ref[h]
        out_ref[2 + h : 3 + h, :bucket_count] = dot_nt(sums[:, :offsets], bucket_hot, highest)[0:1]


def hidden_kernel(*refs, heads):
    att_parts, w_parts = refs[:heads], refs[heads : 2 * heads]
    x_ref, out_ref, att_s, w_s = refs[2 * heads :]
    head = lax.axis_index("head")
    tokens = x_ref.shape[0]
    inner = w_parts[0].shape[0]
    for d in range(heads):
        mine = pl.ds(pl.multiple_of((head ^ d) * inner, inner), inner)
        att_s[mine, :] = att_parts[d][...]
        w_s[mine, :] = w_parts[d][...]
    for i in range(0, tokens, 256):
        rows = pl.ds(i, 256)
        out_ref[rows, :] = x_ref[rows, :].astype(f32) + dot_tn(att_s[:, rows], w_s[...])


def output_kernel(hidden_ref, place_ref, comb_ref, out_ref):
    high, rest = split_two(comb_ref[...])
    for i in range(0, hidden_ref.shape[0], 256):
        rows = pl.ds(i, 256)
        where = place_ref[rows, :]
        out_ref[rows, :] = hidden_ref[rows, :] + (dot(where, high) + dot(where, rest))


def first_norm_kernel(*refs):
    parts = refs[:-9]
    (x_ref, cot_ref, place_ref, dv_ref, gain_ref, keep_ref, got_ref, out_ref, sum_ref) = refs[-9:]
    grad = parts[0][...].astype(f32)
    for part in parts[1:]:
        grad = grad + part[...].astype(f32)
    x = x_ref[...].astype(f32)
    inverse = lax.rsqrt(jnp.mean(x * x, axis=-1, keepdims=True) + EPS)
    scaled = grad * gain_ref[...]
    inner_sum = jnp.mean(scaled * x, axis=-1, keepdims=True)
    high, rest = split_two(dv_ref[...])
    hidden_grad = cot_ref[...].astype(f32) + (dot(place_ref[...], high) + dot(place_ref[...], rest))
    out_ref[...] = (
        hidden_grad + inverse * scaled - x * (inverse * inverse * inverse * inner_sum)
    ).astype(bf16)
    sum_ref[...] = (keep_ref[...] + got_ref[...].astype(f32)).astype(bf16)


def spread_kernel(*refs):
    parts, out_ref = refs[:-1], refs[-1]
    head = lax.axis_index("head")
    part = parts[0].shape[0]
    for d in range(len(parts)):
        mine = pl.ds(pl.multiple_of((head ^ d) * part, part), part)
        out_ref[mine, :] = parts[d][...].astype(f32)


def swap(x, axis, d):
    size = lax.axis_size(axis)
    return lax.ppermute(x, axis, [(i, i ^ d) for i in range(size)])


def share(x, axis):
    return [x] + [swap(x, axis, d) for d in range(1, lax.axis_size(axis))]


def trade(pieces, axis):
    return lax.all_to_all(pieces, axis, split_axis=0, concat_axis=0, tiled=True)


def swap_all(pieces, axis):
    return [pieces[0]] + [swap(pieces[d], axis, d) for d in range(1, len(pieces))]


def bits_of(axis):
    return [b for b in (1 << i for i in range(16)) if b < lax.axis_size(axis)]


def scatter_sum(send, keep, after):
    rows, width = keep.shape
    bits = bits_of("seq")
    for bit in bits[1:]:
        send, keep = call(
            partial(halve_kernel, bit=bit),
            [shape_of(rows // 2, width, bf16), shape_of(rows // 2, width, f32)],
            (keep, swap(send, "seq", bit // 2)),
            scratch=[pltpu.VMEM((rows, width), f32)],
            name="halve",
            after=after,
        )
        rows //= 2
        after = ()
    return keep, swap(send, "seq", bits[-1])


def gather_rows(now, counts, after, later):
    rows, width = now.shape
    for bit in reversed(bits_of("seq")[1:]):
        rows *= 2
        (now,) = call(
            partial(pair_kernel, bit=bit),
            [shape_of(rows, width, bf16)],
            (now, swap(now, "seq", bit)),
            scratch=[pltpu.VMEM((rows, width), f32)],
            name="pair",
            after=after,
        )
        after, later = later, ()
    return call(
        partial(final_kernel, bit=1),
        [shape_of(n, width, f32) for n in counts],
        (now, swap(now, "seq", 1)),
        scratch=[pltpu.VMEM((2 * rows, width), f32)],
        name="weights_out",
    )


def sum_small(x, axes):
    for axis in axes:
        d = 1
        while d < lax.axis_size(axis):
            x = x + swap(x, axis, d)
            d *= 2
    return x


def on_device(
    layer_input, cotangent, norm1_gain, w_query, w_key, w_value, w_attn_out, bias_table,
    norm2_gain, w_router, w_expert_in, w_expert_out, expert_ids, slot_ids, buckets,
):
    tokens, width = layer_input.shape
    shards = lax.axis_size("seq")
    heads = lax.axis_size("head")
    bucket_count, count = bias_table.shape
    inner = w_query.shape[1]
    each = inner // count
    experts = w_router.shape[1]
    rows = experts * SLOT
    hidden_units = w_expert_in.shape[2]
    part = tokens // heads
    chunk = 2 * CAP // heads * shards
    piece_rows = chunk // shards
    span = 2 * tokens
    params = pltpu.CompilerParams(vmem_limit_bytes=VMEM_LIMIT)

    ids = expert_ids.reshape(1, tokens)
    slots = slot_ids.reshape(1, tokens)
    bucket_row = buckets.reshape(1, -1)
    wq_t, wk_t, wv_t = jnp.transpose(w_query), jnp.transpose(w_key), jnp.transpose(w_value)
    router_t, table_t = jnp.transpose(w_router), jnp.transpose(bias_table)
    w_in = w_expert_in.reshape(width, hidden_units)
    w_out = w_expert_out.reshape(hidden_units, width)

    quarter = CAP // heads
    place_in = np.arange(chunk)
    peer, turn = place_in // piece_rows, place_in % piece_rows
    is_grad = (turn >= quarter).astype(np.int32)
    tags = np.zeros((8, chunk), np.int32)
    tags[0], tags[1], tags[2] = peer, turn % quarter, is_grad
    base = np.stack([peer, is_grad * rows + turn % quarter], axis=1).astype(np.int32)

    w_mix = share(w_attn_out, "head")

    low, prob, att, att_t, att_sel = pl.pallas_call(
        attend_kernel,
        grid=(count,),
        out_shape=(
            shape_of(tokens, width, bf16),
            jax.ShapeDtypeStruct((count, tokens, tokens), bf16),
            jax.ShapeDtypeStruct((count, tokens, each), bf16),
            shape_of(inner, tokens, bf16),
            shape_of(rows // 2, 2 * inner, bf16),
        ),
        in_specs=[
            whole((tokens, width)), whole((width,)), whole((inner, width)), whole((inner, width)),
            whole((inner, width)), whole((count, bucket_count)), whole((1, span - 1)),
            whole((1, tokens)), whole((1, tokens)),
        ],
        out_specs=(
            whole((tokens, width)), by_head((1, tokens, tokens)), by_head((1, tokens, each)),
            whole((inner, tokens)), whole((rows // 2, 2 * inner)),
        ),
        scratch_shapes=[
            pltpu.VMEM((count, tokens, each), bf16),
            pltpu.VMEM((inner, tokens), bf16),
            pltpu.VMEM((count, tokens, each), bf16),
            pltpu.VMEM((8, span), f32),
            pltpu.VMEM((BLOCK, span), f32),
            pltpu.VMEM((rows, tokens), bf16),
        ],
        compiler_params=params,
        cost_estimate=NO_COST,
        name="attend",
    )(layer_input, norm1_gain, wq_t, wk_t, wv_t, table_t, bucket_row, ids, slots)

    sel_parts = share(att_sel, "head")
    sel_in, sel_up, place, place_c, x_c, cot_c = call(
        place_kernel,
        [
            shape_of(rows, width, bf16),
            shape_of(rows, width, bf16),
            shape_of(tokens, rows, bf16),
            shape_of(part, rows, bf16),
            shape_of(part, width, bf16),
            shape_of(part, width, bf16),
        ],
        (layer_input, cotangent, ids, slots),
        scratch=[pltpu.VMEM((tokens, rows), f32)],
        name="place",
        after=(att_sel,),
    )
    hidden_sel, normed_sel, probs, pay_pieces, att_on = call(
        partial(route_kernel, shards=shards, heads=heads),
        [
            shape_of(rows, width, f32),
            shape_of(rows, width, f32),
            shape_of(rows, experts, f32),
            jax.ShapeDtypeStruct((shards, SLOT, 2 * width + 128), bf16),
            shape_of(inner, tokens, bf16),
        ],
        tuple(sel_parts) + tuple(w_mix) + (sel_in, sel_up, norm2_gain, router_t, att_t),
        scratch=[
            pltpu.VMEM((heads, rows, inner), bf16),
            pltpu.VMEM((heads, inner, width), bf16),
        ],
        name="route",
    )
    pay_parts = trade(pay_pieces, "seq")
    att_parts = share(att_on, "head")

    dq0, dk0, dv0, offs, wout0, prob_sel, q_sel, k_rows, v_t = pl.pallas_call(
        masked_back_kernel,
        grid=(count,),
        out_shape=(
            jax.ShapeDtypeStruct((count, tokens, each), f32),
            shape_of(inner, tokens, f32),
            shape_of(inner, tokens, f32),
            jax.ShapeDtypeStruct((count, 8, span), f32),
            shape_of(inner, width, f32),
            jax.ShapeDtypeStruct((count, rows, tokens), bf16),
            shape_of(inner, rows, bf16),
            jax.ShapeDtypeStruct((count, tokens, each), bf16),
            shape_of(inner, tokens, bf16),
        ),
        in_specs=[
            whole((tokens, width)), whole((inner, width)), whole((inner, width)),
            whole((inner, width)), whole((inner, width)), whole((tokens, width)),
            whole((tokens, rows)), by_head((1, tokens, each)), by_head((1, tokens, tokens)),
            whole((inner, tokens)), spec(pl.ANY),
        ],
        out_specs=(
            by_head((1, tokens, each)), by_head((each, tokens)), by_head((each, tokens)),
            by_head((1, 8, span)), whole((inner, width)), by_head((1, rows, tokens)),
            whole((inner, rows)), whole((count, tokens, each)), whole((inner, tokens)),
        ),
        scratch_shapes=[
            pltpu.VMEM((count, tokens, each), bf16),
            pltpu.VMEM((inner, tokens), bf16),
            pltpu.VMEM((inner, tokens), bf16),
            pltpu.VMEM((tokens, width), bf16),
            pltpu.VMEM((BLOCK, span), f32),
            pltpu.VMEM((tokens, tokens), bf16),
            pltpu.VMEM((each + rows, tokens), bf16),
        ],
        compiler_params=params,
        cost_estimate=NO_COST,
        name="masked_back",
    )(cotangent, w_attn_out, wq_t, wk_t, wv_t, low, place, att, prob, att_t, pay_pieces)

    done = call(
        partial(expert_kernel, heads=heads),
        [shape_of(chunk, width, bf16)] * heads
        + [
            shape_of(rows, width, bf16),
            shape_of(rows, hidden_units, bf16),
            shape_of(rows, hidden_units, bf16),
            shape_of(rows, width, bf16),
        ],
        (pay_parts, w_in, w_out, jnp.asarray(base)),
        scratch=[pltpu.VMEM((2 * rows, width), bf16)],
        name="expert",
        after=(dq0,) + tuple(att_parts[1:]),
    )
    x_rows, act, pre_low, out_low = done[heads:]
    w_in_grad, w_out_grad = call(
        expert_grad_kernel,
        [
            jax.ShapeDtypeStruct(w_expert_in.shape, f32),
            jax.ShapeDtypeStruct(w_expert_out.shape, f32),
        ],
        (x_rows, pre_low, act, out_low),
        name="expert_grad",
        moved=12 * 2**20,
    )
    returned = call(
        partial(sum_kernel, heads=heads),
        [shape_of(piece_rows, width, bf16)] * shards,
        swap_all(done[:heads], "head"),
        scratch=[pltpu.VMEM((chunk, width), f32)],
        name="sum",
        after=(w_in_grad,),
    )
    (joined,) = call(
        join_kernel,
        [shape_of(chunk, width, bf16)],
        swap_all(returned, "seq"),
        scratch=[pltpu.VMEM((chunk, width), f32)],
        name="join",
    )
    full_parts = share(joined, "head")

    (hidden,) = call(
        partial(hidden_kernel, heads=heads),
        [shape_of(tokens, width, f32)],
        tuple(att_parts) + tuple(w_mix) + (layer_input,),
        scratch=[
            pltpu.VMEM((heads * inner, tokens), bf16),
            pltpu.VMEM((heads * inner, width), bf16),
        ],
        name="hidden",
        after=(joined,),
        moved=16 * 2**20,
    )

    small_rows = 8 + -(-experts // 8) * 8
    dv_sel, comb_sel, small, wout_part, gh_sel, ght_sel, delta_sel = call(
        partial(slot_back_kernel, heads=heads),
        [
            shape_of(rows, width, f32),
            shape_of(rows, width, f32),
            shape_of(small_rows, width, f32),
            shape_of(inner, width, f32),
            jax.ShapeDtypeStruct((count, rows, each), bf16),
            shape_of(inner, rows, bf16),
            jax.ShapeDtypeStruct((count, rows, 1), f32),
        ],
        tuple(full_parts)
        + (jnp.asarray(tags), sel_up, normed_sel, hidden_sel, probs, router_t, norm2_gain)
        + (w_attn_out, att_sel, wout0),
        name="slot_back",
        after=(hidden,),
    )

    back = call(
        partial(sparse_back_kernel, heads=heads),
        [shape_of(part, width, bf16)] * heads
        + [
            jax.ShapeDtypeStruct((count, rows, tokens), bf16),
            shape_of(2 * inner, width, bf16),
            shape_of(2 * inner, width, f32),
            shape_of(small_rows, width, f32),
        ],
        (gh_sel, ght_sel, delta_sel, v_t, k_rows, q_sel, prob_sel, dq0, dk0, dv0, place)
        + (wq_t, wk_t, wv_t, low, norm1_gain, small, wout_part),
        scratch=[
            pltpu.VMEM((rows, inner), f32),
            pltpu.VMEM((tokens, inner), bf16),
            pltpu.VMEM((tokens, inner), bf16),
            pltpu.VMEM((tokens, inner), bf16),
            pltpu.VMEM((inner, tokens), bf16),
            pltpu.VMEM((inner, tokens), bf16),
            pltpu.VMEM((4 * inner, width), f32),
        ],
        name="sparse_back",
    )
    score_sel, send, keep, small = back[heads:]
    first_parts = swap_all(back[:heads], "head")
    (small,) = call(
        partial(bias_grad_kernel, bucket_count=bucket_count),
        [shape_of(small_rows, width, f32)],
        (score_sel, place, offs, bucket_row, small),
        scratch=[pltpu.VMEM((BLOCK, span), f32)],
        name="bias_grad",
        moved=20 * 2**20,
    )
    small_sum = sum_small(small, ("seq",))
    gain1_sum = sum_small(small_sum[1:2], ("head",))
    keep, got = scatter_sum(send, keep, tuple(first_parts[1:-1]) + (small,))

    grad_part, weights = call(
        first_norm_kernel,
        [shape_of(part, width, bf16), shape_of(keep.shape[0], width, bf16)],
        tuple(first_parts) + (x_c, cot_c, place_c, dv_sel, norm1_gain, keep, got),
        name="first_norm",
    )
    grad_parts = share(grad_part, "head")
    (layer_output,) = call(
        output_kernel,
        [shape_of(tokens, width, f32)],
        (hidden, place, comb_sel),
        name="output",
        after=(grad_part,),
        moved=16 * 2**20,
    )
    weight_sums = gather_rows(
        weights, [inner] * 4, tuple(grad_parts[1:-1]) + (layer_output,), tuple(grad_parts[-1:])
    )
    (input_grad,) = call(
        spread_kernel,
        [shape_of(tokens, width, f32)],
        tuple(grad_parts),
        name="spread",
    )

    return (
        layer_output,
        input_grad,
        gain1_sum[0],
        jnp.transpose(weight_sums[0]),
        jnp.transpose(weight_sums[1]),
        jnp.transpose(weight_sums[2]),
        weight_sums[3],
        jnp.transpose(small_sum[2 : 2 + count, :bucket_count]),
        small_sum[0],
        jnp.transpose(small_sum[8 : 8 + experts]),
        w_in_grad,
        w_out_grad,
    )


def solution(mesh):
    return jax.shard_map(
        on_device,
        mesh=mesh,
        in_specs=(
            P("seq", None),
            P("seq", None),
            P(),
            P(None, "head"),
            P(None, "head"),
            P(None, "head"),
            P("head", None),
            P(None, "head"),
            P(),
            P(),
            P("seq", None, "head"),
            P("seq", "head", None),
            P("seq"),
            P("seq"),
            P(),
        ),
        out_specs=(
            P("seq", None),
            P("seq", None),
            P(),
            P(None, "head"),
            P(None, "head"),
            P(None, "head"),
            P("head", None),
            P(None, "head"),
            P(),
            P(),
            P("seq", None, "head"),
            P("seq", "head", None),
        ),
        check_vma=False,
    )
```

```python
from functools import partial

import jax
import jax.numpy as jnp
import numpy as np
from jax import lax
from jax.experimental import pallas as pl
from jax.experimental.pallas import tpu as pltpu
from jax.sharding import PartitionSpec as P

CAP = 20
SLOT = 24
EPS = 1e-06
BLOCK = 128
VMEM_LIMIT = 26 * 1024 * 1024
VMEM_ALL = 60 * 1024 * 1024
NO_COST = pl.CostEstimate(flops=1, bytes_accessed=1, transcendentals=0)

f32 = jnp.float32
bf16 = jnp.bfloat16
highest = lax.Precision.HIGHEST


def dot(a, b):
    return jnp.dot(a, b, preferred_element_type=f32)


def dot_nt(a, b, precision=None):
    return lax.dot_general(
        a, b, (((1,), (1,)), ((), ())), precision=precision, preferred_element_type=f32
    )


def dot_tn(a, b, precision=None):
    return lax.dot_general(
        a, b, (((0,), (0,)), ((), ())), precision=precision, preferred_element_type=f32
    )


def iota(shape, dim):
    return lax.broadcasted_iota(jnp.int32, shape, dim)


def split_two(v):
    high = v.astype(bf16)
    return high, (v - high.astype(f32)).astype(bf16)


def shape_of(rows, cols, dtype):
    return jax.ShapeDtypeStruct((rows, cols), dtype)


def spec(memory):
    return pl.BlockSpec(memory_space=memory)


def call(kernel, outs, args, scratch=(), name=None, after=(), moved=1):
    outs, args = tuple(outs), tuple(args)
    held = sum(int(np.prod(a.shape)) * np.dtype(a.dtype).itemsize for a in args + outs)

    def body(*refs):
        kernel(*refs[: len(args)], *refs[len(args) + len(after) :])

    return pl.pallas_call(
        body,
        out_shape=outs,
        in_specs=[spec(pltpu.VMEM)] * len(args) + [spec(pl.ANY)] * len(after),
        out_specs=tuple(spec(pltpu.VMEM) for _ in outs),
        scratch_shapes=list(scratch),
        compiler_params=pltpu.CompilerParams(
            vmem_limit_bytes=VMEM_LIMIT if 2 * held < VMEM_LIMIT else VMEM_ALL
        ),
        cost_estimate=pl.CostEstimate(flops=1, bytes_accessed=moved, transcendentals=0),
        name=name,
    )(*args, *after)


def whole(shape):
    return pl.BlockSpec(shape, lambda h: (0,) * len(shape))


def by_head(shape):
    return pl.BlockSpec(shape, lambda h: (h,) + (0,) * (len(shape) - 1))


def slot_rows(ids, slots, rows):
    cell = jnp.where(slots < CAP, ids * SLOT + slots, -1)
    return (iota((rows, cell.shape[1]), 0) == cell).astype(f32)


def place_kernel(
    x_ref, cot_ref, ids_ref, slots_ref, sel_in, sel_up, place, place_c, x_c, cot_c, place_s
):
    head = lax.axis_index("head")
    part = x_c.shape[0]
    slot_hot = slot_rows(ids_ref[...], slots_ref[...], sel_in.shape[0])
    place_s[...] = jnp.transpose(slot_hot)
    slot_low = slot_hot.astype(bf16)
    sel_in[...] = dot(slot_low, x_ref[...]).astype(bf16)
    sel_up[...] = dot(slot_low, cot_ref[...]).astype(bf16)
    place[...] = place_s[...].astype(bf16)
    mine = pl.ds(pl.multiple_of(head * part, part), part)
    place_c[...] = place_s[mine, :].astype(bf16)
    x_c[...] = x_ref[mine, :]
    cot_c[...] = cot_ref[mine, :]


def attend_kernel(*refs):
    given, refs = refs[:9], refs[9:]
    low_ref, prob_ref, att_ref, attt_ref, sel_ref = refs[:5]
    q_s, kt_s, v_s, bias_s, skew_s, slot_s = refs[5:11]
    here, sems = refs[11:20], refs[20]
    x_ref, gain_ref, wq_ref, wk_ref, wv_ref, table_ref, buckets_ref, ids_ref, slots_ref = here
    copies = [
        pltpu.make_async_copy(far, near, sems.at[i])
        for i, (far, near) in enumerate(zip(given, here))
    ]
    step = pl.program_id(0)
    tokens = x_ref.shape[0]
    inner = wq_ref.shape[0]
    count = q_s.shape[0]
    width = inner // count

    @pl.when(step == 0)
    def _():
        for copy in copies:
            copy.start()
        for copy in copies:
            copy.wait()
        for i in range(0, tokens, 256):
            rows = pl.ds(i, 256)
            x = x_ref[rows, :].astype(f32)
            inverse = lax.rsqrt(jnp.mean(x * x, axis=-1, keepdims=True) + EPS)
            low_ref[rows, :] = (x * inverse * gain_ref[...]).astype(bf16)
        low = low_ref[...]
        q = dot_nt(low, wq_ref[...]).astype(bf16) * bf16(width ** (-0.5))
        kt_s[...] = dot_nt(wk_ref[...], low).astype(bf16)
        v = dot_nt(low, wv_ref[...]).astype(bf16)
        for h in range(count):
            cols = slice(h * width, (h + 1) * width)
            q_s[h] = q[:, cols]
            v_s[h] = v[:, cols]
        offsets = buckets_ref.shape[1]
        bucket_hot = (iota((table_ref.shape[1], offsets), 0) == buckets_ref[...]).astype(f32)
        slot_s[...] = slot_rows(ids_ref[...], slots_ref[...], slot_s.shape[0]).astype(bf16)
        bias_s[...] = jnp.zeros_like(bias_s)
        bias_s[:count, :offsets] = jnp.dot(
            table_ref[...], bucket_hot, precision=highest, preferred_element_type=f32
        )

    span = skew_s.shape[1]
    row = bias_s[pl.ds(step, 1), :]
    skew_s[...] = pltpu.roll(
        jnp.broadcast_to(row, skew_s.shape), span - (BLOCK - 1), 1, stride=1, stride_axis=0
    )
    head_rows = pl.ds(pl.multiple_of(step * width, width), width)
    for i in range(0, tokens, 2 * BLOCK):
        scores = dot(q_s[step, pl.ds(i, 2 * BLOCK), :], kt_s[head_rows, :])
        for j in range(2):
            start = i + j * BLOCK
            first = tokens - BLOCK - start
            score = scores[j * BLOCK : (j + 1) * BLOCK] + skew_s[:, first : first + tokens]
            top = jnp.max(score, axis=-1, keepdims=True)
            weight = jnp.exp(score - top)
            total = jnp.sum(weight, axis=-1, keepdims=True)
            prob_ref[0, pl.ds(start, BLOCK), :] = (weight * (1.0 / total)).astype(bf16)
    att = dot(prob_ref[0], v_s[step])
    att_low = att.astype(bf16)
    att_ref[0] = att_low
    attt_ref[head_rows, :] = jnp.transpose(att).astype(bf16)
    picked = dot(slot_s[...], att_low).astype(bf16)
    half = sel_ref.shape[0]
    for h in range(count):

        @pl.when(step == h)
        def _():
            for part in range(2):
                start = part * inner + h * width
                sel_ref[:, start : start + width] = picked[part * half : (part + 1) * half]


def route_kernel(*refs, shards, heads):
    att_parts = refs[:heads]
    w_parts = refs[heads : 2 * heads]
    (sel_in, sel_up, gain_ref, router_ref, att_t, hidden_ref, normed_ref, probs_ref, pieces,
     att_on) = refs[2 * heads : 2 * heads + 10]
    att_s, w_s = refs[2 * heads + 10 :]
    head = lax.axis_index("head")
    inner = w_parts[0].shape[0]
    half = att_parts[0].shape[0]
    for d in range(heads):
        att_s[d, 0:half, :] = att_parts[d][:, 0:inner]
        att_s[d, half : 2 * half, :] = att_parts[d][:, inner : 2 * inner]
        w_s[d] = w_parts[d][...]
    mixed = None
    for k in range(heads):
        term = dot(att_s[head ^ k], w_s[head ^ k])
        mixed = term if mixed is None else mixed + term
    hidden = sel_in[...].astype(f32) + mixed
    hidden_ref[...] = hidden
    inverse = lax.rsqrt(jnp.mean(hidden * hidden, axis=-1, keepdims=True) + EPS)
    normed = hidden * inverse * gain_ref[...]
    normed_ref[...] = normed
    logits = dot_nt(normed, router_ref[...], highest)
    logits = logits - jnp.max(logits, axis=-1, keepdims=True)
    powers = jnp.exp(logits)
    probs = powers / jnp.sum(powers, axis=-1, keepdims=True)
    probs_ref[...] = probs
    gate = jnp.sum(jnp.where(chosen_of(probs.shape), probs, 0.0), axis=-1, keepdims=True)
    high = gate.astype(bf16).astype(f32)
    lane = iota((gate.shape[0], 128), 1)
    width = normed.shape[1]
    extra = jnp.where(lane == 0, high, jnp.where(lane == 1, gate - high, 0.0))
    pieces[:, :, :width] = normed.reshape(shards, SLOT, width).astype(bf16)
    pieces[:, :, width : 2 * width] = (
        sel_up[...].astype(f32).reshape(shards, SLOT, width).astype(bf16)
    )
    pieces[:, :, 2 * width :] = extra.reshape(shards, SLOT, 128).astype(bf16)
    att_on[...] = att_t[...]


def chosen_of(shape):
    expert = iota(shape, 1) * SLOT
    slot_row = iota(shape, 0)
    return (slot_row >= expert) & (slot_row < expert + SLOT)


def expert_kernel(pay_ref, w_in, w_out, pieces, x_ref, act_ref, pre_ref, out_ref, *, heads):
    rows, width = x_ref.shape
    pay = pay_ref[...].astype(f32).reshape(rows, pay_ref.shape[2])
    x = pay[:, :width].astype(bf16)
    up = pay[:, width : 2 * width]
    gate = pay[:, 2 * width : 2 * width + 1] + pay[:, 2 * width + 1 : 2 * width + 2]
    out_low = (gate * up).astype(bf16)
    pre = dot(x, w_in[...])
    cdf = 0.5 * (1.0 + lax.erf(pre * (0.5**0.5)))
    act = (pre * cdf).astype(bf16)
    slope = cdf + pre * jnp.exp(-0.5 * pre * pre) * ((2.0 * np.pi) ** (-0.5))
    pre_low = (dot_nt(out_low, w_out[...]) * slope).astype(bf16)
    both = (dot(act, w_out[...]), dot_nt(pre_low, w_in[...]))
    shards, part = rows // SLOT, pieces.shape[2]
    for k in range(heads):
        start = k % (heads // 2) * part
        piece = both[k // (heads // 2)][:, start : start + part]
        pieces[k * shards : (k + 1) * shards] = piece.reshape(shards, SLOT, part).astype(bf16)
    pre_ref[...] = pre_low
    out_ref[...] = out_low
    x_ref[...] = x
    act_ref[...] = act


def expert_grad_kernel(x_ref, pre_ref, act_ref, out_ref, in_grad, out_grad):
    in_grad[0] = dot_tn(x_ref[...], pre_ref[...])
    out_grad[0] = dot_tn(act_ref[...], out_ref[...])


def sum_kernel(parts, out_ref, *, heads):
    shards = parts.shape[0] // heads
    total = parts[0:shards].astype(f32)
    for k in range(1, heads):
        total = total + parts[k * shards : (k + 1) * shards].astype(f32)
    out_ref[...] = total.reshape(out_ref.shape).astype(bf16)


def masked_back_kernel(
    cot_ref, w_ref, wq_ref, wk_ref, wv_ref, low_ref, place_ref, att_ref, prob_ref, attt_ref, _,
    dq_ref, dkt_ref, dvt_ref, offs_ref, wout_ref, psel_ref, qsel_ref, k_ref, vt_ref,
    gh_s, ght_s, qt_s, mcot_s, acc_s, score_s, stack_s,
):
    step = pl.program_id(0)
    count, tokens, width = gh_s.shape
    rows_all = place_ref.shape[1]

    @pl.when(step == 0)
    def _():
        for i in range(0, tokens, 256):
            rows = pl.ds(i, 256)
            where = place_ref[rows, :].astype(f32)
            free = 1.0 - jnp.sum(where, axis=-1, keepdims=True)
            mcot_s[rows, :] = (cot_ref[rows, :].astype(f32) * free).astype(bf16)
            stack_s[width:, rows] = jnp.transpose(where).astype(bf16)
        gh = dot_nt(mcot_s[...], w_ref[...]).astype(bf16)
        ght_s[...] = dot_nt(w_ref[...], mcot_s[...]).astype(bf16)
        k = dot_nt(low_ref[...], wk_ref[...]).astype(bf16)
        qt_s[...] = dot_nt(wq_ref[...], low_ref[...]).astype(bf16) * bf16(width ** (-0.5))
        vt_ref[...] = dot_nt(wv_ref[...], low_ref[...]).astype(bf16)
        for h in range(count):
            cols = slice(h * width, (h + 1) * width)
            gh_s[h] = gh[:, cols]
            k_ref[h] = k[:, cols]
        wout_ref[...] = dot(attt_ref[...], mcot_s[...])
        qsel_ref[...] = dot(qt_s[...], place_ref[...]).astype(bf16)

    acc_s[...] = jnp.zeros_like(acc_s)
    head_rows = pl.ds(pl.multiple_of(step * width, width), width)
    stack_s[0:width, :] = ght_s[head_rows, :]
    for i in range(0, tokens, 2 * BLOCK):
        rows = pl.ds(i, 2 * BLOCK)
        gh = gh_s[step, rows, :]
        delta = jnp.sum(gh.astype(f32) * att_ref[0, rows, :].astype(f32), axis=-1, keepdims=True)
        grads = dot(gh, vt_ref[head_rows, :]) - delta
        for j in range(2):
            start = i + j * BLOCK
            first = tokens - BLOCK - start
            here = pl.ds(start, BLOCK)
            score = prob_ref[0, here, :].astype(f32) * grads[j * BLOCK : (j + 1) * BLOCK]
            acc_s[:, first : first + tokens] += score
            score_s[here, :] = score.astype(bf16)
    dq_ref[0] = dot(score_s[...], k_ref[step]) * (width ** (-0.5))
    dkt_ref[...] = dot(qt_s[head_rows, :], score_s[...])
    both = dot(stack_s[...], prob_ref[0])
    dvt_ref[...] = both[:width]
    psel_ref[0] = both[width:].astype(bf16)
    offs_ref[0] = diagonals(acc_s[...])


def diagonals(acc):
    span = acc.shape[1]
    rows = acc.shape[0] // 2
    while rows >= 8:
        acc = acc[:rows] + pltpu.roll(acc[rows:], span - rows, 1)
        rows //= 2
    total = acc[0:1]
    for r in range(1, 8):
        total = total + pltpu.roll(acc[r : r + 1], span - r, 1)
    return jnp.broadcast_to(pltpu.roll(total, BLOCK - 1, 1), (8, span))


def slot_back_kernel(*refs, heads):
    parts = refs[:heads]
    (up_ref, normed_ref, hidden_ref, probs_ref, router_ref, gain_ref, w_ref, att_ref,
     wout0_ref) = refs[heads : heads + 9]
    dv_ref, comb_ref, small_ref, wout_ref, gh_ref, ght_ref, delta_ref, ret_s = refs[heads + 9 :]
    head = lax.axis_index("head")
    for d in range(heads):
        ret_s[head ^ d] = parts[d][...]
    back = [ret_s[k].astype(f32) for k in range(heads)]
    combined = jnp.concatenate(back[: heads // 2], axis=1)
    grad_buf = jnp.concatenate(back[heads // 2 :], axis=1)
    up = up_ref[...].astype(f32)
    hidden, normed, probs, gain = hidden_ref[...], normed_ref[...], probs_ref[...], gain_ref[...]
    chosen = chosen_of(probs.shape)
    gate = jnp.sum(jnp.where(chosen, probs, 0.0), axis=-1, keepdims=True)
    comb_ref[...] = gate * combined
    gate_grad = jnp.sum(up * combined, axis=-1, keepdims=True)
    marked = jnp.where(chosen, gate_grad, 0.0)
    logit_grad = probs * (marked - jnp.sum(marked * probs, axis=-1, keepdims=True))
    experts = probs.shape[1]
    grad = grad_buf + jnp.dot(
        logit_grad, router_ref[...], precision=highest, preferred_element_type=f32
    )
    inverse = lax.rsqrt(jnp.mean(hidden * hidden, axis=-1, keepdims=True) + EPS)
    scaled = grad * gain
    inner_sum = jnp.mean(scaled * hidden, axis=-1, keepdims=True)
    dv = inverse * scaled - hidden * (inverse * inverse * inverse * inner_sum)
    dv_ref[...] = dv
    small_ref[...] = jnp.zeros_like(small_ref)
    small_ref[0:1, :] = jnp.sum(grad * hidden * inverse, axis=0, keepdims=True)
    small_ref[8 : 8 + experts, :] = dot_tn(logit_grad, normed, highest)
    grad_low = (up + dv).astype(bf16)
    half = att_ref.shape[0]
    inner = w_ref.shape[0]
    att = jnp.concatenate(
        [att_ref[:, 0:inner].astype(f32), att_ref[:, inner : 2 * inner].astype(f32)], axis=0
    )
    wout_ref[...] = wout0_ref[...] + dot_tn(att.astype(bf16), grad_low)
    gh = dot_nt(grad_low, w_ref[...])
    gh_low = gh.astype(bf16)
    count = gh_ref.shape[0]
    each = inner // count
    ght_ref[...] = dot_nt(w_ref[...], grad_low).astype(bf16)
    for h in range(count):
        cols = slice(h * each, (h + 1) * each)
        gh_ref[h] = gh_low[:, cols]
        delta_ref[h] = jnp.sum(
            gh_low[:, cols].astype(f32) * att[:, cols], axis=-1, keepdims=True
        )


def sparse_back_kernel(
    gh_ref, ght_ref, delta_ref, vt_ref, k_ref, qsel_ref, psel_ref, dq0_ref, dkt0_ref, dvt0_ref,
    place_ref, wq_ref, wk_ref, wv_ref, low_ref, gain_ref, small_ref, wout_ref, *refs, heads,
):
    chunks = refs[:heads]
    (score_ref, send_ref, keep_ref, out_ref,
     dq_s, q_low, k_low, v_low, kt_s, vt_s, all_s) = refs[heads:]
    head = lax.axis_index("head")
    count, rows, width = gh_ref.shape
    tokens = vt_ref.shape[1]
    inner = count * width
    for h in range(count):
        cols = slice(h * width, (h + 1) * width)
        grad = dot(gh_ref[h], vt_ref[cols, :])
        prob = psel_ref[h]
        score = (prob.astype(f32) * (grad - delta_ref[h])).astype(bf16)
        score_ref[h] = score
        dq_s[:, cols] = dot(score, k_ref[h]) * (width ** (-0.5))
        dkt = dkt0_ref[cols, :] + dot(qsel_ref[cols, :], score)
        dvt = dvt0_ref[cols, :] + dot(ght_ref[cols, :], prob)
        kt_s[cols, :] = dkt.astype(bf16)
        vt_s[cols, :] = dvt.astype(bf16)
        k_low[:, cols] = jnp.transpose(dkt).astype(bf16)
        v_low[:, cols] = jnp.transpose(dvt).astype(bf16)
    spread = dot(place_ref[...], dq_s[...].astype(bf16))
    for h in range(count):
        cols = slice(h * width, (h + 1) * width)
        q_low[:, cols] = (spread[:, cols] + dq0_ref[h]).astype(bf16)
    part = tokens // heads
    for d in range(heads):
        mine = pl.ds(pl.multiple_of((head ^ d) * part, part), part)
        chunks[d][...] = (
            dot(q_low[mine, :], wq_ref[...])
            + dot(k_low[mine, :], wk_ref[...])
            + dot(v_low[mine, :], wv_ref[...])
        ).astype(bf16)
    low = low_ref[...]
    total = None
    grads = (dot_tn(q_low[...], low), dot(kt_s[...], low), dot(vt_s[...], low))
    for i, (grad, w) in enumerate(zip(grads, (wq_ref, wk_ref, wv_ref))):
        all_s[i * inner : (i + 1) * inner, :] = grad
        term = jnp.sum(grad * w[...].astype(f32), axis=0, keepdims=True)
        total = term if total is None else total + term
    all_s[3 * inner :, :] = wout_ref[...]
    out_ref[...] = small_ref[...]
    out_ref[1:2, :] = total / gain_ref[...]
    split_rows(all_s, 1, send_ref, keep_ref)


def is_upper(bit):
    return (lax.axis_index("seq") & bit) != 0


def split_rows(all_s, bit, send_ref, keep_ref):
    half = send_ref.shape[0]
    low, high = all_s[0:half, :], all_s[half : 2 * half, :]
    keep_ref[...] = jnp.where(is_upper(bit), high, low)
    send_ref[...] = jnp.where(is_upper(bit), low, high).astype(bf16)


def halve_kernel(keep_ref, got_ref, send_ref, out_ref, all_s, *, bit):
    all_s[...] = keep_ref[...] + got_ref[...].astype(f32)
    split_rows(all_s, bit, send_ref, out_ref)


def join_rows(mine_ref, got_ref, all_s, bit):
    half = mine_ref.shape[0]
    mine, got = mine_ref[...].astype(f32), got_ref[...].astype(f32)
    all_s[0:half, :] = jnp.where(is_upper(bit), got, mine)
    all_s[half : 2 * half, :] = jnp.where(is_upper(bit), mine, got)


def pair_kernel(mine_ref, got_ref, out_ref, all_s, *, bit):
    join_rows(mine_ref, got_ref, all_s, bit)
    out_ref[...] = all_s[...].astype(bf16)


def final_kernel(mine_ref, got_ref, *refs, bit):
    outs, all_s = refs[:-1], refs[-1]
    join_rows(mine_ref, got_ref, all_s, bit)
    inner = outs[0].shape[0]
    for i, out in enumerate(outs):
        out[...] = all_s[i * inner : (i + 1) * inner, :]


def bias_grad_kernel(
    score_ref, place_ref, offs_ref, buckets_ref, small_ref, out_ref, acc_s, *, bucket_count
):
    count = score_ref.shape[0]
    tokens = place_ref.shape[0]
    offsets = buckets_ref.shape[1]
    out_ref[...] = small_ref[...]
    bucket_hot = (iota((bucket_count, offsets), 0) == buckets_ref[...]).astype(f32)
    for h in range(count):
        acc_s[...] = jnp.zeros_like(acc_s)
        for i in range(0, tokens, BLOCK):
            first = tokens - BLOCK - i
            acc_s[:, first : first + tokens] += dot(place_ref[i : i + BLOCK, :], score_ref[h])
        sums = diagonals(acc_s[...]) + offs_ref[h]
        out_ref[2 + h : 3 + h, :bucket_count] = dot_nt(sums[:, :offsets], bucket_hot, highest)[0:1]


def hidden_kernel(*refs, heads):
    att_parts, w_parts = refs[:heads], refs[heads : 2 * heads]
    x_ref, out_ref, att_s, w_s = refs[2 * heads :]
    head = lax.axis_index("head")
    tokens = x_ref.shape[0]
    inner = w_parts[0].shape[0]
    for d in range(heads):
        mine = pl.ds(pl.multiple_of((head ^ d) * inner, inner), inner)
        att_s[mine, :] = att_parts[d][...]
        w_s[mine, :] = w_parts[d][...]
    for i in range(0, tokens, 256):
        rows = pl.ds(i, 256)
        out_ref[rows, :] = x_ref[rows, :].astype(f32) + dot_tn(att_s[:, rows], w_s[...])


def output_kernel(hidden_ref, place_ref, comb_ref, out_ref):
    high, rest = split_two(comb_ref[...])
    for i in range(0, hidden_ref.shape[0], 256):
        rows = pl.ds(i, 256)
        where = place_ref[rows, :]
        out_ref[rows, :] = hidden_ref[rows, :] + (dot(where, high) + dot(where, rest))


def first_norm_kernel(*refs):
    parts = refs[:-9]
    (x_ref, cot_ref, place_ref, dv_ref, gain_ref, keep_ref, got_ref, out_ref, sum_ref) = refs[-9:]
    grad = parts[0][...].astype(f32)
    for part in parts[1:]:
        grad = grad + part[...].astype(f32)
    x = x_ref[...].astype(f32)
    inverse = lax.rsqrt(jnp.mean(x * x, axis=-1, keepdims=True) + EPS)
    scaled = grad * gain_ref[...]
    inner_sum = jnp.mean(scaled * x, axis=-1, keepdims=True)
    high, rest = split_two(dv_ref[...])
    hidden_grad = cot_ref[...].astype(f32) + (dot(place_ref[...], high) + dot(place_ref[...], rest))
    out_ref[...] = (
        hidden_grad + inverse * scaled - x * (inverse * inverse * inverse * inner_sum)
    ).astype(bf16)
    sum_ref[...] = (keep_ref[...] + got_ref[...].astype(f32)).astype(bf16)


def spread_kernel(*refs):
    parts, out_ref = refs[:-1], refs[-1]
    head = lax.axis_index("head")
    part = parts[0].shape[0]
    for d in range(len(parts)):
        mine = pl.ds(pl.multiple_of((head ^ d) * part, part), part)
        out_ref[mine, :] = parts[d][...].astype(f32)


def swap(x, axis, d):
    size = lax.axis_size(axis)
    return lax.ppermute(x, axis, [(i, i ^ d) for i in range(size)])


def share(x, axis):
    return [x] + [swap(x, axis, d) for d in range(1, lax.axis_size(axis))]


def trade(pieces, axis):
    return lax.all_to_all(pieces, axis, split_axis=0, concat_axis=0, tiled=True)


def swap_all(pieces, axis):
    return [pieces[0]] + [swap(pieces[d], axis, d) for d in range(1, len(pieces))]


def bits_of(axis):
    return [b for b in (1 << i for i in range(16)) if b < lax.axis_size(axis)]


def scatter_sum(send, keep, after):
    rows, width = keep.shape
    bits = bits_of("seq")
    for bit in bits[1:]:
        send, keep = call(
            partial(halve_kernel, bit=bit),
            [shape_of(rows // 2, width, bf16), shape_of(rows // 2, width, f32)],
            (keep, swap(send, "seq", bit // 2)),
            scratch=[pltpu.VMEM((rows, width), f32)],
            name="halve",
            after=after,
        )
        rows //= 2
        after = ()
    return keep, swap(send, "seq", bits[-1])


def gather_rows(now, counts, after, later):
    rows, width = now.shape
    for bit in reversed(bits_of("seq")[1:]):
        rows *= 2
        (now,) = call(
            partial(pair_kernel, bit=bit),
            [shape_of(rows, width, bf16)],
            (now, swap(now, "seq", bit)),
            scratch=[pltpu.VMEM((rows, width), f32)],
            name="pair",
            after=after,
        )
        after, later = later, ()
    return call(
        partial(final_kernel, bit=1),
        [shape_of(n, width, f32) for n in counts],
        (now, swap(now, "seq", 1)),
        scratch=[pltpu.VMEM((2 * rows, width), f32)],
        name="weights_out",
    )


def sum_small(x, axes):
    for axis in axes:
        d = 1
        while d < lax.axis_size(axis):
            x = x + swap(x, axis, d)
            d *= 2
    return x


def on_device(
    layer_input, cotangent, norm1_gain, w_query, w_key, w_value, w_attn_out, bias_table,
    norm2_gain, w_router, w_expert_in, w_expert_out, expert_ids, slot_ids, buckets,
):
    tokens, width = layer_input.shape
    shards = lax.axis_size("seq")
    heads = lax.axis_size("head")
    bucket_count, count = bias_table.shape
    inner = w_query.shape[1]
    each = inner // count
    experts = w_router.shape[1]
    rows = experts * SLOT
    hidden_units = w_expert_in.shape[2]
    part = tokens // heads
    split = 2 * width // heads
    span = 2 * tokens
    params = pltpu.CompilerParams(vmem_limit_bytes=VMEM_LIMIT if rows <= 256 else VMEM_ALL)

    ids = expert_ids.reshape(1, tokens)
    slots = slot_ids.reshape(1, tokens)
    bucket_row = buckets.reshape(1, -1)
    wq_t, wk_t, wv_t = jnp.transpose(w_query), jnp.transpose(w_key), jnp.transpose(w_value)
    router_t, table_t = jnp.transpose(w_router), jnp.transpose(bias_table)
    w_in = w_expert_in.reshape(width, hidden_units)
    w_out = w_expert_out.reshape(hidden_units, width)

    w_mix = share(w_attn_out, "head")

    low, prob, att, att_t, att_sel = pl.pallas_call(
        attend_kernel,
        grid=(count,),
        out_shape=(
            shape_of(tokens, width, bf16),
            jax.ShapeDtypeStruct((count, tokens, tokens), bf16),
            jax.ShapeDtypeStruct((count, tokens, each), bf16),
            shape_of(inner, tokens, bf16),
            shape_of(rows // 2, 2 * inner, bf16),
        ),
        in_specs=[spec(pltpu.HBM)] * 9,
        out_specs=(
            whole((tokens, width)), by_head((1, tokens, tokens)), by_head((1, tokens, each)),
            whole((inner, tokens)), whole((rows // 2, 2 * inner)),
        ),
        scratch_shapes=[
            pltpu.VMEM((count, tokens, each), bf16),
            pltpu.VMEM((inner, tokens), bf16),
            pltpu.VMEM((count, tokens, each), bf16),
            pltpu.VMEM((8, span), f32),
            pltpu.VMEM((BLOCK, span), f32),
            pltpu.VMEM((rows, tokens), bf16),
            pltpu.VMEM((tokens, width), bf16),
            pltpu.VMEM((width,), f32),
            pltpu.VMEM((inner, width), bf16),
            pltpu.VMEM((inner, width), bf16),
            pltpu.VMEM((inner, width), bf16),
            pltpu.VMEM((count, bucket_count), f32),
            pltpu.VMEM((1, span - 1), jnp.int32),
            pltpu.VMEM((1, tokens), jnp.int32),
            pltpu.VMEM((1, tokens), jnp.int32),
            pltpu.SemaphoreType.DMA((9,)),
        ],
        compiler_params=params,
        cost_estimate=NO_COST,
        name="attend",
    )(
        *(
            pltpu.with_memory_space_constraint(a, pltpu.HBM)
            for a in (layer_input, norm1_gain, wq_t, wk_t, wv_t, table_t, bucket_row, ids, slots)
        )
    )

    sel_parts = share(att_sel, "head")
    sel_in, sel_up, place, place_c, x_c, cot_c = call(
        place_kernel,
        [
            shape_of(rows, width, bf16),
            shape_of(rows, width, bf16),
            shape_of(tokens, rows, bf16),
            shape_of(part, rows, bf16),
            shape_of(part, width, bf16),
            shape_of(part, width, bf16),
        ],
        (layer_input, cotangent, ids, slots),
        scratch=[pltpu.VMEM((tokens, rows), f32)],
        moved=12 * 2**20,
        name="place",
        after=(att_sel,),
    )
    hidden_sel, normed_sel, probs, pay_pieces, att_on = call(
        partial(route_kernel, shards=shards, heads=heads),
        [
            shape_of(rows, width, f32),
            shape_of(rows, width, f32),
            shape_of(rows, experts, f32),
            jax.ShapeDtypeStruct((shards, SLOT, 2 * width + 128), bf16),
            shape_of(inner, tokens, bf16),
        ],
        tuple(sel_parts) + tuple(w_mix) + (sel_in, sel_up, norm2_gain, router_t, att_t),
        scratch=[
            pltpu.VMEM((heads, rows, inner), bf16),
            pltpu.VMEM((heads, inner, width), bf16),
        ],
        name="route",
    )
    pay_parts = trade(pay_pieces, "seq")
    att_parts = share(att_on, "head")

    dq0, dk0, dv0, offs, wout0, prob_sel, q_sel, k_rows, v_t = pl.pallas_call(
        masked_back_kernel,
        grid=(count,),
        out_shape=(
            jax.ShapeDtypeStruct((count, tokens, each), f32),
            shape_of(inner, tokens, f32),
            shape_of(inner, tokens, f32),
            jax.ShapeDtypeStruct((count, 8, span), f32),
            shape_of(inner, width, f32),
            jax.ShapeDtypeStruct((count, rows, tokens), bf16),
            shape_of(inner, rows, bf16),
            jax.ShapeDtypeStruct((count, tokens, each), bf16),
            shape_of(inner, tokens, bf16),
        ),
        in_specs=[
            whole((tokens, width)), whole((inner, width)), whole((inner, width)),
            whole((inner, width)), whole((inner, width)), whole((tokens, width)),
            whole((tokens, rows)), by_head((1, tokens, each)), by_head((1, tokens, tokens)),
            whole((inner, tokens)), spec(pl.ANY),
        ],
        out_specs=(
            by_head((1, tokens, each)), by_head((each, tokens)), by_head((each, tokens)),
            by_head((1, 8, span)), whole((inner, width)), by_head((1, rows, tokens)),
            whole((inner, rows)), whole((count, tokens, each)), whole((inner, tokens)),
        ),
        scratch_shapes=[
            pltpu.VMEM((count, tokens, each), bf16),
            pltpu.VMEM((inner, tokens), bf16),
            pltpu.VMEM((inner, tokens), bf16),
            pltpu.VMEM((tokens, width), bf16),
            pltpu.VMEM((BLOCK, span), f32),
            pltpu.VMEM((tokens, tokens), bf16),
            pltpu.VMEM((each + rows, tokens), bf16),
        ],
        compiler_params=params,
        cost_estimate=NO_COST,
        name="masked_back",
    )(cotangent, w_attn_out, wq_t, wk_t, wv_t, low, place, att, prob, att_t, pay_pieces)

    pieces, x_rows, act, pre_low, out_low = call(
        partial(expert_kernel, heads=heads),
        [
            jax.ShapeDtypeStruct((heads * shards, SLOT, split), bf16),
            shape_of(rows, width, bf16),
            shape_of(rows, hidden_units, bf16),
            shape_of(rows, hidden_units, bf16),
            shape_of(rows, width, bf16),
        ],
        (pay_parts, w_in, w_out),
        name="expert",
        after=(dq0,) + tuple(att_parts[1:]),
    )
    w_in_grad, w_out_grad = call(
        expert_grad_kernel,
        [
            jax.ShapeDtypeStruct(w_expert_in.shape, f32),
            jax.ShapeDtypeStruct(w_expert_out.shape, f32),
        ],
        (x_rows, pre_low, act, out_low),
        name="expert_grad",
        moved=12 * 2**20,
    )
    (hidden,) = call(
        partial(hidden_kernel, heads=heads),
        [shape_of(tokens, width, f32)],
        tuple(att_parts) + tuple(w_mix) + (layer_input,),
        scratch=[
            pltpu.VMEM((heads * inner, tokens), bf16),
            pltpu.VMEM((heads * inner, width), bf16),
        ],
        name="hidden",
        after=(w_in_grad,),
        moved=16 * 2**20,
    )
    (summed,) = call(
        partial(sum_kernel, heads=heads),
        [shape_of(rows, split, bf16)],
        (trade(pieces, ("head", "seq")),),
        name="sum",
        after=(hidden,),
    )
    full_parts = share(summed, "head")

    small_rows = 8 + -(-experts // 8) * 8
    dv_sel, comb_sel, small, wout_part, gh_sel, ght_sel, delta_sel = call(
        partial(slot_back_kernel, heads=heads),
        [
            shape_of(rows, width, f32),
            shape_of(rows, width, f32),
            shape_of(small_rows, width, f32),
            shape_of(inner, width, f32),
            jax.ShapeDtypeStruct((count, rows, each), bf16),
            shape_of(inner, rows, bf16),
            jax.ShapeDtypeStruct((count, rows, 1), f32),
        ],
        tuple(full_parts)
        + (sel_up, normed_sel, hidden_sel, probs, router_t, norm2_gain)
        + (w_attn_out, att_sel, wout0),
        scratch=[pltpu.VMEM((heads, rows, split), bf16)],
        name="slot_back",
    )

    back = call(
        partial(sparse_back_kernel, heads=heads),
        [shape_of(part, width, bf16)] * heads
        + [
            jax.ShapeDtypeStruct((count, rows, tokens), bf16),
            shape_of(2 * inner, width, bf16),
            shape_of(2 * inner, width, f32),
            shape_of(small_rows, width, f32),
        ],
        (gh_sel, ght_sel, delta_sel, v_t, k_rows, q_sel, prob_sel, dq0, dk0, dv0, place)
        + (wq_t, wk_t, wv_t, low, norm1_gain, small, wout_part),
        scratch=[
            pltpu.VMEM((rows, inner), f32),
            pltpu.VMEM((tokens, inner), bf16),
            pltpu.VMEM((tokens, inner), bf16),
            pltpu.VMEM((tokens, inner), bf16),
            pltpu.VMEM((inner, tokens), bf16),
            pltpu.VMEM((inner, tokens), bf16),
            pltpu.VMEM((4 * inner, width), f32),
        ],
        name="sparse_back",
    )
    score_sel, send, keep, small = back[heads:]
    first_parts = swap_all(back[:heads], "head")
    (small,) = call(
        partial(bias_grad_kernel, bucket_count=bucket_count),
        [shape_of(small_rows, width, f32)],
        (score_sel, place, offs, bucket_row, small),
        scratch=[pltpu.VMEM((BLOCK, span), f32)],
        name="bias_grad",
        moved=20 * 2**20,
    )
    small_sum = sum_small(small, ("seq",))
    gain1_sum = sum_small(small_sum[1:2], ("head",))
    keep, got = scatter_sum(send, keep, tuple(first_parts[1:-1]) + (small,))

    grad_part, weights = call(
        first_norm_kernel,
        [shape_of(part, width, bf16), shape_of(keep.shape[0], width, bf16)],
        tuple(first_parts) + (x_c, cot_c, place_c, dv_sel, norm1_gain, keep, got),
        name="first_norm",
        after=(small_sum,),
    )
    grad_parts = share(grad_part, "head")
    (layer_output,) = call(
        output_kernel,
        [shape_of(tokens, width, f32)],
        (hidden, place, comb_sel),
        name="output",
        after=(grad_part,),
        moved=16 * 2**20,
    )
    weight_sums = gather_rows(
        weights,
        [inner] * 4,
        tuple(grad_parts[1:-1]) + (layer_output, gain1_sum),
        tuple(grad_parts[-1:]),
    )
    (input_grad,) = call(
        spread_kernel,
        [shape_of(tokens, width, f32)],
        tuple(grad_parts),
        name="spread",
    )

    return (
        layer_output,
        input_grad,
        gain1_sum[0],
        jnp.transpose(weight_sums[0]),
        jnp.transpose(weight_sums[1]),
        jnp.transpose(weight_sums[2]),
        weight_sums[3],
        jnp.transpose(small_sum[2 : 2 + count, :bucket_count]),
        small_sum[0],
        jnp.transpose(small_sum[8 : 8 + experts]),
        w_in_grad,
        w_out_grad,
    )


def solution(mesh):
    return jax.shard_map(
        on_device,
        mesh=mesh,
        in_specs=(
            P("seq", None),
            P("seq", None),
            P(),
            P(None, "head"),
            P(None, "head"),
            P(None, "head"),
            P("head", None),
            P(None, "head"),
            P(),
            P(),
            P("seq", None, "head"),
            P("seq", "head", None),
            P("seq"),
            P("seq"),
            P(),
        ),
        out_specs=(
            P("seq", None),
            P("seq", None),
            P(),
            P(None, "head"),
            P(None, "head"),
            P(None, "head"),
            P("head", None),
            P(None, "head"),
            P(),
            P(),
            P("seq", None, "head"),
            P("seq", "head", None),
        ),
        check_vma=False,
    )
```

```python
from functools import partial

import jax
import jax.numpy as jnp
import numpy as np
from jax import lax
from jax.experimental import pallas as pl
from jax.experimental.pallas import tpu as pltpu
from jax.sharding import PartitionSpec as P

CAP = 20
SLOT = 24
EPS = 1e-06
BLOCK = 128
VMEM_LIMIT = 26 * 1024 * 1024
VMEM_ALL = 60 * 1024 * 1024
NO_COST = pl.CostEstimate(flops=1, bytes_accessed=1, transcendentals=0)

f32 = jnp.float32
bf16 = jnp.bfloat16
highest = lax.Precision.HIGHEST


def dot(a, b):
    return jnp.dot(a, b, preferred_element_type=f32)


def dot_nt(a, b, precision=None):
    return lax.dot_general(
        a, b, (((1,), (1,)), ((), ())), precision=precision, preferred_element_type=f32
    )


def dot_tn(a, b, precision=None):
    return lax.dot_general(
        a, b, (((0,), (0,)), ((), ())), precision=precision, preferred_element_type=f32
    )


def iota(shape, dim):
    return lax.broadcasted_iota(jnp.int32, shape, dim)


def split_two(v):
    high = v.astype(bf16)
    return high, (v - high.astype(f32)).astype(bf16)


def shape_of(rows, cols, dtype):
    return jax.ShapeDtypeStruct((rows, cols), dtype)


def spec(memory):
    return pl.BlockSpec(memory_space=memory)


def call(kernel, outs, args, scratch=(), name=None, after=(), moved=1, token=False):
    outs, args = tuple(outs), tuple(args)
    held = sum(int(np.prod(a.shape)) * np.dtype(a.dtype).itemsize for a in args + outs)
    if token:
        outs += (shape_of(8, 128, f32),)
    first_out = len(args) + len(after)

    def body(*refs):
        results = refs[first_out : first_out + len(outs)]
        if token:
            results[-1][...] = jnp.zeros((8, 128), f32)
            results = results[:-1]
        kernel(*refs[: len(args)], *results, *refs[first_out + len(outs) :])

    return pl.pallas_call(
        body,
        out_shape=outs,
        in_specs=[spec(pltpu.VMEM)] * len(args) + [spec(pl.ANY)] * len(after),
        out_specs=tuple(spec(pltpu.VMEM) for _ in outs),
        scratch_shapes=list(scratch),
        compiler_params=pltpu.CompilerParams(
            vmem_limit_bytes=VMEM_LIMIT if 2 * held < VMEM_LIMIT else VMEM_ALL
        ),
        cost_estimate=pl.CostEstimate(flops=1, bytes_accessed=moved, transcendentals=0),
        name=name,
    )(*args, *after)


def whole(shape):
    return pl.BlockSpec(shape, lambda h: (0,) * len(shape))


def by_head(shape):
    return pl.BlockSpec(shape, lambda h: (h,) + (0,) * (len(shape) - 1))


def slot_rows(ids, slots, rows):
    cell = jnp.where(slots < CAP, ids * SLOT + slots, -1)
    return (iota((rows, cell.shape[1]), 0) == cell).astype(f32)


def place_kernel(
    x_ref, cot_ref, ids_ref, slots_ref, sel_in, sel_up, place, place_c, x_c, cot_c, place_s
):
    head = lax.axis_index("head")
    part = x_c.shape[0]
    slot_hot = slot_rows(ids_ref[...], slots_ref[...], sel_in.shape[0])
    place_s[...] = jnp.transpose(slot_hot)
    slot_low = slot_hot.astype(bf16)
    sel_in[...] = dot(slot_low, x_ref[...]).astype(bf16)
    sel_up[...] = dot(slot_low, cot_ref[...]).astype(bf16)
    place[...] = place_s[...].astype(bf16)
    mine = pl.ds(pl.multiple_of(head * part, part), part)
    place_c[...] = place_s[mine, :].astype(bf16)
    x_c[...] = x_ref[mine, :]
    cot_c[...] = cot_ref[mine, :]


def attend_kernel(*refs):
    given, refs = refs[:9], refs[9:]
    low_ref, prob_ref, att_ref, attt_ref, sel_ref = refs[:5]
    q_s, kt_s, v_s, bias_s, skew_s, slot_s = refs[5:11]
    here, sems = refs[11:20], refs[20]
    x_ref, gain_ref, wq_ref, wk_ref, wv_ref, table_ref, buckets_ref, ids_ref, slots_ref = here
    copies = [
        pltpu.make_async_copy(far, near, sems.at[i])
        for i, (far, near) in enumerate(zip(given, here))
    ]
    step = pl.program_id(0)
    tokens = x_ref.shape[0]
    inner = wq_ref.shape[0]
    count = q_s.shape[0]
    width = inner // count

    @pl.when(step == 0)
    def _():
        for copy in copies:
            copy.start()
        for copy in copies:
            copy.wait()
        for i in range(0, tokens, 256):
            rows = pl.ds(i, 256)
            x = x_ref[rows, :].astype(f32)
            inverse = lax.rsqrt(jnp.mean(x * x, axis=-1, keepdims=True) + EPS)
            low_ref[rows, :] = (x * inverse * gain_ref[...]).astype(bf16)
        low = low_ref[...]
        q = dot_nt(low, wq_ref[...]).astype(bf16) * bf16(width ** (-0.5))
        kt_s[...] = dot_nt(wk_ref[...], low).astype(bf16)
        v = dot_nt(low, wv_ref[...]).astype(bf16)
        for h in range(count):
            cols = slice(h * width, (h + 1) * width)
            q_s[h] = q[:, cols]
            v_s[h] = v[:, cols]
        offsets = buckets_ref.shape[1]
        bucket_hot = (iota((table_ref.shape[1], offsets), 0) == buckets_ref[...]).astype(f32)
        slot_s[...] = slot_rows(ids_ref[...], slots_ref[...], slot_s.shape[0]).astype(bf16)
        bias_s[...] = jnp.zeros_like(bias_s)
        bias_s[:count, :offsets] = jnp.dot(
            table_ref[...], bucket_hot, precision=highest, preferred_element_type=f32
        )

    span = skew_s.shape[1]
    row = bias_s[pl.ds(step, 1), :]
    skew_s[...] = pltpu.roll(
        jnp.broadcast_to(row, skew_s.shape), span - (BLOCK - 1), 1, stride=1, stride_axis=0
    )
    head_rows = pl.ds(pl.multiple_of(step * width, width), width)
    for i in range(0, tokens, 2 * BLOCK):
        scores = dot(q_s[step, pl.ds(i, 2 * BLOCK), :], kt_s[head_rows, :])
        for j in range(2):
            start = i + j * BLOCK
            first = tokens - BLOCK - start
            score = scores[j * BLOCK : (j + 1) * BLOCK] + skew_s[:, first : first + tokens]
            top = jnp.max(score, axis=-1, keepdims=True)
            weight = jnp.exp(score - top)
            total = jnp.sum(weight, axis=-1, keepdims=True)
            prob_ref[0, pl.ds(start, BLOCK), :] = (weight * (1.0 / total)).astype(bf16)
    att = dot(prob_ref[0], v_s[step])
    att_low = att.astype(bf16)
    att_ref[0] = att_low
    attt_ref[head_rows, :] = jnp.transpose(att).astype(bf16)
    picked = dot(slot_s[...], att_low).astype(bf16)
    half = sel_ref.shape[0]
    for h in range(count):

        @pl.when(step == h)
        def _():
            for part in range(2):
                start = part * inner + h * width
                sel_ref[:, start : start + width] = picked[part * half : (part + 1) * half]


def route_kernel(*refs, shards, heads):
    att_parts = refs[:heads]
    w_parts = refs[heads : 2 * heads]
    (sel_in, sel_up, gain_ref, router_ref, att_t, hidden_ref, normed_ref, probs_ref, att_on
     ) = refs[2 * heads : 2 * heads + 9]
    pieces = refs[2 * heads + 9 : 2 * heads + 9 + shards]
    att_s, w_s, pay_s = refs[2 * heads + 9 + shards :]
    head = lax.axis_index("head")
    inner = w_parts[0].shape[0]
    half = att_parts[0].shape[0]
    for d in range(heads):
        att_s[d, 0:half, :] = att_parts[d][:, 0:inner]
        att_s[d, half : 2 * half, :] = att_parts[d][:, inner : 2 * inner]
        w_s[d] = w_parts[d][...]
    mixed = None
    for k in range(heads):
        term = dot(att_s[head ^ k], w_s[head ^ k])
        mixed = term if mixed is None else mixed + term
    hidden = sel_in[...].astype(f32) + mixed
    hidden_ref[...] = hidden
    inverse = lax.rsqrt(jnp.mean(hidden * hidden, axis=-1, keepdims=True) + EPS)
    normed = hidden * inverse * gain_ref[...]
    normed_ref[...] = normed
    logits = dot_nt(normed, router_ref[...], highest)
    logits = logits - jnp.max(logits, axis=-1, keepdims=True)
    powers = jnp.exp(logits)
    probs = powers / jnp.sum(powers, axis=-1, keepdims=True)
    probs_ref[...] = probs
    gate = jnp.sum(jnp.where(chosen_of(probs.shape), probs, 0.0), axis=-1, keepdims=True)
    high = gate.astype(bf16).astype(f32)
    lane = iota((gate.shape[0], 128), 1)
    width = normed.shape[1]
    extra = jnp.where(lane == 0, high, jnp.where(lane == 1, gate - high, 0.0))
    pay_s[:, :width] = normed
    pay_s[:, width : 2 * width] = sel_up[...].astype(f32)
    pay_s[:, 2 * width :] = extra
    shard = lax.axis_index("seq")
    for j in range(shards):
        first = pl.multiple_of((shard ^ j) * SLOT, SLOT)
        pieces[j][...] = pay_s[pl.ds(first, SLOT), :].astype(bf16)
    att_on[...] = att_t[...]


def chosen_of(shape):
    expert = iota(shape, 1) * SLOT
    slot_row = iota(shape, 0)
    return (slot_row >= expert) & (slot_row < expert + SLOT)


def expert_kernel(*refs, shards, heads):
    parts = refs[:shards]
    w_in, w_out = refs[shards : shards + 2]
    chunks = refs[shards + 2 : shards + 2 + heads]
    x_ref, act_ref, pre_ref, out_ref, pay_s, both_s = refs[shards + 2 + heads :]
    head = lax.axis_index("head")
    width = x_ref.shape[1]
    for j in range(shards):
        pay_s[j * SLOT : (j + 1) * SLOT, :] = parts[j][...].astype(f32)
    x = pay_s[:, :width].astype(bf16)
    up = pay_s[:, width : 2 * width]
    gate = pay_s[:, 2 * width : 2 * width + 1] + pay_s[:, 2 * width + 1 : 2 * width + 2]
    out_low = (gate * up).astype(bf16)
    pre = dot(x, w_in[...])
    cdf = 0.5 * (1.0 + lax.erf(pre * (0.5**0.5)))
    act = (pre * cdf).astype(bf16)
    slope = cdf + pre * jnp.exp(-0.5 * pre * pre) * ((2.0 * np.pi) ** (-0.5))
    pre_low = (dot_nt(out_low, w_out[...]) * slope).astype(bf16)
    both = (dot(act, w_out[...]), dot_nt(pre_low, w_in[...]))
    part = both_s.shape[2]
    for k in range(heads):
        start = k % (heads // 2) * part
        both_s[k] = both[k // (heads // 2)][:, start : start + part].astype(bf16)
    for d in range(heads):
        chunks[d][...] = both_s[head ^ d]
    pre_ref[...] = pre_low
    out_ref[...] = out_low
    x_ref[...] = x
    act_ref[...] = act


def expert_grad_kernel(x_ref, pre_ref, act_ref, out_ref, in_grad, out_grad):
    in_grad[0] = dot_tn(x_ref[...], pre_ref[...])
    out_grad[0] = dot_tn(act_ref[...], out_ref[...])


def sum_kernel(*refs, heads):
    parts, pieces, sum_s = refs[:heads], refs[heads:-1], refs[-1]
    total = parts[0][...].astype(f32)
    for d in range(1, heads):
        total = total + parts[d][...].astype(f32)
    sum_s[...] = total
    for j, piece in enumerate(pieces):
        piece[...] = sum_s[j * SLOT : (j + 1) * SLOT, :].astype(bf16)


def join_kernel(*refs):
    parts, out_ref, sum_s = refs[:-2], refs[-2], refs[-1]
    shard = lax.axis_index("seq")
    for j, part in enumerate(parts):
        first = pl.multiple_of((shard ^ j) * SLOT, SLOT)
        sum_s[pl.ds(first, SLOT), :] = part[...].astype(f32)
    out_ref[...] = sum_s[...].astype(bf16)


def prep_kernel(
    cot_ref, w_ref, wq_ref, wk_ref, wv_ref, low_ref, place_ref, attt_ref,
    gh_ref, stack_ref, k_ref, qt_ref, vt_ref, wout_ref, qsel_ref, ght_s, mcot_s,
):
    count, tokens, width = gh_ref.shape
    for i in range(0, tokens, 256):
        rows = pl.ds(i, 256)
        where = place_ref[rows, :].astype(f32)
        free = 1.0 - jnp.sum(where, axis=-1, keepdims=True)
        mcot_s[rows, :] = (cot_ref[rows, :].astype(f32) * free).astype(bf16)
        slots = jnp.transpose(where).astype(bf16)
        for h in range(count):
            stack_ref[h, width:, rows] = slots
    gh = dot_nt(mcot_s[...], w_ref[...]).astype(bf16)
    ght_s[...] = dot_nt(w_ref[...], mcot_s[...]).astype(bf16)
    k = dot_nt(low_ref[...], wk_ref[...]).astype(bf16)
    qt_ref[...] = dot_nt(wq_ref[...], low_ref[...]).astype(bf16) * bf16(width ** (-0.5))
    vt_ref[...] = dot_nt(wv_ref[...], low_ref[...]).astype(bf16)
    for h in range(count):
        cols = slice(h * width, (h + 1) * width)
        gh_ref[h] = gh[:, cols]
        k_ref[h] = k[:, cols]
        stack_ref[h, 0:width, :] = ght_s[cols, :]
    wout_ref[...] = dot(attt_ref[...], mcot_s[...])
    qsel_ref[...] = dot(qt_ref[...], place_ref[...]).astype(bf16)


def masked_back_kernel(
    gh_ref, stack_ref, k_ref, qt_ref, vt_ref, att_ref, prob_ref,
    dq_ref, dkt_ref, dvt_ref, offs_ref, psel_ref, acc_s, score_s, *, h,
):
    tokens, width = dq_ref.shape
    acc_s[...] = jnp.zeros_like(acc_s)
    cols = slice(h * width, (h + 1) * width)
    for i in range(0, tokens, 2 * BLOCK):
        rows = pl.ds(i, 2 * BLOCK)
        gh = gh_ref[h, rows, :]
        delta = jnp.sum(gh.astype(f32) * att_ref[h, rows, :].astype(f32), axis=-1, keepdims=True)
        grads = dot(gh, vt_ref[cols, :]) - delta
        for j in range(2):
            start = i + j * BLOCK
            first = tokens - BLOCK - start
            here = pl.ds(start, BLOCK)
            score = prob_ref[h, here, :].astype(f32) * grads[j * BLOCK : (j + 1) * BLOCK]
            acc_s[:, first : first + tokens] += score
            score_s[here, :] = score.astype(bf16)
    dq_ref[...] = dot(score_s[...], k_ref[h]) * (width ** (-0.5))
    dkt_ref[...] = dot(qt_ref[cols, :], score_s[...])
    both = dot(stack_ref[h], prob_ref[h])
    dvt_ref[...] = both[:width]
    psel_ref[...] = both[width:].astype(bf16)
    offs_ref[...] = diagonals(acc_s[...])


def diagonals(acc):
    span = acc.shape[1]
    rows = acc.shape[0] // 2
    while rows >= 8:
        acc = acc[:rows] + pltpu.roll(acc[rows:], span - rows, 1)
        rows //= 2
    total = acc[0:1]
    for r in range(1, 8):
        total = total + pltpu.roll(acc[r : r + 1], span - r, 1)
    return jnp.broadcast_to(pltpu.roll(total, BLOCK - 1, 1), (8, span))


def slot_back_kernel(*refs, heads):
    parts = refs[:heads]
    (up_ref, normed_ref, hidden_ref, probs_ref, router_ref, gain_ref, w_ref, att_ref,
     wout0_ref) = refs[heads : heads + 9]
    dv_ref, comb_ref, small_ref, wout_ref, gh_ref, ght_ref, delta_ref, ret_s = refs[heads + 9 :]
    head = lax.axis_index("head")
    for d in range(heads):
        ret_s[head ^ d] = parts[d][...]
    back = [ret_s[k].astype(f32) for k in range(heads)]
    combined = jnp.concatenate(back[: heads // 2], axis=1)
    grad_buf = jnp.concatenate(back[heads // 2 :], axis=1)
    up = up_ref[...].astype(f32)
    hidden, normed, probs, gain = hidden_ref[...], normed_ref[...], probs_ref[...], gain_ref[...]
    chosen = chosen_of(probs.shape)
    gate = jnp.sum(jnp.where(chosen, probs, 0.0), axis=-1, keepdims=True)
    comb_ref[...] = gate * combined
    gate_grad = jnp.sum(up * combined, axis=-1, keepdims=True)
    marked = jnp.where(chosen, gate_grad, 0.0)
    logit_grad = probs * (marked - jnp.sum(marked * probs, axis=-1, keepdims=True))
    experts = probs.shape[1]
    grad = grad_buf + jnp.dot(
        logit_grad, router_ref[...], precision=highest, preferred_element_type=f32
    )
    inverse = lax.rsqrt(jnp.mean(hidden * hidden, axis=-1, keepdims=True) + EPS)
    scaled = grad * gain
    inner_sum = jnp.mean(scaled * hidden, axis=-1, keepdims=True)
    dv = inverse * scaled - hidden * (inverse * inverse * inverse * inner_sum)
    dv_ref[...] = dv
    small_ref[...] = jnp.zeros_like(small_ref)
    small_ref[0:1, :] = jnp.sum(grad * hidden * inverse, axis=0, keepdims=True)
    small_ref[8 : 8 + experts, :] = dot_tn(logit_grad, normed, highest)
    grad_low = (up + dv).astype(bf16)
    half = att_ref.shape[0]
    inner = w_ref.shape[0]
    att = jnp.concatenate(
        [att_ref[:, 0:inner].astype(f32), att_ref[:, inner : 2 * inner].astype(f32)], axis=0
    )
    wout_ref[...] = wout0_ref[...] + dot_tn(att.astype(bf16), grad_low)
    gh = dot_nt(grad_low, w_ref[...])
    gh_low = gh.astype(bf16)
    count = gh_ref.shape[0]
    each = inner // count
    ght_ref[...] = dot_nt(w_ref[...], grad_low).astype(bf16)
    for h in range(count):
        cols = slice(h * each, (h + 1) * each)
        gh_ref[h] = gh_low[:, cols]
        delta_ref[h] = jnp.sum(
            gh_low[:, cols].astype(f32) * att[:, cols], axis=-1, keepdims=True
        )


def sparse_back_kernel(
    gh_ref, ght_ref, delta_ref, vt_ref, k_ref, qsel_ref,
    place_ref, wq_ref, wk_ref, wv_ref, low_ref, gain_ref, small_ref, wout_ref, *refs, heads,
):
    per_head, refs = refs[: 4 * gh_ref.shape[0]], refs[4 * gh_ref.shape[0] :]
    psels, dq0s, dkt0s, dvt0s = (per_head[i :: 4] for i in range(4))
    chunks = refs[:heads]
    (score_ref, send_ref, keep_ref, out_ref,
     dq_s, q_low, k_low, v_low, kt_s, vt_s, all_s) = refs[heads:]
    head = lax.axis_index("head")
    count, rows, width = gh_ref.shape
    tokens = vt_ref.shape[1]
    inner = count * width
    for h in range(count):
        cols = slice(h * width, (h + 1) * width)
        grad = dot(gh_ref[h], vt_ref[cols, :])
        prob = psels[h][...]
        score = (prob.astype(f32) * (grad - delta_ref[h])).astype(bf16)
        score_ref[h] = score
        dq_s[:, cols] = dot(score, k_ref[h]) * (width ** (-0.5))
        dkt = dkt0s[h][...] + dot(qsel_ref[cols, :], score)
        dvt = dvt0s[h][...] + dot(ght_ref[cols, :], prob)
        kt_s[cols, :] = dkt.astype(bf16)
        vt_s[cols, :] = dvt.astype(bf16)
        k_low[:, cols] = jnp.transpose(dkt).astype(bf16)
        v_low[:, cols] = jnp.transpose(dvt).astype(bf16)
    spread = dot(place_ref[...], dq_s[...].astype(bf16))
    for h in range(count):
        cols = slice(h * width, (h + 1) * width)
        q_low[:, cols] = (spread[:, cols] + dq0s[h][...]).astype(bf16)
    part = tokens // heads
    for d in range(heads):
        mine = pl.ds(pl.multiple_of((head ^ d) * part, part), part)
        chunks[d][...] = (
            dot(q_low[mine, :], wq_ref[...])
            + dot(k_low[mine, :], wk_ref[...])
            + dot(v_low[mine, :], wv_ref[...])
        ).astype(bf16)
    low = low_ref[...]
    total = None
    grads = (dot_tn(q_low[...], low), dot(kt_s[...], low), dot(vt_s[...], low))
    for i, (grad, w) in enumerate(zip(grads, (wq_ref, wk_ref, wv_ref))):
        all_s[i * inner : (i + 1) * inner, :] = grad
        term = jnp.sum(grad * w[...].astype(f32), axis=0, keepdims=True)
        total = term if total is None else total + term
    all_s[3 * inner :, :] = wout_ref[...]
    out_ref[...] = small_ref[...]
    out_ref[1:2, :] = total / gain_ref[...]
    split_rows(all_s, 1, send_ref, keep_ref)


def is_upper(bit):
    return (lax.axis_index("seq") & bit) != 0


def split_rows(all_s, bit, send_ref, keep_ref):
    half = send_ref.shape[0]
    low, high = all_s[0:half, :], all_s[half : 2 * half, :]
    keep_ref[...] = jnp.where(is_upper(bit), high, low)
    send_ref[...] = jnp.where(is_upper(bit), low, high).astype(bf16)


def halve_kernel(keep_ref, got_ref, send_ref, out_ref, all_s, *, bit):
    all_s[...] = keep_ref[...] + got_ref[...].astype(f32)
    split_rows(all_s, bit, send_ref, out_ref)


def join_rows(mine_ref, got_ref, all_s, bit):
    half = mine_ref.shape[0]
    mine, got = mine_ref[...].astype(f32), got_ref[...].astype(f32)
    all_s[0:half, :] = jnp.where(is_upper(bit), got, mine)
    all_s[half : 2 * half, :] = jnp.where(is_upper(bit), mine, got)


def pair_kernel(mine_ref, got_ref, out_ref, all_s, *, bit):
    join_rows(mine_ref, got_ref, all_s, bit)
    out_ref[...] = all_s[...].astype(bf16)


def final_kernel(mine_ref, got_ref, *refs, bit):
    outs, all_s = refs[:-1], refs[-1]
    join_rows(mine_ref, got_ref, all_s, bit)
    inner = outs[0].shape[0]
    for i, out in enumerate(outs):
        out[...] = all_s[i * inner : (i + 1) * inner, :]


def bias_grad_kernel(
    score_ref, place_ref, buckets_ref, small_ref, *refs, bucket_count
):
    count = score_ref.shape[0]
    offs, out_ref, acc_s = refs[:count], refs[count], refs[count + 1]
    tokens = place_ref.shape[0]
    offsets = buckets_ref.shape[1]
    out_ref[...] = small_ref[...]
    bucket_hot = (iota((bucket_count, offsets), 0) == buckets_ref[...]).astype(f32)
    for h in range(count):
        acc_s[...] = jnp.zeros_like(acc_s)
        for i in range(0, tokens, BLOCK):
            first = tokens - BLOCK - i
            acc_s[:, first : first + tokens] += dot(place_ref[i : i + BLOCK, :], score_ref[h])
        sums = diagonals(acc_s[...]) + offs[h][...]
        out_ref[2 + h : 3 + h, :bucket_count] = dot_nt(sums[:, :offsets], bucket_hot, highest)[0:1]


def hidden_kernel(*refs, heads):
    att_parts, w_parts = refs[:heads], refs[heads : 2 * heads]
    x_ref, out_ref, att_s, w_s = refs[2 * heads :]
    head = lax.axis_index("head")
    tokens = x_ref.shape[0]
    inner = w_parts[0].shape[0]
    for d in range(heads):
        mine = pl.ds(pl.multiple_of((head ^ d) * inner, inner), inner)
        att_s[mine, :] = att_parts[d][...]
        w_s[mine, :] = w_parts[d][...]
    for i in range(0, tokens, 256):
        rows = pl.ds(i, 256)
        out_ref[rows, :] = x_ref[rows, :].astype(f32) + dot_tn(att_s[:, rows], w_s[...])


def output_kernel(hidden_ref, place_ref, comb_ref, out_ref):
    high, rest = split_two(comb_ref[...])
    for i in range(0, hidden_ref.shape[0], 256):
        rows = pl.ds(i, 256)
        where = place_ref[rows, :]
        out_ref[rows, :] = hidden_ref[rows, :] + (dot(where, high) + dot(where, rest))


def first_norm_kernel(*refs):
    parts = refs[:-9]
    (x_ref, cot_ref, place_ref, dv_ref, gain_ref, keep_ref, got_ref, out_ref, sum_ref) = refs[-9:]
    grad = parts[0][...].astype(f32)
    for part in parts[1:]:
        grad = grad + part[...].astype(f32)
    x = x_ref[...].astype(f32)
    inverse = lax.rsqrt(jnp.mean(x * x, axis=-1, keepdims=True) + EPS)
    scaled = grad * gain_ref[...]
    inner_sum = jnp.mean(scaled * x, axis=-1, keepdims=True)
    high, rest = split_two(dv_ref[...])
    hidden_grad = cot_ref[...].astype(f32) + (dot(place_ref[...], high) + dot(place_ref[...], rest))
    out_ref[...] = (
        hidden_grad + inverse * scaled - x * (inverse * inverse * inverse * inner_sum)
    ).astype(bf16)
    sum_ref[...] = (keep_ref[...] + got_ref[...].astype(f32)).astype(bf16)


def spread_kernel(*refs):
    parts, out_ref = refs[:-1], refs[-1]
    head = lax.axis_index("head")
    part = parts[0].shape[0]
    for d in range(len(parts)):
        mine = pl.ds(pl.multiple_of((head ^ d) * part, part), part)
        out_ref[mine, :] = parts[d][...].astype(f32)


def swap(x, axis, d):
    size = lax.axis_size(axis)
    return lax.ppermute(x, axis, [(i, i ^ d) for i in range(size)])


def share(x, axis):
    return [x] + [swap(x, axis, d) for d in range(1, lax.axis_size(axis))]


def trade(pieces, axis):
    return lax.all_to_all(pieces, axis, split_axis=0, concat_axis=0, tiled=True)


def swap_all(pieces, axis):
    return [pieces[0]] + [swap(pieces[d], axis, d) for d in range(1, len(pieces))]


def bits_of(axis):
    return [b for b in (1 << i for i in range(16)) if b < lax.axis_size(axis)]


def scatter_sum(send, keep, after, later):
    rows, width = keep.shape
    bits = bits_of("seq")
    for bit in bits[1:]:
        send, keep = call(
            partial(halve_kernel, bit=bit),
            [shape_of(rows // 2, width, bf16), shape_of(rows // 2, width, f32)],
            (keep, swap(send, "seq", bit // 2)),
            scratch=[pltpu.VMEM((rows, width), f32)],
            name="halve",
            after=after,
        )
        rows //= 2
        after, later = later, ()
    return keep, swap(send, "seq", bits[-1])


def gather_rows(now, counts, after, later):
    rows, width = now.shape
    for bit in reversed(bits_of("seq")[1:]):
        rows *= 2
        (now,) = call(
            partial(pair_kernel, bit=bit),
            [shape_of(rows, width, bf16)],
            (now, swap(now, "seq", bit)),
            scratch=[pltpu.VMEM((rows, width), f32)],
            name="pair",
            after=after,
        )
        after, later = later, ()
    return call(
        partial(final_kernel, bit=1),
        [shape_of(n, width, f32) for n in counts],
        (now, swap(now, "seq", 1)),
        scratch=[pltpu.VMEM((2 * rows, width), f32)],
        name="weights_out",
    )


def sum_small(x, axes):
    for axis in axes:
        d = 1
        while d < lax.axis_size(axis):
            x = x + swap(x, axis, d)
            d *= 2
    return x


def on_device(
    layer_input, cotangent, norm1_gain, w_query, w_key, w_value, w_attn_out, bias_table,
    norm2_gain, w_router, w_expert_in, w_expert_out, expert_ids, slot_ids, buckets,
):
    tokens, width = layer_input.shape
    shards = lax.axis_size("seq")
    heads = lax.axis_size("head")
    bucket_count, count = bias_table.shape
    inner = w_query.shape[1]
    each = inner // count
    experts = w_router.shape[1]
    rows = experts * SLOT
    hidden_units = w_expert_in.shape[2]
    part = tokens // heads
    split = 2 * width // heads
    span = 2 * tokens
    params = pltpu.CompilerParams(vmem_limit_bytes=VMEM_LIMIT if rows <= 256 else VMEM_ALL)

    ids = expert_ids.reshape(1, tokens)
    slots = slot_ids.reshape(1, tokens)
    bucket_row = buckets.reshape(1, -1)
    wq_t, wk_t, wv_t = jnp.transpose(w_query), jnp.transpose(w_key), jnp.transpose(w_value)
    router_t, table_t = jnp.transpose(w_router), jnp.transpose(bias_table)
    w_in = w_expert_in.reshape(width, hidden_units)
    w_out = w_expert_out.reshape(hidden_units, width)

    w_mix = share(w_attn_out, "head")

    low, prob, att, att_t, att_sel = pl.pallas_call(
        attend_kernel,
        grid=(count,),
        out_shape=(
            shape_of(tokens, width, bf16),
            jax.ShapeDtypeStruct((count, tokens, tokens), bf16),
            jax.ShapeDtypeStruct((count, tokens, each), bf16),
            shape_of(inner, tokens, bf16),
            shape_of(rows // 2, 2 * inner, bf16),
        ),
        in_specs=[spec(pltpu.HBM)] * 9,
        out_specs=(
            whole((tokens, width)), by_head((1, tokens, tokens)), by_head((1, tokens, each)),
            whole((inner, tokens)), whole((rows // 2, 2 * inner)),
        ),
        scratch_shapes=[
            pltpu.VMEM((count, tokens, each), bf16),
            pltpu.VMEM((inner, tokens), bf16),
            pltpu.VMEM((count, tokens, each), bf16),
            pltpu.VMEM((8, span), f32),
            pltpu.VMEM((BLOCK, span), f32),
            pltpu.VMEM((rows, tokens), bf16),
            pltpu.VMEM((tokens, width), bf16),
            pltpu.VMEM((width,), f32),
            pltpu.VMEM((inner, width), bf16),
            pltpu.VMEM((inner, width), bf16),
            pltpu.VMEM((inner, width), bf16),
            pltpu.VMEM((count, bucket_count), f32),
            pltpu.VMEM((1, span - 1), jnp.int32),
            pltpu.VMEM((1, tokens), jnp.int32),
            pltpu.VMEM((1, tokens), jnp.int32),
            pltpu.SemaphoreType.DMA((9,)),
        ],
        compiler_params=params,
        cost_estimate=NO_COST,
        name="attend",
    )(
        *(
            pltpu.with_memory_space_constraint(a, pltpu.HBM)
            for a in (layer_input, norm1_gain, wq_t, wk_t, wv_t, table_t, bucket_row, ids, slots)
        )
    )

    sel_parts = share(att_sel, "head")
    sel_in, sel_up, place, place_c, x_c, cot_c = call(
        place_kernel,
        [
            shape_of(rows, width, bf16),
            shape_of(rows, width, bf16),
            shape_of(tokens, rows, bf16),
            shape_of(part, rows, bf16),
            shape_of(part, width, bf16),
            shape_of(part, width, bf16),
        ],
        (layer_input, cotangent, ids, slots),
        scratch=[pltpu.VMEM((tokens, rows), f32)],
        moved=12 * 2**20,
        name="place",
        after=(att_sel,),
    )
    routed = call(
        partial(route_kernel, shards=shards, heads=heads),
        [
            shape_of(rows, width, f32),
            shape_of(rows, width, f32),
            shape_of(rows, experts, f32),
            shape_of(inner, tokens, bf16),
        ]
        + [shape_of(SLOT, 2 * width + 128, bf16)] * shards,
        tuple(sel_parts) + tuple(w_mix) + (sel_in, sel_up, norm2_gain, router_t, att_t),
        scratch=[
            pltpu.VMEM((heads, rows, inner), bf16),
            pltpu.VMEM((heads, inner, width), bf16),
            pltpu.VMEM((rows, 2 * width + 128), f32),
        ],
        name="route",
        token=True,
    )
    hidden_sel, normed_sel, probs, att_on = routed[:4]
    pay_parts = swap_all(routed[4:-1], "seq")
    att_parts = share(att_on, "head")

    gh, stack, k_rows, q_t, v_t, wout0, q_sel, prepared = call(
        prep_kernel,
        [
            jax.ShapeDtypeStruct((count, tokens, each), bf16),
            jax.ShapeDtypeStruct((count, each + rows, tokens), bf16),
            jax.ShapeDtypeStruct((count, tokens, each), bf16),
            shape_of(inner, tokens, bf16),
            shape_of(inner, tokens, bf16),
            shape_of(inner, width, f32),
            shape_of(inner, rows, bf16),
        ],
        (cotangent, w_attn_out, wq_t, wk_t, wv_t, low, place, att_t),
        scratch=[pltpu.VMEM((inner, tokens), bf16), pltpu.VMEM((tokens, width), bf16)],
        name="prep",
        after=(routed[-1],),
        moved=8 * 2**20,
        token=True,
    )

    def masked_back(h, after):
        return call(
            partial(masked_back_kernel, h=h),
            [
                shape_of(tokens, each, f32),
                shape_of(each, tokens, f32),
                shape_of(each, tokens, f32),
                shape_of(8, span, f32),
                shape_of(rows, tokens, bf16),
            ],
            (gh, stack, k_rows, q_t, v_t, att, prob),
            scratch=[pltpu.VMEM((BLOCK, span), f32), pltpu.VMEM((tokens, tokens), bf16)],
            name="masked_back",
            after=after,
            moved=11 * 2**20,
            token=True,
        )

    done = call(
        partial(expert_kernel, shards=shards, heads=heads),
        [shape_of(rows, split, bf16)] * heads
        + [
            shape_of(rows, width, bf16),
            shape_of(rows, hidden_units, bf16),
            shape_of(rows, hidden_units, bf16),
            shape_of(rows, width, bf16),
        ],
        tuple(pay_parts) + (w_in, w_out),
        scratch=[
            pltpu.VMEM((rows, 2 * width + 128), f32),
            pltpu.VMEM((heads, rows, split), bf16),
        ],
        name="expert",
        after=(prepared,) + tuple(att_parts[1:-1]),
        token=True,
    )
    x_rows, act, pre_low, out_low, token = done[heads:]
    masked = []
    for h in range(count - 2):
        masked.append(masked_back(h, (token,)))
        token = masked[-1][-1]
    returned = call(
        partial(sum_kernel, heads=heads),
        [shape_of(SLOT, split, bf16)] * shards,
        swap_all(done[:heads], "head"),
        scratch=[pltpu.VMEM((rows, split), f32)],
        name="sum",
        after=(token,),
        token=True,
    )
    masked.append(masked_back(count - 2, (returned[-1],)))
    joined, token = call(
        join_kernel,
        [shape_of(rows, split, bf16)],
        swap_all(returned[:-1], "seq"),
        scratch=[pltpu.VMEM((rows, split), f32)],
        name="join",
        after=(masked[-1][-1], att_parts[-1]),
        token=True,
    )
    masked.append(masked_back(count - 1, (token,)))
    full_parts = share(joined, "head")

    small_rows = 8 + -(-experts // 8) * 8
    dv_sel, comb_sel, small, wout_part, gh_sel, ght_sel, delta_sel = call(
        partial(slot_back_kernel, heads=heads),
        [
            shape_of(rows, width, f32),
            shape_of(rows, width, f32),
            shape_of(small_rows, width, f32),
            shape_of(inner, width, f32),
            jax.ShapeDtypeStruct((count, rows, each), bf16),
            shape_of(inner, rows, bf16),
            jax.ShapeDtypeStruct((count, rows, 1), f32),
        ],
        tuple(full_parts)
        + (sel_up, normed_sel, hidden_sel, probs, router_t, norm2_gain)
        + (w_attn_out, att_sel, wout0),
        scratch=[pltpu.VMEM((heads, rows, split), bf16)],
        name="slot_back",
        after=(masked[-1][-1],),
    )

    back = call(
        partial(sparse_back_kernel, heads=heads),
        [shape_of(part, width, bf16)] * heads
        + [
            jax.ShapeDtypeStruct((count, rows, tokens), bf16),
            shape_of(2 * inner, width, bf16),
            shape_of(2 * inner, width, f32),
            shape_of(small_rows, width, f32),
        ],
        (gh_sel, ght_sel, delta_sel, v_t, k_rows, q_sel, place)
        + (wq_t, wk_t, wv_t, low, norm1_gain, small, wout_part)
        + tuple(a for m in masked for a in (m[4], m[0], m[1], m[2])),
        scratch=[
            pltpu.VMEM((rows, inner), f32),
            pltpu.VMEM((tokens, inner), bf16),
            pltpu.VMEM((tokens, inner), bf16),
            pltpu.VMEM((tokens, inner), bf16),
            pltpu.VMEM((inner, tokens), bf16),
            pltpu.VMEM((inner, tokens), bf16),
            pltpu.VMEM((4 * inner, width), f32),
        ],
        name="sparse_back",
    )
    score_sel, send, keep, small = back[heads:]
    first_parts = swap_all(back[:heads], "head")
    (small,) = call(
        partial(bias_grad_kernel, bucket_count=bucket_count),
        [shape_of(small_rows, width, f32)],
        (score_sel, place, bucket_row, small) + tuple(m[3] for m in masked),
        scratch=[pltpu.VMEM((BLOCK, span), f32)],
        name="bias_grad",
        moved=16 * 2**20,
    )
    w_in_grad, w_out_grad, token = call(
        expert_grad_kernel,
        [
            jax.ShapeDtypeStruct(w_expert_in.shape, f32),
            jax.ShapeDtypeStruct(w_expert_out.shape, f32),
        ],
        (x_rows, pre_low, act, out_low),
        name="expert_grad",
        after=(small,),
        moved=10 * 2**20,
        token=True,
    )
    small_sum = sum_small(small, ("seq",))
    gain1_sum = sum_small(small_sum[1:2], ("head",))
    keep, got = scatter_sum(send, keep, (small,), tuple(first_parts[1:-1]) + (token,))
    (hidden, token) = call(
        partial(hidden_kernel, heads=heads),
        [shape_of(tokens, width, f32)],
        tuple(att_parts) + tuple(w_mix) + (layer_input,),
        scratch=[
            pltpu.VMEM((heads * inner, tokens), bf16),
            pltpu.VMEM((heads * inner, width), bf16),
        ],
        name="hidden",
        after=(token,),
        moved=6 * 2**20,
        token=True,
    )

    grad_part, weights, token = call(
        first_norm_kernel,
        [shape_of(part, width, bf16), shape_of(keep.shape[0], width, bf16)],
        tuple(first_parts) + (x_c, cot_c, place_c, dv_sel, norm1_gain, keep, got),
        name="first_norm",
        after=(small_sum, token),
        token=True,
    )
    grad_parts = share(grad_part, "head")
    layer_output, token = call(
        output_kernel,
        [shape_of(tokens, width, f32)],
        (hidden, place, comb_sel),
        name="output",
        after=(token,),
        moved=10 * 2**20,
        token=True,
    )
    weight_sums = gather_rows(
        weights,
        [inner] * 4,
        tuple(grad_parts[1:-1]) + (token, gain1_sum),
        tuple(grad_parts[-1:]),
    )
    (input_grad,) = call(
        spread_kernel,
        [shape_of(tokens, width, f32)],
        tuple(grad_parts),
        name="spread",
    )

    return (
        layer_output,
        input_grad,
        gain1_sum[0],
        jnp.transpose(weight_sums[0]),
        jnp.transpose(weight_sums[1]),
        jnp.transpose(weight_sums[2]),
        weight_sums[3],
        jnp.transpose(small_sum[2 : 2 + count, :bucket_count]),
        small_sum[0],
        jnp.transpose(small_sum[8 : 8 + experts]),
        w_in_grad,
        w_out_grad,
    )


def solution(mesh):
    return jax.shard_map(
        on_device,
        mesh=mesh,
        in_specs=(
            P("seq", None),
            P("seq", None),
            P(),
            P(None, "head"),
            P(None, "head"),
            P(None, "head"),
            P("head", None),
            P(None, "head"),
            P(),
            P(),
            P("seq", None, "head"),
            P("seq", "head", None),
            P("seq"),
            P("seq"),
            P(),
        ),
        out_specs=(
            P("seq", None),
            P("seq", None),
            P(),
            P(None, "head"),
            P(None, "head"),
            P(None, "head"),
            P("head", None),
            P(None, "head"),
            P(),
            P(),
            P("seq", None, "head"),
            P("seq", "head", None),
        ),
        check_vma=False,
    )
```

```python
from functools import partial

import jax
import jax.numpy as jnp
import numpy as np
from jax import lax
from jax.experimental import pallas as pl
from jax.experimental.pallas import tpu as pltpu
from jax.sharding import PartitionSpec as P

CAP = 20
SLOT = 24
EPS = 1e-06
BLOCK = 128
ROWS = 16
VMEM_LIMIT = 26 * 1024 * 1024
VMEM_ALL = 60 * 1024 * 1024
NO_COST = pl.CostEstimate(flops=1, bytes_accessed=1, transcendentals=0)

f32 = jnp.float32
bf16 = jnp.bfloat16
highest = lax.Precision.HIGHEST


def dot(a, b):
    return jnp.dot(a, b, preferred_element_type=f32)


def dot_nt(a, b, precision=None):
    return lax.dot_general(
        a, b, (((1,), (1,)), ((), ())), precision=precision, preferred_element_type=f32
    )


def dot_tn(a, b, precision=None):
    return lax.dot_general(
        a, b, (((0,), (0,)), ((), ())), precision=precision, preferred_element_type=f32
    )


def iota(shape, dim):
    return lax.broadcasted_iota(jnp.int32, shape, dim)


def split_two(v):
    high = v.astype(bf16)
    return high, (v - high.astype(f32)).astype(bf16)


def shape_of(rows, cols, dtype):
    return jax.ShapeDtypeStruct((rows, cols), dtype)


def spec(memory):
    return pl.BlockSpec(memory_space=memory)


def call(kernel, outs, args, scratch=(), name=None, after=(), moved=1, token=False):
    outs, args = tuple(outs), tuple(args)
    held = sum(int(np.prod(a.shape)) * np.dtype(a.dtype).itemsize for a in args + outs)
    if token:
        outs += (shape_of(8, 128, f32),)
    first_out = len(args) + len(after)

    def body(*refs):
        results = refs[first_out : first_out + len(outs)]
        if token:
            results[-1][...] = jnp.zeros((8, 128), f32)
            results = results[:-1]
        kernel(*refs[: len(args)], *results, *refs[first_out + len(outs) :])

    return pl.pallas_call(
        body,
        out_shape=outs,
        in_specs=[spec(pltpu.VMEM)] * len(args) + [spec(pl.ANY)] * len(after),
        out_specs=tuple(spec(pltpu.VMEM) for _ in outs),
        scratch_shapes=list(scratch),
        compiler_params=pltpu.CompilerParams(
            vmem_limit_bytes=VMEM_LIMIT if 2 * held < VMEM_LIMIT else VMEM_ALL
        ),
        cost_estimate=pl.CostEstimate(flops=1, bytes_accessed=moved, transcendentals=0),
        name=name,
    )(*args, *after)


def whole(shape):
    return pl.BlockSpec(shape, lambda h: (0,) * len(shape))


def by_head(shape):
    return pl.BlockSpec(shape, lambda h: (h,) + (0,) * (len(shape) - 1))


def slot_rows(ids, slots, rows):
    cell = jnp.where(slots < CAP, ids * SLOT + slots, -1)
    return (iota((rows, cell.shape[1]), 0) == cell).astype(f32)


def place_kernel(
    x_ref, cot_ref, ids_ref, slots_ref, sel_in, sel_up, place, place_c, x_c, cot_c, place_s
):
    head = lax.axis_index("head")
    part = x_c.shape[0]
    slot_hot = slot_rows(ids_ref[...], slots_ref[...], sel_in.shape[0])
    place_s[...] = jnp.transpose(slot_hot)
    slot_low = slot_hot.astype(bf16)
    sel_in[...] = dot(slot_low, x_ref[...]).astype(bf16)
    sel_up[...] = dot(slot_low, cot_ref[...]).astype(bf16)
    place[...] = place_s[...].astype(bf16)
    mine = pl.ds(pl.multiple_of(head * part, part), part)
    place_c[...] = place_s[mine, :].astype(bf16)
    x_c[...] = x_ref[mine, :]
    cot_c[...] = cot_ref[mine, :]


def attend_kernel(*refs):
    given, refs = refs[:9], refs[9:]
    low_ref, prob_ref, att_ref, attt_ref, sel_ref = refs[:5]
    q_s, kt_s, v_s, bias_s, skew_s, slot_s, score_s = refs[5:12]
    here, sems = refs[12:21], refs[21]
    x_ref, gain_ref, wq_ref, wk_ref, wv_ref, table_ref, buckets_ref, ids_ref, slots_ref = here
    copies = [
        pltpu.make_async_copy(far, near, sems.at[i])
        for i, (far, near) in enumerate(zip(given, here))
    ]
    step = pl.program_id(0)
    tokens = x_ref.shape[0]
    inner = wq_ref.shape[0]
    count = q_s.shape[0]
    width = inner // count

    @pl.when(step == 0)
    def _():
        for copy in copies:
            copy.start()
        for copy in copies:
            copy.wait()
        for i in range(0, tokens, 256):
            rows = pl.ds(i, 256)
            x = x_ref[rows, :].astype(f32)
            inverse = lax.rsqrt(jnp.mean(x * x, axis=-1, keepdims=True) + EPS)
            low_ref[rows, :] = (x * inverse * gain_ref[...]).astype(bf16)
        low = low_ref[...]
        q = dot_nt(low, wq_ref[...]).astype(bf16) * bf16(width ** (-0.5))
        kt_s[...] = dot_nt(wk_ref[...], low).astype(bf16)
        v = dot_nt(low, wv_ref[...]).astype(bf16)
        for h in range(count):
            cols = slice(h * width, (h + 1) * width)
            q_s[h] = q[:, cols]
            v_s[h] = v[:, cols]
        offsets = buckets_ref.shape[1]
        bucket_hot = (iota((table_ref.shape[1], offsets), 0) == buckets_ref[...]).astype(f32)
        slot_s[...] = slot_rows(ids_ref[...], slots_ref[...], slot_s.shape[0]).astype(bf16)
        bias_s[...] = jnp.zeros_like(bias_s)
        bias_s[:count, :offsets] = jnp.dot(
            table_ref[...], bucket_hot, precision=highest, preferred_element_type=f32
        )

    span = skew_s.shape[1]
    row = bias_s[pl.ds(step, 1), :]
    skew_s[...] = pltpu.roll(
        jnp.broadcast_to(row, skew_s.shape), span - (BLOCK - 1), 1, stride=1, stride_axis=0
    )
    head_rows = pl.ds(pl.multiple_of(step * width, width), width)
    for i in range(0, tokens, 2 * BLOCK):
        score_s[...] = dot(q_s[step, pl.ds(i, 2 * BLOCK), :], kt_s[head_rows, :])
        for j in range(0, 2 * BLOCK, ROWS):
            first = tokens - BLOCK - (i + j) // BLOCK * BLOCK
            bias = skew_s[j % BLOCK : j % BLOCK + ROWS, first : first + tokens]
            score = score_s[j : j + ROWS, :] + bias
            weight = jnp.exp(score - jnp.max(score, axis=-1, keepdims=True))
            total = jnp.sum(weight, axis=-1, keepdims=True)
            prob_ref[0, pl.ds(i + j, ROWS), :] = (weight * (1.0 / total)).astype(bf16)
    att = dot(prob_ref[0], v_s[step])
    att_low = att.astype(bf16)
    att_ref[0] = att_low
    attt_ref[head_rows, :] = jnp.transpose(att).astype(bf16)
    picked = dot(slot_s[...], att_low).astype(bf16)
    half = sel_ref.shape[0]
    for h in range(count):

        @pl.when(step == h)
        def _():
            for part in range(2):
                start = part * inner + h * width
                sel_ref[:, start : start + width] = picked[part * half : (part + 1) * half]


def mix_kernel(att_ref, *refs, heads):
    w_parts, att_on, w_ref = refs[:heads], refs[heads], refs[heads + 1]
    att_on[...] = att_ref[...]
    head = lax.axis_index("head")
    inner = w_parts[0].shape[0]
    for d in range(heads):
        mine = pl.ds(pl.multiple_of((head ^ d) * inner, inner), inner)
        w_ref[mine, :] = w_parts[d][...]


def route_kernel(*refs, shards, heads):
    att_parts, w_ref = refs[:heads], refs[heads]
    (sel_in, sel_up, gain_ref, router_ref, att_t, hidden_ref, normed_ref, probs_ref, att_on
     ) = refs[heads + 1 : heads + 10]
    pieces = refs[heads + 10 : heads + 10 + shards]
    att_s, pay_s = refs[heads + 10 + shards :]
    head = lax.axis_index("head")
    half = att_parts[0].shape[0]
    inner = w_ref.shape[0] // heads
    for d in range(heads):
        att_s[d, 0:half, :] = att_parts[d][:, 0:inner]
        att_s[d, half : 2 * half, :] = att_parts[d][:, inner : 2 * inner]
    mixed = None
    for k in range(heads):
        term = dot(att_s[head ^ k], w_ref[k * inner : (k + 1) * inner, :])
        mixed = term if mixed is None else mixed + term
    hidden = sel_in[...].astype(f32) + mixed
    hidden_ref[...] = hidden
    inverse = lax.rsqrt(jnp.mean(hidden * hidden, axis=-1, keepdims=True) + EPS)
    normed = hidden * inverse * gain_ref[...]
    normed_ref[...] = normed
    logits = dot_nt(normed, router_ref[...], highest)
    logits = logits - jnp.max(logits, axis=-1, keepdims=True)
    powers = jnp.exp(logits)
    probs = powers / jnp.sum(powers, axis=-1, keepdims=True)
    probs_ref[...] = probs
    gate = jnp.sum(jnp.where(chosen_of(probs.shape), probs, 0.0), axis=-1, keepdims=True)
    high = gate.astype(bf16).astype(f32)
    lane = iota((gate.shape[0], 128), 1)
    width = normed.shape[1]
    extra = jnp.where(lane == 0, high, jnp.where(lane == 1, gate - high, 0.0))
    pay_s[:, :width] = normed
    pay_s[:, width : 2 * width] = sel_up[...].astype(f32)
    pay_s[:, 2 * width :] = extra
    shard = lax.axis_index("seq")
    for j in range(shards):
        first = pl.multiple_of((shard ^ j) * SLOT, SLOT)
        pieces[j][...] = pay_s[pl.ds(first, SLOT), :].astype(bf16)
    att_on[...] = att_t[...]


def chosen_of(shape):
    expert = iota(shape, 1) * SLOT
    slot_row = iota(shape, 0)
    return (slot_row >= expert) & (slot_row < expert + SLOT)


def expert_kernel(*refs, shards, heads):
    parts = refs[:shards]
    w_in, w_out = refs[shards : shards + 2]
    chunks = refs[shards + 2 : shards + 2 + heads]
    x_ref, act_ref, pre_ref, out_ref, pay_s, both_s = refs[shards + 2 + heads :]
    head = lax.axis_index("head")
    width = x_ref.shape[1]
    for j in range(shards):
        pay_s[j * SLOT : (j + 1) * SLOT, :] = parts[j][...].astype(f32)
    x = pay_s[:, :width].astype(bf16)
    up = pay_s[:, width : 2 * width]
    gate = pay_s[:, 2 * width : 2 * width + 1] + pay_s[:, 2 * width + 1 : 2 * width + 2]
    out_low = (gate * up).astype(bf16)
    pre = dot(x, w_in[...])
    cdf = 0.5 * (1.0 + lax.erf(pre * (0.5**0.5)))
    act = (pre * cdf).astype(bf16)
    slope = cdf + pre * jnp.exp(-0.5 * pre * pre) * ((2.0 * np.pi) ** (-0.5))
    pre_low = (dot_nt(out_low, w_out[...]) * slope).astype(bf16)
    both = (dot(act, w_out[...]), dot_nt(pre_low, w_in[...]))
    part = both_s.shape[2]
    for k in range(heads):
        start = k % (heads // 2) * part
        both_s[k] = both[k // (heads // 2)][:, start : start + part].astype(bf16)
    for d in range(heads):
        chunks[d][...] = both_s[head ^ d]
    pre_ref[...] = pre_low
    out_ref[...] = out_low
    x_ref[...] = x
    act_ref[...] = act


def expert_grad_kernel(x_ref, pre_ref, act_ref, out_ref, in_grad, out_grad):
    in_grad[0] = dot_tn(x_ref[...], pre_ref[...])
    out_grad[0] = dot_tn(act_ref[...], out_ref[...])


def sum_kernel(att_ref, *refs, heads):
    parts, att_on, pieces, sum_s = refs[:heads], refs[heads], refs[heads + 1 : -1], refs[-1]
    att_on[...] = att_ref[...]
    total = parts[0][...].astype(f32)
    for d in range(1, heads):
        total = total + parts[d][...].astype(f32)
    sum_s[...] = total
    for j, piece in enumerate(pieces):
        piece[...] = sum_s[j * SLOT : (j + 1) * SLOT, :].astype(bf16)


def join_kernel(*refs):
    parts, out_ref, sum_s = refs[:-2], refs[-2], refs[-1]
    shard = lax.axis_index("seq")
    for j, part in enumerate(parts):
        first = pl.multiple_of((shard ^ j) * SLOT, SLOT)
        sum_s[pl.ds(first, SLOT), :] = part[...].astype(f32)
    out_ref[...] = sum_s[...].astype(bf16)


def prep_kernel(
    cot_ref, w_ref, wq_ref, wk_ref, wv_ref, low_ref, place_ref, attt_ref,
    gh_ref, stack_ref, k_ref, qt_ref, vt_ref, wout_ref, qsel_ref, ght_s, mcot_s,
):
    count, tokens, width = gh_ref.shape
    for i in range(0, tokens, 256):
        rows = pl.ds(i, 256)
        where = place_ref[rows, :].astype(f32)
        free = 1.0 - jnp.sum(where, axis=-1, keepdims=True)
        mcot_s[rows, :] = (cot_ref[rows, :].astype(f32) * free).astype(bf16)
        slots = jnp.transpose(where).astype(bf16)
        for h in range(count):
            stack_ref[h, width:, rows] = slots
    gh = dot_nt(mcot_s[...], w_ref[...]).astype(bf16)
    ght_s[...] = dot_nt(w_ref[...], mcot_s[...]).astype(bf16)
    k = dot_nt(low_ref[...], wk_ref[...]).astype(bf16)
    qt_ref[...] = dot_nt(wq_ref[...], low_ref[...]).astype(bf16) * bf16(width ** (-0.5))
    vt_ref[...] = dot_nt(wv_ref[...], low_ref[...]).astype(bf16)
    for h in range(count):
        cols = slice(h * width, (h + 1) * width)
        gh_ref[h] = gh[:, cols]
        k_ref[h] = k[:, cols]
        stack_ref[h, 0:width, :] = ght_s[cols, :]
    wout_ref[...] = dot(attt_ref[...], mcot_s[...])
    qsel_ref[...] = dot(qt_ref[...], place_ref[...]).astype(bf16)


def masked_back_kernel(
    gh_ref, stack_ref, k_ref, qt_ref, vt_ref, att_ref, prob_ref,
    dq_ref, dkt_ref, dvt_ref, offs_ref, psel_ref, acc_s, score_s, *, h,
):
    tokens, width = dq_ref.shape
    acc_s[...] = jnp.zeros_like(acc_s)
    cols = slice(h * width, (h + 1) * width)
    for i in range(0, tokens, 2 * BLOCK):
        rows = pl.ds(i, 2 * BLOCK)
        gh = gh_ref[h, rows, :]
        delta = jnp.sum(gh.astype(f32) * att_ref[h, rows, :].astype(f32), axis=-1, keepdims=True)
        grads = dot(gh, vt_ref[cols, :]) - delta
        for j in range(2):
            start = i + j * BLOCK
            first = tokens - BLOCK - start
            here = pl.ds(start, BLOCK)
            score = prob_ref[h, here, :].astype(f32) * grads[j * BLOCK : (j + 1) * BLOCK]
            acc_s[:, first : first + tokens] += score
            score_s[here, :] = score.astype(bf16)
    dq_ref[...] = dot(score_s[...], k_ref[h]) * (width ** (-0.5))
    dkt_ref[...] = dot(qt_ref[cols, :], score_s[...])
    both = dot(stack_ref[h], prob_ref[h])
    dvt_ref[...] = both[:width]
    psel_ref[...] = both[width:].astype(bf16)
    offs_ref[...] = diagonals(acc_s[...])


def diagonals(acc):
    span = acc.shape[1]
    rows = acc.shape[0] // 2
    while rows >= 8:
        acc = acc[:rows] + pltpu.roll(acc[rows:], span - rows, 1)
        rows //= 2
    total = acc[0:1]
    for r in range(1, 8):
        total = total + pltpu.roll(acc[r : r + 1], span - r, 1)
    return jnp.broadcast_to(pltpu.roll(total, BLOCK - 1, 1), (8, span))


def slot_back_kernel(*refs, heads):
    parts = refs[:heads]
    (up_ref, normed_ref, hidden_ref, probs_ref, router_ref, gain_ref, w_ref, att_ref,
     wout0_ref) = refs[heads : heads + 9]
    dv_ref, comb_ref, small_ref, wout_ref, gh_ref, ght_ref, delta_ref, ret_s = refs[heads + 9 :]
    head = lax.axis_index("head")
    for d in range(heads):
        ret_s[head ^ d] = parts[d][...]
    back = [ret_s[k].astype(f32) for k in range(heads)]
    combined = jnp.concatenate(back[: heads // 2], axis=1)
    grad_buf = jnp.concatenate(back[heads // 2 :], axis=1)
    up = up_ref[...].astype(f32)
    hidden, normed, probs, gain = hidden_ref[...], normed_ref[...], probs_ref[...], gain_ref[...]
    chosen = chosen_of(probs.shape)
    gate = jnp.sum(jnp.where(chosen, probs, 0.0), axis=-1, keepdims=True)
    comb_ref[...] = gate * combined
    gate_grad = jnp.sum(up * combined, axis=-1, keepdims=True)
    marked = jnp.where(chosen, gate_grad, 0.0)
    logit_grad = probs * (marked - jnp.sum(marked * probs, axis=-1, keepdims=True))
    experts = probs.shape[1]
    grad = grad_buf + jnp.dot(
        logit_grad, router_ref[...], precision=highest, preferred_element_type=f32
    )
    inverse = lax.rsqrt(jnp.mean(hidden * hidden, axis=-1, keepdims=True) + EPS)
    scaled = grad * gain
    inner_sum = jnp.mean(scaled * hidden, axis=-1, keepdims=True)
    dv = inverse * scaled - hidden * (inverse * inverse * inverse * inner_sum)
    dv_ref[...] = dv
    small_ref[...] = jnp.zeros_like(small_ref)
    small_ref[0:1, :] = jnp.sum(grad * hidden * inverse, axis=0, keepdims=True)
    small_ref[8 : 8 + experts, :] = dot_tn(logit_grad, normed, highest)
    grad_low = (up + dv).astype(bf16)
    half = att_ref.shape[0]
    inner = w_ref.shape[0]
    att = jnp.concatenate(
        [att_ref[:, 0:inner].astype(f32), att_ref[:, inner : 2 * inner].astype(f32)], axis=0
    )
    wout_ref[...] = wout0_ref[...] + dot_tn(att.astype(bf16), grad_low)
    gh = dot_nt(grad_low, w_ref[...])
    gh_low = gh.astype(bf16)
    count = gh_ref.shape[0]
    each = inner // count
    ght_ref[...] = dot_nt(w_ref[...], grad_low).astype(bf16)
    for h in range(count):
        cols = slice(h * each, (h + 1) * each)
        gh_ref[h] = gh_low[:, cols]
        delta_ref[h] = jnp.sum(
            gh_low[:, cols].astype(f32) * att[:, cols], axis=-1, keepdims=True
        )


def sparse_back_kernel(
    gh_ref, ght_ref, delta_ref, vt_ref, k_ref, qsel_ref,
    place_ref, wq_ref, wk_ref, wv_ref, low_ref, gain_ref, small_ref, wout_ref, *refs, heads,
):
    per_head, refs = refs[: 4 * gh_ref.shape[0]], refs[4 * gh_ref.shape[0] :]
    psels, dq0s, dkt0s, dvt0s = (per_head[i :: 4] for i in range(4))
    chunks = refs[:heads]
    (score_ref, send_ref, keep_ref, out_ref,
     dq_s, q_low, k_low, v_low, kt_s, vt_s, all_s) = refs[heads:]
    head = lax.axis_index("head")
    count, rows, width = gh_ref.shape
    tokens = vt_ref.shape[1]
    inner = count * width
    for h in range(count):
        cols = slice(h * width, (h + 1) * width)
        grad = dot(gh_ref[h], vt_ref[cols, :])
        prob = psels[h][...]
        score = (prob.astype(f32) * (grad - delta_ref[h])).astype(bf16)
        score_ref[h] = score
        dq_s[:, cols] = dot(score, k_ref[h]) * (width ** (-0.5))
        dkt = dkt0s[h][...] + dot(qsel_ref[cols, :], score)
        dvt = dvt0s[h][...] + dot(ght_ref[cols, :], prob)
        kt_s[cols, :] = dkt.astype(bf16)
        vt_s[cols, :] = dvt.astype(bf16)
        k_low[:, cols] = jnp.transpose(dkt).astype(bf16)
        v_low[:, cols] = jnp.transpose(dvt).astype(bf16)
    spread = dot(place_ref[...], dq_s[...].astype(bf16))
    for h in range(count):
        cols = slice(h * width, (h + 1) * width)
        q_low[:, cols] = (spread[:, cols] + dq0s[h][...]).astype(bf16)
    part = tokens // heads
    for d in range(heads):
        mine = pl.ds(pl.multiple_of((head ^ d) * part, part), part)
        chunks[d][...] = (
            dot(q_low[mine, :], wq_ref[...])
            + dot(k_low[mine, :], wk_ref[...])
            + dot(v_low[mine, :], wv_ref[...])
        ).astype(bf16)
    low = low_ref[...]
    total = None
    grads = (dot_tn(q_low[...], low), dot(kt_s[...], low), dot(vt_s[...], low))
    for i, (grad, w) in enumerate(zip(grads, (wq_ref, wk_ref, wv_ref))):
        all_s[i * inner : (i + 1) * inner, :] = grad
        term = jnp.sum(grad * w[...].astype(f32), axis=0, keepdims=True)
        total = term if total is None else total + term
    all_s[3 * inner :, :] = wout_ref[...]
    out_ref[...] = small_ref[...]
    out_ref[1:2, :] = total / gain_ref[...]
    split_rows(all_s, 1, send_ref, keep_ref)


def is_upper(bit):
    return (lax.axis_index("seq") & bit) != 0


def split_rows(all_s, bit, send_ref, keep_ref):
    half = send_ref.shape[0]
    low, high = all_s[0:half, :], all_s[half : 2 * half, :]
    keep_ref[...] = jnp.where(is_upper(bit), high, low)
    send_ref[...] = jnp.where(is_upper(bit), low, high).astype(bf16)


def halve_kernel(keep_ref, got_ref, *refs, bit):
    send_ref, out_ref, all_s = refs[-3:]
    if len(refs) > 3:
        refs[1][...] = refs[0][...]
    all_s[...] = keep_ref[...] + got_ref[...].astype(f32)
    split_rows(all_s, bit, send_ref, out_ref)


def join_rows(mine_ref, got_ref, all_s, bit):
    half = mine_ref.shape[0]
    mine, got = mine_ref[...].astype(f32), got_ref[...].astype(f32)
    all_s[0:half, :] = jnp.where(is_upper(bit), got, mine)
    all_s[half : 2 * half, :] = jnp.where(is_upper(bit), mine, got)


def pair_kernel(mine_ref, got_ref, *refs, bit):
    out_ref, all_s = refs[-2:]
    if len(refs) > 2:
        refs[1][...] = refs[0][...]
    join_rows(mine_ref, got_ref, all_s, bit)
    out_ref[...] = all_s[...].astype(bf16)


def final_kernel(mine_ref, got_ref, *refs, bit):
    outs, all_s = refs[:-1], refs[-1]
    join_rows(mine_ref, got_ref, all_s, bit)
    inner = outs[0].shape[0]
    for i, out in enumerate(outs):
        out[...] = all_s[i * inner : (i + 1) * inner, :]


def bias_grad_kernel(
    score_ref, place_ref, buckets_ref, small_ref, *refs, bucket_count
):
    count = score_ref.shape[0]
    offs, out_ref, acc_s = refs[:count], refs[count], refs[count + 1]
    tokens = place_ref.shape[0]
    offsets = buckets_ref.shape[1]
    out_ref[...] = small_ref[...]
    bucket_hot = (iota((bucket_count, offsets), 0) == buckets_ref[...]).astype(f32)
    for h in range(count):
        acc_s[...] = jnp.zeros_like(acc_s)
        for i in range(0, tokens, BLOCK):
            first = tokens - BLOCK - i
            acc_s[:, first : first + tokens] += dot(place_ref[i : i + BLOCK, :], score_ref[h])
        sums = diagonals(acc_s[...]) + offs[h][...]
        out_ref[2 + h : 3 + h, :bucket_count] = dot_nt(sums[:, :offsets], bucket_hot, highest)[0:1]


def hidden_kernel(*refs, heads):
    att_parts, w_ref, x_ref, out_ref, att_s = refs[:heads], *refs[heads:]
    head = lax.axis_index("head")
    tokens = x_ref.shape[0]
    inner = att_parts[0].shape[0]
    for d in range(heads):
        mine = pl.ds(pl.multiple_of((head ^ d) * inner, inner), inner)
        att_s[mine, :] = att_parts[d][...]
    for i in range(0, tokens, 256):
        rows = pl.ds(i, 256)
        out_ref[rows, :] = x_ref[rows, :].astype(f32) + dot_tn(att_s[:, rows], w_ref[...])


def output_kernel(hidden_ref, place_ref, comb_ref, out_ref):
    high, rest = split_two(comb_ref[...])
    for i in range(0, hidden_ref.shape[0], 256):
        rows = pl.ds(i, 256)
        where = place_ref[rows, :]
        out_ref[rows, :] = hidden_ref[rows, :] + (dot(where, high) + dot(where, rest))


def first_norm_kernel(*refs):
    parts = refs[:-9]
    (x_ref, cot_ref, place_ref, dv_ref, gain_ref, keep_ref, got_ref, out_ref, sum_ref) = refs[-9:]
    grad = parts[0][...].astype(f32)
    for part in parts[1:]:
        grad = grad + part[...].astype(f32)
    x = x_ref[...].astype(f32)
    inverse = lax.rsqrt(jnp.mean(x * x, axis=-1, keepdims=True) + EPS)
    scaled = grad * gain_ref[...]
    inner_sum = jnp.mean(scaled * x, axis=-1, keepdims=True)
    high, rest = split_two(dv_ref[...])
    hidden_grad = cot_ref[...].astype(f32) + (dot(place_ref[...], high) + dot(place_ref[...], rest))
    out_ref[...] = (
        hidden_grad + inverse * scaled - x * (inverse * inverse * inverse * inner_sum)
    ).astype(bf16)
    sum_ref[...] = (keep_ref[...] + got_ref[...].astype(f32)).astype(bf16)


def spread_kernel(*refs):
    parts, out_ref = refs[:-1], refs[-1]
    head = lax.axis_index("head")
    part = parts[0].shape[0]
    for d in range(len(parts)):
        mine = pl.ds(pl.multiple_of((head ^ d) * part, part), part)
        out_ref[mine, :] = parts[d][...].astype(f32)


def swap(x, axis, d):
    size = lax.axis_size(axis)
    return lax.ppermute(x, axis, [(i, i ^ d) for i in range(size)])


def share(x, axis):
    return [x] + [swap(x, axis, d) for d in range(1, lax.axis_size(axis))]


def trade(pieces, axis):
    return lax.all_to_all(pieces, axis, split_axis=0, concat_axis=0, tiled=True)


def swap_all(pieces, axis):
    return [pieces[0]] + [swap(pieces[d], axis, d) for d in range(1, len(pieces))]


def bits_of(axis):
    return [b for b in (1 << i for i in range(16)) if b < lax.axis_size(axis)]


def halve(send, keep, bit, after, passed=()):
    rows, width = keep.shape
    return call(
        partial(halve_kernel, bit=bit),
        [shape_of(*a.shape, a.dtype) for a in passed]
        + [shape_of(rows // 2, width, bf16), shape_of(rows // 2, width, f32)],
        (keep, swap(send, "seq", bit // 2)) + tuple(passed),
        scratch=[pltpu.VMEM((rows, width), f32)],
        name="halve",
        after=after,
        token=True,
    )


def pair(now, bit, after, passed=()):
    rows, width = now.shape
    return call(
        partial(pair_kernel, bit=bit),
        [shape_of(*a.shape, a.dtype) for a in passed] + [shape_of(2 * rows, width, bf16)],
        (now, swap(now, "seq", bit)) + tuple(passed),
        scratch=[pltpu.VMEM((2 * rows, width), f32)],
        name="pair",
        after=after,
        token=True,
    )


def sum_small(x, axes):
    for axis in axes:
        d = 1
        while d < lax.axis_size(axis):
            x = x + swap(x, axis, d)
            d *= 2
    return x


def on_device(
    layer_input, cotangent, norm1_gain, w_query, w_key, w_value, w_attn_out, bias_table,
    norm2_gain, w_router, w_expert_in, w_expert_out, expert_ids, slot_ids, buckets,
):
    tokens, width = layer_input.shape
    shards = lax.axis_size("seq")
    heads = lax.axis_size("head")
    bucket_count, count = bias_table.shape
    inner = w_query.shape[1]
    each = inner // count
    experts = w_router.shape[1]
    rows = experts * SLOT
    hidden_units = w_expert_in.shape[2]
    part = tokens // heads
    split = 2 * width // heads
    span = 2 * tokens
    params = pltpu.CompilerParams(vmem_limit_bytes=VMEM_LIMIT if rows <= 256 else VMEM_ALL)

    ids = expert_ids.reshape(1, tokens)
    slots = slot_ids.reshape(1, tokens)
    bucket_row = buckets.reshape(1, -1)
    wq_t, wk_t, wv_t = jnp.transpose(w_query), jnp.transpose(w_key), jnp.transpose(w_value)
    router_t, table_t = jnp.transpose(w_router), jnp.transpose(bias_table)
    w_in = w_expert_in.reshape(width, hidden_units)
    w_out = w_expert_out.reshape(hidden_units, width)

    w_mix = share(w_attn_out, "head")

    low, prob, att, att_t, att_sel = pl.pallas_call(
        attend_kernel,
        grid=(count,),
        out_shape=(
            shape_of(tokens, width, bf16),
            jax.ShapeDtypeStruct((count, tokens, tokens), bf16),
            jax.ShapeDtypeStruct((count, tokens, each), bf16),
            shape_of(inner, tokens, bf16),
            shape_of(rows // 2, 2 * inner, bf16),
        ),
        in_specs=[spec(pltpu.HBM)] * 9,
        out_specs=(
            whole((tokens, width)), by_head((1, tokens, tokens)), by_head((1, tokens, each)),
            whole((inner, tokens)), whole((rows // 2, 2 * inner)),
        ),
        scratch_shapes=[
            pltpu.VMEM((count, tokens, each), bf16),
            pltpu.VMEM((inner, tokens), bf16),
            pltpu.VMEM((count, tokens, each), bf16),
            pltpu.VMEM((8, span), f32),
            pltpu.VMEM((BLOCK, span), f32),
            pltpu.VMEM((rows, tokens), bf16),
            pltpu.VMEM((2 * BLOCK, tokens), f32),
            pltpu.VMEM((tokens, width), bf16),
            pltpu.VMEM((width,), f32),
            pltpu.VMEM((inner, width), bf16),
            pltpu.VMEM((inner, width), bf16),
            pltpu.VMEM((inner, width), bf16),
            pltpu.VMEM((count, bucket_count), f32),
            pltpu.VMEM((1, span - 1), jnp.int32),
            pltpu.VMEM((1, tokens), jnp.int32),
            pltpu.VMEM((1, tokens), jnp.int32),
            pltpu.SemaphoreType.DMA((9,)),
        ],
        compiler_params=params,
        cost_estimate=NO_COST,
        name="attend",
    )(
        *(
            pltpu.with_memory_space_constraint(a, pltpu.HBM)
            for a in (layer_input, norm1_gain, wq_t, wk_t, wv_t, table_t, bucket_row, ids, slots)
        )
    )

    att_sel, w_full = call(
        partial(mix_kernel, heads=heads),
        [shape_of(rows // 2, 2 * inner, bf16), shape_of(heads * inner, width, bf16)],
        (att_sel,) + tuple(w_mix),
        name="mix",
    )
    sel_parts = share(att_sel, "head")
    sel_in, sel_up, place, place_c, x_c, cot_c = call(
        place_kernel,
        [
            shape_of(rows, width, bf16),
            shape_of(rows, width, bf16),
            shape_of(tokens, rows, bf16),
            shape_of(part, rows, bf16),
            shape_of(part, width, bf16),
            shape_of(part, width, bf16),
        ],
        (layer_input, cotangent, ids, slots),
        scratch=[pltpu.VMEM((tokens, rows), f32)],
        moved=12 * 2**20,
        name="place",
        after=(att_sel,),
    )
    routed = call(
        partial(route_kernel, shards=shards, heads=heads),
        [
            shape_of(rows, width, f32),
            shape_of(rows, width, f32),
            shape_of(rows, experts, f32),
            shape_of(inner, tokens, bf16),
        ]
        + [shape_of(SLOT, 2 * width + 128, bf16)] * shards,
        tuple(sel_parts) + (w_full, sel_in, sel_up, norm2_gain, router_t, att_t),
        scratch=[
            pltpu.VMEM((heads, rows, inner), bf16),
            pltpu.VMEM((rows, 2 * width + 128), f32),
        ],
        name="route",
        token=True,
    )
    hidden_sel, normed_sel, probs, att_on = routed[:4]
    pay_parts = swap_all(routed[4:-1], "seq")
    att_parts = [att_t] + [swap(att_on, "head", d) for d in range(1, heads - 1)]

    gh, stack, k_rows, q_t, v_t, wout0, q_sel, prepared = call(
        prep_kernel,
        [
            jax.ShapeDtypeStruct((count, tokens, each), bf16),
            jax.ShapeDtypeStruct((count, each + rows, tokens), bf16),
            jax.ShapeDtypeStruct((count, tokens, each), bf16),
            shape_of(inner, tokens, bf16),
            shape_of(inner, tokens, bf16),
            shape_of(inner, width, f32),
            shape_of(inner, rows, bf16),
        ],
        (cotangent, w_attn_out, wq_t, wk_t, wv_t, low, place, att_t),
        scratch=[pltpu.VMEM((inner, tokens), bf16), pltpu.VMEM((tokens, width), bf16)],
        name="prep",
        after=(routed[-1],),
        moved=8 * 2**20,
        token=True,
    )

    def masked_back(h, after):
        return call(
            partial(masked_back_kernel, h=h),
            [
                shape_of(tokens, each, f32),
                shape_of(each, tokens, f32),
                shape_of(each, tokens, f32),
                shape_of(8, span, f32),
                shape_of(rows, tokens, bf16),
            ],
            (gh, stack, k_rows, q_t, v_t, att, prob),
            scratch=[pltpu.VMEM((BLOCK, span), f32), pltpu.VMEM((tokens, tokens), bf16)],
            name="masked_back",
            after=after,
            moved=11 * 2**20,
            token=True,
        )

    done = call(
        partial(expert_kernel, shards=shards, heads=heads),
        [shape_of(rows, split, bf16)] * heads
        + [
            shape_of(rows, width, bf16),
            shape_of(rows, hidden_units, bf16),
            shape_of(rows, hidden_units, bf16),
            shape_of(rows, width, bf16),
        ],
        tuple(pay_parts) + (w_in, w_out),
        scratch=[
            pltpu.VMEM((rows, 2 * width + 128), f32),
            pltpu.VMEM((heads, rows, split), bf16),
        ],
        name="expert",
        after=(prepared,) + tuple(att_parts[1:]),
        token=True,
    )
    x_rows, act, pre_low, out_low, token = done[heads:]
    masked = []
    for h in range(count - 2):
        masked.append(masked_back(h, (token,)))
        token = masked[-1][-1]
    returned = call(
        partial(sum_kernel, heads=heads),
        [shape_of(inner, tokens, bf16)] + [shape_of(SLOT, split, bf16)] * shards,
        [att_t] + swap_all(done[:heads], "head"),
        scratch=[pltpu.VMEM((rows, split), f32)],
        name="sum",
        after=(token,),
        token=True,
    )
    masked.append(masked_back(count - 2, (returned[-1],)))
    att_parts.append(swap(returned[0], "head", heads - 1))
    joined, token = call(
        join_kernel,
        [shape_of(rows, split, bf16)],
        swap_all(returned[1:-1], "seq"),
        scratch=[pltpu.VMEM((rows, split), f32)],
        name="join",
        after=(masked[-1][-1], att_parts[-1]),
        token=True,
    )
    masked.append(masked_back(count - 1, (token,)))
    full_parts = share(joined, "head")

    small_rows = 8 + -(-experts // 8) * 8
    dv_sel, comb_sel, small, wout_part, gh_sel, ght_sel, delta_sel = call(
        partial(slot_back_kernel, heads=heads),
        [
            shape_of(rows, width, f32),
            shape_of(rows, width, f32),
            shape_of(small_rows, width, f32),
            shape_of(inner, width, f32),
            jax.ShapeDtypeStruct((count, rows, each), bf16),
            shape_of(inner, rows, bf16),
            jax.ShapeDtypeStruct((count, rows, 1), f32),
        ],
        tuple(full_parts)
        + (sel_up, normed_sel, hidden_sel, probs, router_t, norm2_gain)
        + (w_attn_out, att_sel, wout0),
        scratch=[pltpu.VMEM((heads, rows, split), bf16)],
        name="slot_back",
        after=(masked[-1][-1],),
    )

    back = call(
        partial(sparse_back_kernel, heads=heads),
        [shape_of(part, width, bf16)] * heads
        + [
            jax.ShapeDtypeStruct((count, rows, tokens), bf16),
            shape_of(2 * inner, width, bf16),
            shape_of(2 * inner, width, f32),
            shape_of(small_rows, width, f32),
        ],
        (gh_sel, ght_sel, delta_sel, v_t, k_rows, q_sel, place)
        + (wq_t, wk_t, wv_t, low, norm1_gain, small, wout_part)
        + tuple(a for m in masked for a in (m[4], m[0], m[1], m[2])),
        scratch=[
            pltpu.VMEM((rows, inner), f32),
            pltpu.VMEM((tokens, inner), bf16),
            pltpu.VMEM((tokens, inner), bf16),
            pltpu.VMEM((tokens, inner), bf16),
            pltpu.VMEM((inner, tokens), bf16),
            pltpu.VMEM((inner, tokens), bf16),
            pltpu.VMEM((4 * inner, width), f32),
        ],
        name="sparse_back",
    )
    score_sel, send, keep, small = back[heads:]
    chunks = back[:heads]
    first_parts = [chunks[0]] + [swap(chunks[d], "head", d) for d in range(1, heads - 1)]

    bits = bits_of("seq")
    send, keep, token = halve(send, keep, bits[1], ())
    small, token = call(
        partial(bias_grad_kernel, bucket_count=bucket_count),
        [shape_of(small_rows, width, f32)],
        (score_sel, place, bucket_row, small) + tuple(m[3] for m in masked),
        scratch=[pltpu.VMEM((BLOCK, span), f32)],
        name="bias_grad",
        after=(token,),
        moved=16 * 2**20,
        token=True,
    )
    small_sum = sum_small(small, ("seq",))
    gain1_sum = sum_small(small_sum[1:2], ("head",))
    chunk, send, keep, token = halve(
        send, keep, bits[2], tuple(first_parts[1:]) + (token,), (chunks[-1],)
    )
    first_parts.append(swap(chunk, "head", heads - 1))
    w_in_grad, w_out_grad, token = call(
        expert_grad_kernel,
        [
            jax.ShapeDtypeStruct(w_expert_in.shape, f32),
            jax.ShapeDtypeStruct(w_expert_out.shape, f32),
        ],
        (x_rows, pre_low, act, out_low),
        name="expert_grad",
        after=(token,),
        moved=10 * 2**20,
        token=True,
    )
    hidden, token = call(
        partial(hidden_kernel, heads=heads),
        [shape_of(tokens, width, f32)],
        tuple(att_parts) + (w_full, layer_input),
        scratch=[pltpu.VMEM((heads * inner, tokens), bf16)],
        name="hidden",
        after=(token,),
        moved=6 * 2**20,
        token=True,
    )
    for bit in bits[3:]:
        send, keep, token = halve(send, keep, bit, (token,))

    grad_part, weights, token = call(
        first_norm_kernel,
        [shape_of(part, width, bf16), shape_of(keep.shape[0], width, bf16)],
        tuple(first_parts)
        + (x_c, cot_c, place_c, dv_sel, norm1_gain, keep, swap(send, "seq", bits[-1])),
        name="first_norm",
        after=(token,),
        token=True,
    )
    grad_parts = [grad_part] + [swap(grad_part, "head", d) for d in range(1, heads - 1)]
    layer_output, token = call(
        output_kernel,
        [shape_of(tokens, width, f32)],
        (hidden, place, comb_sel),
        name="output",
        after=(token,),
        moved=10 * 2**20,
        token=True,
    )
    for bit in reversed(bits[3:]):
        weights, token = pair(weights, bit, (token,))
    grad_on, weights, token = pair(
        weights, bits[2], tuple(grad_parts[1:]) + (token, small_sum), (grad_part,)
    )
    grad_parts.append(swap(grad_on, "head", heads - 1))
    weights, token = pair(weights, bits[1], (grad_parts[-1], gain1_sum))
    weight_sums = call(
        partial(final_kernel, bit=bits[0]),
        [shape_of(inner, width, f32)] * 4,
        (weights, swap(weights, "seq", bits[0])),
        scratch=[pltpu.VMEM((4 * inner, width), f32)],
        name="weights_out",
    )
    (input_grad,) = call(
        spread_kernel,
        [shape_of(tokens, width, f32)],
        tuple(grad_parts),
        name="spread",
    )

    return (
        layer_output,
        input_grad,
        gain1_sum[0],
        jnp.transpose(weight_sums[0]),
        jnp.transpose(weight_sums[1]),
        jnp.transpose(weight_sums[2]),
        weight_sums[3],
        jnp.transpose(small_sum[2 : 2 + count, :bucket_count]),
        small_sum[0],
        jnp.transpose(small_sum[8 : 8 + experts]),
        w_in_grad,
        w_out_grad,
    )


def solution(mesh):
    return jax.shard_map(
        on_device,
        mesh=mesh,
        in_specs=(
            P("seq", None),
            P("seq", None),
            P(),
            P(None, "head"),
            P(None, "head"),
            P(None, "head"),
            P("head", None),
            P(None, "head"),
            P(),
            P(),
            P("seq", None, "head"),
            P("seq", "head", None),
            P("seq"),
            P("seq"),
            P(),
        ),
        out_specs=(
            P("seq", None),
            P("seq", None),
            P(),
            P(None, "head"),
            P(None, "head"),
            P(None, "head"),
            P("head", None),
            P(None, "head"),
            P(),
            P(),
            P("seq", None, "head"),
            P("seq", "head", None),
        ),
        check_vma=False,
    )
```

```python
from functools import partial

import jax
import jax.numpy as jnp
import numpy as np
from jax import lax
from jax.experimental import pallas as pl
from jax.experimental.pallas import tpu as pltpu
from jax.sharding import PartitionSpec as P

CAP = 20
SLOT = 24
EPS = 1e-06
BLOCK = 128
ROWS = 16
VMEM_LIMIT = 26 * 1024 * 1024
VMEM_ALL = 60 * 1024 * 1024
NO_COST = pl.CostEstimate(flops=1, bytes_accessed=1, transcendentals=0)

f32 = jnp.float32
bf16 = jnp.bfloat16
highest = lax.Precision.HIGHEST


def dot(a, b):
    return jnp.dot(a, b, preferred_element_type=f32)


def dot_nt(a, b, precision=None):
    return lax.dot_general(
        a, b, (((1,), (1,)), ((), ())), precision=precision, preferred_element_type=f32
    )


def dot_tn(a, b, precision=None):
    return lax.dot_general(
        a, b, (((0,), (0,)), ((), ())), precision=precision, preferred_element_type=f32
    )


def iota(shape, dim):
    return lax.broadcasted_iota(jnp.int32, shape, dim)


def split_two(v):
    high = v.astype(bf16)
    return high, (v - high.astype(f32)).astype(bf16)


def shape_of(rows, cols, dtype):
    return jax.ShapeDtypeStruct((rows, cols), dtype)


def spec(memory):
    return pl.BlockSpec(memory_space=memory)


def call(kernel, outs, args, scratch=(), name=None, after=(), moved=1, token=False):
    outs, args = tuple(outs), tuple(args)
    held = sum(int(np.prod(a.shape)) * np.dtype(a.dtype).itemsize for a in args + outs)
    if token:
        outs += (shape_of(8, 128, f32),)
    first_out = len(args) + len(after)

    def body(*refs):
        results = refs[first_out : first_out + len(outs)]
        if token:
            results[-1][...] = jnp.zeros((8, 128), f32)
            results = results[:-1]
        kernel(*refs[: len(args)], *results, *refs[first_out + len(outs) :])

    return pl.pallas_call(
        body,
        out_shape=outs,
        in_specs=[spec(pltpu.VMEM)] * len(args) + [spec(pl.ANY)] * len(after),
        out_specs=tuple(spec(pltpu.VMEM) for _ in outs),
        scratch_shapes=list(scratch),
        compiler_params=pltpu.CompilerParams(
            vmem_limit_bytes=VMEM_LIMIT if 2 * held < VMEM_LIMIT else VMEM_ALL
        ),
        cost_estimate=pl.CostEstimate(flops=1, bytes_accessed=moved, transcendentals=0),
        name=name,
    )(*args, *after)


def whole(shape):
    return pl.BlockSpec(shape, lambda h: (0,) * len(shape))


def by_head(shape):
    return pl.BlockSpec(shape, lambda h: (h,) + (0,) * (len(shape) - 1))


def slot_rows(ids, slots, rows, each):
    cell = jnp.where(slots < CAP, ids * each + slots, -1)
    return (iota((rows, cell.shape[1]), 0) == cell).astype(f32)


def place_kernel(
    x_ref, cot_ref, ids_ref, slots_ref, sel_in, sel_up, place, place_c, x_c, cot_c, place_s
):
    head = lax.axis_index("head")
    part = x_c.shape[0]
    slot_hot = slot_rows(ids_ref[...], slots_ref[...], sel_in.shape[0], SLOT)
    place_s[...] = jnp.transpose(slot_hot)
    slot_low = slot_hot.astype(bf16)
    sel_in[...] = dot(slot_low, x_ref[...]).astype(bf16)
    sel_up[...] = dot(slot_low, cot_ref[...]).astype(bf16)
    place[...] = place_s[...].astype(bf16)
    mine = pl.ds(pl.multiple_of(head * part, part), part)
    place_c[...] = place_s[mine, :].astype(bf16)
    x_c[...] = x_ref[mine, :]
    cot_c[...] = cot_ref[mine, :]


def attend_kernel(*refs):
    given, refs = refs[:9], refs[9:]
    low_ref, prob_ref, att_ref, attt_ref, sel_ref = refs[:5]
    q_s, kt_s, v_s, bias_s, skew_s, slot_s, score_s = refs[5:12]
    here, sems = refs[12:21], refs[21]
    x_ref, gain_ref, wq_ref, wk_ref, wv_ref, table_ref, buckets_ref, ids_ref, slots_ref = here
    copies = [
        pltpu.make_async_copy(far, near, sems.at[i])
        for i, (far, near) in enumerate(zip(given, here))
    ]
    step = pl.program_id(0)
    tokens = x_ref.shape[0]
    inner = wq_ref.shape[0]
    count = q_s.shape[0]
    width = inner // count

    @pl.when(step == 0)
    def _():
        for copy in copies:
            copy.start()
        for copy in copies:
            copy.wait()
        for i in range(0, tokens, 256):
            rows = pl.ds(i, 256)
            x = x_ref[rows, :].astype(f32)
            inverse = lax.rsqrt(jnp.mean(x * x, axis=-1, keepdims=True) + EPS)
            low_ref[rows, :] = (x * inverse * gain_ref[...]).astype(bf16)
        low = low_ref[...]
        q = dot_nt(low, wq_ref[...]).astype(bf16) * bf16(width ** (-0.5))
        kt_s[...] = dot_nt(wk_ref[...], low).astype(bf16)
        v = dot_nt(low, wv_ref[...]).astype(bf16)
        for h in range(count):
            cols = slice(h * width, (h + 1) * width)
            q_s[h] = q[:, cols]
            v_s[h] = v[:, cols]
        offsets = buckets_ref.shape[1]
        bucket_hot = (iota((table_ref.shape[1], offsets), 0) == buckets_ref[...]).astype(f32)
        slot_s[...] = slot_rows(ids_ref[...], slots_ref[...], slot_s.shape[0], CAP).astype(bf16)
        bias_s[...] = jnp.zeros_like(bias_s)
        bias_s[:count, :offsets] = jnp.dot(
            table_ref[...], bucket_hot, precision=highest, preferred_element_type=f32
        )

    span = skew_s.shape[1]
    row = bias_s[pl.ds(step, 1), :]
    skew_s[...] = pltpu.roll(
        jnp.broadcast_to(row, skew_s.shape), span - (BLOCK - 1), 1, stride=1, stride_axis=0
    )
    head_rows = pl.ds(pl.multiple_of(step * width, width), width)
    for i in range(0, tokens, 2 * BLOCK):
        score_s[...] = dot(q_s[step, pl.ds(i, 2 * BLOCK), :], kt_s[head_rows, :])
        for j in range(0, 2 * BLOCK, ROWS):
            first = tokens - BLOCK - (i + j) // BLOCK * BLOCK
            bias = skew_s[j % BLOCK : j % BLOCK + ROWS, first : first + tokens]
            score = score_s[j : j + ROWS, :] + bias
            weight = jnp.exp(score - jnp.max(score, axis=-1, keepdims=True))
            total = jnp.sum(weight, axis=-1, keepdims=True)
            prob_ref[0, pl.ds(i + j, ROWS), :] = (weight * (1.0 / total)).astype(bf16)
    att = dot(prob_ref[0], v_s[step])
    att_low = att.astype(bf16)
    att_ref[0] = att_low
    attt_ref[head_rows, :] = jnp.transpose(att).astype(bf16)
    picked = dot(slot_s[...], att_low).astype(bf16)
    half = sel_ref.shape[0]
    for h in range(count):

        @pl.when(step == h)
        def _():
            for part in range(2):
                start = part * inner + h * width
                sel_ref[:, start : start + width] = picked[part * half : (part + 1) * half]


def mix_kernel(att_ref, *refs, heads):
    w_parts, att_on, w_ref = refs[:heads], refs[heads], refs[heads + 1]
    att_on[...] = att_ref[...]
    head = lax.axis_index("head")
    inner = w_parts[0].shape[0]
    for d in range(heads):
        mine = pl.ds(pl.multiple_of((head ^ d) * inner, inner), inner)
        w_ref[mine, :] = w_parts[d][...]


def widen(rows, wide_s):
    wide_s[...] = jnp.zeros_like(wide_s)
    for e in range(rows.shape[0] // CAP):
        wide_s[e * SLOT : e * SLOT + CAP, :] = rows[e * CAP : (e + 1) * CAP]
    return wide_s[...]


def route_kernel(*refs, shards, heads):
    att_parts, w_ref = refs[:heads], refs[heads]
    (sel_in, sel_up, gain_ref, router_ref, att_t, hidden_ref, normed_ref, probs_ref, att_on
     ) = refs[heads + 1 : heads + 10]
    pieces = refs[heads + 10 : heads + 10 + shards]
    att_s, pay_s, wide_s = refs[heads + 10 + shards :]
    head = lax.axis_index("head")
    half = att_parts[0].shape[0]
    inner = w_ref.shape[0] // heads
    for d in range(heads):
        att_s[d, 0:half, :] = att_parts[d][:, 0:inner]
        att_s[d, half : 2 * half, :] = att_parts[d][:, inner : 2 * inner]
    mixed = None
    for k in range(heads):
        term = dot(att_s[head ^ k], w_ref[k * inner : (k + 1) * inner, :])
        mixed = term if mixed is None else mixed + term
    hidden = sel_in[...].astype(f32) + widen(mixed, wide_s)
    hidden_ref[...] = hidden
    inverse = lax.rsqrt(jnp.mean(hidden * hidden, axis=-1, keepdims=True) + EPS)
    normed = hidden * inverse * gain_ref[...]
    normed_ref[...] = normed
    logits = dot_nt(normed, router_ref[...], highest)
    logits = logits - jnp.max(logits, axis=-1, keepdims=True)
    powers = jnp.exp(logits)
    probs = powers / jnp.sum(powers, axis=-1, keepdims=True)
    probs_ref[...] = probs
    gate = jnp.sum(jnp.where(chosen_of(probs.shape), probs, 0.0), axis=-1, keepdims=True)
    high = gate.astype(bf16).astype(f32)
    lane = iota((gate.shape[0], 128), 1)
    width = normed.shape[1]
    extra = jnp.where(lane == 0, high, jnp.where(lane == 1, gate - high, 0.0))
    pay_s[:, :width] = normed
    pay_s[:, width : 2 * width] = sel_up[...].astype(f32)
    pay_s[:, 2 * width :] = extra
    shard = lax.axis_index("seq")
    for j in range(shards):
        first = pl.multiple_of((shard ^ j) * SLOT, SLOT)
        pieces[j][...] = pay_s[pl.ds(first, SLOT), :].astype(bf16)
    att_on[...] = att_t[...]


def chosen_of(shape):
    expert = iota(shape, 1) * SLOT
    slot_row = iota(shape, 0)
    return (slot_row >= expert) & (slot_row < expert + SLOT)


def expert_kernel(*refs, shards, heads):
    parts = refs[:shards]
    w_in, w_out = refs[shards : shards + 2]
    chunks = refs[shards + 2 : shards + 2 + heads]
    x_ref, act_ref, pre_ref, out_ref, pay_s, both_s = refs[shards + 2 + heads :]
    head = lax.axis_index("head")
    width = x_ref.shape[1]
    for j in range(shards):
        pay_s[j * SLOT : (j + 1) * SLOT, :] = parts[j][...].astype(f32)
    x = pay_s[:, :width].astype(bf16)
    up = pay_s[:, width : 2 * width]
    gate = pay_s[:, 2 * width : 2 * width + 1] + pay_s[:, 2 * width + 1 : 2 * width + 2]
    out_low = (gate * up).astype(bf16)
    pre = dot(x, w_in[...])
    cdf = 0.5 * (1.0 + lax.erf(pre * (0.5**0.5)))
    act = (pre * cdf).astype(bf16)
    slope = cdf + pre * jnp.exp(-0.5 * pre * pre) * ((2.0 * np.pi) ** (-0.5))
    pre_low = (dot_nt(out_low, w_out[...]) * slope).astype(bf16)
    both = (dot(act, w_out[...]), dot_nt(pre_low, w_in[...]))
    part = both_s.shape[2]
    for k in range(heads):
        start = k % (heads // 2) * part
        for j in range(shards):
            both_s[k, j * CAP : (j + 1) * CAP, :] = both[k // (heads // 2)][
                j * SLOT : j * SLOT + CAP, start : start + part
            ]
    for d in range(heads):
        chunks[d][...] = both_s[head ^ d].astype(bf16)
    pre_ref[...] = pre_low
    out_ref[...] = out_low
    x_ref[...] = x
    act_ref[...] = act


def expert_grad_kernel(x_ref, pre_ref, act_ref, out_ref, in_grad, out_grad):
    in_grad[0] = dot_tn(x_ref[...], pre_ref[...])
    out_grad[0] = dot_tn(act_ref[...], out_ref[...])


def sum_kernel(att_ref, *refs, heads):
    parts, att_on, pieces, sum_s = refs[:heads], refs[heads], refs[heads + 1 : -1], refs[-1]
    att_on[...] = att_ref[...]
    total = parts[0][...].astype(f32)
    for d in range(1, heads):
        total = total + parts[d][...].astype(f32)
    sum_s[...] = total
    for j, piece in enumerate(pieces):
        piece[...] = sum_s[j * CAP : (j + 1) * CAP, :].astype(bf16)


def join_kernel(*refs):
    parts, out_ref, sum_s = refs[:-2], refs[-2], refs[-1]
    for j, part in enumerate(parts):
        sum_s[j * CAP : (j + 1) * CAP, :] = part[...].astype(f32)
    out_ref[...] = sum_s[...].astype(bf16)


def prep_kernel(
    cot_ref, w_ref, wq_ref, wk_ref, wv_ref, low_ref, place_ref, attt_ref,
    gh_ref, stack_ref, k_ref, qt_ref, vt_ref, wout_ref, qsel_ref, ght_s, mcot_s,
):
    count, tokens, width = gh_ref.shape
    for i in range(0, tokens, 256):
        rows = pl.ds(i, 256)
        where = place_ref[rows, :].astype(f32)
        free = 1.0 - jnp.sum(where, axis=-1, keepdims=True)
        mcot_s[rows, :] = (cot_ref[rows, :].astype(f32) * free).astype(bf16)
        slots = jnp.transpose(where).astype(bf16)
        for h in range(count):
            stack_ref[h, width:, rows] = slots
    gh = dot_nt(mcot_s[...], w_ref[...]).astype(bf16)
    ght_s[...] = dot_nt(w_ref[...], mcot_s[...]).astype(bf16)
    k = dot_nt(low_ref[...], wk_ref[...]).astype(bf16)
    qt_ref[...] = dot_nt(wq_ref[...], low_ref[...]).astype(bf16) * bf16(width ** (-0.5))
    vt_ref[...] = dot_nt(wv_ref[...], low_ref[...]).astype(bf16)
    for h in range(count):
        cols = slice(h * width, (h + 1) * width)
        gh_ref[h] = gh[:, cols]
        k_ref[h] = k[:, cols]
        stack_ref[h, 0:width, :] = ght_s[cols, :]
    wout_ref[...] = dot(attt_ref[...], mcot_s[...])
    qsel_ref[...] = dot(qt_ref[...], place_ref[...]).astype(bf16)


def masked_back_kernel(
    gh_ref, stack_ref, k_ref, qt_ref, vt_ref, att_ref, prob_ref,
    dq_ref, dkt_ref, dvt_ref, offs_ref, psel_ref, acc_s, score_s, *, h,
):
    tokens, width = dq_ref.shape
    acc_s[...] = jnp.zeros_like(acc_s)
    cols = slice(h * width, (h + 1) * width)
    for i in range(0, tokens, 2 * BLOCK):
        rows = pl.ds(i, 2 * BLOCK)
        gh = gh_ref[h, rows, :]
        delta = jnp.sum(gh.astype(f32) * att_ref[h, rows, :].astype(f32), axis=-1, keepdims=True)
        grads = dot(gh, vt_ref[cols, :]) - delta
        for j in range(2):
            start = i + j * BLOCK
            first = tokens - BLOCK - start
            here = pl.ds(start, BLOCK)
            score = prob_ref[h, here, :].astype(f32) * grads[j * BLOCK : (j + 1) * BLOCK]
            acc_s[:, first : first + tokens] += score
            score_s[here, :] = score.astype(bf16)
    dq_ref[...] = dot(score_s[...], k_ref[h]) * (width ** (-0.5))
    dkt_ref[...] = dot(qt_ref[cols, :], score_s[...])
    both = dot(stack_ref[h], prob_ref[h])
    dvt_ref[...] = both[:width]
    psel_ref[...] = both[width:].astype(bf16)
    offs_ref[...] = diagonals(acc_s[...])


def diagonals(acc):
    span = acc.shape[1]
    rows = acc.shape[0] // 2
    while rows >= 8:
        acc = acc[:rows] + pltpu.roll(acc[rows:], span - rows, 1)
        rows //= 2
    total = acc[0:1]
    for r in range(1, 8):
        total = total + pltpu.roll(acc[r : r + 1], span - r, 1)
    return jnp.broadcast_to(pltpu.roll(total, BLOCK - 1, 1), (8, span))


def slot_back_kernel(*refs, heads):
    parts = refs[:heads]
    (up_ref, normed_ref, hidden_ref, probs_ref, router_ref, gain_ref, w_ref, att_ref,
     wout0_ref) = refs[heads : heads + 9]
    (dv_ref, comb_ref, small_ref, wout_ref, gh_ref, ght_ref, delta_ref, ret_s, wide_s
     ) = refs[heads + 9 :]
    head, shard = lax.axis_index("head"), lax.axis_index("seq")
    ret_s[...] = jnp.zeros_like(ret_s)
    for d in range(heads):
        part = parts[d][...].astype(f32)
        for j in range(part.shape[0] // CAP):
            first = pl.multiple_of((shard ^ j) * SLOT, SLOT)
            ret_s[head ^ d, pl.ds(first, CAP), :] = part[j * CAP : (j + 1) * CAP]
    back = [ret_s[k] for k in range(heads)]
    combined = jnp.concatenate(back[: heads // 2], axis=1)
    grad_buf = jnp.concatenate(back[heads // 2 :], axis=1)
    up = up_ref[...].astype(f32)
    hidden, normed, probs, gain = hidden_ref[...], normed_ref[...], probs_ref[...], gain_ref[...]
    chosen = chosen_of(probs.shape)
    gate = jnp.sum(jnp.where(chosen, probs, 0.0), axis=-1, keepdims=True)
    comb_ref[...] = gate * combined
    gate_grad = jnp.sum(up * combined, axis=-1, keepdims=True)
    marked = jnp.where(chosen, gate_grad, 0.0)
    logit_grad = probs * (marked - jnp.sum(marked * probs, axis=-1, keepdims=True))
    experts = probs.shape[1]
    grad = grad_buf + jnp.dot(
        logit_grad, router_ref[...], precision=highest, preferred_element_type=f32
    )
    inverse = lax.rsqrt(jnp.mean(hidden * hidden, axis=-1, keepdims=True) + EPS)
    scaled = grad * gain
    inner_sum = jnp.mean(scaled * hidden, axis=-1, keepdims=True)
    dv = inverse * scaled - hidden * (inverse * inverse * inverse * inner_sum)
    dv_ref[...] = dv
    small_ref[...] = jnp.zeros_like(small_ref)
    small_ref[0:1, :] = jnp.sum(grad * hidden * inverse, axis=0, keepdims=True)
    small_ref[8 : 8 + experts, :] = dot_tn(logit_grad, normed, highest)
    grad_low = (up + dv).astype(bf16)
    half = att_ref.shape[0]
    inner = w_ref.shape[0]
    att = jnp.concatenate(
        [att_ref[:, 0:inner].astype(f32), att_ref[:, inner : 2 * inner].astype(f32)], axis=0
    )
    att = widen(att, wide_s)
    wout_ref[...] = wout0_ref[...] + dot_tn(att.astype(bf16), grad_low)
    gh = dot_nt(grad_low, w_ref[...])
    gh_low = gh.astype(bf16)
    count = gh_ref.shape[0]
    each = inner // count
    ght_ref[...] = dot_nt(w_ref[...], grad_low).astype(bf16)
    for h in range(count):
        cols = slice(h * each, (h + 1) * each)
        gh_ref[h] = gh_low[:, cols]
        delta_ref[h] = jnp.sum(
            gh_low[:, cols].astype(f32) * att[:, cols], axis=-1, keepdims=True
        )


def sparse_back_kernel(
    gh_ref, ght_ref, delta_ref, vt_ref, k_ref, qsel_ref,
    place_ref, wq_ref, wk_ref, wv_ref, low_ref, gain_ref, small_ref, wout_ref, *refs, heads,
):
    per_head, refs = refs[: 4 * gh_ref.shape[0]], refs[4 * gh_ref.shape[0] :]
    psels, dq0s, dkt0s, dvt0s = (per_head[i :: 4] for i in range(4))
    chunks = refs[:5]
    (score_ref, send_ref, keep_ref, out_ref,
     dq_s, q_low, k_low, v_low, kt_s, vt_s, all_s) = refs[5:]
    head = lax.axis_index("head")
    count, rows, width = gh_ref.shape
    tokens = vt_ref.shape[1]
    inner = count * width
    for h in range(count):
        cols = slice(h * width, (h + 1) * width)
        grad = dot(gh_ref[h], vt_ref[cols, :])
        prob = psels[h][...]
        score = (prob.astype(f32) * (grad - delta_ref[h])).astype(bf16)
        score_ref[h] = score
        dq_s[:, cols] = dot(score, k_ref[h]) * (width ** (-0.5))
        dkt = dkt0s[h][...] + dot(qsel_ref[cols, :], score)
        dvt = dvt0s[h][...] + dot(ght_ref[cols, :], prob)
        kt_s[cols, :] = dkt.astype(bf16)
        vt_s[cols, :] = dvt.astype(bf16)
        k_low[:, cols] = jnp.transpose(dkt).astype(bf16)
        v_low[:, cols] = jnp.transpose(dvt).astype(bf16)
    spread = dot(place_ref[...], dq_s[...].astype(bf16))
    for h in range(count):
        cols = slice(h * width, (h + 1) * width)
        q_low[:, cols] = (spread[:, cols] + dq0s[h][...]).astype(bf16)
    part = tokens // heads
    half = part // 2
    own, to_1, to_2, rest_1, rest_2 = chunks
    places = (
        ((own, 0), (own, half)),
        ((to_1, 0), (rest_1, 0)),
        ((rest_2, 0), (to_2, 0)),
        ((to_1, half), (to_2, half)),
    )
    for d in range(heads):
        mine = pl.ds(pl.multiple_of((head ^ d) * part, part), part)
        rows_part = (
            dot(q_low[mine, :], wq_ref[...])
            + dot(k_low[mine, :], wk_ref[...])
            + dot(v_low[mine, :], wv_ref[...])
        ).astype(bf16)
        for n, (ref, first) in enumerate(places[d]):
            ref[first : first + half, :] = rows_part[n * half : (n + 1) * half]
    low = low_ref[...]
    total = None
    grads = (dot_tn(q_low[...], low), dot(kt_s[...], low), dot(vt_s[...], low))
    for i, (grad, w) in enumerate(zip(grads, (wq_ref, wk_ref, wv_ref))):
        all_s[i * inner : (i + 1) * inner, :] = grad
        term = jnp.sum(grad * w[...].astype(f32), axis=0, keepdims=True)
        total = term if total is None else total + term
    all_s[3 * inner :, :] = wout_ref[...]
    out_ref[...] = small_ref[...]
    out_ref[1:2, :] = total / gain_ref[...]
    split_rows(all_s, 1, send_ref, keep_ref)


def is_upper(bit):
    return (lax.axis_index("seq") & bit) != 0


def split_rows(all_s, bit, send_ref, keep_ref):
    half = send_ref.shape[0]
    low, high = all_s[0:half, :], all_s[half : 2 * half, :]
    keep_ref[...] = jnp.where(is_upper(bit), high, low)
    send_ref[...] = jnp.where(is_upper(bit), low, high).astype(bf16)


def halve_kernel(keep_ref, got_ref, *refs, bit):
    send_ref, out_ref, all_s = refs[-3:]
    if len(refs) > 3:
        rest_1, got_1, rest_2, got_2, next_1, next_2 = refs[:-3]
        half = rest_1.shape[0]
        for rest, got, onward in ((rest_1, got_2, next_1), (rest_2, got_1, next_2)):
            onward[...] = (rest[...].astype(f32) + got[half:, :].astype(f32)).astype(bf16)
    all_s[...] = keep_ref[...] + got_ref[...].astype(f32)
    split_rows(all_s, bit, send_ref, out_ref)


def join_rows(mine_ref, got_ref, all_s, bit):
    half = mine_ref.shape[0]
    mine, got = mine_ref[...].astype(f32), got_ref[...].astype(f32)
    all_s[0:half, :] = jnp.where(is_upper(bit), got, mine)
    all_s[half : 2 * half, :] = jnp.where(is_upper(bit), mine, got)


def pair_kernel(mine_ref, got_ref, *refs, bit):
    out_ref, all_s = refs[-2:]
    if len(refs) > 2:
        got_1, got_2, next_1, next_2 = refs[:-2]
        half = next_1.shape[0]
        next_2[...] = got_1[0:half, :]
        next_1[...] = got_2[half:, :]
    join_rows(mine_ref, got_ref, all_s, bit)
    out_ref[...] = all_s[...].astype(bf16)


def final_kernel(mine_ref, got_ref, *refs, bit):
    outs, all_s = refs[:-1], refs[-1]
    join_rows(mine_ref, got_ref, all_s, bit)
    inner = outs[0].shape[0]
    for i, out in enumerate(outs):
        out[...] = all_s[i * inner : (i + 1) * inner, :]


def bias_grad_kernel(
    score_ref, place_ref, buckets_ref, small_ref, *refs, bucket_count
):
    count = score_ref.shape[0]
    offs, out_ref, acc_s = refs[:count], refs[count], refs[count + 1]
    tokens = place_ref.shape[0]
    offsets = buckets_ref.shape[1]
    out_ref[...] = small_ref[...]
    bucket_hot = (iota((bucket_count, offsets), 0) == buckets_ref[...]).astype(f32)
    for h in range(count):
        acc_s[...] = jnp.zeros_like(acc_s)
        for i in range(0, tokens, BLOCK):
            first = tokens - BLOCK - i
            acc_s[:, first : first + tokens] += dot(place_ref[i : i + BLOCK, :], score_ref[h])
        sums = diagonals(acc_s[...]) + offs[h][...]
        out_ref[2 + h : 3 + h, :bucket_count] = dot_nt(sums[:, :offsets], bucket_hot, highest)[0:1]


def hidden_kernel(*refs, heads):
    att_parts, w_ref, x_ref, out_ref, att_s = refs[:heads], *refs[heads:]
    head = lax.axis_index("head")
    tokens = x_ref.shape[0]
    inner = att_parts[0].shape[0]
    for d in range(heads):
        mine = pl.ds(pl.multiple_of((head ^ d) * inner, inner), inner)
        att_s[mine, :] = att_parts[d][...]
    for i in range(0, tokens, 256):
        rows = pl.ds(i, 256)
        out_ref[rows, :] = x_ref[rows, :].astype(f32) + dot_tn(att_s[:, rows], w_ref[...])


def output_kernel(hidden_ref, place_ref, comb_ref, out_ref):
    high, rest = split_two(comb_ref[...])
    for i in range(0, hidden_ref.shape[0], 256):
        rows = pl.ds(i, 256)
        where = place_ref[rows, :]
        out_ref[rows, :] = hidden_ref[rows, :] + (dot(where, high) + dot(where, rest))


def first_norm_kernel(
    own, got_1, got_2, last_1, last_2,
    x_ref, cot_ref, place_ref, dv_ref, gain_ref, keep_ref, got_ref, out_ref, sum_ref,
):
    half = last_1.shape[0]
    high, rest = split_two(dv_ref[...])
    for first, near, far in ((0, got_1, last_2), (half, got_2, last_1)):
        rows = pl.ds(first, half)
        grad = own[rows, :].astype(f32) + near[0:half, :].astype(f32) + far[...].astype(f32)
        x = x_ref[rows, :].astype(f32)
        inverse = lax.rsqrt(jnp.mean(x * x, axis=-1, keepdims=True) + EPS)
        scaled = grad * gain_ref[...]
        inner_sum = jnp.mean(scaled * x, axis=-1, keepdims=True)
        where = place_ref[rows, :]
        hidden_grad = cot_ref[rows, :].astype(f32) + (dot(where, high) + dot(where, rest))
        out_ref[rows, :] = (
            hidden_grad + inverse * scaled - x * (inverse * inverse * inverse * inner_sum)
        ).astype(bf16)
    sum_ref[...] = (keep_ref[...] + got_ref[...].astype(f32)).astype(bf16)


def spread_kernel(own, got_1, got_2, last_1, last_2, out_ref):
    head = lax.axis_index("head")
    part, half = own.shape[0], last_1.shape[0]
    for d, piece in enumerate((own, got_1, got_2)):
        mine = pl.ds(pl.multiple_of((head ^ d) * part, part), part)
        out_ref[mine, :] = piece[...].astype(f32)
    for n, piece in enumerate((last_2, last_1)):
        mine = pl.ds(pl.multiple_of((head ^ 3) * part + n * half, half), half)
        out_ref[mine, :] = piece[...].astype(f32)


def small_kernel(sum_ref, gain_ref, gain1_ref, gain2_ref, table_ref, router_ref):
    gain1_ref[...] = gain_ref[0, :]
    gain2_ref[...] = sum_ref[0, :]
    count, buckets = table_ref.shape
    table_ref[...] = sum_ref[2 : 2 + count, :buckets]
    router_ref[...] = sum_ref[8 : 8 + router_ref.shape[0], :]


def swap(x, axis, d):
    size = lax.axis_size(axis)
    return lax.ppermute(x, axis, [(i, i ^ d) for i in range(size)])


def share(x, axis):
    return [x] + [swap(x, axis, d) for d in range(1, lax.axis_size(axis))]


def trade(pieces, axis):
    return lax.all_to_all(pieces, axis, split_axis=0, concat_axis=0, tiled=True)


def swap_all(pieces, axis):
    return [pieces[0]] + [swap(pieces[d], axis, d) for d in range(1, len(pieces))]


def bits_of(axis):
    return [b for b in (1 << i for i in range(16)) if b < lax.axis_size(axis)]


def halve(send, keep, bit, after, onward=()):
    rows, width = keep.shape
    outs = [shape_of(*onward[0].shape, bf16)] * 2 if onward else []
    return call(
        partial(halve_kernel, bit=bit),
        outs + [shape_of(rows // 2, width, bf16), shape_of(rows // 2, width, f32)],
        (keep, swap(send, "seq", bit // 2)) + tuple(onward),
        scratch=[pltpu.VMEM((rows, width), f32)],
        name="halve",
        after=after,
        token=True,
    )


def pair(now, bit, after, onward=()):
    rows, width = now.shape
    outs = [shape_of(onward[0].shape[0] // 2, width, bf16)] * 2 if onward else []
    return call(
        partial(pair_kernel, bit=bit),
        outs + [shape_of(2 * rows, width, bf16)],
        (now, swap(now, "seq", bit)) + tuple(onward),
        scratch=[pltpu.VMEM((2 * rows, width), f32)],
        name="pair",
        after=after,
        token=True,
    )


def sum_steps(x, axis):
    steps = []
    for bit in bits_of(axis):
        x = x + swap(x, axis, bit)
        steps.append(x)
    return steps


def on_device(
    layer_input, cotangent, norm1_gain, w_query, w_key, w_value, w_attn_out, bias_table,
    norm2_gain, w_router, w_expert_in, w_expert_out, expert_ids, slot_ids, buckets,
):
    tokens, width = layer_input.shape
    shards = lax.axis_size("seq")
    heads = lax.axis_size("head")
    bucket_count, count = bias_table.shape
    inner = w_query.shape[1]
    each = inner // count
    experts = w_router.shape[1]
    rows, filled = experts * SLOT, experts * CAP
    hidden_units = w_expert_in.shape[2]
    part = tokens // heads
    split = 2 * width // heads
    span = 2 * tokens
    params = pltpu.CompilerParams(vmem_limit_bytes=VMEM_LIMIT if rows <= 256 else VMEM_ALL)

    ids = expert_ids.reshape(1, tokens)
    slots = slot_ids.reshape(1, tokens)
    bucket_row = buckets.reshape(1, -1)
    wq_t, wk_t, wv_t = jnp.transpose(w_query), jnp.transpose(w_key), jnp.transpose(w_value)
    router_t, table_t = jnp.transpose(w_router), jnp.transpose(bias_table)
    w_in = w_expert_in.reshape(width, hidden_units)
    w_out = w_expert_out.reshape(hidden_units, width)

    w_mix = share(w_attn_out, "head")

    low, prob, att, att_t, att_sel = pl.pallas_call(
        attend_kernel,
        grid=(count,),
        out_shape=(
            shape_of(tokens, width, bf16),
            jax.ShapeDtypeStruct((count, tokens, tokens), bf16),
            jax.ShapeDtypeStruct((count, tokens, each), bf16),
            shape_of(inner, tokens, bf16),
            shape_of(filled // 2, 2 * inner, bf16),
        ),
        in_specs=[spec(pltpu.HBM)] * 9,
        out_specs=(
            whole((tokens, width)), by_head((1, tokens, tokens)), by_head((1, tokens, each)),
            whole((inner, tokens)), whole((filled // 2, 2 * inner)),
        ),
        scratch_shapes=[
            pltpu.VMEM((count, tokens, each), bf16),
            pltpu.VMEM((inner, tokens), bf16),
            pltpu.VMEM((count, tokens, each), bf16),
            pltpu.VMEM((8, span), f32),
            pltpu.VMEM((BLOCK, span), f32),
            pltpu.VMEM((filled, tokens), bf16),
            pltpu.VMEM((2 * BLOCK, tokens), f32),
            pltpu.VMEM((tokens, width), bf16),
            pltpu.VMEM((width,), f32),
            pltpu.VMEM((inner, width), bf16),
            pltpu.VMEM((inner, width), bf16),
            pltpu.VMEM((inner, width), bf16),
            pltpu.VMEM((count, bucket_count), f32),
            pltpu.VMEM((1, span - 1), jnp.int32),
            pltpu.VMEM((1, tokens), jnp.int32),
            pltpu.VMEM((1, tokens), jnp.int32),
            pltpu.SemaphoreType.DMA((9,)),
        ],
        compiler_params=params,
        cost_estimate=NO_COST,
        name="attend",
    )(
        *(
            pltpu.with_memory_space_constraint(a, pltpu.HBM)
            for a in (layer_input, norm1_gain, wq_t, wk_t, wv_t, table_t, bucket_row, ids, slots)
        )
    )

    att_sel, w_full = call(
        partial(mix_kernel, heads=heads),
        [shape_of(filled // 2, 2 * inner, bf16), shape_of(heads * inner, width, bf16)],
        (att_sel,) + tuple(w_mix),
        name="mix",
    )
    sel_parts = share(att_sel, "head")
    sel_in, sel_up, place, place_c, x_c, cot_c = call(
        place_kernel,
        [
            shape_of(rows, width, bf16),
            shape_of(rows, width, bf16),
            shape_of(tokens, rows, bf16),
            shape_of(part, rows, bf16),
            shape_of(part, width, bf16),
            shape_of(part, width, bf16),
        ],
        (layer_input, cotangent, ids, slots),
        scratch=[pltpu.VMEM((tokens, rows), f32)],
        moved=12 * 2**20,
        name="place",
        after=(att_sel,),
    )
    routed = call(
        partial(route_kernel, shards=shards, heads=heads),
        [
            shape_of(rows, width, f32),
            shape_of(rows, width, f32),
            shape_of(rows, experts, f32),
            shape_of(inner, tokens, bf16),
        ]
        + [shape_of(SLOT, 2 * width + 128, bf16)] * shards,
        tuple(sel_parts) + (w_full, sel_in, sel_up, norm2_gain, router_t, att_t),
        scratch=[
            pltpu.VMEM((heads, filled, inner), bf16),
            pltpu.VMEM((rows, 2 * width + 128), f32),
            pltpu.VMEM((rows, width), f32),
        ],
        name="route",
        token=True,
    )
    hidden_sel, normed_sel, probs, att_on = routed[:4]
    pay_parts = swap_all(routed[4:-1], "seq")
    att_parts = [att_t] + [swap(att_on, "head", d) for d in range(1, heads - 1)]

    gh, stack, k_rows, q_t, v_t, wout0, q_sel, prepared = call(
        prep_kernel,
        [
            jax.ShapeDtypeStruct((count, tokens, each), bf16),
            jax.ShapeDtypeStruct((count, each + rows, tokens), bf16),
            jax.ShapeDtypeStruct((count, tokens, each), bf16),
            shape_of(inner, tokens, bf16),
            shape_of(inner, tokens, bf16),
            shape_of(inner, width, f32),
            shape_of(inner, rows, bf16),
        ],
        (cotangent, w_attn_out, wq_t, wk_t, wv_t, low, place, att_t),
        scratch=[pltpu.VMEM((inner, tokens), bf16), pltpu.VMEM((tokens, width), bf16)],
        name="prep",
        after=(routed[-1],),
        moved=8 * 2**20,
        token=True,
    )

    def masked_back(h, after):
        return call(
            partial(masked_back_kernel, h=h),
            [
                shape_of(tokens, each, f32),
                shape_of(each, tokens, f32),
                shape_of(each, tokens, f32),
                shape_of(8, span, f32),
                shape_of(rows, tokens, bf16),
            ],
            (gh, stack, k_rows, q_t, v_t, att, prob),
            scratch=[pltpu.VMEM((BLOCK, span), f32), pltpu.VMEM((tokens, tokens), bf16)],
            name="masked_back",
            after=after,
            moved=11 * 2**20,
            token=True,
        )

    done = call(
        partial(expert_kernel, shards=shards, heads=heads),
        [shape_of(filled, split, bf16)] * heads
        + [
            shape_of(rows, width, bf16),
            shape_of(rows, hidden_units, bf16),
            shape_of(rows, hidden_units, bf16),
            shape_of(rows, width, bf16),
        ],
        tuple(pay_parts) + (w_in, w_out),
        scratch=[
            pltpu.VMEM((rows, 2 * width + 128), f32),
            pltpu.VMEM((heads, filled, split), f32),
        ],
        name="expert",
        after=(prepared,) + tuple(att_parts[1:]),
        token=True,
    )
    x_rows, act, pre_low, out_low, token = done[heads:]
    masked = []
    for h in range(count - 2):
        masked.append(masked_back(h, (token,)))
        token = masked[-1][-1]
    returned = call(
        partial(sum_kernel, heads=heads),
        [shape_of(inner, tokens, bf16)] + [shape_of(CAP, split, bf16)] * shards,
        [att_t] + swap_all(done[:heads], "head"),
        scratch=[pltpu.VMEM((filled, split), f32)],
        name="sum",
        after=(token,),
        token=True,
    )
    masked.append(masked_back(count - 2, (returned[-1],)))
    att_parts.append(swap(returned[0], "head", heads - 1))
    joined, token = call(
        join_kernel,
        [shape_of(filled, split, bf16)],
        swap_all(returned[1:-1], "seq"),
        scratch=[pltpu.VMEM((filled, split), f32)],
        name="join",
        after=(masked[-1][-1], att_parts[-1]),
        token=True,
    )
    masked.append(masked_back(count - 1, (token,)))
    full_parts = share(joined, "head")

    small_rows = 8 + -(-experts // 8) * 8
    dv_sel, comb_sel, small, wout_part, gh_sel, ght_sel, delta_sel = call(
        partial(slot_back_kernel, heads=heads),
        [
            shape_of(rows, width, f32),
            shape_of(rows, width, f32),
            shape_of(small_rows, width, f32),
            shape_of(inner, width, f32),
            jax.ShapeDtypeStruct((count, rows, each), bf16),
            shape_of(inner, rows, bf16),
            jax.ShapeDtypeStruct((count, rows, 1), f32),
        ],
        tuple(full_parts)
        + (sel_up, normed_sel, hidden_sel, probs, router_t, norm2_gain)
        + (w_attn_out, att_sel, wout0),
        scratch=[pltpu.VMEM((heads, rows, split), f32), pltpu.VMEM((rows, inner), f32)],
        name="slot_back",
        after=(masked[-1][-1],),
    )

    back = call(
        partial(sparse_back_kernel, heads=heads),
        [shape_of(part, width, bf16)] * 3
        + [shape_of(part // 2, width, bf16)] * 2
        + [
            jax.ShapeDtypeStruct((count, rows, tokens), bf16),
            shape_of(2 * inner, width, bf16),
            shape_of(2 * inner, width, f32),
            shape_of(small_rows, width, f32),
        ],
        (gh_sel, ght_sel, delta_sel, v_t, k_rows, q_sel, place)
        + (wq_t, wk_t, wv_t, low, norm1_gain, small, wout_part)
        + tuple(a for m in masked for a in (m[4], m[0], m[1], m[2])),
        scratch=[
            pltpu.VMEM((rows, inner), f32),
            pltpu.VMEM((tokens, inner), bf16),
            pltpu.VMEM((tokens, inner), bf16),
            pltpu.VMEM((tokens, inner), bf16),
            pltpu.VMEM((inner, tokens), bf16),
            pltpu.VMEM((inner, tokens), bf16),
            pltpu.VMEM((4 * inner, width), f32),
        ],
        name="sparse_back",
    )
    score_sel, send, keep, small = back[5:]
    own, to_1, to_2, rest_1, rest_2 = back[:5]
    got_1, got_2 = swap(to_1, "head", 1), swap(to_2, "head", 2)

    bits = bits_of("seq")
    send, keep, token = halve(send, keep, bits[1], ())
    small, token = call(
        partial(bias_grad_kernel, bucket_count=bucket_count),
        [shape_of(small_rows, width, f32)],
        (score_sel, place, bucket_row, small) + tuple(m[3] for m in masked),
        scratch=[pltpu.VMEM((BLOCK, span), f32)],
        name="bias_grad",
        after=(token,),
        moved=16 * 2**20,
        token=True,
    )
    sums = sum_steps(small, "seq")
    gains = sum_steps(sums[-1][1:2], "head")
    next_1, next_2, send, keep, token = halve(
        send, keep, bits[2], (token, sums[0]), (rest_1, got_1, rest_2, got_2)
    )
    last_1, last_2 = swap(next_1, "head", 1), swap(next_2, "head", 2)
    w_in_grad, w_out_grad, token = call(
        expert_grad_kernel,
        [
            jax.ShapeDtypeStruct(w_expert_in.shape, f32),
            jax.ShapeDtypeStruct(w_expert_out.shape, f32),
        ],
        (x_rows, pre_low, act, out_low),
        name="expert_grad",
        after=(token,),
        moved=10 * 2**20,
        token=True,
    )
    hidden, token = call(
        partial(hidden_kernel, heads=heads),
        [shape_of(tokens, width, f32)],
        tuple(att_parts) + (w_full, layer_input),
        scratch=[pltpu.VMEM((heads * inner, tokens), bf16)],
        name="hidden",
        after=(token,),
        moved=6 * 2**20,
        token=True,
    )
    for bit in bits[3:]:
        send, keep, token = halve(send, keep, bit, (token,))

    grad_part, weights, token = call(
        first_norm_kernel,
        [shape_of(part, width, bf16), shape_of(keep.shape[0], width, bf16)],
        (own, got_1, got_2, last_1, last_2, x_c, cot_c, place_c, dv_sel, norm1_gain)
        + (keep, swap(send, "seq", bits[-1])),
        name="first_norm",
        after=(token, sums[-1]),
        token=True,
    )
    grad_1, grad_2 = swap(grad_part, "head", 1), swap(grad_part, "head", 2)
    layer_output, token = call(
        output_kernel,
        [shape_of(tokens, width, f32)],
        (hidden, place, comb_sel),
        name="output",
        after=(token,),
        moved=10 * 2**20,
        token=True,
    )
    for bit in reversed(bits[3:]):
        weights, token = pair(weights, bit, (token,))
    next_1, next_2, weights, token = pair(
        weights, bits[2], (token, gains[0]), (grad_1, grad_2)
    )
    grad_3 = (swap(next_1, "head", 1), swap(next_2, "head", 2))
    gain1_sum, gain2_sum, table_sum, router_sum, token = call(
        small_kernel,
        [
            jax.ShapeDtypeStruct((width,), f32),
            jax.ShapeDtypeStruct((width,), f32),
            shape_of(count, bucket_count, f32),
            shape_of(experts, width, f32),
        ],
        (sums[-1], gains[-1]),
        name="small",
        token=True,
    )
    weights, token = pair(weights, bits[1], grad_3 + (token,))
    weight_sums = call(
        partial(final_kernel, bit=bits[0]),
        [shape_of(inner, width, f32)] * 4,
        (weights, swap(weights, "seq", bits[0])),
        scratch=[pltpu.VMEM((4 * inner, width), f32)],
        name="weights_out",
    )
    (input_grad,) = call(
        spread_kernel,
        [shape_of(tokens, width, f32)],
        (grad_part, grad_1, grad_2) + grad_3,
        name="spread",
    )

    return (
        layer_output,
        input_grad,
        gain1_sum,
        jnp.transpose(weight_sums[0]),
        jnp.transpose(weight_sums[1]),
        jnp.transpose(weight_sums[2]),
        weight_sums[3],
        jnp.transpose(table_sum),
        gain2_sum,
        jnp.transpose(router_sum),
        w_in_grad,
        w_out_grad,
    )


def solution(mesh):
    return jax.shard_map(
        on_device,
        mesh=mesh,
        in_specs=(
            P("seq", None),
            P("seq", None),
            P(),
            P(None, "head"),
            P(None, "head"),
            P(None, "head"),
            P("head", None),
            P(None, "head"),
            P(),
            P(),
            P("seq", None, "head"),
            P("seq", "head", None),
            P("seq"),
            P("seq"),
            P(),
        ),
        out_specs=(
            P("seq", None),
            P("seq", None),
            P(),
            P(None, "head"),
            P(None, "head"),
            P(None, "head"),
            P("head", None),
            P(None, "head"),
            P(),
            P(),
            P("seq", None, "head"),
            P("seq", "head", None),
        ),
        check_vma=False,
    )
```

```python
from functools import partial

import jax
import jax.numpy as jnp
import numpy as np
from jax import lax
from jax.experimental import pallas as pl
from jax.experimental.pallas import tpu as pltpu
from jax.sharding import PartitionSpec as P

CAP = 20
SLOT = 24
EPS = 1e-06
BLOCK = 128
ROWS = 16
EXTRA = 16
VMEM_LIMIT = 26 * 1024 * 1024
VMEM_ALL = 60 * 1024 * 1024
NO_COST = pl.CostEstimate(flops=1, bytes_accessed=1, transcendentals=0)

f32 = jnp.float32
bf16 = jnp.bfloat16
highest = lax.Precision.HIGHEST


def dot(a, b):
    return jnp.dot(a, b, preferred_element_type=f32)


def dot_nt(a, b, precision=None):
    return lax.dot_general(
        a, b, (((1,), (1,)), ((), ())), precision=precision, preferred_element_type=f32
    )


def dot_tn(a, b, precision=None):
    return lax.dot_general(
        a, b, (((0,), (0,)), ((), ())), precision=precision, preferred_element_type=f32
    )


def iota(shape, dim):
    return lax.broadcasted_iota(jnp.int32, shape, dim)


def split_two(v):
    high = v.astype(bf16)
    return high, (v - high.astype(f32)).astype(bf16)


def shape_of(rows, cols, dtype):
    return jax.ShapeDtypeStruct((rows, cols), dtype)


def spec(memory):
    return pl.BlockSpec(memory_space=memory)


def call(kernel, outs, args, scratch=(), name=None, after=(), moved=1, token=False):
    outs, args = tuple(outs), tuple(args)
    held = sum(int(np.prod(a.shape)) * np.dtype(a.dtype).itemsize for a in args + outs)
    if token:
        outs += (shape_of(8, 128, f32),)
    first_out = len(args) + len(after)

    def body(*refs):
        results = refs[first_out : first_out + len(outs)]
        if token:
            results[-1][...] = jnp.zeros((8, 128), f32)
            results = results[:-1]
        kernel(*refs[: len(args)], *results, *refs[first_out + len(outs) :])

    return pl.pallas_call(
        body,
        out_shape=outs,
        in_specs=[spec(pltpu.VMEM)] * len(args) + [spec(pl.ANY)] * len(after),
        out_specs=tuple(spec(pltpu.VMEM) for _ in outs),
        scratch_shapes=list(scratch),
        compiler_params=pltpu.CompilerParams(
            vmem_limit_bytes=VMEM_LIMIT if 2 * held < VMEM_LIMIT else VMEM_ALL
        ),
        cost_estimate=pl.CostEstimate(flops=1, bytes_accessed=moved, transcendentals=0),
        name=name,
    )(*args, *after)


def slot_rows(ids, slots, rows, each):
    cell = jnp.where(slots < CAP, ids * each + slots, -1)
    return (iota((rows, cell.shape[1]), 0) == cell).astype(f32)


def place_kernel(
    x_ref, cot_ref, ids_ref, slots_ref, sel_in, sel_up, place, place_c, x_c, cot_c, place_s
):
    head = lax.axis_index("head")
    part = x_c.shape[0]
    slot_hot = slot_rows(ids_ref[...], slots_ref[...], sel_in.shape[0], SLOT)
    place_s[...] = jnp.transpose(slot_hot)
    slot_low = slot_hot.astype(bf16)
    sel_in[...] = dot(slot_low, x_ref[...]).astype(bf16)
    sel_up[...] = dot(slot_low, cot_ref[...]).astype(bf16)
    place[...] = place_s[...].astype(bf16)
    mine = pl.ds(pl.multiple_of(head * part, part), part)
    place_c[...] = place_s[mine, :].astype(bf16)
    x_c[...] = x_ref[mine, :]
    cot_c[...] = cot_ref[mine, :]


def attend_kernel(*refs):
    given, refs = refs[:9], refs[9:]
    low_ref, prob_ref, att_ref, attt_ref, sel_ref = refs[:5]
    q_s, kt_s, v_s, bias_s, skew_s, slot_s, score_s = refs[5:12]
    here, sems = refs[12:21], refs[21]
    x_ref, gain_ref, wq_ref, wk_ref, wv_ref, table_ref, buckets_ref, ids_ref, slots_ref = here
    copies = [
        pltpu.make_async_copy(far, near, sems.at[i])
        for i, (far, near) in enumerate(zip(given, here))
    ]
    tokens = x_ref.shape[0]
    inner = wq_ref.shape[0]
    count = q_s.shape[0]
    width = inner // count
    span = skew_s.shape[2]
    tall = 2 * BLOCK
    for copy in copies:
        copy.start()
    for copy in copies[5:]:
        copy.wait()
    slot_s[...] = slot_rows(ids_ref[...], slots_ref[...], slot_s.shape[0], CAP).astype(bf16)
    offsets = buckets_ref.shape[1]
    bucket_hot = (iota((table_ref.shape[1], offsets), 0) == buckets_ref[...]).astype(f32)
    bias_s[...] = jnp.zeros_like(bias_s)
    bias_s[:count, :offsets] = jnp.dot(
        table_ref[...], bucket_hot, precision=highest, preferred_element_type=f32
    )
    for copy in copies[:2]:
        copy.wait()
    for i in range(0, tokens, 256):
        rows = pl.ds(i, 256)
        x = x_ref[rows, :].astype(f32)
        inverse = lax.rsqrt(jnp.mean(x * x, axis=-1, keepdims=True) + EPS)
        low_ref[rows, :] = (x * inverse * gain_ref[...]).astype(bf16)
    for copy in copies[2:5]:
        copy.wait()
    low = low_ref[...]
    q = dot_nt(low, wq_ref[...]).astype(bf16) * bf16(width ** (-0.5))
    kt_s[...] = dot_nt(wk_ref[...], low).astype(bf16)
    v = dot_nt(low, wv_ref[...]).astype(bf16)
    for h in range(count):
        cols = slice(h * width, (h + 1) * width)
        q_s[h] = q[:, cols]
        v_s[h] = v[:, cols]

    def lay_bias(h):
        skew_s[h % 2] = pltpu.roll(
            jnp.broadcast_to(bias_s[h : h + 1, :], skew_s.shape[1:]),
            span - (BLOCK - 1), 1, stride=1, stride_axis=0,
        )

    def scores(h, n):
        score_s[n % 2] = dot(
            q_s[h, pl.ds(n * tall, tall), :], kt_s[h * width : (h + 1) * width, :]
        )

    def weights(h, n):
        for j in range(0, tall, ROWS):
            row = n * tall + j
            first = tokens - BLOCK - row // BLOCK * BLOCK
            bias = skew_s[h % 2, j % BLOCK : j % BLOCK + ROWS, first : first + tokens]
            score = score_s[n % 2, j : j + ROWS, :] + bias
            weight = jnp.exp(score - jnp.max(score, axis=-1, keepdims=True))
            total = jnp.sum(weight, axis=-1, keepdims=True)
            prob_ref[h, pl.ds(row, ROWS), :] = (weight * (1.0 / total)).astype(bf16)

    blocks = tokens // tall
    half = sel_ref.shape[0]
    lay_bias(0)
    scores(0, 0)
    for h in range(count):
        for n in range(blocks):
            if n + 1 < blocks:
                scores(h, n + 1)
            elif h + 1 < count:
                lay_bias(h + 1)
                scores(h + 1, 0)
            weights(h, n)
        att = dot(prob_ref[h], v_s[h])
        att_low = att.astype(bf16)
        att_ref[h] = att_low
        attt_ref[h * width : (h + 1) * width, :] = jnp.transpose(att).astype(bf16)
        picked = dot(slot_s[...], att_low).astype(bf16)
        for part in range(2):
            start = part * inner + h * width
            sel_ref[:, start : start + width] = picked[part * half : (part + 1) * half]


def mix_kernel(att_ref, *refs, heads):
    w_parts, att_on, w_ref = refs[:heads], refs[heads], refs[heads + 1]
    att_on[...] = att_ref[...]
    head = lax.axis_index("head")
    inner = w_parts[0].shape[0]
    for d in range(heads):
        mine = pl.ds(pl.multiple_of((head ^ d) * inner, inner), inner)
        w_ref[mine, :] = w_parts[d][...]


def widen(rows, wide_s):
    wide_s[...] = jnp.zeros_like(wide_s)
    for e in range(rows.shape[0] // CAP):
        wide_s[e * SLOT : e * SLOT + CAP, :] = rows[e * CAP : (e + 1) * CAP]
    return wide_s[...]


def route_kernel(*refs, shards, heads):
    att_parts, w_ref = refs[:heads], refs[heads]
    (sel_in, sel_up, gain_ref, router_ref, att_t, hidden_ref, normed_ref, probs_ref, att_on
     ) = refs[heads + 1 : heads + 10]
    pieces = refs[heads + 10 : heads + 10 + shards]
    att_s, pay_s, wide_s = refs[heads + 10 + shards :]
    head = lax.axis_index("head")
    half = att_parts[0].shape[0]
    inner = w_ref.shape[0] // heads
    for d in range(heads):
        att_s[d, 0:half, :] = att_parts[d][:, 0:inner]
        att_s[d, half : 2 * half, :] = att_parts[d][:, inner : 2 * inner]
    mixed = None
    for k in range(heads):
        term = dot(att_s[head ^ k], w_ref[k * inner : (k + 1) * inner, :])
        mixed = term if mixed is None else mixed + term
    hidden = sel_in[...].astype(f32) + widen(mixed, wide_s)
    hidden_ref[...] = hidden
    inverse = lax.rsqrt(jnp.mean(hidden * hidden, axis=-1, keepdims=True) + EPS)
    normed = hidden * inverse * gain_ref[...]
    normed_ref[...] = normed
    logits = dot_nt(normed, router_ref[...], highest)
    logits = logits - jnp.max(logits, axis=-1, keepdims=True)
    powers = jnp.exp(logits)
    probs = powers / jnp.sum(powers, axis=-1, keepdims=True)
    probs_ref[...] = probs
    gate = jnp.sum(jnp.where(chosen_of(probs.shape), probs, 0.0), axis=-1, keepdims=True)
    high = gate.astype(bf16).astype(f32)
    lane = iota((gate.shape[0], 128), 1)
    width = normed.shape[1]
    extra = jnp.where(lane == 0, high, jnp.where(lane == 1, gate - high, 0.0))
    pay_s[:, :width] = normed
    pay_s[:, width : 2 * width] = sel_up[...].astype(f32)
    pay_s[:, 2 * width :] = extra
    shard = lax.axis_index("seq")
    for j in range(shards):
        first = pl.multiple_of((shard ^ j) * SLOT, SLOT)
        pieces[j][...] = pay_s[pl.ds(first, SLOT), :].astype(bf16)
    att_on[...] = att_t[...]


def chosen_of(shape):
    expert = iota(shape, 1) * SLOT
    slot_row = iota(shape, 0)
    return (slot_row >= expert) & (slot_row < expert + SLOT)


def expert_kernel(*refs, shards, heads):
    parts = refs[:shards]
    w_in, w_out = refs[shards : shards + 2]
    chunks = refs[shards + 2 : shards + 2 + heads]
    x_ref, act_ref, pre_ref, out_ref, pay_s, both_s = refs[shards + 2 + heads :]
    head = lax.axis_index("head")
    width = x_ref.shape[1]
    for j in range(shards):
        pay_s[j * SLOT : (j + 1) * SLOT, :] = parts[j][...].astype(f32)
    x = pay_s[:, :width].astype(bf16)
    up = pay_s[:, width : 2 * width]
    gate = pay_s[:, 2 * width : 2 * width + 1] + pay_s[:, 2 * width + 1 : 2 * width + 2]
    out_low = (gate * up).astype(bf16)
    pre = dot(x, w_in[...])
    cdf = 0.5 * (1.0 + lax.erf(pre * (0.5**0.5)))
    act = (pre * cdf).astype(bf16)
    slope = cdf + pre * jnp.exp(-0.5 * pre * pre) * ((2.0 * np.pi) ** (-0.5))
    pre_low = (dot_nt(out_low, w_out[...]) * slope).astype(bf16)
    both = (dot(act, w_out[...]), dot_nt(pre_low, w_in[...]))
    part = both_s.shape[2]
    for k in range(heads):
        start = k % (heads // 2) * part
        for j in range(shards):
            both_s[k, j * CAP : (j + 1) * CAP, :] = both[k // (heads // 2)][
                j * SLOT : j * SLOT + CAP, start : start + part
            ]
    for d in range(heads):
        chunks[d][...] = both_s[head ^ d].astype(bf16)
    pre_ref[...] = pre_low
    out_ref[...] = out_low
    x_ref[...] = x
    act_ref[...] = act


def expert_grad_kernel(x_ref, pre_ref, act_ref, out_ref, in_grad, out_grad):
    in_grad[0] = dot_tn(x_ref[...], pre_ref[...])
    out_grad[0] = dot_tn(act_ref[...], out_ref[...])


def sum_kernel(att_ref, *refs, heads):
    parts, att_on, pieces, sum_s = refs[:heads], refs[heads], refs[heads + 1 : -1], refs[-1]
    att_on[...] = att_ref[...]
    total = parts[0][...].astype(f32)
    for d in range(1, heads):
        total = total + parts[d][...].astype(f32)
    sum_s[...] = total
    for j, piece in enumerate(pieces):
        piece[...] = sum_s[j * CAP : (j + 1) * CAP, :].astype(bf16)


def join_kernel(*refs):
    parts, out_ref, sum_s = refs[:-2], refs[-2], refs[-1]
    for j, part in enumerate(parts):
        sum_s[j * CAP : (j + 1) * CAP, :] = part[...].astype(f32)
    out_ref[...] = sum_s[...].astype(bf16)


def prep_kernel(
    cot_ref, w_ref, wq_ref, wk_ref, wv_ref, low_ref, place_ref, attt_ref,
    gh_ref, stack_ref, k_ref, qt_ref, vt_ref, wout_ref, qsel_ref, ght_s, mcot_s,
):
    count, tokens, width = gh_ref.shape
    for i in range(0, tokens, 256):
        rows = pl.ds(i, 256)
        where = place_ref[rows, :].astype(f32)
        free = 1.0 - jnp.sum(where, axis=-1, keepdims=True)
        mcot_s[rows, :] = (cot_ref[rows, :].astype(f32) * free).astype(bf16)
        slots = jnp.transpose(where).astype(bf16)
        for h in range(count):
            stack_ref[h, width:, rows] = slots
    gh = dot_nt(mcot_s[...], w_ref[...]).astype(bf16)
    ght_s[...] = dot_nt(w_ref[...], mcot_s[...]).astype(bf16)
    k = dot_nt(low_ref[...], wk_ref[...]).astype(bf16)
    qt_ref[...] = dot_nt(wq_ref[...], low_ref[...]).astype(bf16) * bf16(width ** (-0.5))
    vt_ref[...] = dot_nt(wv_ref[...], low_ref[...]).astype(bf16)
    for h in range(count):
        cols = slice(h * width, (h + 1) * width)
        gh_ref[h] = gh[:, cols]
        k_ref[h] = k[:, cols]
        stack_ref[h, 0:width, :] = ght_s[cols, :]
    wout_ref[...] = dot(attt_ref[...], mcot_s[...])
    qsel_ref[...] = dot(qt_ref[...], place_ref[...]).astype(bf16)


def masked_back_kernel(
    gh_ref, stack_ref, k_ref, qt_ref, vt_ref, att_ref, prob_ref,
    dq_ref, dkt_ref, dvt_ref, offs_ref, psel_ref, acc_s, score_s, *, h,
):
    tokens, width = dq_ref.shape
    acc_s[...] = jnp.zeros_like(acc_s)
    cols = slice(h * width, (h + 1) * width)
    for i in range(0, tokens, 2 * BLOCK):
        rows = pl.ds(i, 2 * BLOCK)
        gh = gh_ref[h, rows, :]
        delta = jnp.sum(gh.astype(f32) * att_ref[h, rows, :].astype(f32), axis=-1, keepdims=True)
        grads = dot(gh, vt_ref[cols, :]) - delta
        for j in range(2):
            start = i + j * BLOCK
            first = tokens - BLOCK - start
            here = pl.ds(start, BLOCK)
            score = prob_ref[h, here, :].astype(f32) * grads[j * BLOCK : (j + 1) * BLOCK]
            acc_s[:, first : first + tokens] += score
            score_s[here, :] = score.astype(bf16)
    dq_ref[...] = dot(score_s[...], k_ref[h]) * (width ** (-0.5))
    dkt_ref[...] = dot(qt_ref[cols, :], score_s[...])
    both = dot(stack_ref[h], prob_ref[h])
    dvt_ref[...] = both[:width]
    psel_ref[...] = both[width:].astype(bf16)
    offs_ref[...] = diagonals(acc_s[...])


def diagonals(acc):
    span = acc.shape[1]
    rows = acc.shape[0] // 2
    while rows >= 8:
        acc = acc[:rows] + pltpu.roll(acc[rows:], span - rows, 1)
        rows //= 2
    total = acc[0:1]
    for r in range(1, 8):
        total = total + pltpu.roll(acc[r : r + 1], span - r, 1)
    return jnp.broadcast_to(pltpu.roll(total, BLOCK - 1, 1), (8, span))


def slot_back_kernel(*refs, heads):
    parts = refs[:heads]
    (up_ref, normed_ref, hidden_ref, probs_ref, router_ref, gain_ref, w_ref, att_ref,
     wout0_ref) = refs[heads : heads + 9]
    (dv_ref, comb_ref, small_ref, wout_ref, gh_ref, ght_ref, delta_ref, ret_s, wide_s
     ) = refs[heads + 9 :]
    head, shard = lax.axis_index("head"), lax.axis_index("seq")
    ret_s[...] = jnp.zeros_like(ret_s)
    for d in range(heads):
        part = parts[d][...].astype(f32)
        for j in range(part.shape[0] // CAP):
            first = pl.multiple_of((shard ^ j) * SLOT, SLOT)
            ret_s[head ^ d, pl.ds(first, CAP), :] = part[j * CAP : (j + 1) * CAP]
    back = [ret_s[k] for k in range(heads)]
    combined = jnp.concatenate(back[: heads // 2], axis=1)
    grad_buf = jnp.concatenate(back[heads // 2 :], axis=1)
    up = up_ref[...].astype(f32)
    hidden, normed, probs, gain = hidden_ref[...], normed_ref[...], probs_ref[...], gain_ref[...]
    chosen = chosen_of(probs.shape)
    gate = jnp.sum(jnp.where(chosen, probs, 0.0), axis=-1, keepdims=True)
    comb_ref[...] = gate * combined
    gate_grad = jnp.sum(up * combined, axis=-1, keepdims=True)
    marked = jnp.where(chosen, gate_grad, 0.0)
    logit_grad = probs * (marked - jnp.sum(marked * probs, axis=-1, keepdims=True))
    experts = probs.shape[1]
    grad = grad_buf + jnp.dot(
        logit_grad, router_ref[...], precision=highest, preferred_element_type=f32
    )
    inverse = lax.rsqrt(jnp.mean(hidden * hidden, axis=-1, keepdims=True) + EPS)
    scaled = grad * gain
    inner_sum = jnp.mean(scaled * hidden, axis=-1, keepdims=True)
    dv = inverse * scaled - hidden * (inverse * inverse * inverse * inner_sum)
    dv_ref[...] = dv
    small_ref[...] = jnp.zeros_like(small_ref)
    small_ref[0:1, :] = jnp.sum(grad * hidden * inverse, axis=0, keepdims=True)
    small_ref[8 : 8 + experts, :] = dot_tn(logit_grad, normed, highest)
    grad_low = (up + dv).astype(bf16)
    half = att_ref.shape[0]
    inner = w_ref.shape[0]
    att = jnp.concatenate(
        [att_ref[:, 0:inner].astype(f32), att_ref[:, inner : 2 * inner].astype(f32)], axis=0
    )
    att = widen(att, wide_s)
    wout_ref[...] = wout0_ref[...] + dot_tn(att.astype(bf16), grad_low)
    gh = dot_nt(grad_low, w_ref[...])
    gh_low = gh.astype(bf16)
    count = gh_ref.shape[0]
    each = inner // count
    ght_ref[...] = dot_nt(w_ref[...], grad_low).astype(bf16)
    for h in range(count):
        cols = slice(h * each, (h + 1) * each)
        gh_ref[h] = gh_low[:, cols]
        delta_ref[h] = jnp.sum(
            gh_low[:, cols].astype(f32) * att[:, cols], axis=-1, keepdims=True
        )


def sparse_back_kernel(
    gh_ref, ght_ref, delta_ref, vt_ref, k_ref, qsel_ref,
    place_ref, wq_ref, wk_ref, wv_ref, low_ref, gain_ref, small_ref, wout_ref, *refs, heads,
):
    per_head, refs = refs[: 4 * gh_ref.shape[0]], refs[4 * gh_ref.shape[0] :]
    psels, dq0s, dkt0s, dvt0s = (per_head[i :: 4] for i in range(4))
    chunks = refs[:5]
    (score_ref, send_ref, keep_ref, out_ref,
     dq_s, q_low, k_low, v_low, kt_s, vt_s, all_s) = refs[5:]
    head = lax.axis_index("head")
    count, rows, width = gh_ref.shape
    tokens = vt_ref.shape[1]
    inner = count * width
    for h in range(count):
        cols = slice(h * width, (h + 1) * width)
        grad = dot(gh_ref[h], vt_ref[cols, :])
        prob = psels[h][...]
        score = (prob.astype(f32) * (grad - delta_ref[h])).astype(bf16)
        score_ref[h] = score
        dq_s[:, cols] = dot(score, k_ref[h]) * (width ** (-0.5))
        dkt = dkt0s[h][...] + dot(qsel_ref[cols, :], score)
        dvt = dvt0s[h][...] + dot(ght_ref[cols, :], prob)
        kt_s[cols, :] = dkt.astype(bf16)
        vt_s[cols, :] = dvt.astype(bf16)
        k_low[:, cols] = jnp.transpose(dkt).astype(bf16)
        v_low[:, cols] = jnp.transpose(dvt).astype(bf16)
    spread = dot(place_ref[...], dq_s[...].astype(bf16))
    for h in range(count):
        cols = slice(h * width, (h + 1) * width)
        q_low[:, cols] = (spread[:, cols] + dq0s[h][...]).astype(bf16)
    part = tokens // heads
    half = part // 2
    own, to_1, to_2, rest_1, rest_2 = chunks
    to_1[part:, :] = jnp.zeros((EXTRA, to_1.shape[1]), bf16)
    places = (
        ((own, 0), (own, half)),
        ((to_1, 0), (rest_1, 0)),
        ((rest_2, 0), (to_2, 0)),
        ((to_1, half), (to_2, half)),
    )
    for d in range(heads):
        mine = pl.ds(pl.multiple_of((head ^ d) * part, part), part)
        rows_part = (
            dot(q_low[mine, :], wq_ref[...])
            + dot(k_low[mine, :], wk_ref[...])
            + dot(v_low[mine, :], wv_ref[...])
        ).astype(bf16)
        for n, (ref, first) in enumerate(places[d]):
            ref[first : first + half, :] = rows_part[n * half : (n + 1) * half]
    low = low_ref[...]
    total = None
    grads = (dot_tn(q_low[...], low), dot(kt_s[...], low), dot(vt_s[...], low))
    for i, (grad, w) in enumerate(zip(grads, (wq_ref, wk_ref, wv_ref))):
        all_s[i * inner : (i + 1) * inner, :] = grad
        term = jnp.sum(grad * w[...].astype(f32), axis=0, keepdims=True)
        total = term if total is None else total + term
    all_s[3 * inner :, :] = wout_ref[...]
    out_ref[...] = small_ref[...]
    out_ref[1:2, :] = total / gain_ref[...]
    to_1[part : part + 1, :] = (total / gain_ref[...]).astype(bf16)
    split_rows(all_s, 1, send_ref, keep_ref)


def is_upper(bit):
    return (lax.axis_index("seq") & bit) != 0


def split_rows(all_s, bit, send_ref, keep_ref):
    half = send_ref.shape[0]
    low, high = all_s[0:half, :], all_s[half : 2 * half, :]
    keep_ref[...] = jnp.where(is_upper(bit), high, low)
    send_ref[...] = jnp.where(is_upper(bit), low, high).astype(bf16)


def halve_kernel(keep_ref, got_ref, *refs, bit):
    send_ref, out_ref, all_s = refs[-3:]
    if len(refs) > 3:
        rest_1, got_1, rest_2, got_2, small_ref, next_1, next_2 = refs[:-3]
        half = rest_1.shape[0]
        for rest, got, onward in ((rest_1, got_2, next_1), (rest_2, got_1, next_2)):
            got_rest = got[half : 2 * half, :].astype(f32)
            onward[0:half, :] = (rest[...].astype(f32) + got_rest).astype(bf16)
        mine = small_ref[1:2, :].astype(bf16).astype(f32)
        next_2[half:, :] = jnp.zeros((EXTRA, next_2.shape[1]), bf16)
        next_2[half : half + 1, :] = (mine + got_1[2 * half : 2 * half + 1, :].astype(f32)).astype(bf16)
    all_s[...] = keep_ref[...] + got_ref[...].astype(f32)
    split_rows(all_s, bit, send_ref, out_ref)


def join_rows(mine_ref, got_ref, all_s, bit, count):
    mine, got = mine_ref[...].astype(f32), got_ref[...].astype(f32)
    all_s[0:count, :] = jnp.where(is_upper(bit), got[:count], mine[:count])
    all_s[count : 2 * count, :] = jnp.where(is_upper(bit), mine[:count], got[:count])
    all_s[2 * count :, :] = mine[count:] + got[count:]


def pair_kernel(mine_ref, got_ref, *refs, bit, count):
    out_ref, all_s = refs[-2:]
    if len(refs) > 2:
        got_1, got_2, next_1, next_2 = refs[:-2]
        half = next_1.shape[0]
        next_2[...] = got_1[0:half, :]
        next_1[...] = got_2[half:, :]
    join_rows(mine_ref, got_ref, all_s, bit, count)
    out_ref[...] = all_s[...].astype(bf16)


def final_kernel(mine_ref, got_ref, *refs, bit, count):
    gain1_ref, gain2_ref, table_ref, router_ref, all_s = refs[-5:]
    outs = refs[:-5]
    join_rows(mine_ref, got_ref, all_s, bit, count)
    inner = outs[0].shape[0]
    for i, out in enumerate(outs):
        out[...] = all_s[i * inner : (i + 1) * inner, :]
    small = all_s[2 * count :, :]
    gain1_ref[...] = small[1, :]
    gain2_ref[...] = small[0, :]
    heads, buckets = table_ref.shape
    table_ref[...] = small[2 : 2 + heads, :buckets]
    router_ref[...] = small[8 : 8 + router_ref.shape[0], :]


def bias_grad_kernel(
    score_ref, place_ref, buckets_ref, small_ref, *refs, bucket_count
):
    count = score_ref.shape[0]
    offs, out_ref, acc_s = refs[:count], refs[count], refs[count + 1]
    tokens = place_ref.shape[0]
    offsets = buckets_ref.shape[1]
    out_ref[...] = small_ref[...]
    bucket_hot = (iota((bucket_count, offsets), 0) == buckets_ref[...]).astype(f32)
    for h in range(count):
        acc_s[...] = jnp.zeros_like(acc_s)
        for i in range(0, tokens, BLOCK):
            first = tokens - BLOCK - i
            acc_s[:, first : first + tokens] += dot(place_ref[i : i + BLOCK, :], score_ref[h])
        sums = diagonals(acc_s[...]) + offs[h][...]
        out_ref[2 + h : 3 + h, :bucket_count] = dot_nt(sums[:, :offsets], bucket_hot, highest)[0:1]


def hidden_kernel(*refs, heads):
    att_parts, w_ref, x_ref, out_ref, att_s = refs[:heads], *refs[heads:]
    head = lax.axis_index("head")
    tokens = x_ref.shape[0]
    inner = att_parts[0].shape[0]
    for d in range(heads):
        mine = pl.ds(pl.multiple_of((head ^ d) * inner, inner), inner)
        att_s[mine, :] = att_parts[d][...]
    for i in range(0, tokens, 256):
        rows = pl.ds(i, 256)
        out_ref[rows, :] = x_ref[rows, :].astype(f32) + dot_tn(att_s[:, rows], w_ref[...])


def output_kernel(hidden_ref, place_ref, comb_ref, out_ref):
    high, rest = split_two(comb_ref[...])
    for i in range(0, hidden_ref.shape[0], 256):
        rows = pl.ds(i, 256)
        where = place_ref[rows, :]
        out_ref[rows, :] = hidden_ref[rows, :] + (dot(where, high) + dot(where, rest))


def first_norm_kernel(
    own, got_1, got_2, last_1, last_2, next_2, small_ref,
    x_ref, cot_ref, place_ref, dv_ref, gain_ref, keep_ref, got_ref, out_ref, sum_ref,
):
    half = last_1.shape[0]
    high, rest = split_two(dv_ref[...])
    for first, near, far in ((0, got_1, last_2), (half, got_2, last_1)):
        rows = pl.ds(first, half)
        grad = own[rows, :].astype(f32) + near[0:half, :].astype(f32)
        grad = grad + far[0:half, :].astype(f32)
        x = x_ref[rows, :].astype(f32)
        inverse = lax.rsqrt(jnp.mean(x * x, axis=-1, keepdims=True) + EPS)
        scaled = grad * gain_ref[...]
        inner_sum = jnp.mean(scaled * x, axis=-1, keepdims=True)
        where = place_ref[rows, :]
        hidden_grad = cot_ref[rows, :].astype(f32) + (dot(where, high) + dot(where, rest))
        out_ref[rows, :] = (
            hidden_grad + inverse * scaled - x * (inverse * inverse * inverse * inner_sum)
        ).astype(bf16)
    count = keep_ref.shape[0]
    sum_ref[0:count, :] = (keep_ref[...] + got_ref[...].astype(f32)).astype(bf16)
    gain1 = next_2[half:, :].astype(f32)[0:1] + last_2[half:, :].astype(f32)[0:1]
    small = small_ref[...]
    sum_ref[count:, :] = jnp.where(iota(small.shape, 0) == 1, gain1, small).astype(bf16)


def spread_kernel(own, got_1, got_2, last_1, last_2, out_ref):
    head = lax.axis_index("head")
    part, half = own.shape[0], last_1.shape[0]
    for d, piece in enumerate((own, got_1, got_2)):
        mine = pl.ds(pl.multiple_of((head ^ d) * part, part), part)
        out_ref[mine, :] = piece[...].astype(f32)
    for n, piece in enumerate((last_2, last_1)):
        mine = pl.ds(pl.multiple_of((head ^ 3) * part + n * half, half), half)
        out_ref[mine, :] = piece[...].astype(f32)


def swap(x, axis, d):
    size = lax.axis_size(axis)
    return lax.ppermute(x, axis, [(i, i ^ d) for i in range(size)])


def share(x, axis):
    return [x] + [swap(x, axis, d) for d in range(1, lax.axis_size(axis))]


def trade(pieces, axis):
    return lax.all_to_all(pieces, axis, split_axis=0, concat_axis=0, tiled=True)


def swap_all(pieces, axis):
    return [pieces[0]] + [swap(pieces[d], axis, d) for d in range(1, len(pieces))]


def bits_of(axis):
    return [b for b in (1 << i for i in range(16)) if b < lax.axis_size(axis)]


def halve(send, keep, bit, after, onward=()):
    rows, width = keep.shape
    outs = []
    if onward:
        half = onward[0].shape[0]
        outs = [shape_of(half, width, bf16), shape_of(half + EXTRA, width, bf16)]
    return call(
        partial(halve_kernel, bit=bit),
        outs + [shape_of(rows // 2, width, bf16), shape_of(rows // 2, width, f32)],
        (keep, swap(send, "seq", bit // 2)) + tuple(onward),
        scratch=[pltpu.VMEM((rows, width), f32)],
        name="halve",
        after=after,
        token=True,
    )


def pair(now, small_rows, bit, after, onward=()):
    rows, width = now.shape
    count = rows - small_rows
    outs = [shape_of(onward[0].shape[0] // 2, width, bf16)] * 2 if onward else []
    return call(
        partial(pair_kernel, bit=bit, count=count),
        outs + [shape_of(rows + count, width, bf16)],
        (now, swap(now, "seq", bit)) + tuple(onward),
        scratch=[pltpu.VMEM((rows + count, width), f32)],
        name="pair",
        after=after,
        token=True,
    )


def on_device(
    layer_input, cotangent, norm1_gain, w_query, w_key, w_value, w_attn_out, bias_table,
    norm2_gain, w_router, w_expert_in, w_expert_out, expert_ids, slot_ids, buckets,
):
    tokens, width = layer_input.shape
    shards = lax.axis_size("seq")
    heads = lax.axis_size("head")
    bucket_count, count = bias_table.shape
    inner = w_query.shape[1]
    each = inner // count
    experts = w_router.shape[1]
    rows, filled = experts * SLOT, experts * CAP
    hidden_units = w_expert_in.shape[2]
    part = tokens // heads
    split = 2 * width // heads
    span = 2 * tokens
    params = pltpu.CompilerParams(vmem_limit_bytes=VMEM_LIMIT if rows <= 256 else VMEM_ALL)

    ids = expert_ids.reshape(1, tokens)
    slots = slot_ids.reshape(1, tokens)
    bucket_row = buckets.reshape(1, -1)
    wq_t, wk_t, wv_t = jnp.transpose(w_query), jnp.transpose(w_key), jnp.transpose(w_value)
    router_t, table_t = jnp.transpose(w_router), jnp.transpose(bias_table)
    w_in = w_expert_in.reshape(width, hidden_units)
    w_out = w_expert_out.reshape(hidden_units, width)

    w_mix = share(w_attn_out, "head")

    low, prob, att, att_t, att_sel = pl.pallas_call(
        attend_kernel,
        out_shape=(
            shape_of(tokens, width, bf16),
            jax.ShapeDtypeStruct((count, tokens, tokens), bf16),
            jax.ShapeDtypeStruct((count, tokens, each), bf16),
            shape_of(inner, tokens, bf16),
            shape_of(filled // 2, 2 * inner, bf16),
        ),
        in_specs=[spec(pltpu.HBM)] * 9,
        out_specs=(spec(pltpu.VMEM),) * 5,
        scratch_shapes=[
            pltpu.VMEM((count, tokens, each), bf16),
            pltpu.VMEM((inner, tokens), bf16),
            pltpu.VMEM((count, tokens, each), bf16),
            pltpu.VMEM((8, span), f32),
            pltpu.VMEM((2, BLOCK, span), f32),
            pltpu.VMEM((filled, tokens), bf16),
            pltpu.VMEM((2, 2 * BLOCK, tokens), f32),
            pltpu.VMEM((tokens, width), bf16),
            pltpu.VMEM((width,), f32),
            pltpu.VMEM((inner, width), bf16),
            pltpu.VMEM((inner, width), bf16),
            pltpu.VMEM((inner, width), bf16),
            pltpu.VMEM((count, bucket_count), f32),
            pltpu.VMEM((1, span - 1), jnp.int32),
            pltpu.VMEM((1, tokens), jnp.int32),
            pltpu.VMEM((1, tokens), jnp.int32),
            pltpu.SemaphoreType.DMA((9,)),
        ],
        compiler_params=params,
        cost_estimate=NO_COST,
        name="attend",
    )(
        *(
            pltpu.with_memory_space_constraint(a, pltpu.HBM)
            for a in (layer_input, norm1_gain, wq_t, wk_t, wv_t, table_t, bucket_row, ids, slots)
        )
    )

    att_sel, w_full = call(
        partial(mix_kernel, heads=heads),
        [shape_of(filled // 2, 2 * inner, bf16), shape_of(heads * inner, width, bf16)],
        (att_sel,) + tuple(w_mix),
        name="mix",
    )
    sel_parts = share(att_sel, "head")
    sel_in, sel_up, place, place_c, x_c, cot_c = call(
        place_kernel,
        [
            shape_of(rows, width, bf16),
            shape_of(rows, width, bf16),
            shape_of(tokens, rows, bf16),
            shape_of(part, rows, bf16),
            shape_of(part, width, bf16),
            shape_of(part, width, bf16),
        ],
        (layer_input, cotangent, ids, slots),
        scratch=[pltpu.VMEM((tokens, rows), f32)],
        moved=12 * 2**20,
        name="place",
        after=(att_sel,),
    )
    routed = call(
        partial(route_kernel, shards=shards, heads=heads),
        [
            shape_of(rows, width, f32),
            shape_of(rows, width, f32),
            shape_of(rows, experts, f32),
            shape_of(inner, tokens, bf16),
        ]
        + [shape_of(SLOT, 2 * width + 128, bf16)] * shards,
        tuple(sel_parts) + (w_full, sel_in, sel_up, norm2_gain, router_t, att_t),
        scratch=[
            pltpu.VMEM((heads, filled, inner), bf16),
            pltpu.VMEM((rows, 2 * width + 128), f32),
            pltpu.VMEM((rows, width), f32),
        ],
        name="route",
        token=True,
    )
    hidden_sel, normed_sel, probs, att_on = routed[:4]
    pay_parts = swap_all(routed[4:-1], "seq")
    att_parts = [att_t] + [swap(att_on, "head", d) for d in range(1, heads - 1)]

    gh, stack, k_rows, q_t, v_t, wout0, q_sel, prepared = call(
        prep_kernel,
        [
            jax.ShapeDtypeStruct((count, tokens, each), bf16),
            jax.ShapeDtypeStruct((count, each + rows, tokens), bf16),
            jax.ShapeDtypeStruct((count, tokens, each), bf16),
            shape_of(inner, tokens, bf16),
            shape_of(inner, tokens, bf16),
            shape_of(inner, width, f32),
            shape_of(inner, rows, bf16),
        ],
        (cotangent, w_attn_out, wq_t, wk_t, wv_t, low, place, att_t),
        scratch=[pltpu.VMEM((inner, tokens), bf16), pltpu.VMEM((tokens, width), bf16)],
        name="prep",
        after=(routed[-1],),
        moved=8 * 2**20,
        token=True,
    )

    def masked_back(h, after):
        return call(
            partial(masked_back_kernel, h=h),
            [
                shape_of(tokens, each, f32),
                shape_of(each, tokens, f32),
                shape_of(each, tokens, f32),
                shape_of(8, span, f32),
                shape_of(rows, tokens, bf16),
            ],
            (gh, stack, k_rows, q_t, v_t, att, prob),
            scratch=[pltpu.VMEM((BLOCK, span), f32), pltpu.VMEM((tokens, tokens), bf16)],
            name="masked_back",
            after=after,
            moved=11 * 2**20,
            token=True,
        )

    done = call(
        partial(expert_kernel, shards=shards, heads=heads),
        [shape_of(filled, split, bf16)] * heads
        + [
            shape_of(rows, width, bf16),
            shape_of(rows, hidden_units, bf16),
            shape_of(rows, hidden_units, bf16),
            shape_of(rows, width, bf16),
        ],
        tuple(pay_parts) + (w_in, w_out),
        scratch=[
            pltpu.VMEM((rows, 2 * width + 128), f32),
            pltpu.VMEM((heads, filled, split), f32),
        ],
        name="expert",
        after=(prepared,) + tuple(att_parts[1:]),
        token=True,
    )
    x_rows, act, pre_low, out_low, token = done[heads:]
    masked = []
    for h in range(count - 2):
        masked.append(masked_back(h, (token,)))
        token = masked[-1][-1]
    returned = call(
        partial(sum_kernel, heads=heads),
        [shape_of(inner, tokens, bf16)] + [shape_of(CAP, split, bf16)] * shards,
        [att_t] + swap_all(done[:heads], "head"),
        scratch=[pltpu.VMEM((filled, split), f32)],
        name="sum",
        after=(token,),
        token=True,
    )
    masked.append(masked_back(count - 2, (returned[-1],)))
    att_parts.append(swap(returned[0], "head", heads - 1))
    joined, token = call(
        join_kernel,
        [shape_of(filled, split, bf16)],
        swap_all(returned[1:-1], "seq"),
        scratch=[pltpu.VMEM((filled, split), f32)],
        name="join",
        after=(masked[-1][-1], att_parts[-1]),
        token=True,
    )
    masked.append(masked_back(count - 1, (token,)))
    full_parts = share(joined, "head")

    small_rows = 8 + -(-experts // 8) * 8
    dv_sel, comb_sel, small, wout_part, gh_sel, ght_sel, delta_sel = call(
        partial(slot_back_kernel, heads=heads),
        [
            shape_of(rows, width, f32),
            shape_of(rows, width, f32),
            shape_of(small_rows, width, f32),
            shape_of(inner, width, f32),
            jax.ShapeDtypeStruct((count, rows, each), bf16),
            shape_of(inner, rows, bf16),
            jax.ShapeDtypeStruct((count, rows, 1), f32),
        ],
        tuple(full_parts)
        + (sel_up, normed_sel, hidden_sel, probs, router_t, norm2_gain)
        + (w_attn_out, att_sel, wout0),
        scratch=[pltpu.VMEM((heads, rows, split), f32), pltpu.VMEM((rows, inner), f32)],
        name="slot_back",
        after=(masked[-1][-1],),
    )

    back = call(
        partial(sparse_back_kernel, heads=heads),
        [shape_of(part, width, bf16), shape_of(part + EXTRA, width, bf16)]
        + [shape_of(part, width, bf16)]
        + [shape_of(part // 2, width, bf16)] * 2
        + [
            jax.ShapeDtypeStruct((count, rows, tokens), bf16),
            shape_of(2 * inner, width, bf16),
            shape_of(2 * inner, width, f32),
            shape_of(small_rows, width, f32),
        ],
        (gh_sel, ght_sel, delta_sel, v_t, k_rows, q_sel, place)
        + (wq_t, wk_t, wv_t, low, norm1_gain, small, wout_part)
        + tuple(a for m in masked for a in (m[4], m[0], m[1], m[2])),
        scratch=[
            pltpu.VMEM((rows, inner), f32),
            pltpu.VMEM((tokens, inner), bf16),
            pltpu.VMEM((tokens, inner), bf16),
            pltpu.VMEM((tokens, inner), bf16),
            pltpu.VMEM((inner, tokens), bf16),
            pltpu.VMEM((inner, tokens), bf16),
            pltpu.VMEM((4 * inner, width), f32),
        ],
        name="sparse_back",
    )
    score_sel, send, keep, small = back[5:]
    own, to_1, to_2, rest_1, rest_2 = back[:5]
    got_1, got_2 = swap(to_1, "head", 1), swap(to_2, "head", 2)

    bits = bits_of("seq")
    send, keep, token = halve(send, keep, bits[1], ())
    small_part = small
    small, token = call(
        partial(bias_grad_kernel, bucket_count=bucket_count),
        [shape_of(small_rows, width, f32)],
        (score_sel, place, bucket_row, small) + tuple(m[3] for m in masked),
        scratch=[pltpu.VMEM((BLOCK, span), f32)],
        name="bias_grad",
        after=(token,),
        moved=16 * 2**20,
        token=True,
    )
    next_1, next_2, send, keep, token = halve(
        send, keep, bits[2], (token,), (rest_1, got_1, rest_2, got_2, small_part)
    )
    last_1, last_2 = swap(next_1, "head", 1), swap(next_2, "head", 2)
    w_in_grad, w_out_grad, token = call(
        expert_grad_kernel,
        [
            jax.ShapeDtypeStruct(w_expert_in.shape, f32),
            jax.ShapeDtypeStruct(w_expert_out.shape, f32),
        ],
        (x_rows, pre_low, act, out_low),
        name="expert_grad",
        after=(token,),
        moved=10 * 2**20,
        token=True,
    )
    hidden, token = call(
        partial(hidden_kernel, heads=heads),
        [shape_of(tokens, width, f32)],
        tuple(att_parts) + (w_full, layer_input),
        scratch=[pltpu.VMEM((heads * inner, tokens), bf16)],
        name="hidden",
        after=(token,),
        moved=6 * 2**20,
        token=True,
    )
    for bit in bits[3:]:
        send, keep, token = halve(send, keep, bit, (token,))

    grad_part, weights, token = call(
        first_norm_kernel,
        [shape_of(part, width, bf16), shape_of(keep.shape[0] + small_rows, width, bf16)],
        (own, got_1, got_2, last_1, last_2, next_2, small)
        + (x_c, cot_c, place_c, dv_sel, norm1_gain)
        + (keep, swap(send, "seq", bits[-1])),
        name="first_norm",
        after=(token,),
        token=True,
    )
    grad_1, grad_2 = swap(grad_part, "head", 1), swap(grad_part, "head", 2)
    layer_output, token = call(
        output_kernel,
        [shape_of(tokens, width, f32)],
        (hidden, place, comb_sel),
        name="output",
        after=(token,),
        moved=10 * 2**20,
        token=True,
    )
    for bit in reversed(bits[3:]):
        weights, token = pair(weights, small_rows, bit, (token,))
    next_1, next_2, weights, token = pair(
        weights, small_rows, bits[2], (token,), (grad_1, grad_2)
    )
    grad_3 = (swap(next_1, "head", 1), swap(next_2, "head", 2))
    weights, token = pair(weights, small_rows, bits[1], grad_3)
    last = call(
        partial(final_kernel, bit=bits[0], count=2 * inner),
        [shape_of(inner, width, f32)] * 4
        + [
            jax.ShapeDtypeStruct((width,), f32),
            jax.ShapeDtypeStruct((width,), f32),
            shape_of(count, bucket_count, f32),
            shape_of(experts, width, f32),
        ],
        (weights, swap(weights, "seq", bits[0])),
        scratch=[pltpu.VMEM((4 * inner + small_rows, width), f32)],
        name="weights_out",
    )
    weight_sums = last[:4]
    gain1_sum, gain2_sum, table_sum, router_sum = last[4:]
    (input_grad,) = call(
        spread_kernel,
        [shape_of(tokens, width, f32)],
        (grad_part, grad_1, grad_2) + grad_3,
        name="spread",
    )

    return (
        layer_output,
        input_grad,
        gain1_sum,
        jnp.transpose(weight_sums[0]),
        jnp.transpose(weight_sums[1]),
        jnp.transpose(weight_sums[2]),
        weight_sums[3],
        jnp.transpose(table_sum),
        gain2_sum,
        jnp.transpose(router_sum),
        w_in_grad,
        w_out_grad,
    )


def solution(mesh):
    return jax.shard_map(
        on_device,
        mesh=mesh,
        in_specs=(
            P("seq", None),
            P("seq", None),
            P(),
            P(None, "head"),
            P(None, "head"),
            P(None, "head"),
            P("head", None),
            P(None, "head"),
            P(),
            P(),
            P("seq", None, "head"),
            P("seq", "head", None),
            P("seq"),
            P("seq"),
            P(),
        ),
        out_specs=(
            P("seq", None),
            P("seq", None),
            P(),
            P(None, "head"),
            P(None, "head"),
            P(None, "head"),
            P("head", None),
            P(None, "head"),
            P(),
            P(),
            P("seq", None, "head"),
            P("seq", "head", None),
        ),
        check_vma=False,
    )
```

```python
from functools import partial

import jax
import jax.numpy as jnp
import numpy as np
from jax import lax
from jax.experimental import pallas as pl
from jax.experimental.pallas import tpu as pltpu
from jax.sharding import PartitionSpec as P

CAP = 20
SLOT = 24
EPS = 1e-06
BLOCK = 128
ROWS = 16
EXTRA = 16
VMEM_LIMIT = 26 * 1024 * 1024
VMEM_ALL = 60 * 1024 * 1024
NO_COST = pl.CostEstimate(flops=1, bytes_accessed=1, transcendentals=0)

f32 = jnp.float32
bf16 = jnp.bfloat16
highest = lax.Precision.HIGHEST


def dot(a, b):
    return jnp.dot(a, b, preferred_element_type=f32)


def dot_nt(a, b, precision=None):
    return lax.dot_general(
        a, b, (((1,), (1,)), ((), ())), precision=precision, preferred_element_type=f32
    )


def dot_tn(a, b, precision=None):
    return lax.dot_general(
        a, b, (((0,), (0,)), ((), ())), precision=precision, preferred_element_type=f32
    )


def iota(shape, dim):
    return lax.broadcasted_iota(jnp.int32, shape, dim)


def split_two(v):
    high = v.astype(bf16)
    return high, (v - high.astype(f32)).astype(bf16)


def shape_of(rows, cols, dtype):
    return jax.ShapeDtypeStruct((rows, cols), dtype)


def spec(memory):
    return pl.BlockSpec(memory_space=memory)


def call(kernel, outs, args, scratch=(), name=None, after=(), moved=1, token=False):
    outs, args = tuple(outs), tuple(args)
    held = sum(int(np.prod(a.shape)) * np.dtype(a.dtype).itemsize for a in args + outs)
    if token:
        outs += (shape_of(8, 128, f32),)
    first_out = len(args) + len(after)

    def body(*refs):
        results = refs[first_out : first_out + len(outs)]
        if token:
            results[-1][...] = jnp.zeros((8, 128), f32)
            results = results[:-1]
        kernel(*refs[: len(args)], *results, *refs[first_out + len(outs) :])

    return pl.pallas_call(
        body,
        out_shape=outs,
        in_specs=[spec(pltpu.VMEM)] * len(args) + [spec(pl.ANY)] * len(after),
        out_specs=tuple(spec(pltpu.VMEM) for _ in outs),
        scratch_shapes=list(scratch),
        compiler_params=pltpu.CompilerParams(
            vmem_limit_bytes=VMEM_LIMIT if 2 * held < VMEM_LIMIT else VMEM_ALL
        ),
        cost_estimate=pl.CostEstimate(flops=1, bytes_accessed=moved, transcendentals=0),
        name=name,
    )(*args, *after)


def slot_rows(ids, slots, rows, each):
    cell = jnp.where(slots < CAP, ids * each + slots, -1)
    return (iota((rows, cell.shape[1]), 0) == cell).astype(f32)


def place_kernel(x_ref, cot_ref, ids_ref, slots_ref, *refs, heads):
    w_parts = refs[:heads]
    sel_in, sel_up, place, place_c, x_c, cot_c, w_ref, place_s = refs[heads:]
    head = lax.axis_index("head")
    part = x_c.shape[0]
    slot_hot = slot_rows(ids_ref[...], slots_ref[...], sel_in.shape[0], SLOT)
    place_s[...] = jnp.transpose(slot_hot)
    slot_low = slot_hot.astype(bf16)
    sel_in[...] = dot(slot_low, x_ref[...]).astype(bf16)
    sel_up[...] = dot(slot_low, cot_ref[...]).astype(bf16)
    place[...] = place_s[...].astype(bf16)
    mine = pl.ds(pl.multiple_of(head * part, part), part)
    place_c[...] = place_s[mine, :].astype(bf16)
    x_c[...] = x_ref[mine, :]
    cot_c[...] = cot_ref[mine, :]
    inner = w_parts[0].shape[0]
    for d in range(heads):
        rows = pl.ds(pl.multiple_of((head ^ d) * inner, inner), inner)
        w_ref[rows, :] = w_parts[d][...]


def attend_kernel(*refs):
    given, refs = refs[:9], refs[9:]
    low_ref, prob_ref, att_ref, attt_ref, sel_ref = refs[:5]
    q_s, kt_s, v_s, bias_s, skew_s, slot_s, score_s = refs[5:12]
    here, sems = refs[12:21], refs[21]
    x_ref, gain_ref, wq_ref, wk_ref, wv_ref, table_ref, buckets_ref, ids_ref, slots_ref = here
    copies = [
        pltpu.make_async_copy(far, near, sems.at[i])
        for i, (far, near) in enumerate(zip(given, here))
    ]
    tokens = x_ref.shape[0]
    inner = wq_ref.shape[0]
    count = q_s.shape[0]
    width = inner // count
    span = skew_s.shape[1]
    tall = 2 * BLOCK
    for copy in copies:
        copy.start()
    for copy in copies[5:]:
        copy.wait()
    slot_s[...] = slot_rows(ids_ref[...], slots_ref[...], slot_s.shape[0], CAP).astype(bf16)
    offsets = buckets_ref.shape[1]
    bucket_hot = (iota((table_ref.shape[1], offsets), 0) == buckets_ref[...]).astype(f32)
    bias_s[...] = jnp.zeros_like(bias_s)
    bias_s[:count, :offsets] = jnp.dot(
        table_ref[...], bucket_hot, precision=highest, preferred_element_type=f32
    )
    for copy in copies[:2]:
        copy.wait()
    for i in range(0, tokens, 256):
        rows = pl.ds(i, 256)
        x = x_ref[rows, :].astype(f32)
        inverse = lax.rsqrt(jnp.mean(x * x, axis=-1, keepdims=True) + EPS)
        low_ref[rows, :] = (x * inverse * gain_ref[...]).astype(bf16)
    for copy in copies[2:5]:
        copy.wait()
    low = low_ref[...]
    q = dot_nt(low, wq_ref[...]).astype(bf16) * bf16(width ** (-0.5))
    kt_s[...] = dot_nt(wk_ref[...], low).astype(bf16)
    v = dot_nt(low, wv_ref[...]).astype(bf16)
    for h in range(count):
        cols = slice(h * width, (h + 1) * width)
        q_s[h] = q[:, cols]
        v_s[h] = v[:, cols]

    blocks = tokens // tall
    half = sel_ref.shape[0]

    def one_head(h, carry):
        head_rows = pl.ds(pl.multiple_of(h * width, width), width)
        skew_s[...] = pltpu.roll(
            jnp.broadcast_to(bias_s[pl.ds(h, 1), :], skew_s.shape),
            span - (BLOCK - 1), 1, stride=1, stride_axis=0,
        )

        def scores(n):
            score_s[n % 2] = dot(q_s[h, pl.ds(n * tall, tall), :], kt_s[head_rows, :])

        scores(0)
        for n in range(blocks):
            if n + 1 < blocks:
                scores(n + 1)
            for j in range(0, tall, ROWS):
                row = n * tall + j
                first = tokens - BLOCK - row // BLOCK * BLOCK
                bias = skew_s[j % BLOCK : j % BLOCK + ROWS, first : first + tokens]
                score = score_s[n % 2, j : j + ROWS, :] + bias
                weight = jnp.exp(score - jnp.max(score, axis=-1, keepdims=True))
                total = jnp.sum(weight, axis=-1, keepdims=True)
                prob_ref[h, pl.ds(row, ROWS), :] = (weight * (1.0 / total)).astype(bf16)
        att = dot(prob_ref[h], v_s[h])
        att_low = att.astype(bf16)
        att_ref[h] = att_low
        attt_ref[head_rows, :] = jnp.transpose(att).astype(bf16)
        picked = dot(slot_s[...], att_low).astype(bf16)
        for k in range(count):

            @pl.when(h == k)
            def _():
                for part in range(2):
                    start = part * inner + k * width
                    sel_ref[:, start : start + width] = picked[part * half : (part + 1) * half]

        return carry

    lax.fori_loop(0, count, one_head, 0)


def pass_kernel(given, passed):
    passed[...] = given[...]


def widen(rows, wide_s):
    wide_s[...] = jnp.zeros_like(wide_s)
    for e in range(rows.shape[0] // CAP):
        wide_s[e * SLOT : e * SLOT + CAP, :] = rows[e * CAP : (e + 1) * CAP]
    return wide_s[...]


def route_kernel(*refs, shards, heads):
    att_parts, w_ref = refs[:heads], refs[heads]
    (sel_in, sel_up, gain_ref, router_ref, att_t, hidden_ref, normed_ref, probs_ref, att_on
     ) = refs[heads + 1 : heads + 10]
    pieces = refs[heads + 10 : heads + 10 + shards]
    att_s, pay_s, wide_s = refs[heads + 10 + shards :]
    head = lax.axis_index("head")
    half = att_parts[0].shape[0]
    inner = w_ref.shape[0] // heads
    for d in range(heads):
        att_s[d, 0:half, :] = att_parts[d][:, 0:inner]
        att_s[d, half : 2 * half, :] = att_parts[d][:, inner : 2 * inner]
    mixed = None
    for k in range(heads):
        term = dot(att_s[head ^ k], w_ref[k * inner : (k + 1) * inner, :])
        mixed = term if mixed is None else mixed + term
    hidden = sel_in[...].astype(f32) + widen(mixed, wide_s)
    hidden_ref[...] = hidden
    inverse = lax.rsqrt(jnp.mean(hidden * hidden, axis=-1, keepdims=True) + EPS)
    normed = hidden * inverse * gain_ref[...]
    normed_ref[...] = normed
    logits = dot_nt(normed, router_ref[...], highest)
    logits = logits - jnp.max(logits, axis=-1, keepdims=True)
    powers = jnp.exp(logits)
    probs = powers / jnp.sum(powers, axis=-1, keepdims=True)
    probs_ref[...] = probs
    gate = jnp.sum(jnp.where(chosen_of(probs.shape), probs, 0.0), axis=-1, keepdims=True)
    high = gate.astype(bf16).astype(f32)
    lane = iota((gate.shape[0], 128), 1)
    width = normed.shape[1]
    extra = jnp.where(lane == 0, high, jnp.where(lane == 1, gate - high, 0.0))
    pay_s[:, :width] = normed
    pay_s[:, width : 2 * width] = sel_up[...].astype(f32)
    pay_s[:, 2 * width :] = extra
    shard = lax.axis_index("seq")
    for j in range(shards):
        first = pl.multiple_of((shard ^ j) * SLOT, SLOT)
        pieces[j][...] = pay_s[pl.ds(first, SLOT), :].astype(bf16)
    att_on[...] = att_t[...]


def chosen_of(shape):
    expert = iota(shape, 1) * SLOT
    slot_row = iota(shape, 0)
    return (slot_row >= expert) & (slot_row < expert + SLOT)


def expert_kernel(*refs, shards, heads):
    parts = refs[:shards]
    w_in, w_out = refs[shards : shards + 2]
    chunks = refs[shards + 2 : shards + 2 + heads]
    x_ref, act_ref, pre_ref, out_ref, pay_s, both_s = refs[shards + 2 + heads :]
    head = lax.axis_index("head")
    width = x_ref.shape[1]
    for j in range(shards):
        pay_s[j * SLOT : (j + 1) * SLOT, :] = parts[j][...].astype(f32)
    x = pay_s[:, :width].astype(bf16)
    up = pay_s[:, width : 2 * width]
    gate = pay_s[:, 2 * width : 2 * width + 1] + pay_s[:, 2 * width + 1 : 2 * width + 2]
    out_low = (gate * up).astype(bf16)
    pre = dot(x, w_in[...])
    cdf = 0.5 * (1.0 + lax.erf(pre * (0.5**0.5)))
    act = (pre * cdf).astype(bf16)
    slope = cdf + pre * jnp.exp(-0.5 * pre * pre) * ((2.0 * np.pi) ** (-0.5))
    pre_low = (dot_nt(out_low, w_out[...]) * slope).astype(bf16)
    both = (dot(act, w_out[...]), dot_nt(pre_low, w_in[...]))
    part = both_s.shape[2]
    for k in range(heads):
        start = k % (heads // 2) * part
        for j in range(shards):
            both_s[k, j * CAP : (j + 1) * CAP, :] = both[k // (heads // 2)][
                j * SLOT : j * SLOT + CAP, start : start + part
            ]
    for d in range(heads):
        chunks[d][...] = both_s[head ^ d].astype(bf16)
    pre_ref[...] = pre_low
    out_ref[...] = out_low
    x_ref[...] = x
    act_ref[...] = act


def expert_grad_kernel(x_ref, pre_ref, act_ref, out_ref, in_grad, out_grad):
    in_grad[0] = dot_tn(x_ref[...], pre_ref[...])
    out_grad[0] = dot_tn(act_ref[...], out_ref[...])


def sum_kernel(att_ref, *refs, heads):
    parts, att_on, pieces, sum_s = refs[:heads], refs[heads], refs[heads + 1 : -1], refs[-1]
    att_on[...] = att_ref[...]
    total = parts[0][...].astype(f32)
    for d in range(1, heads):
        total = total + parts[d][...].astype(f32)
    sum_s[...] = total
    for j, piece in enumerate(pieces):
        piece[...] = sum_s[j * CAP : (j + 1) * CAP, :].astype(bf16)


def join_kernel(*refs):
    parts, out_ref, sum_s = refs[:-2], refs[-2], refs[-1]
    for j, part in enumerate(parts):
        sum_s[j * CAP : (j + 1) * CAP, :] = part[...].astype(f32)
    out_ref[...] = sum_s[...].astype(bf16)


def prep_kernel(
    cot_ref, w_ref, wq_ref, wk_ref, wv_ref, low_ref, place_ref, attt_ref,
    gh_ref, stack_ref, k_ref, qt_ref, vt_ref, wout_ref, qsel_ref, ght_s, mcot_s,
):
    count, tokens, width = gh_ref.shape
    for i in range(0, tokens, 256):
        rows = pl.ds(i, 256)
        where = place_ref[rows, :].astype(f32)
        free = 1.0 - jnp.sum(where, axis=-1, keepdims=True)
        mcot_s[rows, :] = (cot_ref[rows, :].astype(f32) * free).astype(bf16)
        slots = jnp.transpose(where).astype(bf16)
        for h in range(count):
            stack_ref[h, width:, rows] = slots
    gh = dot_nt(mcot_s[...], w_ref[...]).astype(bf16)
    ght_s[...] = dot_nt(w_ref[...], mcot_s[...]).astype(bf16)
    k = dot_nt(low_ref[...], wk_ref[...]).astype(bf16)
    qt_ref[...] = dot_nt(wq_ref[...], low_ref[...]).astype(bf16) * bf16(width ** (-0.5))
    vt_ref[...] = dot_nt(wv_ref[...], low_ref[...]).astype(bf16)
    for h in range(count):
        cols = slice(h * width, (h + 1) * width)
        gh_ref[h] = gh[:, cols]
        k_ref[h] = k[:, cols]
        stack_ref[h, 0:width, :] = ght_s[cols, :]
    wout_ref[...] = dot(attt_ref[...], mcot_s[...])
    qsel_ref[...] = dot(qt_ref[...], place_ref[...]).astype(bf16)


def masked_back_kernel(
    gh_ref, stack_ref, k_ref, qt_ref, vt_ref, att_ref, prob_ref,
    dq_ref, dkt_ref, dvt_ref, offs_ref, psel_ref, acc_s, score_s, *, h,
):
    tokens, width = dq_ref.shape
    acc_s[...] = jnp.zeros_like(acc_s)
    cols = slice(h * width, (h + 1) * width)
    for i in range(0, tokens, 2 * BLOCK):
        rows = pl.ds(i, 2 * BLOCK)
        gh = gh_ref[h, rows, :]
        delta = jnp.sum(gh.astype(f32) * att_ref[h, rows, :].astype(f32), axis=-1, keepdims=True)
        grads = dot(gh, vt_ref[cols, :]) - delta
        for j in range(2):
            start = i + j * BLOCK
            first = tokens - BLOCK - start
            here = pl.ds(start, BLOCK)
            score = prob_ref[h, here, :].astype(f32) * grads[j * BLOCK : (j + 1) * BLOCK]
            acc_s[:, first : first + tokens] += score
            score_s[here, :] = score.astype(bf16)
    dq_ref[...] = dot(score_s[...], k_ref[h]) * (width ** (-0.5))
    dkt_ref[...] = dot(qt_ref[cols, :], score_s[...])
    both = dot(stack_ref[h], prob_ref[h])
    dvt_ref[...] = both[:width]
    psel_ref[...] = both[width:].astype(bf16)
    offs_ref[...] = diagonals(acc_s[...])


def diagonals(acc):
    span = acc.shape[1]
    rows = acc.shape[0] // 2
    while rows >= 8:
        acc = acc[:rows] + pltpu.roll(acc[rows:], span - rows, 1)
        rows //= 2
    total = acc[0:1]
    for r in range(1, 8):
        total = total + pltpu.roll(acc[r : r + 1], span - r, 1)
    return jnp.broadcast_to(pltpu.roll(total, BLOCK - 1, 1), (8, span))


def slot_back_kernel(*refs, heads):
    parts = refs[:heads]
    (up_ref, normed_ref, hidden_ref, probs_ref, router_ref, gain_ref, w_ref, att_ref,
     wout0_ref) = refs[heads : heads + 9]
    (dv_ref, comb_ref, small_ref, wout_ref, gh_ref, ght_ref, delta_ref, ret_s, wide_s
     ) = refs[heads + 9 :]
    head, shard = lax.axis_index("head"), lax.axis_index("seq")
    ret_s[...] = jnp.zeros_like(ret_s)
    for d in range(heads):
        part = parts[d][...].astype(f32)
        for j in range(part.shape[0] // CAP):
            first = pl.multiple_of((shard ^ j) * SLOT, SLOT)
            ret_s[head ^ d, pl.ds(first, CAP), :] = part[j * CAP : (j + 1) * CAP]
    back = [ret_s[k] for k in range(heads)]
    combined = jnp.concatenate(back[: heads // 2], axis=1)
    grad_buf = jnp.concatenate(back[heads // 2 :], axis=1)
    up = up_ref[...].astype(f32)
    hidden, normed, probs, gain = hidden_ref[...], normed_ref[...], probs_ref[...], gain_ref[...]
    chosen = chosen_of(probs.shape)
    gate = jnp.sum(jnp.where(chosen, probs, 0.0), axis=-1, keepdims=True)
    comb_ref[...] = gate * combined
    gate_grad = jnp.sum(up * combined, axis=-1, keepdims=True)
    marked = jnp.where(chosen, gate_grad, 0.0)
    logit_grad = probs * (marked - jnp.sum(marked * probs, axis=-1, keepdims=True))
    experts = probs.shape[1]
    grad = grad_buf + jnp.dot(
        logit_grad, router_ref[...], precision=highest, preferred_element_type=f32
    )
    inverse = lax.rsqrt(jnp.mean(hidden * hidden, axis=-1, keepdims=True) + EPS)
    scaled = grad * gain
    inner_sum = jnp.mean(scaled * hidden, axis=-1, keepdims=True)
    dv = inverse * scaled - hidden * (inverse * inverse * inverse * inner_sum)
    dv_ref[...] = dv
    small_ref[...] = jnp.zeros_like(small_ref)
    small_ref[0:1, :] = jnp.sum(grad * hidden * inverse, axis=0, keepdims=True)
    small_ref[8 : 8 + experts, :] = dot_tn(logit_grad, normed, highest)
    grad_low = (up + dv).astype(bf16)
    half = att_ref.shape[0]
    inner = w_ref.shape[0]
    att = jnp.concatenate(
        [att_ref[:, 0:inner].astype(f32), att_ref[:, inner : 2 * inner].astype(f32)], axis=0
    )
    att = widen(att, wide_s)
    wout_ref[...] = wout0_ref[...] + dot_tn(att.astype(bf16), grad_low)
    gh = dot_nt(grad_low, w_ref[...])
    gh_low = gh.astype(bf16)
    count = gh_ref.shape[0]
    each = inner // count
    ght_ref[...] = dot_nt(w_ref[...], grad_low).astype(bf16)
    for h in range(count):
        cols = slice(h * each, (h + 1) * each)
        gh_ref[h] = gh_low[:, cols]
        delta_ref[h] = jnp.sum(
            gh_low[:, cols].astype(f32) * att[:, cols], axis=-1, keepdims=True
        )


def sparse_back_kernel(
    gh_ref, ght_ref, delta_ref, vt_ref, k_ref, qsel_ref,
    place_ref, wq_ref, wk_ref, wv_ref, low_ref, gain_ref, small_ref, wout_ref, *refs, heads,
):
    per_head, refs = refs[: 4 * gh_ref.shape[0]], refs[4 * gh_ref.shape[0] :]
    psels, dq0s, dkt0s, dvt0s = (per_head[i :: 4] for i in range(4))
    chunks = refs[:5]
    (score_ref, send_ref, keep_ref, out_ref,
     dq_s, q_low, k_low, v_low, kt_s, vt_s, all_s) = refs[5:]
    head = lax.axis_index("head")
    count, rows, width = gh_ref.shape
    tokens = vt_ref.shape[1]
    inner = count * width
    for h in range(count):
        cols = slice(h * width, (h + 1) * width)
        grad = dot(gh_ref[h], vt_ref[cols, :])
        prob = psels[h][...]
        score = (prob.astype(f32) * (grad - delta_ref[h])).astype(bf16)
        score_ref[h] = score
        dq_s[:, cols] = dot(score, k_ref[h]) * (width ** (-0.5))
        dkt = dkt0s[h][...] + dot(qsel_ref[cols, :], score)
        dvt = dvt0s[h][...] + dot(ght_ref[cols, :], prob)
        kt_s[cols, :] = dkt.astype(bf16)
        vt_s[cols, :] = dvt.astype(bf16)
        k_low[:, cols] = jnp.transpose(dkt).astype(bf16)
        v_low[:, cols] = jnp.transpose(dvt).astype(bf16)
    spread = dot(place_ref[...], dq_s[...].astype(bf16))
    for h in range(count):
        cols = slice(h * width, (h + 1) * width)
        q_low[:, cols] = (spread[:, cols] + dq0s[h][...]).astype(bf16)
    part = tokens // heads
    half = part // 2
    own, to_1, to_2, rest_1, rest_2 = chunks
    to_1[part:, :] = jnp.zeros((EXTRA, to_1.shape[1]), bf16)
    places = (
        ((own, 0), (own, half)),
        ((to_1, 0), (rest_1, 0)),
        ((rest_2, 0), (to_2, 0)),
        ((to_1, half), (to_2, half)),
    )
    for d in range(heads):
        mine = pl.ds(pl.multiple_of((head ^ d) * part, part), part)
        rows_part = (
            dot(q_low[mine, :], wq_ref[...])
            + dot(k_low[mine, :], wk_ref[...])
            + dot(v_low[mine, :], wv_ref[...])
        ).astype(bf16)
        for n, (ref, first) in enumerate(places[d]):
            ref[first : first + half, :] = rows_part[n * half : (n + 1) * half]
    low = low_ref[...]
    total = None
    grads = (dot_tn(q_low[...], low), dot(kt_s[...], low), dot(vt_s[...], low))
    for i, (grad, w) in enumerate(zip(grads, (wq_ref, wk_ref, wv_ref))):
        all_s[i * inner : (i + 1) * inner, :] = grad
        term = jnp.sum(grad * w[...].astype(f32), axis=0, keepdims=True)
        total = term if total is None else total + term
    all_s[3 * inner :, :] = wout_ref[...]
    out_ref[...] = small_ref[...]
    out_ref[1:2, :] = total / gain_ref[...]
    to_1[part : part + 1, :] = (total / gain_ref[...]).astype(bf16)
    split_rows(all_s, 1, send_ref, keep_ref)


def is_upper(bit):
    return (lax.axis_index("seq") & bit) != 0


def split_rows(all_s, bit, send_ref, keep_ref):
    half = send_ref.shape[0]
    low, high = all_s[0:half, :], all_s[half : 2 * half, :]
    keep_ref[...] = jnp.where(is_upper(bit), high, low)
    send_ref[...] = jnp.where(is_upper(bit), low, high).astype(bf16)


def halve_kernel(keep_ref, got_ref, *refs, bit):
    send_ref, out_ref, all_s = refs[-3:]
    if len(refs) > 3:
        rest_1, got_1, rest_2, got_2, small_ref, next_1, next_2 = refs[:-3]
        half = rest_1.shape[0]
        for rest, got, onward in ((rest_1, got_2, next_1), (rest_2, got_1, next_2)):
            got_rest = got[half : 2 * half, :].astype(f32)
            onward[0:half, :] = (rest[...].astype(f32) + got_rest).astype(bf16)
        mine = small_ref[1:2, :].astype(bf16).astype(f32)
        next_2[half:, :] = jnp.zeros((EXTRA, next_2.shape[1]), bf16)
        next_2[half : half + 1, :] = (mine + got_1[2 * half : 2 * half + 1, :].astype(f32)).astype(bf16)
    all_s[...] = keep_ref[...] + got_ref[...].astype(f32)
    split_rows(all_s, bit, send_ref, out_ref)


def join_rows(mine_ref, got_ref, all_s, bit, count):
    mine, got = mine_ref[...].astype(f32), got_ref[...].astype(f32)
    all_s[0:count, :] = jnp.where(is_upper(bit), got[:count], mine[:count])
    all_s[count : 2 * count, :] = jnp.where(is_upper(bit), mine[:count], got[:count])
    all_s[2 * count :, :] = mine[count:] + got[count:]


def pair_kernel(mine_ref, got_ref, *refs, bit, count):
    out_ref, all_s = refs[-2:]
    if len(refs) > 2:
        got_1, got_2, next_1, next_2 = refs[:-2]
        half = next_1.shape[0]
        next_2[...] = got_1[0:half, :]
        next_1[...] = got_2[half:, :]
    join_rows(mine_ref, got_ref, all_s, bit, count)
    out_ref[...] = all_s[...].astype(bf16)


def final_kernel(mine_ref, got_ref, *refs, bit, count):
    gain1_ref, gain2_ref, table_ref, router_ref, all_s = refs[-5:]
    outs = refs[:-5]
    join_rows(mine_ref, got_ref, all_s, bit, count)
    inner = outs[0].shape[0]
    for i, out in enumerate(outs):
        out[...] = all_s[i * inner : (i + 1) * inner, :]
    small = all_s[2 * count :, :]
    gain1_ref[...] = small[1, :]
    gain2_ref[...] = small[0, :]
    heads, buckets = table_ref.shape
    table_ref[...] = small[2 : 2 + heads, :buckets]
    router_ref[...] = small[8 : 8 + router_ref.shape[0], :]


def bias_grad_kernel(
    score_ref, place_ref, buckets_ref, small_ref, *refs, bucket_count
):
    count = score_ref.shape[0]
    offs, out_ref, acc_s = refs[:count], refs[count], refs[count + 1]
    tokens = place_ref.shape[0]
    offsets = buckets_ref.shape[1]
    out_ref[...] = small_ref[...]
    bucket_hot = (iota((bucket_count, offsets), 0) == buckets_ref[...]).astype(f32)
    for h in range(count):
        acc_s[...] = jnp.zeros_like(acc_s)
        for i in range(0, tokens, BLOCK):
            first = tokens - BLOCK - i
            acc_s[:, first : first + tokens] += dot(place_ref[i : i + BLOCK, :], score_ref[h])
        sums = diagonals(acc_s[...]) + offs[h][...]
        out_ref[2 + h : 3 + h, :bucket_count] = dot_nt(sums[:, :offsets], bucket_hot, highest)[0:1]


def hidden_kernel(*refs, heads):
    att_parts, w_ref, x_ref, out_ref, att_s = refs[:heads], *refs[heads:]
    head = lax.axis_index("head")
    tokens = x_ref.shape[0]
    inner = att_parts[0].shape[0]
    for d in range(heads):
        mine = pl.ds(pl.multiple_of((head ^ d) * inner, inner), inner)
        att_s[mine, :] = att_parts[d][...]
    for i in range(0, tokens, 256):
        rows = pl.ds(i, 256)
        out_ref[rows, :] = x_ref[rows, :].astype(f32) + dot_tn(att_s[:, rows], w_ref[...])


def output_kernel(hidden_ref, place_ref, comb_ref, out_ref):
    high, rest = split_two(comb_ref[...])
    for i in range(0, hidden_ref.shape[0], 256):
        rows = pl.ds(i, 256)
        where = place_ref[rows, :]
        out_ref[rows, :] = hidden_ref[rows, :] + (dot(where, high) + dot(where, rest))


def first_norm_kernel(
    own, got_1, got_2, last_1, last_2, next_2, small_ref,
    x_ref, cot_ref, place_ref, dv_ref, gain_ref, keep_ref, got_ref, out_ref, sum_ref,
):
    half = last_1.shape[0]
    high, rest = split_two(dv_ref[...])
    for first, near, far in ((0, got_1, last_2), (half, got_2, last_1)):
        rows = pl.ds(first, half)
        grad = own[rows, :].astype(f32) + near[0:half, :].astype(f32)
        grad = grad + far[0:half, :].astype(f32)
        x = x_ref[rows, :].astype(f32)
        inverse = lax.rsqrt(jnp.mean(x * x, axis=-1, keepdims=True) + EPS)
        scaled = grad * gain_ref[...]
        inner_sum = jnp.mean(scaled * x, axis=-1, keepdims=True)
        where = place_ref[rows, :]
        hidden_grad = cot_ref[rows, :].astype(f32) + (dot(where, high) + dot(where, rest))
        out_ref[rows, :] = (
            hidden_grad + inverse * scaled - x * (inverse * inverse * inverse * inner_sum)
        ).astype(bf16)
    count = keep_ref.shape[0]
    sum_ref[0:count, :] = (keep_ref[...] + got_ref[...].astype(f32)).astype(bf16)
    gain1 = next_2[half:, :].astype(f32)[0:1] + last_2[half:, :].astype(f32)[0:1]
    small = small_ref[...]
    sum_ref[count:, :] = jnp.where(iota(small.shape, 0) == 1, gain1, small).astype(bf16)


def spread_kernel(own, got_1, got_2, last_1, last_2, out_ref):
    head = lax.axis_index("head")
    part, half = own.shape[0], last_1.shape[0]
    for d, piece in enumerate((own, got_1, got_2)):
        mine = pl.ds(pl.multiple_of((head ^ d) * part, part), part)
        out_ref[mine, :] = piece[...].astype(f32)
    for n, piece in enumerate((last_2, last_1)):
        mine = pl.ds(pl.multiple_of((head ^ 3) * part + n * half, half), half)
        out_ref[mine, :] = piece[...].astype(f32)


def swap(x, axis, d):
    size = lax.axis_size(axis)
    return lax.ppermute(x, axis, [(i, i ^ d) for i in range(size)])


def share(x, axis):
    return [x] + [swap(x, axis, d) for d in range(1, lax.axis_size(axis))]


def trade(pieces, axis):
    return lax.all_to_all(pieces, axis, split_axis=0, concat_axis=0, tiled=True)


def swap_all(pieces, axis):
    return [pieces[0]] + [swap(pieces[d], axis, d) for d in range(1, len(pieces))]


def bits_of(axis):
    return [b for b in (1 << i for i in range(16)) if b < lax.axis_size(axis)]


def halve(send, keep, bit, after, onward=()):
    rows, width = keep.shape
    outs = []
    if onward:
        half = onward[0].shape[0]
        outs = [shape_of(half, width, bf16), shape_of(half + EXTRA, width, bf16)]
    return call(
        partial(halve_kernel, bit=bit),
        outs + [shape_of(rows // 2, width, bf16), shape_of(rows // 2, width, f32)],
        (keep, swap(send, "seq", bit // 2)) + tuple(onward),
        scratch=[pltpu.VMEM((rows, width), f32)],
        name="halve",
        after=after,
        token=True,
    )


def pair(now, small_rows, bit, after, onward=()):
    rows, width = now.shape
    count = rows - small_rows
    outs = [shape_of(onward[0].shape[0] // 2, width, bf16)] * 2 if onward else []
    return call(
        partial(pair_kernel, bit=bit, count=count),
        outs + [shape_of(rows + count, width, bf16)],
        (now, swap(now, "seq", bit)) + tuple(onward),
        scratch=[pltpu.VMEM((rows + count, width), f32)],
        name="pair",
        after=after,
        token=True,
    )


def on_device(
    layer_input, cotangent, norm1_gain, w_query, w_key, w_value, w_attn_out, bias_table,
    norm2_gain, w_router, w_expert_in, w_expert_out, expert_ids, slot_ids, buckets,
):
    tokens, width = layer_input.shape
    shards = lax.axis_size("seq")
    heads = lax.axis_size("head")
    bucket_count, count = bias_table.shape
    inner = w_query.shape[1]
    each = inner // count
    experts = w_router.shape[1]
    rows, filled = experts * SLOT, experts * CAP
    hidden_units = w_expert_in.shape[2]
    part = tokens // heads
    split = 2 * width // heads
    span = 2 * tokens
    params = pltpu.CompilerParams(vmem_limit_bytes=VMEM_LIMIT if rows <= 256 else VMEM_ALL)

    ids = expert_ids.reshape(1, tokens)
    slots = slot_ids.reshape(1, tokens)
    bucket_row = buckets.reshape(1, -1)
    wq_t, wk_t, wv_t = jnp.transpose(w_query), jnp.transpose(w_key), jnp.transpose(w_value)
    router_t, table_t = jnp.transpose(w_router), jnp.transpose(bias_table)
    w_in = w_expert_in.reshape(width, hidden_units)
    w_out = w_expert_out.reshape(hidden_units, width)

    w_mix = share(w_attn_out, "head")

    low, prob, att, att_t, att_sel = pl.pallas_call(
        attend_kernel,
        out_shape=(
            shape_of(tokens, width, bf16),
            jax.ShapeDtypeStruct((count, tokens, tokens), bf16),
            jax.ShapeDtypeStruct((count, tokens, each), bf16),
            shape_of(inner, tokens, bf16),
            shape_of(filled // 2, 2 * inner, bf16),
        ),
        in_specs=[spec(pltpu.HBM)] * 9,
        out_specs=(spec(pltpu.VMEM),) * 5,
        scratch_shapes=[
            pltpu.VMEM((count, tokens, each), bf16),
            pltpu.VMEM((inner, tokens), bf16),
            pltpu.VMEM((count, tokens, each), bf16),
            pltpu.VMEM((8, span), f32),
            pltpu.VMEM((BLOCK, span), f32),
            pltpu.VMEM((filled, tokens), bf16),
            pltpu.VMEM((2, 2 * BLOCK, tokens), f32),
            pltpu.VMEM((tokens, width), bf16),
            pltpu.VMEM((width,), f32),
            pltpu.VMEM((inner, width), bf16),
            pltpu.VMEM((inner, width), bf16),
            pltpu.VMEM((inner, width), bf16),
            pltpu.VMEM((count, bucket_count), f32),
            pltpu.VMEM((1, span - 1), jnp.int32),
            pltpu.VMEM((1, tokens), jnp.int32),
            pltpu.VMEM((1, tokens), jnp.int32),
            pltpu.SemaphoreType.DMA((9,)),
        ],
        compiler_params=params,
        cost_estimate=NO_COST,
        name="attend",
    )(
        *(
            pltpu.with_memory_space_constraint(a, pltpu.HBM)
            for a in (layer_input, norm1_gain, wq_t, wk_t, wv_t, table_t, bucket_row, ids, slots)
        )
    )

    (att_sel,) = call(
        pass_kernel,
        [shape_of(filled // 2, 2 * inner, bf16)],
        (att_sel,),
        name="pass",
        after=(w_mix[1],),
    )
    sel_parts = share(att_sel, "head")
    sel_in, sel_up, place, place_c, x_c, cot_c, w_full = call(
        partial(place_kernel, heads=heads),
        [
            shape_of(rows, width, bf16),
            shape_of(rows, width, bf16),
            shape_of(tokens, rows, bf16),
            shape_of(part, rows, bf16),
            shape_of(part, width, bf16),
            shape_of(part, width, bf16),
            shape_of(heads * inner, width, bf16),
        ],
        (layer_input, cotangent, ids, slots) + tuple(w_mix),
        scratch=[pltpu.VMEM((tokens, rows), f32)],
        moved=12 * 2**20,
        name="place",
        after=(att_sel,),
    )
    routed = call(
        partial(route_kernel, shards=shards, heads=heads),
        [
            shape_of(rows, width, f32),
            shape_of(rows, width, f32),
            shape_of(rows, experts, f32),
            shape_of(inner, tokens, bf16),
        ]
        + [shape_of(SLOT, 2 * width + 128, bf16)] * shards,
        tuple(sel_parts) + (w_full, sel_in, sel_up, norm2_gain, router_t, att_t),
        scratch=[
            pltpu.VMEM((heads, filled, inner), bf16),
            pltpu.VMEM((rows, 2 * width + 128), f32),
            pltpu.VMEM((rows, width), f32),
        ],
        name="route",
    )
    hidden_sel, normed_sel, probs, att_on = routed[:4]
    pay_parts = swap_all(routed[4:], "seq")
    att_parts = [att_t] + [swap(att_on, "head", d) for d in range(1, heads - 1)]

    def masked_back(h, after):
        return call(
            partial(masked_back_kernel, h=h),
            [
                shape_of(tokens, each, f32),
                shape_of(each, tokens, f32),
                shape_of(each, tokens, f32),
                shape_of(8, span, f32),
                shape_of(rows, tokens, bf16),
            ],
            (gh, stack, k_rows, q_t, v_t, att, prob),
            scratch=[pltpu.VMEM((BLOCK, span), f32), pltpu.VMEM((tokens, tokens), bf16)],
            name="masked_back",
            after=after,
            moved=11 * 2**20,
            token=True,
        )

    done = call(
        partial(expert_kernel, shards=shards, heads=heads),
        [shape_of(filled, split, bf16)] * heads
        + [
            shape_of(rows, width, bf16),
            shape_of(rows, hidden_units, bf16),
            shape_of(rows, hidden_units, bf16),
            shape_of(rows, width, bf16),
        ],
        tuple(pay_parts) + (w_in, w_out),
        scratch=[
            pltpu.VMEM((rows, 2 * width + 128), f32),
            pltpu.VMEM((heads, filled, split), f32),
        ],
        name="expert",
        after=tuple(att_parts[1:]),
        token=True,
    )
    x_rows, act, pre_low, out_low, token = done[heads:]
    gh, stack, k_rows, q_t, v_t, wout0, q_sel, token = call(
        prep_kernel,
        [
            jax.ShapeDtypeStruct((count, tokens, each), bf16),
            jax.ShapeDtypeStruct((count, each + rows, tokens), bf16),
            jax.ShapeDtypeStruct((count, tokens, each), bf16),
            shape_of(inner, tokens, bf16),
            shape_of(inner, tokens, bf16),
            shape_of(inner, width, f32),
            shape_of(inner, rows, bf16),
        ],
        (cotangent, w_attn_out, wq_t, wk_t, wv_t, low, place, att_t),
        scratch=[pltpu.VMEM((inner, tokens), bf16), pltpu.VMEM((tokens, width), bf16)],
        name="prep",
        after=(token,),
        moved=8 * 2**20,
        token=True,
    )

    masked = []
    for h in range(count - 2):
        masked.append(masked_back(h, (token,)))
        token = masked[-1][-1]
    returned = call(
        partial(sum_kernel, heads=heads),
        [shape_of(inner, tokens, bf16)] + [shape_of(CAP, split, bf16)] * shards,
        [att_t] + swap_all(done[:heads], "head"),
        scratch=[pltpu.VMEM((filled, split), f32)],
        name="sum",
        after=(token,),
        token=True,
    )
    masked.append(masked_back(count - 2, (returned[-1],)))
    att_parts.append(swap(returned[0], "head", heads - 1))
    joined, token = call(
        join_kernel,
        [shape_of(filled, split, bf16)],
        swap_all(returned[1:-1], "seq"),
        scratch=[pltpu.VMEM((filled, split), f32)],
        name="join",
        after=(masked[-1][-1], att_parts[-1]),
        token=True,
    )
    masked.append(masked_back(count - 1, (token,)))
    full_parts = share(joined, "head")

    small_rows = 8 + -(-experts // 8) * 8
    dv_sel, comb_sel, small, wout_part, gh_sel, ght_sel, delta_sel = call(
        partial(slot_back_kernel, heads=heads),
        [
            shape_of(rows, width, f32),
            shape_of(rows, width, f32),
            shape_of(small_rows, width, f32),
            shape_of(inner, width, f32),
            jax.ShapeDtypeStruct((count, rows, each), bf16),
            shape_of(inner, rows, bf16),
            jax.ShapeDtypeStruct((count, rows, 1), f32),
        ],
        tuple(full_parts)
        + (sel_up, normed_sel, hidden_sel, probs, router_t, norm2_gain)
        + (w_attn_out, att_sel, wout0),
        scratch=[pltpu.VMEM((heads, rows, split), f32), pltpu.VMEM((rows, inner), f32)],
        name="slot_back",
        after=(masked[-1][-1],),
    )

    back = call(
        partial(sparse_back_kernel, heads=heads),
        [shape_of(part, width, bf16), shape_of(part + EXTRA, width, bf16)]
        + [shape_of(part, width, bf16)]
        + [shape_of(part // 2, width, bf16)] * 2
        + [
            jax.ShapeDtypeStruct((count, rows, tokens), bf16),
            shape_of(2 * inner, width, bf16),
            shape_of(2 * inner, width, f32),
            shape_of(small_rows, width, f32),
        ],
        (gh_sel, ght_sel, delta_sel, v_t, k_rows, q_sel, place)
        + (wq_t, wk_t, wv_t, low, norm1_gain, small, wout_part)
        + tuple(a for m in masked for a in (m[4], m[0], m[1], m[2])),
        scratch=[
            pltpu.VMEM((rows, inner), f32),
            pltpu.VMEM((tokens, inner), bf16),
            pltpu.VMEM((tokens, inner), bf16),
            pltpu.VMEM((tokens, inner), bf16),
            pltpu.VMEM((inner, tokens), bf16),
            pltpu.VMEM((inner, tokens), bf16),
            pltpu.VMEM((4 * inner, width), f32),
        ],
        name="sparse_back",
    )
    score_sel, send, keep, small = back[5:]
    own, to_1, to_2, rest_1, rest_2 = back[:5]
    got_1, got_2 = swap(to_1, "head", 1), swap(to_2, "head", 2)

    bits = bits_of("seq")
    send, keep, token = halve(send, keep, bits[1], ())
    small_part = small
    small, token = call(
        partial(bias_grad_kernel, bucket_count=bucket_count),
        [shape_of(small_rows, width, f32)],
        (score_sel, place, bucket_row, small) + tuple(m[3] for m in masked),
        scratch=[pltpu.VMEM((BLOCK, span), f32)],
        name="bias_grad",
        after=(token,),
        moved=16 * 2**20,
        token=True,
    )
    next_1, next_2, send, keep, token = halve(
        send, keep, bits[2], (token,), (rest_1, got_1, rest_2, got_2, small_part)
    )
    last_1, last_2 = swap(next_1, "head", 1), swap(next_2, "head", 2)
    w_in_grad, w_out_grad, token = call(
        expert_grad_kernel,
        [
            jax.ShapeDtypeStruct(w_expert_in.shape, f32),
            jax.ShapeDtypeStruct(w_expert_out.shape, f32),
        ],
        (x_rows, pre_low, act, out_low),
        name="expert_grad",
        after=(token,),
        moved=10 * 2**20,
        token=True,
    )
    hidden, token = call(
        partial(hidden_kernel, heads=heads),
        [shape_of(tokens, width, f32)],
        tuple(att_parts) + (w_full, layer_input),
        scratch=[pltpu.VMEM((heads * inner, tokens), bf16)],
        name="hidden",
        after=(token,),
        moved=6 * 2**20,
        token=True,
    )
    for bit in bits[3:]:
        send, keep, token = halve(send, keep, bit, (token,))

    grad_part, weights, token = call(
        first_norm_kernel,
        [shape_of(part, width, bf16), shape_of(keep.shape[0] + small_rows, width, bf16)],
        (own, got_1, got_2, last_1, last_2, next_2, small)
        + (x_c, cot_c, place_c, dv_sel, norm1_gain)
        + (keep, swap(send, "seq", bits[-1])),
        name="first_norm",
        after=(token,),
        token=True,
    )
    grad_1, grad_2 = swap(grad_part, "head", 1), swap(grad_part, "head", 2)
    layer_output, token = call(
        output_kernel,
        [shape_of(tokens, width, f32)],
        (hidden, place, comb_sel),
        name="output",
        after=(token,),
        moved=10 * 2**20,
        token=True,
    )
    for bit in reversed(bits[3:]):
        weights, token = pair(weights, small_rows, bit, (token,))
    next_1, next_2, weights, token = pair(
        weights, small_rows, bits[2], (token,), (grad_1, grad_2)
    )
    grad_3 = (swap(next_1, "head", 1), swap(next_2, "head", 2))
    weights, token = pair(weights, small_rows, bits[1], grad_3)
    last = call(
        partial(final_kernel, bit=bits[0], count=2 * inner),
        [shape_of(inner, width, f32)] * 4
        + [
            jax.ShapeDtypeStruct((width,), f32),
            jax.ShapeDtypeStruct((width,), f32),
            shape_of(count, bucket_count, f32),
            shape_of(experts, width, f32),
        ],
        (weights, swap(weights, "seq", bits[0])),
        scratch=[pltpu.VMEM((4 * inner + small_rows, width), f32)],
        name="weights_out",
    )
    weight_sums = last[:4]
    gain1_sum, gain2_sum, table_sum, router_sum = last[4:]
    (input_grad,) = call(
        spread_kernel,
        [shape_of(tokens, width, f32)],
        (grad_part, grad_1, grad_2) + grad_3,
        name="spread",
    )

    return (
        layer_output,
        input_grad,
        gain1_sum,
        jnp.transpose(weight_sums[0]),
        jnp.transpose(weight_sums[1]),
        jnp.transpose(weight_sums[2]),
        weight_sums[3],
        jnp.transpose(table_sum),
        gain2_sum,
        jnp.transpose(router_sum),
        w_in_grad,
        w_out_grad,
    )


def solution(mesh):
    return jax.shard_map(
        on_device,
        mesh=mesh,
        in_specs=(
            P("seq", None),
            P("seq", None),
            P(),
            P(None, "head"),
            P(None, "head"),
            P(None, "head"),
            P("head", None),
            P(None, "head"),
            P(),
            P(),
            P("seq", None, "head"),
            P("seq", "head", None),
            P("seq"),
            P("seq"),
            P(),
        ),
        out_specs=(
            P("seq", None),
            P("seq", None),
            P(),
            P(None, "head"),
            P(None, "head"),
            P(None, "head"),
            P("head", None),
            P(None, "head"),
            P(),
            P(),
            P("seq", None, "head"),
            P("seq", "head", None),
        ),
        check_vma=False,
    )
```

```python
from functools import partial

import jax
import jax.numpy as jnp
import numpy as np
from jax import lax
from jax.experimental import pallas as pl
from jax.experimental.pallas import tpu as pltpu
from jax.sharding import PartitionSpec as P

CAP = 20
SLOT = 24
EPS = 1e-06
BLOCK = 128
ROWS = 16
EXTRA = 16
TALL = 16
VMEM_LIMIT = 26 * 1024 * 1024
VMEM_ALL = 60 * 1024 * 1024
NO_COST = pl.CostEstimate(flops=1, bytes_accessed=1, transcendentals=0)

f32 = jnp.float32
bf16 = jnp.bfloat16
highest = lax.Precision.HIGHEST


def dot(a, b):
    return jnp.dot(a, b, preferred_element_type=f32)


def dot_nt(a, b, precision=None):
    return lax.dot_general(
        a, b, (((1,), (1,)), ((), ())), precision=precision, preferred_element_type=f32
    )


def dot_tn(a, b, precision=None):
    return lax.dot_general(
        a, b, (((0,), (0,)), ((), ())), precision=precision, preferred_element_type=f32
    )


def iota(shape, dim):
    return lax.broadcasted_iota(jnp.int32, shape, dim)


def split_two(v):
    high = v.astype(bf16)
    return high, (v - high.astype(f32)).astype(bf16)


def shape_of(rows, cols, dtype):
    return jax.ShapeDtypeStruct((rows, cols), dtype)


def spec(memory):
    return pl.BlockSpec(memory_space=memory)


def call(kernel, outs, args, scratch=(), name=None, after=(), moved=1, token=False):
    outs, args = tuple(outs), tuple(args)
    held = sum(int(np.prod(a.shape)) * np.dtype(a.dtype).itemsize for a in args + outs)
    if token:
        outs += (shape_of(8, 128, f32),)
    first_out = len(args) + len(after)

    def body(*refs):
        results = refs[first_out : first_out + len(outs)]
        if token:
            results[-1][...] = jnp.zeros((8, 128), f32)
            results = results[:-1]
        kernel(*refs[: len(args)], *results, *refs[first_out + len(outs) :])

    return pl.pallas_call(
        body,
        out_shape=outs,
        in_specs=[spec(pltpu.VMEM)] * len(args) + [spec(pl.ANY)] * len(after),
        out_specs=tuple(spec(pltpu.VMEM) for _ in outs),
        scratch_shapes=list(scratch),
        compiler_params=pltpu.CompilerParams(
            vmem_limit_bytes=VMEM_LIMIT if 2 * held < VMEM_LIMIT else VMEM_ALL
        ),
        cost_estimate=pl.CostEstimate(flops=1, bytes_accessed=moved, transcendentals=0),
        name=name,
    )(*args, *after)


def slot_rows(ids, slots, rows, each):
    cell = jnp.where(slots < CAP, ids * each + slots, -1)
    return (iota((rows, cell.shape[1]), 0) == cell).astype(f32)


def place_kernel(x_ref, cot_ref, ids_ref, slots_ref, *refs, heads):
    w_parts = refs[:heads]
    sel_in, sel_up, place, place_c, x_c, cot_c, w_ref, place_s = refs[heads:]
    head = lax.axis_index("head")
    part = x_c.shape[0]
    slot_hot = slot_rows(ids_ref[...], slots_ref[...], sel_in.shape[0], SLOT)
    place_s[...] = jnp.transpose(slot_hot)
    slot_low = slot_hot.astype(bf16)
    sel_in[...] = dot(slot_low, x_ref[...]).astype(bf16)
    sel_up[...] = dot(slot_low, cot_ref[...]).astype(bf16)
    place[...] = place_s[...].astype(bf16)
    mine = pl.ds(pl.multiple_of(head * part, part), part)
    place_c[...] = place_s[mine, :].astype(bf16)
    x_c[...] = x_ref[mine, :]
    cot_c[...] = cot_ref[mine, :]
    inner = w_parts[0].shape[0]
    for d in range(heads):
        rows = pl.ds(pl.multiple_of((head ^ d) * inner, inner), inner)
        w_ref[rows, :] = w_parts[d][...]


def attend_kernel(*refs):
    given, refs = refs[:9], refs[9:]
    low_ref, prob_ref, att_ref, attt_ref, sel_ref = refs[:5]
    q_s, kt_s, v_s, bias_s, skew_s, slot_s, score_s = refs[5:12]
    here, sems = refs[12:21], refs[21]
    x_ref, gain_ref, wq_ref, wk_ref, wv_ref, table_ref, buckets_ref, ids_ref, slots_ref = here
    copies = [
        pltpu.make_async_copy(far, near, sems.at[i])
        for i, (far, near) in enumerate(zip(given, here))
    ]
    tokens = x_ref.shape[0]
    inner = wq_ref.shape[0]
    count = q_s.shape[0]
    width = inner // count
    span = skew_s.shape[2]
    tall = 2 * BLOCK
    for copy in copies:
        copy.start()
    for copy in copies[5:]:
        copy.wait()
    slot_s[...] = slot_rows(ids_ref[...], slots_ref[...], slot_s.shape[0], CAP).astype(bf16)
    offsets = buckets_ref.shape[1]
    bucket_hot = (iota((table_ref.shape[1], offsets), 0) == buckets_ref[...]).astype(f32)
    bias_s[...] = jnp.zeros_like(bias_s)
    bias_s[:count, :offsets] = jnp.dot(
        table_ref[...], bucket_hot, precision=highest, preferred_element_type=f32
    )
    for copy in copies[:2]:
        copy.wait()
    for i in range(0, tokens, 256):
        rows = pl.ds(i, 256)
        x = x_ref[rows, :].astype(f32)
        inverse = lax.rsqrt(jnp.mean(x * x, axis=-1, keepdims=True) + EPS)
        low_ref[rows, :] = (x * inverse * gain_ref[...]).astype(bf16)
    for copy in copies[2:5]:
        copy.wait()
    low = low_ref[...]
    q = dot_nt(low, wq_ref[...]).astype(bf16) * bf16(width ** (-0.5))
    kt_s[...] = dot_nt(wk_ref[...], low).astype(bf16)
    v = dot_nt(low, wv_ref[...]).astype(bf16)
    for h in range(count):
        cols = slice(h * width, (h + 1) * width)
        q_s[h] = q[:, cols]
        v_s[h] = v[:, cols]

    blocks = tokens // tall
    half = sel_ref.shape[0]

    def lay_bias(h):
        skew_s[h % 2] = pltpu.roll(
            jnp.broadcast_to(bias_s[h : h + 1, :], skew_s.shape[1:]),
            span - (BLOCK - 1), 1, stride=1, stride_axis=0,
        )

    def scores(h, n):
        score_s[n % 2] = dot(
            q_s[h, pl.ds(n * tall, tall), :], kt_s[h * width : (h + 1) * width, :]
        )

    def weights(h, n):
        for j in range(0, tall, ROWS):
            row = n * tall + j
            first = tokens - BLOCK - row // BLOCK * BLOCK
            bias = skew_s[h % 2, j % BLOCK : j % BLOCK + ROWS, first : first + tokens]
            score = score_s[n % 2, j : j + ROWS, :] + bias
            weight = jnp.exp(score - jnp.max(score, axis=-1, keepdims=True))
            total = jnp.sum(weight, axis=-1, keepdims=True)
            prob_ref[h, pl.ds(row, ROWS), :] = (weight * (1.0 / total)).astype(bf16)

    lay_bias(0)
    scores(0, 0)
    for h in range(count):
        for n in range(blocks):
            if n + 1 < blocks:
                scores(h, n + 1)
            elif h + 1 < count:
                lay_bias(h + 1)
                scores(h + 1, 0)
            weights(h, n)
        att = dot(prob_ref[h], v_s[h])
        att_low = att.astype(bf16)
        att_ref[h] = att_low
        attt_ref[h * width : (h + 1) * width, :] = jnp.transpose(att).astype(bf16)
        picked = dot(slot_s[...], att_low).astype(bf16)
        for part in range(2):
            start = part * inner + h * width
            sel_ref[:, start : start + width] = picked[part * half : (part + 1) * half]


def pass_kernel(given, passed):
    passed[...] = given[...]


def widen(rows, wide_s):
    wide_s[...] = jnp.zeros_like(wide_s)
    for e in range(rows.shape[0] // CAP):
        wide_s[e * SLOT : e * SLOT + CAP, :] = rows[e * CAP : (e + 1) * CAP]
    return wide_s[...]


def packed_width(width):
    return 2 * width + width // 2 + 128


def short_rows(width):
    each = width // 2
    for i in range(CAP - TALL):
        for k in range(4):
            yield TALL + i, slice(k * each, (k + 1) * each), 4 * i + k


def route_kernel(*refs, shards, heads):
    att_parts, w_ref = refs[:heads], refs[heads]
    (sel_in, sel_up, gain_ref, router_ref, att_t, hidden_ref, normed_ref, probs_ref, att_on
     ) = refs[heads + 1 : heads + 10]
    pieces = refs[heads + 10 : heads + 10 + shards]
    att_s, pay_s, wide_s, pack_s = refs[heads + 10 + shards :]
    head = lax.axis_index("head")
    half = att_parts[0].shape[0]
    inner = w_ref.shape[0] // heads
    for d in range(heads):
        att_s[d, 0:half, :] = att_parts[d][:, 0:inner]
        att_s[d, half : 2 * half, :] = att_parts[d][:, inner : 2 * inner]
    mixed = None
    for k in range(heads):
        term = dot(att_s[head ^ k], w_ref[k * inner : (k + 1) * inner, :])
        mixed = term if mixed is None else mixed + term
    hidden = sel_in[...].astype(f32) + widen(mixed, wide_s)
    hidden_ref[...] = hidden
    inverse = lax.rsqrt(jnp.mean(hidden * hidden, axis=-1, keepdims=True) + EPS)
    normed = hidden * inverse * gain_ref[...]
    normed_ref[...] = normed
    logits = dot_nt(normed, router_ref[...], highest)
    logits = logits - jnp.max(logits, axis=-1, keepdims=True)
    powers = jnp.exp(logits)
    probs = powers / jnp.sum(powers, axis=-1, keepdims=True)
    probs_ref[...] = probs
    gate = jnp.sum(jnp.where(chosen_of(probs.shape), probs, 0.0), axis=-1, keepdims=True)
    high = gate.astype(bf16).astype(f32)
    lane = iota((gate.shape[0], 128), 1)
    width = normed.shape[1]
    rest = gate - high
    first_gates = jnp.where(lane == 0, high, jnp.where(lane == 1, rest, 0.0))
    last_gates = jnp.where(lane == 2, high, jnp.where(lane == 3, rest, 0.0))
    pay_s[:, :width] = normed
    pay_s[:, width:] = sel_up[...].astype(f32)
    full, side = 2 * width, 2 * width + width // 2
    for e in range(shards):
        rows, packed = e * SLOT, e * TALL
        pack_s[packed : packed + TALL, :full] = pay_s[rows : rows + TALL, :]
        for row, lanes, to in short_rows(width):
            pack_s[packed + to : packed + to + 1, full:side] = pay_s[
                rows + row : rows + row + 1, lanes
            ]
        pack_s[packed : packed + 8, side:] = (
            first_gates[rows : rows + 8] + last_gates[rows + TALL : rows + SLOT]
        )
        pack_s[packed + 8 : packed + TALL, side:] = first_gates[rows + 8 : rows + TALL]
    shard = lax.axis_index("seq")
    for j in range(shards):
        first = pl.multiple_of((shard ^ j) * TALL, TALL)
        pieces[j][...] = pack_s[pl.ds(first, TALL), :].astype(bf16)
    att_on[...] = att_t[...]


def chosen_of(shape):
    expert = iota(shape, 1) * SLOT
    slot_row = iota(shape, 0)
    return (slot_row >= expert) & (slot_row < expert + SLOT)


def expert_kernel(*refs, shards, heads):
    parts = refs[:shards]
    w_in, w_out = refs[shards : shards + 2]
    chunks = refs[shards + 2 : shards + 2 + heads]
    x_ref, act_ref, pre_ref, out_ref, pay_s, gate_s, both_s = refs[shards + 2 + heads :]
    head = lax.axis_index("head")
    width = x_ref.shape[1]
    full, side = 2 * width, 2 * width + width // 2
    for j in range(shards):
        rows = j * SLOT
        part = parts[j][...].astype(f32)
        pay_s[rows : rows + TALL, :] = part[:, :full]
        pay_s[rows + TALL : rows + SLOT, :] = jnp.zeros((SLOT - TALL, full), f32)
        for row, lanes, place in short_rows(width):
            pay_s[rows + row : rows + row + 1, lanes] = part[place : place + 1, full:side]
        gate_s[rows : rows + TALL, :] = part[:, side : side + 1] + part[:, side + 1 : side + 2]
        gate_s[rows + TALL : rows + SLOT, :] = (
            part[:8, side + 2 : side + 3] + part[:8, side + 3 : side + 4]
        )
    x = pay_s[:, :width].astype(bf16)
    up = pay_s[:, width:]
    gate = gate_s[...]
    out_low = (gate * up).astype(bf16)
    pre = dot(x, w_in[...])
    cdf = 0.5 * (1.0 + lax.erf(pre * (0.5**0.5)))
    act = (pre * cdf).astype(bf16)
    slope = cdf + pre * jnp.exp(-0.5 * pre * pre) * ((2.0 * np.pi) ** (-0.5))
    pre_low = (dot_nt(out_low, w_out[...]) * slope).astype(bf16)
    both = (dot(act, w_out[...]), dot_nt(pre_low, w_in[...]))
    part = both_s.shape[2]
    for k in range(heads):
        start = k % (heads // 2) * part
        for j in range(shards):
            both_s[k, j * CAP : (j + 1) * CAP, :] = both[k // (heads // 2)][
                j * SLOT : j * SLOT + CAP, start : start + part
            ]
    for d in range(heads):
        chunks[d][...] = both_s[head ^ d].astype(bf16)
    pre_ref[...] = pre_low
    out_ref[...] = out_low
    x_ref[...] = x
    act_ref[...] = act


def expert_grad_kernel(x_ref, pre_ref, act_ref, out_ref, in_grad, out_grad):
    in_grad[0] = dot_tn(x_ref[...], pre_ref[...])
    out_grad[0] = dot_tn(act_ref[...], out_ref[...])


def sum_kernel(att_ref, *refs, heads):
    parts, att_on, pieces, sum_s = refs[:heads], refs[heads], refs[heads + 1 : -1], refs[-1]
    att_on[...] = att_ref[...]
    total = parts[0][...].astype(f32)
    for d in range(1, heads):
        total = total + parts[d][...].astype(f32)
    sum_s[...] = total
    for j, piece in enumerate(pieces):
        piece[...] = sum_s[j * CAP : (j + 1) * CAP, :].astype(bf16)


def join_kernel(*refs):
    parts, out_ref, sum_s = refs[:-2], refs[-2], refs[-1]
    for j, part in enumerate(parts):
        sum_s[j * CAP : (j + 1) * CAP, :] = part[...].astype(f32)
    out_ref[...] = sum_s[...].astype(bf16)


def prep_kernel(
    cot_ref, w_ref, wq_ref, wk_ref, wv_ref, low_ref, place_ref, attt_ref,
    gh_ref, stack_ref, k_ref, qt_ref, vt_ref, wout_ref, qsel_ref, ght_s, mcot_s,
):
    count, tokens, width = gh_ref.shape
    for i in range(0, tokens, 256):
        rows = pl.ds(i, 256)
        where = place_ref[rows, :].astype(f32)
        free = 1.0 - jnp.sum(where, axis=-1, keepdims=True)
        mcot_s[rows, :] = (cot_ref[rows, :].astype(f32) * free).astype(bf16)
        slots = jnp.transpose(where).astype(bf16)
        for h in range(count):
            stack_ref[h, width:, rows] = slots
    gh = dot_nt(mcot_s[...], w_ref[...]).astype(bf16)
    ght_s[...] = dot_nt(w_ref[...], mcot_s[...]).astype(bf16)
    k = dot_nt(low_ref[...], wk_ref[...]).astype(bf16)
    qt_ref[...] = dot_nt(wq_ref[...], low_ref[...]).astype(bf16) * bf16(width ** (-0.5))
    vt_ref[...] = dot_nt(wv_ref[...], low_ref[...]).astype(bf16)
    for h in range(count):
        cols = slice(h * width, (h + 1) * width)
        gh_ref[h] = gh[:, cols]
        k_ref[h] = k[:, cols]
        stack_ref[h, 0:width, :] = ght_s[cols, :]
    wout_ref[...] = dot(attt_ref[...], mcot_s[...])
    qsel_ref[...] = dot(qt_ref[...], place_ref[...]).astype(bf16)


def masked_back_kernel(
    gh_ref, stack_ref, k_ref, qt_ref, vt_ref, att_ref, prob_ref,
    dq_ref, dkt_ref, dvt_ref, offs_ref, psel_ref, acc_s, score_s, *, h,
):
    tokens, width = dq_ref.shape
    acc_s[...] = jnp.zeros_like(acc_s)
    cols = slice(h * width, (h + 1) * width)
    for i in range(0, tokens, 2 * BLOCK):
        rows = pl.ds(i, 2 * BLOCK)
        gh = gh_ref[h, rows, :]
        delta = jnp.sum(gh.astype(f32) * att_ref[h, rows, :].astype(f32), axis=-1, keepdims=True)
        grads = dot(gh, vt_ref[cols, :]) - delta
        for j in range(2):
            start = i + j * BLOCK
            first = tokens - BLOCK - start
            here = pl.ds(start, BLOCK)
            score = prob_ref[h, here, :].astype(f32) * grads[j * BLOCK : (j + 1) * BLOCK]
            acc_s[:, first : first + tokens] += score
            score_s[here, :] = score.astype(bf16)
    dq_ref[...] = dot(score_s[...], k_ref[h]) * (width ** (-0.5))
    dkt_ref[...] = dot(qt_ref[cols, :], score_s[...])
    both = dot(stack_ref[h], prob_ref[h])
    dvt_ref[...] = both[:width]
    psel_ref[...] = both[width:].astype(bf16)
    offs_ref[...] = diagonals(acc_s[...])


def diagonals(acc):
    span = acc.shape[1]
    rows = acc.shape[0] // 2
    while rows >= 8:
        acc = acc[:rows] + pltpu.roll(acc[rows:], span - rows, 1)
        rows //= 2
    total = acc[0:1]
    for r in range(1, 8):
        total = total + pltpu.roll(acc[r : r + 1], span - r, 1)
    return jnp.broadcast_to(pltpu.roll(total, BLOCK - 1, 1), (8, span))


def slot_back_kernel(*refs, heads):
    parts = refs[:heads]
    (up_ref, normed_ref, hidden_ref, probs_ref, router_ref, gain_ref, w_ref, att_ref,
     wout0_ref) = refs[heads : heads + 9]
    (dv_ref, comb_ref, small_ref, wout_ref, gh_ref, ght_ref, delta_ref, ret_s, wide_s
     ) = refs[heads + 9 :]
    head, shard = lax.axis_index("head"), lax.axis_index("seq")
    ret_s[...] = jnp.zeros_like(ret_s)
    for d in range(heads):
        part = parts[d][...].astype(f32)
        for j in range(part.shape[0] // CAP):
            first = pl.multiple_of((shard ^ j) * SLOT, SLOT)
            ret_s[head ^ d, pl.ds(first, CAP), :] = part[j * CAP : (j + 1) * CAP]
    back = [ret_s[k] for k in range(heads)]
    combined = jnp.concatenate(back[: heads // 2], axis=1)
    grad_buf = jnp.concatenate(back[heads // 2 :], axis=1)
    up = up_ref[...].astype(f32)
    hidden, normed, probs, gain = hidden_ref[...], normed_ref[...], probs_ref[...], gain_ref[...]
    chosen = chosen_of(probs.shape)
    gate = jnp.sum(jnp.where(chosen, probs, 0.0), axis=-1, keepdims=True)
    comb_ref[...] = gate * combined
    gate_grad = jnp.sum(up * combined, axis=-1, keepdims=True)
    marked = jnp.where(chosen, gate_grad, 0.0)
    logit_grad = probs * (marked - jnp.sum(marked * probs, axis=-1, keepdims=True))
    experts = probs.shape[1]
    grad = grad_buf + jnp.dot(
        logit_grad, router_ref[...], precision=highest, preferred_element_type=f32
    )
    inverse = lax.rsqrt(jnp.mean(hidden * hidden, axis=-1, keepdims=True) + EPS)
    scaled = grad * gain
    inner_sum = jnp.mean(scaled * hidden, axis=-1, keepdims=True)
    dv = inverse * scaled - hidden * (inverse * inverse * inverse * inner_sum)
    dv_ref[...] = dv
    small_ref[...] = jnp.zeros_like(small_ref)
    small_ref[0:1, :] = jnp.sum(grad * hidden * inverse, axis=0, keepdims=True)
    small_ref[8 : 8 + experts, :] = dot_tn(logit_grad, normed, highest)
    grad_low = (up + dv).astype(bf16)
    half = att_ref.shape[0]
    inner = w_ref.shape[0]
    att = jnp.concatenate(
        [att_ref[:, 0:inner].astype(f32), att_ref[:, inner : 2 * inner].astype(f32)], axis=0
    )
    att = widen(att, wide_s)
    wout_ref[...] = wout0_ref[...] + dot_tn(att.astype(bf16), grad_low)
    gh = dot_nt(grad_low, w_ref[...])
    gh_low = gh.astype(bf16)
    count = gh_ref.shape[0]
    each = inner // count
    ght_ref[...] = dot_nt(w_ref[...], grad_low).astype(bf16)
    for h in range(count):
        cols = slice(h * each, (h + 1) * each)
        gh_ref[h] = gh_low[:, cols]
        delta_ref[h] = jnp.sum(
            gh_low[:, cols].astype(f32) * att[:, cols], axis=-1, keepdims=True
        )


def sparse_back_kernel(
    gh_ref, ght_ref, delta_ref, vt_ref, k_ref, qsel_ref,
    place_ref, wq_ref, wk_ref, wv_ref, low_ref, gain_ref, small_ref, wout_ref, *refs, heads,
):
    per_head, refs = refs[: 4 * gh_ref.shape[0]], refs[4 * gh_ref.shape[0] :]
    psels, dq0s, dkt0s, dvt0s = (per_head[i :: 4] for i in range(4))
    chunks = refs[:5]
    (score_ref, send_ref, keep_ref, out_ref,
     dq_s, q_low, k_low, v_low, kt_s, vt_s, all_s) = refs[5:]
    head = lax.axis_index("head")
    count, rows, width = gh_ref.shape
    tokens = vt_ref.shape[1]
    inner = count * width
    for h in range(count):
        cols = slice(h * width, (h + 1) * width)
        grad = dot(gh_ref[h], vt_ref[cols, :])
        prob = psels[h][...]
        score = (prob.astype(f32) * (grad - delta_ref[h])).astype(bf16)
        score_ref[h] = score
        dq_s[:, cols] = dot(score, k_ref[h]) * (width ** (-0.5))
        dkt = dkt0s[h][...] + dot(qsel_ref[cols, :], score)
        dvt = dvt0s[h][...] + dot(ght_ref[cols, :], prob)
        kt_s[cols, :] = dkt.astype(bf16)
        vt_s[cols, :] = dvt.astype(bf16)
        k_low[:, cols] = jnp.transpose(dkt).astype(bf16)
        v_low[:, cols] = jnp.transpose(dvt).astype(bf16)
    spread = dot(place_ref[...], dq_s[...].astype(bf16))
    for h in range(count):
        cols = slice(h * width, (h + 1) * width)
        q_low[:, cols] = (spread[:, cols] + dq0s[h][...]).astype(bf16)
    part = tokens // heads
    half = part // 2
    own, to_1, to_2, rest_1, rest_2 = chunks
    to_1[part:, :] = jnp.zeros((EXTRA, to_1.shape[1]), bf16)
    places = (
        ((own, 0), (own, half)),
        ((to_1, 0), (rest_1, 0)),
        ((rest_2, 0), (to_2, 0)),
        ((to_1, half), (to_2, half)),
    )
    for d in range(heads):
        mine = pl.ds(pl.multiple_of((head ^ d) * part, part), part)
        rows_part = (
            dot(q_low[mine, :], wq_ref[...])
            + dot(k_low[mine, :], wk_ref[...])
            + dot(v_low[mine, :], wv_ref[...])
        ).astype(bf16)
        for n, (ref, first) in enumerate(places[d]):
            ref[first : first + half, :] = rows_part[n * half : (n + 1) * half]
    low = low_ref[...]
    total = None
    grads = (dot_tn(q_low[...], low), dot(kt_s[...], low), dot(vt_s[...], low))
    for i, (grad, w) in enumerate(zip(grads, (wq_ref, wk_ref, wv_ref))):
        all_s[i * inner : (i + 1) * inner, :] = grad
        term = jnp.sum(grad * w[...].astype(f32), axis=0, keepdims=True)
        total = term if total is None else total + term
    all_s[3 * inner :, :] = wout_ref[...]
    out_ref[...] = small_ref[...]
    out_ref[1:2, :] = total / gain_ref[...]
    to_1[part : part + 1, :] = (total / gain_ref[...]).astype(bf16)
    split_rows(all_s, 1, send_ref, keep_ref)


def is_upper(bit):
    return (lax.axis_index("seq") & bit) != 0


def split_rows(all_s, bit, send_ref, keep_ref):
    half = send_ref.shape[0]
    low, high = all_s[0:half, :], all_s[half : 2 * half, :]
    keep_ref[...] = jnp.where(is_upper(bit), high, low)
    send_ref[...] = jnp.where(is_upper(bit), low, high).astype(bf16)


def halve_kernel(keep_ref, got_ref, *refs, bit):
    send_ref, out_ref, all_s = refs[-3:]
    if len(refs) > 3:
        rest_1, got_1, rest_2, got_2, small_ref, next_1, next_2 = refs[:-3]
        half = rest_1.shape[0]
        for rest, got, onward in ((rest_1, got_2, next_1), (rest_2, got_1, next_2)):
            got_rest = got[half : 2 * half, :].astype(f32)
            onward[0:half, :] = (rest[...].astype(f32) + got_rest).astype(bf16)
        mine = small_ref[1:2, :].astype(bf16).astype(f32)
        next_2[half:, :] = jnp.zeros((EXTRA, next_2.shape[1]), bf16)
        next_2[half : half + 1, :] = (mine + got_1[2 * half : 2 * half + 1, :].astype(f32)).astype(bf16)
    all_s[...] = keep_ref[...] + got_ref[...].astype(f32)
    split_rows(all_s, bit, send_ref, out_ref)


def join_rows(mine_ref, got_ref, all_s, bit, count):
    mine, got = mine_ref[...].astype(f32), got_ref[...].astype(f32)
    all_s[0:count, :] = jnp.where(is_upper(bit), got[:count], mine[:count])
    all_s[count : 2 * count, :] = jnp.where(is_upper(bit), mine[:count], got[:count])
    all_s[2 * count :, :] = mine[count:] + got[count:]


def pair_kernel(mine_ref, got_ref, *refs, bit, count):
    out_ref, all_s = refs[-2:]
    if len(refs) > 2:
        got_1, got_2, next_1, next_2 = refs[:-2]
        half = next_1.shape[0]
        next_2[...] = got_1[0:half, :]
        next_1[...] = got_2[half:, :]
    join_rows(mine_ref, got_ref, all_s, bit, count)
    out_ref[...] = all_s[...].astype(bf16)


def final_kernel(mine_ref, got_ref, *refs, bit, count):
    gain1_ref, gain2_ref, table_ref, router_ref, all_s = refs[-5:]
    outs = refs[:-5]
    join_rows(mine_ref, got_ref, all_s, bit, count)
    inner = outs[0].shape[0]
    for i, out in enumerate(outs):
        out[...] = all_s[i * inner : (i + 1) * inner, :]
    small = all_s[2 * count :, :]
    gain1_ref[...] = small[1, :]
    gain2_ref[...] = small[0, :]
    heads, buckets = table_ref.shape
    table_ref[...] = small[2 : 2 + heads, :buckets]
    router_ref[...] = small[8 : 8 + router_ref.shape[0], :]


def bias_grad_kernel(
    score_ref, place_ref, buckets_ref, small_ref, *refs, bucket_count
):
    count = score_ref.shape[0]
    offs, out_ref, acc_s, sums_s = refs[:count], *refs[count:]
    tokens = place_ref.shape[0]
    offsets = buckets_ref.shape[1]
    out_ref[...] = small_ref[...]
    bucket_hot = (iota((bucket_count, offsets), 0) == buckets_ref[...]).astype(f32)

    def one_head(h, carry):
        acc_s[...] = jnp.zeros_like(acc_s)
        for i in range(0, tokens, BLOCK):
            first = tokens - BLOCK - i
            acc_s[:, first : first + tokens] += dot(place_ref[i : i + BLOCK, :], score_ref[h])
        sums_s[h] = diagonals(acc_s[...])
        return carry

    lax.fori_loop(0, count, one_head, 0)
    for h in range(count):
        sums = sums_s[h] + offs[h][...]
        out_ref[2 + h : 3 + h, :bucket_count] = dot_nt(sums[:, :offsets], bucket_hot, highest)[0:1]


def hidden_kernel(*refs, heads):
    att_parts, w_ref, x_ref, out_ref, att_s = refs[:heads], *refs[heads:]
    head = lax.axis_index("head")
    tokens = x_ref.shape[0]
    inner = att_parts[0].shape[0]
    for d in range(heads):
        mine = pl.ds(pl.multiple_of((head ^ d) * inner, inner), inner)
        att_s[mine, :] = att_parts[d][...]

    def block(i, carry):
        rows = pl.ds(pl.multiple_of(i * 256, 256), 256)
        out_ref[rows, :] = x_ref[rows, :].astype(f32) + dot_tn(att_s[:, rows], w_ref[...])
        return carry

    lax.fori_loop(0, tokens // 256, block, 0)


def output_kernel(hidden_ref, place_ref, comb_ref, out_ref):
    high, rest = split_two(comb_ref[...])

    def block(i, carry):
        rows = pl.ds(pl.multiple_of(i * 256, 256), 256)
        where = place_ref[rows, :]
        out_ref[rows, :] = hidden_ref[rows, :] + (dot(where, high) + dot(where, rest))
        return carry

    lax.fori_loop(0, hidden_ref.shape[0] // 256, block, 0)


def first_norm_kernel(
    own, got_1, got_2, last_1, last_2, next_2, small_ref,
    x_ref, cot_ref, place_ref, dv_ref, gain_ref, keep_ref, got_ref, out_ref, sum_ref,
):
    half = last_1.shape[0]
    high, rest = split_two(dv_ref[...])
    for first, near, far in ((0, got_1, last_2), (half, got_2, last_1)):
        rows = pl.ds(first, half)
        grad = own[rows, :].astype(f32) + near[0:half, :].astype(f32)
        grad = grad + far[0:half, :].astype(f32)
        x = x_ref[rows, :].astype(f32)
        inverse = lax.rsqrt(jnp.mean(x * x, axis=-1, keepdims=True) + EPS)
        scaled = grad * gain_ref[...]
        inner_sum = jnp.mean(scaled * x, axis=-1, keepdims=True)
        where = place_ref[rows, :]
        hidden_grad = cot_ref[rows, :].astype(f32) + (dot(where, high) + dot(where, rest))
        out_ref[rows, :] = (
            hidden_grad + inverse * scaled - x * (inverse * inverse * inverse * inner_sum)
        ).astype(bf16)
    count = keep_ref.shape[0]
    sum_ref[0:count, :] = (keep_ref[...] + got_ref[...].astype(f32)).astype(bf16)
    gain1 = next_2[half:, :].astype(f32)[0:1] + last_2[half:, :].astype(f32)[0:1]
    small = small_ref[...]
    sum_ref[count:, :] = jnp.where(iota(small.shape, 0) == 1, gain1, small).astype(bf16)


def spread_near_kernel(own, got_1, got_2, out_ref, token, wide_s, sems):
    head = lax.axis_index("head")
    part = own.shape[0]
    copies = []
    for d, piece in enumerate((own, got_1, got_2)):
        wide_s[d] = piece[...].astype(f32)
        mine = pl.ds(pl.multiple_of((head ^ d) * part, part), part)
        copies.append(pltpu.make_async_copy(wide_s.at[d], out_ref.at[mine], sems.at[d]))
        copies[-1].start()
    token[...] = jnp.zeros_like(token)
    for copy in copies:
        copy.wait()


def spread_far_kernel(last_1, last_2, given, out_ref, wide_s, sem):
    head = lax.axis_index("head")
    half = last_1.shape[0]
    wide_s[0:half, :] = last_2[...].astype(f32)
    wide_s[half:, :] = last_1[...].astype(f32)
    mine = pl.ds(pl.multiple_of((head ^ 3) * 2 * half, 2 * half), 2 * half)
    copy = pltpu.make_async_copy(wide_s, out_ref.at[mine], sem)
    copy.start()
    copy.wait()


def swap(x, axis, d):
    size = lax.axis_size(axis)
    return lax.ppermute(x, axis, [(i, i ^ d) for i in range(size)])


def share(x, axis):
    return [x] + [swap(x, axis, d) for d in range(1, lax.axis_size(axis))]


def trade(pieces, axis):
    return lax.all_to_all(pieces, axis, split_axis=0, concat_axis=0, tiled=True)


def swap_all(pieces, axis):
    return [pieces[0]] + [swap(pieces[d], axis, d) for d in range(1, len(pieces))]


def bits_of(axis):
    return [b for b in (1 << i for i in range(16)) if b < lax.axis_size(axis)]


def halve(send, keep, bit, after, onward=()):
    rows, width = keep.shape
    outs = []
    if onward:
        half = onward[0].shape[0]
        outs = [shape_of(half, width, bf16), shape_of(half + EXTRA, width, bf16)]
    return call(
        partial(halve_kernel, bit=bit),
        outs + [shape_of(rows // 2, width, bf16), shape_of(rows // 2, width, f32)],
        (keep, swap(send, "seq", bit // 2)) + tuple(onward),
        scratch=[pltpu.VMEM((rows, width), f32)],
        name="halve",
        after=after,
        token=True,
    )


def pair(now, small_rows, bit, after, onward=()):
    rows, width = now.shape
    count = rows - small_rows
    outs = [shape_of(onward[0].shape[0] // 2, width, bf16)] * 2 if onward else []
    return call(
        partial(pair_kernel, bit=bit, count=count),
        outs + [shape_of(rows + count, width, bf16)],
        (now, swap(now, "seq", bit)) + tuple(onward),
        scratch=[pltpu.VMEM((rows + count, width), f32)],
        name="pair",
        after=after,
        token=True,
    )


def on_device(
    layer_input, cotangent, norm1_gain, w_query, w_key, w_value, w_attn_out, bias_table,
    norm2_gain, w_router, w_expert_in, w_expert_out, expert_ids, slot_ids, buckets,
):
    tokens, width = layer_input.shape
    shards = lax.axis_size("seq")
    heads = lax.axis_size("head")
    bucket_count, count = bias_table.shape
    inner = w_query.shape[1]
    each = inner // count
    experts = w_router.shape[1]
    rows, filled = experts * SLOT, experts * CAP
    hidden_units = w_expert_in.shape[2]
    part = tokens // heads
    split = 2 * width // heads
    span = 2 * tokens
    params = pltpu.CompilerParams(vmem_limit_bytes=VMEM_LIMIT if rows <= 256 else VMEM_ALL)

    ids = expert_ids.reshape(1, tokens)
    slots = slot_ids.reshape(1, tokens)
    bucket_row = buckets.reshape(1, -1)
    wq_t, wk_t, wv_t = jnp.transpose(w_query), jnp.transpose(w_key), jnp.transpose(w_value)
    router_t, table_t = jnp.transpose(w_router), jnp.transpose(bias_table)
    w_in = w_expert_in.reshape(width, hidden_units)
    w_out = w_expert_out.reshape(hidden_units, width)

    w_mix = share(w_attn_out, "head")

    low, prob, att, att_t, att_sel = pl.pallas_call(
        attend_kernel,
        out_shape=(
            shape_of(tokens, width, bf16),
            jax.ShapeDtypeStruct((count, tokens, tokens), bf16),
            jax.ShapeDtypeStruct((count, tokens, each), bf16),
            shape_of(inner, tokens, bf16),
            shape_of(filled // 2, 2 * inner, bf16),
        ),
        in_specs=[spec(pltpu.HBM)] * 9,
        out_specs=(spec(pltpu.VMEM),) * 5,
        scratch_shapes=[
            pltpu.VMEM((count, tokens, each), bf16),
            pltpu.VMEM((inner, tokens), bf16),
            pltpu.VMEM((count, tokens, each), bf16),
            pltpu.VMEM((8, span), f32),
            pltpu.VMEM((2, BLOCK, span), f32),
            pltpu.VMEM((filled, tokens), bf16),
            pltpu.VMEM((2, 2 * BLOCK, tokens), f32),
            pltpu.VMEM((tokens, width), bf16),
            pltpu.VMEM((width,), f32),
            pltpu.VMEM((inner, width), bf16),
            pltpu.VMEM((inner, width), bf16),
            pltpu.VMEM((inner, width), bf16),
            pltpu.VMEM((count, bucket_count), f32),
            pltpu.VMEM((1, span - 1), jnp.int32),
            pltpu.VMEM((1, tokens), jnp.int32),
            pltpu.VMEM((1, tokens), jnp.int32),
            pltpu.SemaphoreType.DMA((9,)),
        ],
        compiler_params=params,
        cost_estimate=NO_COST,
        name="attend",
    )(
        *(
            pltpu.with_memory_space_constraint(a, pltpu.HBM)
            for a in (layer_input, norm1_gain, wq_t, wk_t, wv_t, table_t, bucket_row, ids, slots)
        )
    )

    (att_sel,) = call(
        pass_kernel,
        [shape_of(filled // 2, 2 * inner, bf16)],
        (att_sel,),
        name="pass",
        after=(w_mix[1],),
    )
    sel_parts = share(att_sel, "head")
    sel_in, sel_up, place, place_c, x_c, cot_c, w_full = call(
        partial(place_kernel, heads=heads),
        [
            shape_of(rows, width, bf16),
            shape_of(rows, width, bf16),
            shape_of(tokens, rows, bf16),
            shape_of(part, rows, bf16),
            shape_of(part, width, bf16),
            shape_of(part, width, bf16),
            shape_of(heads * inner, width, bf16),
        ],
        (layer_input, cotangent, ids, slots) + tuple(w_mix),
        scratch=[pltpu.VMEM((tokens, rows), f32)],
        moved=12 * 2**20,
        name="place",
        after=(att_sel,),
    )
    routed = call(
        partial(route_kernel, shards=shards, heads=heads),
        [
            shape_of(rows, width, f32),
            shape_of(rows, width, f32),
            shape_of(rows, experts, f32),
            shape_of(inner, tokens, bf16),
        ]
        + [shape_of(TALL, packed_width(width), bf16)] * shards,
        tuple(sel_parts) + (w_full, sel_in, sel_up, norm2_gain, router_t, att_t),
        scratch=[
            pltpu.VMEM((heads, filled, inner), bf16),
            pltpu.VMEM((rows, 2 * width), f32),
            pltpu.VMEM((rows, width), f32),
            pltpu.VMEM((shards * TALL, packed_width(width)), f32),
        ],
        name="route",
    )
    hidden_sel, normed_sel, probs, att_on = routed[:4]
    pay_parts = swap_all(routed[4:], "seq")
    att_parts = [att_t] + [swap(att_on, "head", d) for d in range(1, heads - 1)]

    def masked_back(h, after):
        return call(
            partial(masked_back_kernel, h=h),
            [
                shape_of(tokens, each, f32),
                shape_of(each, tokens, f32),
                shape_of(each, tokens, f32),
                shape_of(8, span, f32),
                shape_of(rows, tokens, bf16),
            ],
            (gh, stack, k_rows, q_t, v_t, att, prob),
            scratch=[pltpu.VMEM((BLOCK, span), f32), pltpu.VMEM((tokens, tokens), bf16)],
            name="masked_back",
            after=after,
            moved=11 * 2**20,
            token=True,
        )

    done = call(
        partial(expert_kernel, shards=shards, heads=heads),
        [shape_of(filled, split, bf16)] * heads
        + [
            shape_of(rows, width, bf16),
            shape_of(rows, hidden_units, bf16),
            shape_of(rows, hidden_units, bf16),
            shape_of(rows, width, bf16),
        ],
        tuple(pay_parts) + (w_in, w_out),
        scratch=[
            pltpu.VMEM((rows, 2 * width), f32),
            pltpu.VMEM((rows, 1), f32),
            pltpu.VMEM((heads, filled, split), f32),
        ],
        name="expert",
        after=tuple(att_parts[1:]),
        token=True,
    )
    x_rows, act, pre_low, out_low, token = done[heads:]
    gh, stack, k_rows, q_t, v_t, wout0, q_sel, token = call(
        prep_kernel,
        [
            jax.ShapeDtypeStruct((count, tokens, each), bf16),
            jax.ShapeDtypeStruct((count, each + rows, tokens), bf16),
            jax.ShapeDtypeStruct((count, tokens, each), bf16),
            shape_of(inner, tokens, bf16),
            shape_of(inner, tokens, bf16),
            shape_of(inner, width, f32),
            shape_of(inner, rows, bf16),
        ],
        (cotangent, w_attn_out, wq_t, wk_t, wv_t, low, place, att_t),
        scratch=[pltpu.VMEM((inner, tokens), bf16), pltpu.VMEM((tokens, width), bf16)],
        name="prep",
        after=(token,),
        moved=8 * 2**20,
        token=True,
    )

    masked = []
    for h in range(count - 2):
        masked.append(masked_back(h, (token,)))
        token = masked[-1][-1]
    returned = call(
        partial(sum_kernel, heads=heads),
        [shape_of(inner, tokens, bf16)] + [shape_of(CAP, split, bf16)] * shards,
        [att_t] + swap_all(done[:heads], "head"),
        scratch=[pltpu.VMEM((filled, split), f32)],
        name="sum",
        after=(token,),
        token=True,
    )
    masked.append(masked_back(count - 2, (returned[-1],)))
    att_parts.append(swap(returned[0], "head", heads - 1))
    joined, token = call(
        join_kernel,
        [shape_of(filled, split, bf16)],
        swap_all(returned[1:-1], "seq"),
        scratch=[pltpu.VMEM((filled, split), f32)],
        name="join",
        after=(masked[-1][-1], att_parts[-1]),
        token=True,
    )
    masked.append(masked_back(count - 1, (token,)))
    full_parts = share(joined, "head")

    small_rows = 8 + -(-experts // 8) * 8
    dv_sel, comb_sel, small, wout_part, gh_sel, ght_sel, delta_sel = call(
        partial(slot_back_kernel, heads=heads),
        [
            shape_of(rows, width, f32),
            shape_of(rows, width, f32),
            shape_of(small_rows, width, f32),
            shape_of(inner, width, f32),
            jax.ShapeDtypeStruct((count, rows, each), bf16),
            shape_of(inner, rows, bf16),
            jax.ShapeDtypeStruct((count, rows, 1), f32),
        ],
        tuple(full_parts)
        + (sel_up, normed_sel, hidden_sel, probs, router_t, norm2_gain)
        + (w_attn_out, att_sel, wout0),
        scratch=[pltpu.VMEM((heads, rows, split), f32), pltpu.VMEM((rows, inner), f32)],
        name="slot_back",
        after=(masked[-1][-1],),
    )

    back = call(
        partial(sparse_back_kernel, heads=heads),
        [shape_of(part, width, bf16), shape_of(part + EXTRA, width, bf16)]
        + [shape_of(part, width, bf16)]
        + [shape_of(part // 2, width, bf16)] * 2
        + [
            jax.ShapeDtypeStruct((count, rows, tokens), bf16),
            shape_of(2 * inner, width, bf16),
            shape_of(2 * inner, width, f32),
            shape_of(small_rows, width, f32),
        ],
        (gh_sel, ght_sel, delta_sel, v_t, k_rows, q_sel, place)
        + (wq_t, wk_t, wv_t, low, norm1_gain, small, wout_part)
        + tuple(a for m in masked for a in (m[4], m[0], m[1], m[2])),
        scratch=[
            pltpu.VMEM((rows, inner), f32),
            pltpu.VMEM((tokens, inner), bf16),
            pltpu.VMEM((tokens, inner), bf16),
            pltpu.VMEM((tokens, inner), bf16),
            pltpu.VMEM((inner, tokens), bf16),
            pltpu.VMEM((inner, tokens), bf16),
            pltpu.VMEM((4 * inner, width), f32),
        ],
        name="sparse_back",
    )
    score_sel, send, keep, small = back[5:]
    own, to_1, to_2, rest_1, rest_2 = back[:5]
    got_1, got_2 = swap(to_1, "head", 1), swap(to_2, "head", 2)

    bits = bits_of("seq")
    send, keep, token = halve(send, keep, bits[1], ())
    small_part = small
    small, token = call(
        partial(bias_grad_kernel, bucket_count=bucket_count),
        [shape_of(small_rows, width, f32)],
        (score_sel, place, bucket_row, small) + tuple(m[3] for m in masked),
        scratch=[pltpu.VMEM((BLOCK, span), f32), pltpu.VMEM((count, 8, span), f32)],
        name="bias_grad",
        after=(token,),
        moved=16 * 2**20,
        token=True,
    )
    next_1, next_2, send, keep, token = halve(
        send, keep, bits[2], (token,), (rest_1, got_1, rest_2, got_2, small_part)
    )
    last_1, last_2 = swap(next_1, "head", 1), swap(next_2, "head", 2)
    w_in_grad, w_out_grad, token = call(
        expert_grad_kernel,
        [
            jax.ShapeDtypeStruct(w_expert_in.shape, f32),
            jax.ShapeDtypeStruct(w_expert_out.shape, f32),
        ],
        (x_rows, pre_low, act, out_low),
        name="expert_grad",
        after=(token,),
        moved=10 * 2**20,
        token=True,
    )
    hidden, token = call(
        partial(hidden_kernel, heads=heads),
        [shape_of(tokens, width, f32)],
        tuple(att_parts) + (w_full, layer_input),
        scratch=[pltpu.VMEM((heads * inner, tokens), bf16)],
        name="hidden",
        after=(token,),
        moved=6 * 2**20,
        token=True,
    )
    for bit in bits[3:]:
        send, keep, token = halve(send, keep, bit, (token,))

    grad_part, weights, token = call(
        first_norm_kernel,
        [shape_of(part, width, bf16), shape_of(keep.shape[0] + small_rows, width, bf16)],
        (own, got_1, got_2, last_1, last_2, next_2, small)
        + (x_c, cot_c, place_c, dv_sel, norm1_gain)
        + (keep, swap(send, "seq", bits[-1])),
        name="first_norm",
        after=(token,),
        token=True,
    )
    grad_1, grad_2 = swap(grad_part, "head", 1), swap(grad_part, "head", 2)
    layer_output, token = call(
        output_kernel,
        [shape_of(tokens, width, f32)],
        (hidden, place, comb_sel),
        name="output",
        after=(token,),
        moved=10 * 2**20,
        token=True,
    )
    for bit in reversed(bits[3:]):
        weights, token = pair(weights, small_rows, bit, (token,))
    next_1, next_2, weights, token = pair(
        weights, small_rows, bits[2], (token,), (grad_1, grad_2)
    )
    grad_3 = (swap(next_1, "head", 1), swap(next_2, "head", 2))
    near, token = pl.pallas_call(
        spread_near_kernel,
        out_shape=(shape_of(tokens, width, f32), shape_of(8, 128, f32)),
        in_specs=[spec(pltpu.VMEM)] * 3,
        out_specs=(spec(pltpu.HBM), spec(pltpu.VMEM)),
        scratch_shapes=[pltpu.VMEM((3, part, width), f32), pltpu.SemaphoreType.DMA((3,))],
        compiler_params=params,
        cost_estimate=pl.CostEstimate(flops=1, bytes_accessed=5 * 2**20, transcendentals=0),
        name="spread_near",
    )(grad_part, grad_1, grad_2)
    weights, token = pair(weights, small_rows, bits[1], grad_3 + (token,))
    last = call(
        partial(final_kernel, bit=bits[0], count=2 * inner),
        [shape_of(inner, width, f32)] * 4
        + [
            jax.ShapeDtypeStruct((width,), f32),
            jax.ShapeDtypeStruct((width,), f32),
            shape_of(count, bucket_count, f32),
            shape_of(experts, width, f32),
        ],
        (weights, swap(weights, "seq", bits[0])),
        scratch=[pltpu.VMEM((4 * inner + small_rows, width), f32)],
        name="weights_out",
    )
    weight_sums = last[:4]
    gain1_sum, gain2_sum, table_sum, router_sum = last[4:]
    input_grad = pl.pallas_call(
        spread_far_kernel,
        out_shape=shape_of(tokens, width, f32),
        in_specs=[spec(pltpu.VMEM), spec(pltpu.VMEM), spec(pltpu.HBM)],
        out_specs=spec(pltpu.HBM),
        scratch_shapes=[pltpu.VMEM((part, width), f32), pltpu.SemaphoreType.DMA(())],
        input_output_aliases={2: 0},
        compiler_params=params,
        cost_estimate=NO_COST,
        name="spread_far",
    )(*grad_3, near)

    return (
        layer_output,
        input_grad,
        gain1_sum,
        jnp.transpose(weight_sums[0]),
        jnp.transpose(weight_sums[1]),
        jnp.transpose(weight_sums[2]),
        weight_sums[3],
        jnp.transpose(table_sum),
        gain2_sum,
        jnp.transpose(router_sum),
        w_in_grad,
        w_out_grad,
    )


def solution(mesh):
    return jax.shard_map(
        on_device,
        mesh=mesh,
        in_specs=(
            P("seq", None),
            P("seq", None),
            P(),
            P(None, "head"),
            P(None, "head"),
            P(None, "head"),
            P("head", None),
            P(None, "head"),
            P(),
            P(),
            P("seq", None, "head"),
            P("seq", "head", None),
            P("seq"),
            P("seq"),
            P(),
        ),
        out_specs=(
            P("seq", None),
            P("seq", None),
            P(),
            P(None, "head"),
            P(None, "head"),
            P(None, "head"),
            P("head", None),
            P(None, "head"),
            P(),
            P(),
            P("seq", None, "head"),
            P("seq", "head", None),
        ),
        check_vma=False,
    )
```

```python
from functools import partial

import jax
import jax.numpy as jnp
import numpy as np
from jax import lax
from jax.experimental import pallas as pl
from jax.experimental.pallas import tpu as pltpu
from jax.sharding import PartitionSpec as P

CAP = 20
SLOT = 24
EPS = 1e-06
BLOCK = 128
ROWS = 32
EXTRA = 16
TALL = 16
VMEM_LIMIT = 26 * 1024 * 1024
VMEM_ALL = 60 * 1024 * 1024
NO_COST = pl.CostEstimate(flops=1, bytes_accessed=1, transcendentals=0)

f32 = jnp.float32
bf16 = jnp.bfloat16
highest = lax.Precision.HIGHEST


def dot(a, b):
    return jnp.dot(a, b, preferred_element_type=f32)


def dot_nt(a, b, precision=None):
    return lax.dot_general(
        a, b, (((1,), (1,)), ((), ())), precision=precision, preferred_element_type=f32
    )


def dot_tn(a, b, precision=None):
    return lax.dot_general(
        a, b, (((0,), (0,)), ((), ())), precision=precision, preferred_element_type=f32
    )


def iota(shape, dim):
    return lax.broadcasted_iota(jnp.int32, shape, dim)


def split_two(v):
    high = v.astype(bf16)
    return high, (v - high.astype(f32)).astype(bf16)


def shape_of(rows, cols, dtype):
    return jax.ShapeDtypeStruct((rows, cols), dtype)


def spec(memory):
    return pl.BlockSpec(memory_space=memory)


def call(kernel, outs, args, scratch=(), name=None, after=(), moved=1, token=False):
    outs, args = tuple(outs), tuple(args)
    held = sum(int(np.prod(a.shape)) * np.dtype(a.dtype).itemsize for a in args + outs)
    if token:
        outs += (shape_of(8, 128, f32),)
    first_out = len(args) + len(after)

    def body(*refs):
        results = refs[first_out : first_out + len(outs)]
        if token:
            results[-1][...] = jnp.zeros((8, 128), f32)
            results = results[:-1]
        kernel(*refs[: len(args)], *results, *refs[first_out + len(outs) :])

    return pl.pallas_call(
        body,
        out_shape=outs,
        in_specs=[spec(pltpu.VMEM)] * len(args) + [spec(pl.ANY)] * len(after),
        out_specs=tuple(spec(pltpu.VMEM) for _ in outs),
        scratch_shapes=list(scratch),
        compiler_params=pltpu.CompilerParams(
            vmem_limit_bytes=VMEM_LIMIT if 2 * held < VMEM_LIMIT else VMEM_ALL
        ),
        cost_estimate=pl.CostEstimate(flops=1, bytes_accessed=moved, transcendentals=0),
        name=name,
    )(*args, *after)


def slot_rows(ids, slots, rows, each):
    cell = jnp.where(slots < CAP, ids * each + slots, -1)
    return (iota((rows, cell.shape[1]), 0) == cell).astype(f32)


def place_kernel(x_ref, cot_ref, ids_ref, slots_ref, *refs, heads):
    w_parts = refs[:heads]
    sel_in, sel_up, place, place_c, x_c, cot_c, w_ref, place_s = refs[heads:]
    head = lax.axis_index("head")
    part = x_c.shape[0]
    slot_hot = slot_rows(ids_ref[...], slots_ref[...], sel_in.shape[0], SLOT)
    place_s[...] = jnp.transpose(slot_hot)
    slot_low = slot_hot.astype(bf16)
    sel_in[...] = dot(slot_low, x_ref[...]).astype(bf16)
    sel_up[...] = dot(slot_low, cot_ref[...]).astype(bf16)
    place[...] = place_s[...].astype(bf16)
    mine = pl.ds(pl.multiple_of(head * part, part), part)
    place_c[...] = place_s[mine, :].astype(bf16)
    x_c[...] = x_ref[mine, :]
    cot_c[...] = cot_ref[mine, :]
    inner = w_parts[0].shape[0]
    for d in range(heads):
        rows = pl.ds(pl.multiple_of((head ^ d) * inner, inner), inner)
        w_ref[rows, :] = w_parts[d][...]


def attend_kernel(*refs):
    given, refs = refs[:9], refs[9:]
    low_ref, prob_ref, att_ref, attt_ref, sel_ref = refs[:5]
    q_s, kt_s, v_s, bias_s, skew_s, slot_s, score_s = refs[5:12]
    here, sems = refs[12:21], refs[21]
    x_ref, gain_ref, wq_ref, wk_ref, wv_ref, table_ref, buckets_ref, ids_ref, slots_ref = here
    tokens = x_ref.shape[0]
    copies = [
        pltpu.make_async_copy(far, near, sems.at[i])
        for i, (far, near) in enumerate(zip(given, here))
        if i > 0
    ]
    x_copies = [
        pltpu.make_async_copy(
            given[0].at[pl.ds(i * 256, 256)], x_ref.at[pl.ds(i * 256, 256)], sems.at[9 + i]
        )
        for i in range(tokens // 256)
    ]
    inner = wq_ref.shape[0]
    count = q_s.shape[0]
    width = inner // count
    span = skew_s.shape[2]
    tall = 2 * BLOCK
    for copy in x_copies + copies:
        copy.start()
    for copy in copies[4:]:
        copy.wait()
    slot_s[...] = slot_rows(ids_ref[...], slots_ref[...], slot_s.shape[0], CAP).astype(bf16)
    offsets = buckets_ref.shape[1]
    bucket_hot = (iota((table_ref.shape[1], offsets), 0) == buckets_ref[...]).astype(f32)
    bias_s[...] = jnp.zeros_like(bias_s)
    bias_s[:count, :offsets] = jnp.dot(
        table_ref[...], bucket_hot, precision=highest, preferred_element_type=f32
    )
    copies[0].wait()
    for i in range(0, tokens, 256):
        rows = pl.ds(i, 256)
        x_copies[i // 256].wait()
        x = x_ref[rows, :].astype(f32)
        inverse = lax.rsqrt(jnp.mean(x * x, axis=-1, keepdims=True) + EPS)
        low_ref[rows, :] = (x * inverse * gain_ref[...]).astype(bf16)
    for copy in copies[1:4]:
        copy.wait()
    low = low_ref[...]
    q = dot_nt(low, wq_ref[...]).astype(bf16) * bf16(width ** (-0.5))
    kt_s[...] = dot_nt(wk_ref[...], low).astype(bf16)
    v = dot_nt(low, wv_ref[...]).astype(bf16)
    for h in range(count):
        cols = slice(h * width, (h + 1) * width)
        q_s[h] = q[:, cols]
        v_s[h] = v[:, cols]

    blocks = tokens // tall
    half = sel_ref.shape[0]

    def lay_bias(h):
        skew_s[h % 2] = pltpu.roll(
            jnp.broadcast_to(bias_s[h : h + 1, :], skew_s.shape[1:]),
            span - (BLOCK - 1), 1, stride=1, stride_axis=0,
        )

    def scores(h, n):
        score_s[n % 2] = dot(
            q_s[h, pl.ds(n * tall, tall), :], kt_s[h * width : (h + 1) * width, :]
        )

    def weights(h, n):
        for j in range(0, tall, ROWS):
            row = n * tall + j
            first = tokens - BLOCK - row // BLOCK * BLOCK
            bias = skew_s[h % 2, j % BLOCK : j % BLOCK + ROWS, first : first + tokens]
            score = score_s[n % 2, j : j + ROWS, :] + bias
            weight = jnp.exp(score - jnp.max(score, axis=-1, keepdims=True))
            total = jnp.sum(weight, axis=-1, keepdims=True)
            prob_ref[h, pl.ds(row, ROWS), :] = (weight * (1.0 / total)).astype(bf16)

    lay_bias(0)
    scores(0, 0)
    for h in range(count):
        for n in range(blocks):
            if n + 1 < blocks:
                scores(h, n + 1)
            elif h + 1 < count:
                lay_bias(h + 1)
                scores(h + 1, 0)
            weights(h, n)
        att = dot(prob_ref[h], v_s[h])
        att_low = att.astype(bf16)
        att_ref[h] = att_low
        attt_ref[h * width : (h + 1) * width, :] = jnp.transpose(att).astype(bf16)
        picked = dot(slot_s[...], att_low).astype(bf16)
        for part in range(2):
            start = part * inner + h * width
            sel_ref[:, start : start + width] = picked[part * half : (part + 1) * half]


def pass_kernel(given, passed):
    passed[...] = given[...]


def widen(rows, wide_s):
    wide_s[...] = jnp.zeros_like(wide_s)
    for e in range(rows.shape[0] // CAP):
        wide_s[e * SLOT : e * SLOT + CAP, :] = rows[e * CAP : (e + 1) * CAP]
    return wide_s[...]


def packed_width(width):
    return 2 * width + width // 2 + 128


def short_rows(width):
    each = width // 2
    for i in range(CAP - TALL):
        for k in range(4):
            yield TALL + i, slice(k * each, (k + 1) * each), 4 * i + k


def route_kernel(*refs, shards, heads):
    att_parts, w_ref = refs[:heads], refs[heads]
    (sel_in, sel_up, gain_ref, router_ref, att_t, hidden_ref, normed_ref, probs_ref, att_on
     ) = refs[heads + 1 : heads + 10]
    pieces = refs[heads + 10 : heads + 10 + shards]
    att_s, pay_s, wide_s, pack_s = refs[heads + 10 + shards :]
    head = lax.axis_index("head")
    half = att_parts[0].shape[0]
    inner = w_ref.shape[0] // heads
    for d in range(heads):
        att_s[d, 0:half, :] = att_parts[d][:, 0:inner]
        att_s[d, half : 2 * half, :] = att_parts[d][:, inner : 2 * inner]
    mixed = None
    for k in range(heads):
        term = dot(att_s[head ^ k], w_ref[k * inner : (k + 1) * inner, :])
        mixed = term if mixed is None else mixed + term
    hidden = sel_in[...].astype(f32) + widen(mixed, wide_s)
    hidden_ref[...] = hidden
    inverse = lax.rsqrt(jnp.mean(hidden * hidden, axis=-1, keepdims=True) + EPS)
    normed = hidden * inverse * gain_ref[...]
    normed_ref[...] = normed
    logits = dot_nt(normed, router_ref[...], highest)
    logits = logits - jnp.max(logits, axis=-1, keepdims=True)
    powers = jnp.exp(logits)
    probs = powers / jnp.sum(powers, axis=-1, keepdims=True)
    probs_ref[...] = probs
    gate = jnp.sum(jnp.where(chosen_of(probs.shape), probs, 0.0), axis=-1, keepdims=True)
    high = gate.astype(bf16).astype(f32)
    lane = iota((gate.shape[0], 128), 1)
    width = normed.shape[1]
    rest = gate - high
    first_gates = jnp.where(lane == 0, high, jnp.where(lane == 1, rest, 0.0))
    last_gates = jnp.where(lane == 2, high, jnp.where(lane == 3, rest, 0.0))
    pay_s[:, :width] = normed
    pay_s[:, width:] = sel_up[...].astype(f32)
    full, side = 2 * width, 2 * width + width // 2
    for e in range(shards):
        rows, packed = e * SLOT, e * TALL
        pack_s[packed : packed + TALL, :full] = pay_s[rows : rows + TALL, :]
        for row, lanes, to in short_rows(width):
            pack_s[packed + to : packed + to + 1, full:side] = pay_s[
                rows + row : rows + row + 1, lanes
            ]
        pack_s[packed : packed + 8, side:] = (
            first_gates[rows : rows + 8] + last_gates[rows + TALL : rows + SLOT]
        )
        pack_s[packed + 8 : packed + TALL, side:] = first_gates[rows + 8 : rows + TALL]
    shard = lax.axis_index("seq")
    for j in range(shards):
        first = pl.multiple_of((shard ^ j) * TALL, TALL)
        pieces[j][...] = pack_s[pl.ds(first, TALL), :].astype(bf16)
    att_on[...] = att_t[...]


def chosen_of(shape):
    expert = iota(shape, 1) * SLOT
    slot_row = iota(shape, 0)
    return (slot_row >= expert) & (slot_row < expert + SLOT)


def expert_kernel(*refs, shards, heads):
    parts = refs[:shards]
    w_in, w_out = refs[shards : shards + 2]
    chunks = refs[shards + 2 : shards + 2 + heads]
    x_ref, act_ref, pre_ref, out_ref, pay_s, gate_s, both_s = refs[shards + 2 + heads :]
    head = lax.axis_index("head")
    width = x_ref.shape[1]
    full, side = 2 * width, 2 * width + width // 2
    for j in range(shards):
        rows = j * SLOT
        part = parts[j][...].astype(f32)
        pay_s[rows : rows + TALL, :] = part[:, :full]
        pay_s[rows + TALL : rows + SLOT, :] = jnp.zeros((SLOT - TALL, full), f32)
        for row, lanes, place in short_rows(width):
            pay_s[rows + row : rows + row + 1, lanes] = part[place : place + 1, full:side]
        gate_s[rows : rows + TALL, :] = part[:, side : side + 1] + part[:, side + 1 : side + 2]
        gate_s[rows + TALL : rows + SLOT, :] = (
            part[:8, side + 2 : side + 3] + part[:8, side + 3 : side + 4]
        )
    x = pay_s[:, :width].astype(bf16)
    up = pay_s[:, width:]
    gate = gate_s[...]
    out_low = (gate * up).astype(bf16)
    pre = dot(x, w_in[...])
    cdf = 0.5 * (1.0 + lax.erf(pre * (0.5**0.5)))
    act = (pre * cdf).astype(bf16)
    slope = cdf + pre * jnp.exp(-0.5 * pre * pre) * ((2.0 * np.pi) ** (-0.5))
    pre_low = (dot_nt(out_low, w_out[...]) * slope).astype(bf16)
    both = (dot(act, w_out[...]), dot_nt(pre_low, w_in[...]))
    part = both_s.shape[2]
    for k in range(heads):
        start = k % (heads // 2) * part
        for j in range(shards):
            both_s[k, j * CAP : (j + 1) * CAP, :] = both[k // (heads // 2)][
                j * SLOT : j * SLOT + CAP, start : start + part
            ]
    for d in range(heads):
        chunks[d][...] = both_s[head ^ d].astype(bf16)
    pre_ref[...] = pre_low
    out_ref[...] = out_low
    x_ref[...] = x
    act_ref[...] = act


def expert_grad_kernel(x_ref, pre_ref, act_ref, out_ref, in_grad, out_grad):
    in_grad[0] = dot_tn(x_ref[...], pre_ref[...])
    out_grad[0] = dot_tn(act_ref[...], out_ref[...])


def sum_kernel(att_ref, *refs, heads):
    parts, att_on, pieces, sum_s = refs[:heads], refs[heads], refs[heads + 1 : -1], refs[-1]
    att_on[...] = att_ref[...]
    total = parts[0][...].astype(f32)
    for d in range(1, heads):
        total = total + parts[d][...].astype(f32)
    sum_s[...] = total
    for j, piece in enumerate(pieces):
        piece[...] = sum_s[j * CAP : (j + 1) * CAP, :].astype(bf16)


def join_kernel(*refs):
    parts, out_ref, sum_s = refs[:-2], refs[-2], refs[-1]
    for j, part in enumerate(parts):
        sum_s[j * CAP : (j + 1) * CAP, :] = part[...].astype(f32)
    out_ref[...] = sum_s[...].astype(bf16)


def prep_kernel(
    cot_ref, w_ref, wq_ref, wk_ref, wv_ref, low_ref, place_ref, attt_ref,
    gh_ref, stack_ref, k_ref, qt_ref, vt_ref, wout_ref, qsel_ref, ght_s, mcot_s,
):
    count, tokens, width = gh_ref.shape
    for i in range(0, tokens, 256):
        rows = pl.ds(i, 256)
        where = place_ref[rows, :].astype(f32)
        free = 1.0 - jnp.sum(where, axis=-1, keepdims=True)
        mcot_s[rows, :] = (cot_ref[rows, :].astype(f32) * free).astype(bf16)
        slots = jnp.transpose(where).astype(bf16)
        for h in range(count):
            stack_ref[h, width:, rows] = slots
    gh = dot_nt(mcot_s[...], w_ref[...]).astype(bf16)
    ght_s[...] = dot_nt(w_ref[...], mcot_s[...]).astype(bf16)
    k = dot_nt(low_ref[...], wk_ref[...]).astype(bf16)
    qt_ref[...] = dot_nt(wq_ref[...], low_ref[...]).astype(bf16) * bf16(width ** (-0.5))
    vt_ref[...] = dot_nt(wv_ref[...], low_ref[...]).astype(bf16)
    for h in range(count):
        cols = slice(h * width, (h + 1) * width)
        gh_ref[h] = gh[:, cols]
        k_ref[h] = k[:, cols]
        stack_ref[h, 0:width, :] = ght_s[cols, :]
    wout_ref[...] = dot(attt_ref[...], mcot_s[...])
    qsel_ref[...] = dot(qt_ref[...], place_ref[...]).astype(bf16)


def masked_back_kernel(
    gh_ref, stack_ref, k_ref, qt_ref, vt_ref, att_ref, prob_ref,
    dq_ref, dkt_ref, dvt_ref, offs_ref, psel_ref, acc_s, score_s, *, h,
):
    tokens, width = dq_ref.shape
    acc_s[...] = jnp.zeros_like(acc_s)
    cols = slice(h * width, (h + 1) * width)
    for i in range(0, tokens, 2 * BLOCK):
        rows = pl.ds(i, 2 * BLOCK)
        gh = gh_ref[h, rows, :]
        delta = jnp.sum(gh.astype(f32) * att_ref[h, rows, :].astype(f32), axis=-1, keepdims=True)
        grads = dot(gh, vt_ref[cols, :]) - delta
        for j in range(2):
            start = i + j * BLOCK
            first = tokens - BLOCK - start
            here = pl.ds(start, BLOCK)
            score = prob_ref[h, here, :].astype(f32) * grads[j * BLOCK : (j + 1) * BLOCK]
            acc_s[:, first : first + tokens] += score
            score_s[here, :] = score.astype(bf16)
    dq_ref[...] = dot(score_s[...], k_ref[h]) * (width ** (-0.5))
    dkt_ref[...] = dot(qt_ref[cols, :], score_s[...])
    both = dot(stack_ref[h], prob_ref[h])
    dvt_ref[...] = both[:width]
    psel_ref[...] = both[width:].astype(bf16)
    offs_ref[...] = diagonals(acc_s[...])


def diagonals(acc):
    span = acc.shape[1]
    rows = acc.shape[0] // 2
    while rows >= 8:
        acc = acc[:rows] + pltpu.roll(acc[rows:], span - rows, 1)
        rows //= 2
    total = acc[0:1]
    for r in range(1, 8):
        total = total + pltpu.roll(acc[r : r + 1], span - r, 1)
    return jnp.broadcast_to(pltpu.roll(total, BLOCK - 1, 1), (8, span))


def slot_back_kernel(*refs, heads):
    parts = refs[:heads]
    (up_ref, normed_ref, hidden_ref, probs_ref, router_ref, gain_ref, w_ref, att_ref,
     wout0_ref) = refs[heads : heads + 9]
    (dv_ref, comb_ref, small_ref, wout_ref, gh_ref, ght_ref, delta_ref, ret_s, wide_s
     ) = refs[heads + 9 :]
    head, shard = lax.axis_index("head"), lax.axis_index("seq")
    ret_s[...] = jnp.zeros_like(ret_s)
    for d in range(heads):
        part = parts[d][...].astype(f32)
        for j in range(part.shape[0] // CAP):
            first = pl.multiple_of((shard ^ j) * SLOT, SLOT)
            ret_s[head ^ d, pl.ds(first, CAP), :] = part[j * CAP : (j + 1) * CAP]
    back = [ret_s[k] for k in range(heads)]
    combined = jnp.concatenate(back[: heads // 2], axis=1)
    grad_buf = jnp.concatenate(back[heads // 2 :], axis=1)
    up = up_ref[...].astype(f32)
    hidden, normed, probs, gain = hidden_ref[...], normed_ref[...], probs_ref[...], gain_ref[...]
    chosen = chosen_of(probs.shape)
    gate = jnp.sum(jnp.where(chosen, probs, 0.0), axis=-1, keepdims=True)
    comb_ref[...] = gate * combined
    gate_grad = jnp.sum(up * combined, axis=-1, keepdims=True)
    marked = jnp.where(chosen, gate_grad, 0.0)
    logit_grad = probs * (marked - jnp.sum(marked * probs, axis=-1, keepdims=True))
    experts = probs.shape[1]
    grad = grad_buf + jnp.dot(
        logit_grad, router_ref[...], precision=highest, preferred_element_type=f32
    )
    inverse = lax.rsqrt(jnp.mean(hidden * hidden, axis=-1, keepdims=True) + EPS)
    scaled = grad * gain
    inner_sum = jnp.mean(scaled * hidden, axis=-1, keepdims=True)
    dv = inverse * scaled - hidden * (inverse * inverse * inverse * inner_sum)
    dv_ref[...] = dv
    small_ref[...] = jnp.zeros_like(small_ref)
    small_ref[0:1, :] = jnp.sum(grad * hidden * inverse, axis=0, keepdims=True)
    small_ref[8 : 8 + experts, :] = dot_tn(logit_grad, normed, highest)
    grad_low = (up + dv).astype(bf16)
    half = att_ref.shape[0]
    inner = w_ref.shape[0]
    att = jnp.concatenate(
        [att_ref[:, 0:inner].astype(f32), att_ref[:, inner : 2 * inner].astype(f32)], axis=0
    )
    att = widen(att, wide_s)
    wout_ref[...] = wout0_ref[...] + dot_tn(att.astype(bf16), grad_low)
    gh = dot_nt(grad_low, w_ref[...])
    gh_low = gh.astype(bf16)
    count = gh_ref.shape[0]
    each = inner // count
    ght_ref[...] = dot_nt(w_ref[...], grad_low).astype(bf16)
    for h in range(count):
        cols = slice(h * each, (h + 1) * each)
        gh_ref[h] = gh_low[:, cols]
        delta_ref[h] = jnp.sum(
            gh_low[:, cols].astype(f32) * att[:, cols], axis=-1, keepdims=True
        )


def sparse_back_kernel(
    gh_ref, ght_ref, delta_ref, vt_ref, k_ref, qsel_ref,
    place_ref, wq_ref, wk_ref, wv_ref, low_ref, gain_ref, small_ref, wout_ref, *refs, heads,
):
    per_head, refs = refs[: 4 * gh_ref.shape[0]], refs[4 * gh_ref.shape[0] :]
    psels, dq0s, dkt0s, dvt0s = (per_head[i :: 4] for i in range(4))
    chunks = refs[:5]
    (score_ref, send_ref, keep_ref, out_ref,
     dq_s, q_low, k_low, v_low, kt_s, vt_s, all_s) = refs[5:]
    head = lax.axis_index("head")
    count, rows, width = gh_ref.shape
    tokens = vt_ref.shape[1]
    inner = count * width
    for h in range(count):
        cols = slice(h * width, (h + 1) * width)
        grad = dot(gh_ref[h], vt_ref[cols, :])
        prob = psels[h][...]
        score = (prob.astype(f32) * (grad - delta_ref[h])).astype(bf16)
        score_ref[h] = score
        dq_s[:, cols] = dot(score, k_ref[h]) * (width ** (-0.5))
        dkt = dkt0s[h][...] + dot(qsel_ref[cols, :], score)
        dvt = dvt0s[h][...] + dot(ght_ref[cols, :], prob)
        kt_s[cols, :] = dkt.astype(bf16)
        vt_s[cols, :] = dvt.astype(bf16)
        k_low[:, cols] = jnp.transpose(dkt).astype(bf16)
        v_low[:, cols] = jnp.transpose(dvt).astype(bf16)
    spread = dot(place_ref[...], dq_s[...].astype(bf16))
    for h in range(count):
        cols = slice(h * width, (h + 1) * width)
        q_low[:, cols] = (spread[:, cols] + dq0s[h][...]).astype(bf16)
    part = tokens // heads
    half = part // 2
    own, to_1, to_2, rest_1, rest_2 = chunks
    to_1[part:, :] = jnp.zeros((EXTRA, to_1.shape[1]), bf16)
    places = (
        ((own, 0), (own, half)),
        ((to_1, 0), (rest_1, 0)),
        ((rest_2, 0), (to_2, 0)),
        ((to_1, half), (to_2, half)),
    )
    for d in range(heads):
        mine = pl.ds(pl.multiple_of((head ^ d) * part, part), part)
        rows_part = (
            dot(q_low[mine, :], wq_ref[...])
            + dot(k_low[mine, :], wk_ref[...])
            + dot(v_low[mine, :], wv_ref[...])
        ).astype(bf16)
        for n, (ref, first) in enumerate(places[d]):
            ref[first : first + half, :] = rows_part[n * half : (n + 1) * half]
    low = low_ref[...]
    total = None
    grads = (dot_tn(q_low[...], low), dot(kt_s[...], low), dot(vt_s[...], low))
    for i, (grad, w) in enumerate(zip(grads, (wq_ref, wk_ref, wv_ref))):
        all_s[i * inner : (i + 1) * inner, :] = grad
        term = jnp.sum(grad * w[...].astype(f32), axis=0, keepdims=True)
        total = term if total is None else total + term
    all_s[3 * inner :, :] = wout_ref[...]
    out_ref[...] = small_ref[...]
    out_ref[1:2, :] = total / gain_ref[...]
    to_1[part : part + 1, :] = (total / gain_ref[...]).astype(bf16)
    split_rows(all_s, 1, send_ref, keep_ref)


def is_upper(bit):
    return (lax.axis_index("seq") & bit) != 0


def split_rows(all_s, bit, send_ref, keep_ref):
    half = send_ref.shape[0]
    low, high = all_s[0:half, :], all_s[half : 2 * half, :]
    keep_ref[...] = jnp.where(is_upper(bit), high, low)
    send_ref[...] = jnp.where(is_upper(bit), low, high).astype(bf16)


def halve_kernel(keep_ref, got_ref, *refs, bit):
    send_ref, out_ref, all_s = refs[-3:]
    if len(refs) > 3:
        rest_1, got_1, rest_2, got_2, small_ref, next_1, next_2 = refs[:-3]
        half = rest_1.shape[0]
        for rest, got, onward in ((rest_1, got_2, next_1), (rest_2, got_1, next_2)):
            got_rest = got[half : 2 * half, :].astype(f32)
            onward[0:half, :] = (rest[...].astype(f32) + got_rest).astype(bf16)
        mine = small_ref[1:2, :].astype(bf16).astype(f32)
        next_2[half:, :] = jnp.zeros((EXTRA, next_2.shape[1]), bf16)
        next_2[half : half + 1, :] = (mine + got_1[2 * half : 2 * half + 1, :].astype(f32)).astype(bf16)
    all_s[...] = keep_ref[...] + got_ref[...].astype(f32)
    split_rows(all_s, bit, send_ref, out_ref)


def join_rows(mine_ref, got_ref, all_s, bit, count):
    mine, got = mine_ref[...].astype(f32), got_ref[...].astype(f32)
    all_s[0:count, :] = jnp.where(is_upper(bit), got[:count], mine[:count])
    all_s[count : 2 * count, :] = jnp.where(is_upper(bit), mine[:count], got[:count])
    all_s[2 * count :, :] = mine[count:] + got[count:]


def pair_kernel(mine_ref, got_ref, *refs, bit, count):
    out_ref, all_s = refs[-2:]
    if len(refs) > 2:
        got_1, got_2, next_1, next_2 = refs[:-2]
        half = next_1.shape[0]
        next_2[...] = got_1[0:half, :]
        next_1[...] = got_2[half:, :]
    if count % 16:
        join_rows(mine_ref, got_ref, all_s, bit, count)
        out_ref[...] = all_s[...].astype(bf16)
    else:
        for first, upper in ((0, False), (count, True)):
            is_mine = is_upper(bit) if upper else jnp.logical_not(is_upper(bit))
            rows = slice(first, first + count)

            @pl.when(is_mine)
            def _():
                out_ref[rows, :] = mine_ref[0:count, :]

            @pl.when(jnp.logical_not(is_mine))
            def _():
                out_ref[rows, :] = got_ref[0:count, :]

        small = mine_ref[count:, :].astype(f32) + got_ref[count:, :].astype(f32)
        out_ref[2 * count :, :] = small.astype(bf16)


def write_half(rows_ref, outs, upper, wide_s, sems):
    inner = wide_s.shape[1]
    for i in range(2):
        wide_s[i] = rows_ref[i * inner : (i + 1) * inner, :].astype(f32)
    for wanted, pair in ((False, outs[:2]), (True, outs[2:])):

        @pl.when(upper if wanted else jnp.logical_not(upper))
        def _():
            copies = [
                pltpu.make_async_copy(wide_s.at[i], out, sems.at[i]) for i, out in enumerate(pair)
            ]
            for copy in copies:
                copy.start()
            for copy in copies:
                copy.wait()


def final_own_kernel(mine_ref, *refs, bit):
    write_half(mine_ref, refs[:4], is_upper(bit), *refs[4:])


def final_got_kernel(mine_ref, got_ref, *refs, bit, count):
    outs = refs[4:8]
    gain1_ref, gain2_ref, table_ref, router_ref, wide_s, sems = refs[8:]
    small = mine_ref[count:, :].astype(f32) + got_ref[count:, :].astype(f32)
    gain1_ref[...] = small[1, :]
    gain2_ref[...] = small[0, :]
    heads, buckets = table_ref.shape
    table_ref[...] = small[2 : 2 + heads, :buckets]
    router_ref[...] = small[8 : 8 + router_ref.shape[0], :]
    write_half(got_ref, outs, jnp.logical_not(is_upper(bit)), wide_s, sems)


def bias_grad_kernel(
    score_ref, place_ref, buckets_ref, small_ref, *refs, bucket_count
):
    count = score_ref.shape[0]
    offs, out_ref, acc_s, sums_s = refs[:count], *refs[count:]
    tokens = place_ref.shape[0]
    offsets = buckets_ref.shape[1]
    out_ref[...] = small_ref[...]
    bucket_hot = (iota((bucket_count, offsets), 0) == buckets_ref[...]).astype(f32)

    def one_head(h, carry):
        acc_s[...] = jnp.zeros_like(acc_s)
        for i in range(0, tokens, BLOCK):
            first = tokens - BLOCK - i
            acc_s[:, first : first + tokens] += dot(place_ref[i : i + BLOCK, :], score_ref[h])
        sums_s[h] = diagonals(acc_s[...])
        return carry

    lax.fori_loop(0, count, one_head, 0)
    for h in range(count):
        sums = sums_s[h] + offs[h][...]
        out_ref[2 + h : 3 + h, :bucket_count] = dot_nt(sums[:, :offsets], bucket_hot, highest)[0:1]


def hidden_kernel(*refs, heads):
    att_parts, w_ref, x_ref, out_ref, att_s = refs[:heads], *refs[heads:]
    head = lax.axis_index("head")
    tokens = x_ref.shape[0]
    inner = att_parts[0].shape[0]
    for d in range(heads):
        mine = pl.ds(pl.multiple_of((head ^ d) * inner, inner), inner)
        att_s[mine, :] = att_parts[d][...]

    def block(i, carry):
        rows = pl.ds(pl.multiple_of(i * 256, 256), 256)
        out_ref[rows, :] = x_ref[rows, :].astype(f32) + dot_tn(att_s[:, rows], w_ref[...])
        return carry

    lax.fori_loop(0, tokens // 256, block, 0)


def output_kernel(hidden_ref, place_ref, comb_ref, out_ref):
    high, rest = split_two(comb_ref[...])

    def block(i, carry):
        rows = pl.ds(pl.multiple_of(i * 256, 256), 256)
        where = place_ref[rows, :]
        out_ref[rows, :] = hidden_ref[rows, :] + (dot(where, high) + dot(where, rest))
        return carry

    lax.fori_loop(0, hidden_ref.shape[0] // 256, block, 0)


def first_norm_kernel(
    own, got_1, got_2, last_1, last_2, next_2, small_ref,
    x_ref, cot_ref, place_ref, dv_ref, gain_ref, keep_ref, got_ref, out_ref, sum_ref,
):
    half = last_1.shape[0]
    high, rest = split_two(dv_ref[...])
    for first, near, far in ((0, got_1, last_2), (half, got_2, last_1)):
        rows = pl.ds(first, half)
        grad = own[rows, :].astype(f32) + near[0:half, :].astype(f32)
        grad = grad + far[0:half, :].astype(f32)
        x = x_ref[rows, :].astype(f32)
        inverse = lax.rsqrt(jnp.mean(x * x, axis=-1, keepdims=True) + EPS)
        scaled = grad * gain_ref[...]
        inner_sum = jnp.mean(scaled * x, axis=-1, keepdims=True)
        where = place_ref[rows, :]
        hidden_grad = cot_ref[rows, :].astype(f32) + (dot(where, high) + dot(where, rest))
        out_ref[rows, :] = (
            hidden_grad + inverse * scaled - x * (inverse * inverse * inverse * inner_sum)
        ).astype(bf16)
    count = keep_ref.shape[0]
    sum_ref[0:count, :] = (keep_ref[...] + got_ref[...].astype(f32)).astype(bf16)
    gain1 = next_2[half:, :].astype(f32)[0:1] + last_2[half:, :].astype(f32)[0:1]
    small = small_ref[...]
    sum_ref[count:, :] = jnp.where(iota(small.shape, 0) == 1, gain1, small).astype(bf16)


def spread_near_kernel(own, got_1, got_2, out_ref, token, wide_s, sems):
    head = lax.axis_index("head")
    part = own.shape[0]
    copies = []
    for d, piece in enumerate((own, got_1, got_2)):
        wide_s[d] = piece[...].astype(f32)
        mine = pl.ds(pl.multiple_of((head ^ d) * part, part), part)
        copies.append(pltpu.make_async_copy(wide_s.at[d], out_ref.at[mine], sems.at[d]))
        copies[-1].start()
    token[...] = jnp.zeros_like(token)
    for copy in copies:
        copy.wait()


def spread_far_kernel(last_1, last_2, given, out_ref, wide_s, sem):
    head = lax.axis_index("head")
    half = last_1.shape[0]
    wide_s[0:half, :] = last_2[...].astype(f32)
    wide_s[half:, :] = last_1[...].astype(f32)
    mine = pl.ds(pl.multiple_of((head ^ 3) * 2 * half, 2 * half), 2 * half)
    copy = pltpu.make_async_copy(wide_s, out_ref.at[mine], sem)
    copy.start()
    copy.wait()


def swap(x, axis, d):
    size = lax.axis_size(axis)
    return lax.ppermute(x, axis, [(i, i ^ d) for i in range(size)])


def share(x, axis):
    return [x] + [swap(x, axis, d) for d in range(1, lax.axis_size(axis))]


def trade(pieces, axis):
    return lax.all_to_all(pieces, axis, split_axis=0, concat_axis=0, tiled=True)


def swap_all(pieces, axis):
    return [pieces[0]] + [swap(pieces[d], axis, d) for d in range(1, len(pieces))]


def bits_of(axis):
    return [b for b in (1 << i for i in range(16)) if b < lax.axis_size(axis)]


def halve(send, keep, bit, after, onward=()):
    rows, width = keep.shape
    outs = []
    if onward:
        half = onward[0].shape[0]
        outs = [shape_of(half, width, bf16), shape_of(half + EXTRA, width, bf16)]
    return call(
        partial(halve_kernel, bit=bit),
        outs + [shape_of(rows // 2, width, bf16), shape_of(rows // 2, width, f32)],
        (keep, swap(send, "seq", bit // 2)) + tuple(onward),
        scratch=[pltpu.VMEM((rows, width), f32)],
        name="halve",
        after=after,
        token=True,
    )


def pair(now, small_rows, bit, after, onward=()):
    rows, width = now.shape
    count = rows - small_rows
    outs = [shape_of(onward[0].shape[0] // 2, width, bf16)] * 2 if onward else []
    return call(
        partial(pair_kernel, bit=bit, count=count),
        outs + [shape_of(rows + count, width, bf16)],
        (now, swap(now, "seq", bit)) + tuple(onward),
        scratch=[pltpu.VMEM((rows + count, width), f32)],
        name="pair",
        after=after,
        token=True,
    )


def on_device(
    layer_input, cotangent, norm1_gain, w_query, w_key, w_value, w_attn_out, bias_table,
    norm2_gain, w_router, w_expert_in, w_expert_out, expert_ids, slot_ids, buckets,
):
    tokens, width = layer_input.shape
    shards = lax.axis_size("seq")
    heads = lax.axis_size("head")
    bucket_count, count = bias_table.shape
    inner = w_query.shape[1]
    each = inner // count
    experts = w_router.shape[1]
    rows, filled = experts * SLOT, experts * CAP
    hidden_units = w_expert_in.shape[2]
    part = tokens // heads
    split = 2 * width // heads
    span = 2 * tokens
    params = pltpu.CompilerParams(vmem_limit_bytes=VMEM_LIMIT if rows <= 256 else VMEM_ALL)

    ids = expert_ids.reshape(1, tokens)
    slots = slot_ids.reshape(1, tokens)
    bucket_row = buckets.reshape(1, -1)
    wq_t, wk_t, wv_t = jnp.transpose(w_query), jnp.transpose(w_key), jnp.transpose(w_value)
    router_t, table_t = jnp.transpose(w_router), jnp.transpose(bias_table)
    w_in = w_expert_in.reshape(width, hidden_units)
    w_out = w_expert_out.reshape(hidden_units, width)

    w_mix = share(w_attn_out, "head")

    low, prob, att, att_t, att_sel = pl.pallas_call(
        attend_kernel,
        out_shape=(
            shape_of(tokens, width, bf16),
            jax.ShapeDtypeStruct((count, tokens, tokens), bf16),
            jax.ShapeDtypeStruct((count, tokens, each), bf16),
            shape_of(inner, tokens, bf16),
            shape_of(filled // 2, 2 * inner, bf16),
        ),
        in_specs=[spec(pltpu.HBM)] * 9,
        out_specs=(spec(pltpu.VMEM),) * 5,
        scratch_shapes=[
            pltpu.VMEM((count, tokens, each), bf16),
            pltpu.VMEM((inner, tokens), bf16),
            pltpu.VMEM((count, tokens, each), bf16),
            pltpu.VMEM((8, span), f32),
            pltpu.VMEM((2, BLOCK, span), f32),
            pltpu.VMEM((filled, tokens), bf16),
            pltpu.VMEM((2, 2 * BLOCK, tokens), f32),
            pltpu.VMEM((tokens, width), bf16),
            pltpu.VMEM((width,), f32),
            pltpu.VMEM((inner, width), bf16),
            pltpu.VMEM((inner, width), bf16),
            pltpu.VMEM((inner, width), bf16),
            pltpu.VMEM((count, bucket_count), f32),
            pltpu.VMEM((1, span - 1), jnp.int32),
            pltpu.VMEM((1, tokens), jnp.int32),
            pltpu.VMEM((1, tokens), jnp.int32),
            pltpu.SemaphoreType.DMA((9 + tokens // 256,)),
        ],
        compiler_params=params,
        cost_estimate=NO_COST,
        name="attend",
    )(
        *(
            pltpu.with_memory_space_constraint(a, pltpu.HBM)
            for a in (layer_input, norm1_gain, wq_t, wk_t, wv_t, table_t, bucket_row, ids, slots)
        )
    )

    (att_sel,) = call(
        pass_kernel,
        [shape_of(filled // 2, 2 * inner, bf16)],
        (att_sel,),
        name="pass",
        after=(w_mix[1],),
    )
    sel_parts = share(att_sel, "head")
    sel_in, sel_up, place, place_c, x_c, cot_c, w_full = call(
        partial(place_kernel, heads=heads),
        [
            shape_of(rows, width, bf16),
            shape_of(rows, width, bf16),
            shape_of(tokens, rows, bf16),
            shape_of(part, rows, bf16),
            shape_of(part, width, bf16),
            shape_of(part, width, bf16),
            shape_of(heads * inner, width, bf16),
        ],
        (layer_input, cotangent, ids, slots) + tuple(w_mix),
        scratch=[pltpu.VMEM((tokens, rows), f32)],
        moved=12 * 2**20,
        name="place",
        after=(att_sel,),
    )
    routed = call(
        partial(route_kernel, shards=shards, heads=heads),
        [
            shape_of(rows, width, f32),
            shape_of(rows, width, f32),
            shape_of(rows, experts, f32),
            shape_of(inner, tokens, bf16),
        ]
        + [shape_of(TALL, packed_width(width), bf16)] * shards,
        tuple(sel_parts) + (w_full, sel_in, sel_up, norm2_gain, router_t, att_t),
        scratch=[
            pltpu.VMEM((heads, filled, inner), bf16),
            pltpu.VMEM((rows, 2 * width), f32),
            pltpu.VMEM((rows, width), f32),
            pltpu.VMEM((shards * TALL, packed_width(width)), f32),
        ],
        name="route",
    )
    hidden_sel, normed_sel, probs, att_on = routed[:4]
    pay_parts = swap_all(routed[4:], "seq")
    att_parts = [att_t] + [swap(att_on, "head", d) for d in range(1, heads - 1)]

    def masked_back(h, after):
        return call(
            partial(masked_back_kernel, h=h),
            [
                shape_of(tokens, each, f32),
                shape_of(each, tokens, f32),
                shape_of(each, tokens, f32),
                shape_of(8, span, f32),
                shape_of(rows, tokens, bf16),
            ],
            (gh, stack, k_rows, q_t, v_t, att, prob),
            scratch=[pltpu.VMEM((BLOCK, span), f32), pltpu.VMEM((tokens, tokens), bf16)],
            name="masked_back",
            after=after,
            moved=11 * 2**20,
            token=True,
        )

    done = call(
        partial(expert_kernel, shards=shards, heads=heads),
        [shape_of(filled, split, bf16)] * heads
        + [
            shape_of(rows, width, bf16),
            shape_of(rows, hidden_units, bf16),
            shape_of(rows, hidden_units, bf16),
            shape_of(rows, width, bf16),
        ],
        tuple(pay_parts) + (w_in, w_out),
        scratch=[
            pltpu.VMEM((rows, 2 * width), f32),
            pltpu.VMEM((rows, 1), f32),
            pltpu.VMEM((heads, filled, split), f32),
        ],
        name="expert",
        after=tuple(att_parts[1:]),
        token=True,
    )
    x_rows, act, pre_low, out_low, token = done[heads:]
    gh, stack, k_rows, q_t, v_t, wout0, q_sel, token = call(
        prep_kernel,
        [
            jax.ShapeDtypeStruct((count, tokens, each), bf16),
            jax.ShapeDtypeStruct((count, each + rows, tokens), bf16),
            jax.ShapeDtypeStruct((count, tokens, each), bf16),
            shape_of(inner, tokens, bf16),
            shape_of(inner, tokens, bf16),
            shape_of(inner, width, f32),
            shape_of(inner, rows, bf16),
        ],
        (cotangent, w_attn_out, wq_t, wk_t, wv_t, low, place, att_t),
        scratch=[pltpu.VMEM((inner, tokens), bf16), pltpu.VMEM((tokens, width), bf16)],
        name="prep",
        after=(token,),
        moved=8 * 2**20,
        token=True,
    )

    masked = []
    for h in range(count - 2):
        masked.append(masked_back(h, (token,)))
        token = masked[-1][-1]
    returned = call(
        partial(sum_kernel, heads=heads),
        [shape_of(inner, tokens, bf16)] + [shape_of(CAP, split, bf16)] * shards,
        [att_t] + swap_all(done[:heads], "head"),
        scratch=[pltpu.VMEM((filled, split), f32)],
        name="sum",
        after=(token,),
        token=True,
    )
    masked.append(masked_back(count - 2, (returned[-1],)))
    att_parts.append(swap(returned[0], "head", heads - 1))
    joined, token = call(
        join_kernel,
        [shape_of(filled, split, bf16)],
        swap_all(returned[1:-1], "seq"),
        scratch=[pltpu.VMEM((filled, split), f32)],
        name="join",
        after=(masked[-1][-1], att_parts[-1]),
        token=True,
    )
    masked.append(masked_back(count - 1, (token,)))
    full_parts = share(joined, "head")

    small_rows = 8 + -(-experts // 8) * 8
    dv_sel, comb_sel, small, wout_part, gh_sel, ght_sel, delta_sel = call(
        partial(slot_back_kernel, heads=heads),
        [
            shape_of(rows, width, f32),
            shape_of(rows, width, f32),
            shape_of(small_rows, width, f32),
            shape_of(inner, width, f32),
            jax.ShapeDtypeStruct((count, rows, each), bf16),
            shape_of(inner, rows, bf16),
            jax.ShapeDtypeStruct((count, rows, 1), f32),
        ],
        tuple(full_parts)
        + (sel_up, normed_sel, hidden_sel, probs, router_t, norm2_gain)
        + (w_attn_out, att_sel, wout0),
        scratch=[pltpu.VMEM((heads, rows, split), f32), pltpu.VMEM((rows, inner), f32)],
        name="slot_back",
        after=(masked[-1][-1],),
    )

    back = call(
        partial(sparse_back_kernel, heads=heads),
        [shape_of(part, width, bf16), shape_of(part + EXTRA, width, bf16)]
        + [shape_of(part, width, bf16)]
        + [shape_of(part // 2, width, bf16)] * 2
        + [
            jax.ShapeDtypeStruct((count, rows, tokens), bf16),
            shape_of(2 * inner, width, bf16),
            shape_of(2 * inner, width, f32),
            shape_of(small_rows, width, f32),
        ],
        (gh_sel, ght_sel, delta_sel, v_t, k_rows, q_sel, place)
        + (wq_t, wk_t, wv_t, low, norm1_gain, small, wout_part)
        + tuple(a for m in masked for a in (m[4], m[0], m[1], m[2])),
        scratch=[
            pltpu.VMEM((rows, inner), f32),
            pltpu.VMEM((tokens, inner), bf16),
            pltpu.VMEM((tokens, inner), bf16),
            pltpu.VMEM((tokens, inner), bf16),
            pltpu.VMEM((inner, tokens), bf16),
            pltpu.VMEM((inner, tokens), bf16),
            pltpu.VMEM((4 * inner, width), f32),
        ],
        name="sparse_back",
    )
    score_sel, send, keep, small = back[5:]
    own, to_1, to_2, rest_1, rest_2 = back[:5]
    got_1, got_2 = swap(to_1, "head", 1), swap(to_2, "head", 2)

    bits = bits_of("seq")
    send, keep, token = halve(send, keep, bits[1], ())
    small_part = small
    small, token = call(
        partial(bias_grad_kernel, bucket_count=bucket_count),
        [shape_of(small_rows, width, f32)],
        (score_sel, place, bucket_row, small) + tuple(m[3] for m in masked),
        scratch=[pltpu.VMEM((BLOCK, span), f32), pltpu.VMEM((count, 8, span), f32)],
        name="bias_grad",
        after=(token,),
        moved=16 * 2**20,
        token=True,
    )
    next_1, next_2, send, keep, token = halve(
        send, keep, bits[2], (token,), (rest_1, got_1, rest_2, got_2, small_part)
    )
    last_1, last_2 = swap(next_1, "head", 1), swap(next_2, "head", 2)
    w_in_grad, w_out_grad, token = call(
        expert_grad_kernel,
        [
            jax.ShapeDtypeStruct(w_expert_in.shape, f32),
            jax.ShapeDtypeStruct(w_expert_out.shape, f32),
        ],
        (x_rows, pre_low, act, out_low),
        name="expert_grad",
        after=(token,),
        moved=10 * 2**20,
        token=True,
    )
    hidden, token = call(
        partial(hidden_kernel, heads=heads),
        [shape_of(tokens, width, f32)],
        tuple(att_parts) + (w_full, layer_input),
        scratch=[pltpu.VMEM((heads * inner, tokens), bf16)],
        name="hidden",
        after=(token,),
        moved=6 * 2**20,
        token=True,
    )
    for bit in bits[3:]:
        send, keep, token = halve(send, keep, bit, (token,))

    grad_part, weights, token = call(
        first_norm_kernel,
        [shape_of(part, width, bf16), shape_of(keep.shape[0] + small_rows, width, bf16)],
        (own, got_1, got_2, last_1, last_2, next_2, small)
        + (x_c, cot_c, place_c, dv_sel, norm1_gain)
        + (keep, swap(send, "seq", bits[-1])),
        name="first_norm",
        after=(token,),
        token=True,
    )
    grad_1, grad_2 = swap(grad_part, "head", 1), swap(grad_part, "head", 2)
    layer_output, token = call(
        output_kernel,
        [shape_of(tokens, width, f32)],
        (hidden, place, comb_sel),
        name="output",
        after=(token,),
        moved=10 * 2**20,
        token=True,
    )
    for bit in reversed(bits[3:]):
        weights, token = pair(weights, small_rows, bit, (token,))
    next_1, next_2, weights, token = pair(
        weights, small_rows, bits[2], (token,), (grad_1, grad_2)
    )
    grad_3 = (swap(next_1, "head", 1), swap(next_2, "head", 2))
    near, token = pl.pallas_call(
        spread_near_kernel,
        out_shape=(shape_of(tokens, width, f32), shape_of(8, 128, f32)),
        in_specs=[spec(pltpu.VMEM)] * 3,
        out_specs=(spec(pltpu.HBM), spec(pltpu.VMEM)),
        scratch_shapes=[pltpu.VMEM((3, part, width), f32), pltpu.SemaphoreType.DMA((3,))],
        compiler_params=params,
        cost_estimate=pl.CostEstimate(flops=1, bytes_accessed=5 * 2**20, transcendentals=0),
        name="spread_near",
    )(grad_part, grad_1, grad_2)
    weights, token = pair(weights, small_rows, bits[1], grad_3 + (token,))
    got = swap(weights, "seq", bits[0])
    halves = pl.pallas_call(
        partial(final_own_kernel, bit=bits[0]),
        out_shape=(shape_of(inner, width, f32),) * 4,
        in_specs=[spec(pltpu.VMEM)],
        out_specs=(spec(pltpu.HBM),) * 4,
        scratch_shapes=[pltpu.VMEM((2, inner, width), f32), pltpu.SemaphoreType.DMA((2,))],
        compiler_params=params,
        cost_estimate=pl.CostEstimate(flops=1, bytes_accessed=2**20, transcendentals=0),
        name="weights_own",
    )(weights)
    last = pl.pallas_call(
        partial(final_got_kernel, bit=bits[0], count=2 * inner),
        out_shape=(shape_of(inner, width, f32),) * 4
        + (
            jax.ShapeDtypeStruct((width,), f32),
            jax.ShapeDtypeStruct((width,), f32),
            shape_of(count, bucket_count, f32),
            shape_of(experts, width, f32),
        ),
        in_specs=[spec(pltpu.VMEM)] * 2 + [spec(pltpu.HBM)] * 4,
        out_specs=(spec(pltpu.HBM),) * 4 + (spec(pltpu.VMEM),) * 4,
        scratch_shapes=[pltpu.VMEM((2, inner, width), f32), pltpu.SemaphoreType.DMA((2,))],
        input_output_aliases={2: 0, 3: 1, 4: 2, 5: 3},
        compiler_params=params,
        cost_estimate=NO_COST,
        name="weights_got",
    )(weights, got, *halves)
    weight_sums = last[:4]
    gain1_sum, gain2_sum, table_sum, router_sum = last[4:]
    input_grad = pl.pallas_call(
        spread_far_kernel,
        out_shape=shape_of(tokens, width, f32),
        in_specs=[spec(pltpu.VMEM), spec(pltpu.VMEM), spec(pltpu.HBM)],
        out_specs=spec(pltpu.HBM),
        scratch_shapes=[pltpu.VMEM((part, width), f32), pltpu.SemaphoreType.DMA(())],
        input_output_aliases={2: 0},
        compiler_params=params,
        cost_estimate=NO_COST,
        name="spread_far",
    )(*grad_3, near)

    return (
        layer_output,
        input_grad,
        gain1_sum,
        jnp.transpose(weight_sums[0]),
        jnp.transpose(weight_sums[1]),
        jnp.transpose(weight_sums[2]),
        weight_sums[3],
        jnp.transpose(table_sum),
        gain2_sum,
        jnp.transpose(router_sum),
        w_in_grad,
        w_out_grad,
    )


def solution(mesh):
    return jax.shard_map(
        on_device,
        mesh=mesh,
        in_specs=(
            P("seq", None),
            P("seq", None),
            P(),
            P(None, "head"),
            P(None, "head"),
            P(None, "head"),
            P("head", None),
            P(None, "head"),
            P(),
            P(),
            P("seq", None, "head"),
            P("seq", "head", None),
            P("seq"),
            P("seq"),
            P(),
        ),
        out_specs=(
            P("seq", None),
            P("seq", None),
            P(),
            P(None, "head"),
            P(None, "head"),
            P(None, "head"),
            P("head", None),
            P(None, "head"),
            P(),
            P(),
            P("seq", None, "head"),
            P("seq", "head", None),
        ),
        check_vma=False,
    )
```

```python
from functools import partial

import jax
import jax.numpy as jnp
import numpy as np
from jax import lax
from jax.experimental import pallas as pl
from jax.experimental.pallas import tpu as pltpu
from jax.sharding import PartitionSpec as P

CAP = 20
SLOT = 24
EPS = 1e-06
BLOCK = 128
ROWS = 16
EXTRA = 16
TALL = 16
VMEM_LIMIT = 26 * 1024 * 1024
VMEM_ALL = 60 * 1024 * 1024
NO_COST = pl.CostEstimate(flops=1, bytes_accessed=1, transcendentals=0)

f32 = jnp.float32
bf16 = jnp.bfloat16
highest = lax.Precision.HIGHEST


def dot(a, b):
    return jnp.dot(a, b, preferred_element_type=f32)


def dot_nt(a, b, precision=None):
    return lax.dot_general(
        a, b, (((1,), (1,)), ((), ())), precision=precision, preferred_element_type=f32
    )


def dot_tn(a, b, precision=None):
    return lax.dot_general(
        a, b, (((0,), (0,)), ((), ())), precision=precision, preferred_element_type=f32
    )


def iota(shape, dim):
    return lax.broadcasted_iota(jnp.int32, shape, dim)


def split_two(v):
    high = v.astype(bf16)
    return high, (v - high.astype(f32)).astype(bf16)


def shape_of(rows, cols, dtype):
    return jax.ShapeDtypeStruct((rows, cols), dtype)


def spec(memory):
    return pl.BlockSpec(memory_space=memory)


def call(kernel, outs, args, scratch=(), name=None, after=(), moved=1, token=False):
    outs, args = tuple(outs), tuple(args)
    held = sum(int(np.prod(a.shape)) * np.dtype(a.dtype).itemsize for a in args + outs)
    if token:
        outs += (shape_of(8, 128, f32),)
    first_out = len(args) + len(after)

    def body(*refs):
        results = refs[first_out : first_out + len(outs)]
        if token:
            results[-1][...] = jnp.zeros((8, 128), f32)
            results = results[:-1]
        kernel(*refs[: len(args)], *results, *refs[first_out + len(outs) :])

    return pl.pallas_call(
        body,
        out_shape=outs,
        in_specs=[spec(pltpu.VMEM)] * len(args) + [spec(pl.ANY)] * len(after),
        out_specs=tuple(spec(pltpu.VMEM) for _ in outs),
        scratch_shapes=list(scratch),
        compiler_params=pltpu.CompilerParams(
            vmem_limit_bytes=VMEM_LIMIT if 2 * held < VMEM_LIMIT else VMEM_ALL
        ),
        cost_estimate=pl.CostEstimate(flops=1, bytes_accessed=moved, transcendentals=0),
        name=name,
    )(*args, *after)


def slot_rows(ids, slots, rows, each):
    cell = jnp.where(slots < CAP, ids * each + slots, -1)
    return (iota((rows, cell.shape[1]), 0) == cell).astype(f32)


def place_kernel(x_ref, cot_ref, ids_ref, slots_ref, *refs, heads):
    w_parts = refs[:heads]
    sel_in, sel_up, place, place_c, x_c, cot_c, w_ref, place_s = refs[heads:]
    head = lax.axis_index("head")
    part = x_c.shape[0]
    slot_hot = slot_rows(ids_ref[...], slots_ref[...], sel_in.shape[0], SLOT)
    place_s[...] = jnp.transpose(slot_hot)
    slot_low = slot_hot.astype(bf16)
    sel_in[...] = dot(slot_low, x_ref[...]).astype(bf16)
    sel_up[...] = dot(slot_low, cot_ref[...]).astype(bf16)
    place[...] = place_s[...].astype(bf16)
    mine = pl.ds(pl.multiple_of(head * part, part), part)
    place_c[...] = place_s[mine, :].astype(bf16)
    x_c[...] = x_ref[mine, :]
    cot_c[...] = cot_ref[mine, :]
    inner = w_parts[0].shape[0]
    for d in range(heads):
        rows = pl.ds(pl.multiple_of((head ^ d) * inner, inner), inner)
        w_ref[rows, :] = w_parts[d][...]


def attend_kernel(*refs):
    given, refs = refs[:9], refs[9:]
    low_ref, prob_ref, att_ref, attt_ref, sel_ref = refs[:5]
    q_s, kt_s, v_s, bias_s, skew_s, slot_s, score_s = refs[5:12]
    here, sems = refs[12:21], refs[21]
    x_ref, gain_ref, wq_ref, wk_ref, wv_ref, table_ref, buckets_ref, ids_ref, slots_ref = here
    copies = [
        pltpu.make_async_copy(far, near, sems.at[i])
        for i, (far, near) in enumerate(zip(given, here))
    ]
    tokens = x_ref.shape[0]
    inner = wq_ref.shape[0]
    count = q_s.shape[0]
    width = inner // count
    span = skew_s.shape[2]
    tall = 2 * BLOCK
    for copy in copies:
        copy.start()
    for copy in copies[5:]:
        copy.wait()
    slot_s[...] = slot_rows(ids_ref[...], slots_ref[...], slot_s.shape[0], CAP).astype(bf16)
    offsets = buckets_ref.shape[1]
    bucket_hot = (iota((table_ref.shape[1], offsets), 0) == buckets_ref[...]).astype(f32)
    bias_s[...] = jnp.zeros_like(bias_s)
    bias_s[:count, :offsets] = jnp.dot(
        table_ref[...], bucket_hot, precision=highest, preferred_element_type=f32
    )
    for copy in copies[:2]:
        copy.wait()
    for i in range(0, tokens, 256):
        rows = pl.ds(i, 256)
        x = x_ref[rows, :].astype(f32)
        inverse = lax.rsqrt(jnp.mean(x * x, axis=-1, keepdims=True) + EPS)
        low_ref[rows, :] = (x * inverse * gain_ref[...]).astype(bf16)
    for copy in copies[2:5]:
        copy.wait()
    low = low_ref[...]
    q = dot_nt(low, wq_ref[...]).astype(bf16) * bf16(width ** (-0.5))
    kt_s[...] = dot_nt(wk_ref[...], low).astype(bf16)
    v = dot_nt(low, wv_ref[...]).astype(bf16)
    for h in range(count):
        cols = slice(h * width, (h + 1) * width)
        q_s[h] = q[:, cols]
        v_s[h] = v[:, cols]

    blocks = tokens // tall
    half = sel_ref.shape[0]

    def lay_bias(h):
        skew_s[h % 2] = pltpu.roll(
            jnp.broadcast_to(bias_s[h : h + 1, :], skew_s.shape[1:]),
            span - (BLOCK - 1), 1, stride=1, stride_axis=0,
        )

    def scores(h, n):
        score_s[n % 2] = dot(
            q_s[h, pl.ds(n * tall, tall), :], kt_s[h * width : (h + 1) * width, :]
        )

    def weights(h, n):
        for j in range(0, tall, ROWS):
            row = n * tall + j
            first = tokens - BLOCK - row // BLOCK * BLOCK
            bias = skew_s[h % 2, j % BLOCK : j % BLOCK + ROWS, first : first + tokens]
            score = score_s[n % 2, j : j + ROWS, :] + bias
            weight = jnp.exp(score - jnp.max(score, axis=-1, keepdims=True))
            total = jnp.sum(weight, axis=-1, keepdims=True)
            prob_ref[h, pl.ds(row, ROWS), :] = (weight * (1.0 / total)).astype(bf16)

    lay_bias(0)
    scores(0, 0)
    for h in range(count):
        for n in range(blocks):
            if n + 1 < blocks:
                scores(h, n + 1)
            elif h + 1 < count:
                lay_bias(h + 1)
                scores(h + 1, 0)
            weights(h, n)
        att = dot(prob_ref[h], v_s[h])
        att_low = att.astype(bf16)
        att_ref[h] = att_low
        attt_ref[h * width : (h + 1) * width, :] = jnp.transpose(att).astype(bf16)
        picked = dot(slot_s[...], att_low).astype(bf16)
        for part in range(2):
            start = part * inner + h * width
            sel_ref[:, start : start + width] = picked[part * half : (part + 1) * half]


def pass_kernel(given, passed):
    passed[...] = given[...]


def widen(rows, wide_s):
    wide_s[...] = jnp.zeros_like(wide_s)
    for e in range(rows.shape[0] // CAP):
        wide_s[e * SLOT : e * SLOT + CAP, :] = rows[e * CAP : (e + 1) * CAP]
    return wide_s[...]


def packed_width(width):
    return 2 * width + width // 2 + 128


def short_rows(width):
    each = width // 2
    for i in range(CAP - TALL):
        for k in range(4):
            yield TALL + i, slice(k * each, (k + 1) * each), 4 * i + k


def route_kernel(*refs, shards, heads):
    att_parts, w_ref = refs[:heads], refs[heads]
    (sel_in, sel_up, gain_ref, router_ref, att_t, hidden_ref, normed_ref, probs_ref, att_on
     ) = refs[heads + 1 : heads + 10]
    pieces = refs[heads + 10 : heads + 10 + shards]
    att_s, pay_s, wide_s, pack_s = refs[heads + 10 + shards :]
    head = lax.axis_index("head")
    half = att_parts[0].shape[0]
    inner = w_ref.shape[0] // heads
    for d in range(heads):
        att_s[d, 0:half, :] = att_parts[d][:, 0:inner]
        att_s[d, half : 2 * half, :] = att_parts[d][:, inner : 2 * inner]
    mixed = None
    for k in range(heads):
        term = dot(att_s[head ^ k], w_ref[k * inner : (k + 1) * inner, :])
        mixed = term if mixed is None else mixed + term
    hidden = sel_in[...].astype(f32) + widen(mixed, wide_s)
    hidden_ref[...] = hidden
    inverse = lax.rsqrt(jnp.mean(hidden * hidden, axis=-1, keepdims=True) + EPS)
    normed = hidden * inverse * gain_ref[...]
    normed_ref[...] = normed
    logits = dot_nt(normed, router_ref[...], highest)
    logits = logits - jnp.max(logits, axis=-1, keepdims=True)
    powers = jnp.exp(logits)
    probs = powers / jnp.sum(powers, axis=-1, keepdims=True)
    probs_ref[...] = probs
    gate = jnp.sum(jnp.where(chosen_of(probs.shape), probs, 0.0), axis=-1, keepdims=True)
    high = gate.astype(bf16).astype(f32)
    lane = iota((gate.shape[0], 128), 1)
    width = normed.shape[1]
    rest = gate - high
    first_gates = jnp.where(lane == 0, high, jnp.where(lane == 1, rest, 0.0))
    last_gates = jnp.where(lane == 2, high, jnp.where(lane == 3, rest, 0.0))
    pay_s[:, :width] = normed
    pay_s[:, width:] = sel_up[...].astype(f32)
    full, side = 2 * width, 2 * width + width // 2
    for e in range(shards):
        rows, packed = e * SLOT, e * TALL
        pack_s[packed : packed + TALL, :full] = pay_s[rows : rows + TALL, :]
        for row, lanes, to in short_rows(width):
            pack_s[packed + to : packed + to + 1, full:side] = pay_s[
                rows + row : rows + row + 1, lanes
            ]
        pack_s[packed : packed + 8, side:] = (
            first_gates[rows : rows + 8] + last_gates[rows + TALL : rows + SLOT]
        )
        pack_s[packed + 8 : packed + TALL, side:] = first_gates[rows + 8 : rows + TALL]
    shard = lax.axis_index("seq")
    for j in range(shards):
        first = pl.multiple_of((shard ^ j) * TALL, TALL)
        pieces[j][...] = pack_s[pl.ds(first, TALL), :].astype(bf16)
    att_on[...] = att_t[...]


def chosen_of(shape):
    expert = iota(shape, 1) * SLOT
    slot_row = iota(shape, 0)
    return (slot_row >= expert) & (slot_row < expert + SLOT)


def far_first(count):
    return sorted(range(count), key=lambda d: (-(d // 2), -d if d < 2 else d))


def by_partner(refs):
    return [ref for _, ref in sorted(zip(far_first(len(refs)), refs), key=lambda t: t[0])]


def expert_kernel(*refs, shards, heads):
    parts = by_partner(refs[:shards])
    w_in, w_out = refs[shards : shards + 2]
    chunks = refs[shards + 2 : shards + 2 + heads]
    x_ref, act_ref, pre_ref, out_ref, pay_s, gate_s, both_s = refs[shards + 2 + heads :]
    head = lax.axis_index("head")
    width = x_ref.shape[1]
    full, side = 2 * width, 2 * width + width // 2
    for j in range(shards):
        rows = j * SLOT
        part = parts[j][...].astype(f32)
        pay_s[rows : rows + TALL, :] = part[:, :full]
        pay_s[rows + TALL : rows + SLOT, :] = jnp.zeros((SLOT - TALL, full), f32)
        for row, lanes, place in short_rows(width):
            pay_s[rows + row : rows + row + 1, lanes] = part[place : place + 1, full:side]
        gate_s[rows : rows + TALL, :] = part[:, side : side + 1] + part[:, side + 1 : side + 2]
        gate_s[rows + TALL : rows + SLOT, :] = (
            part[:8, side + 2 : side + 3] + part[:8, side + 3 : side + 4]
        )
    x = pay_s[:, :width].astype(bf16)
    up = pay_s[:, width:]
    gate = gate_s[...]
    out_low = (gate * up).astype(bf16)
    pre = dot(x, w_in[...])
    cdf = 0.5 * (1.0 + lax.erf(pre * (0.5**0.5)))
    act = (pre * cdf).astype(bf16)
    slope = cdf + pre * jnp.exp(-0.5 * pre * pre) * ((2.0 * np.pi) ** (-0.5))
    pre_low = (dot_nt(out_low, w_out[...]) * slope).astype(bf16)
    both = (dot(act, w_out[...]), dot_nt(pre_low, w_in[...]))
    part = both_s.shape[2]
    for k in range(heads):
        start = k % (heads // 2) * part
        for j in range(shards):
            both_s[k, j * CAP : (j + 1) * CAP, :] = both[k // (heads // 2)][
                j * SLOT : j * SLOT + CAP, start : start + part
            ]
    for d in range(heads):
        chunks[d][...] = both_s[head ^ d].astype(bf16)
    pre_ref[...] = pre_low
    out_ref[...] = out_low
    x_ref[...] = x
    act_ref[...] = act


def expert_grad_kernel(x_ref, pre_ref, act_ref, out_ref, in_grad, out_grad):
    in_grad[0] = dot_tn(x_ref[...], pre_ref[...])
    out_grad[0] = dot_tn(act_ref[...], out_ref[...])


def sum_kernel(att_ref, *refs, heads):
    parts, att_on, pieces, sum_s = refs[:heads], refs[heads], refs[heads + 1 : -1], refs[-1]
    att_on[...] = att_ref[...]
    total = parts[0][...].astype(f32)
    for d in range(1, heads):
        total = total + parts[d][...].astype(f32)
    sum_s[...] = total
    for j, piece in enumerate(pieces):
        piece[...] = sum_s[j * CAP : (j + 1) * CAP, :].astype(bf16)


def join_kernel(*refs):
    parts, out_ref, sum_s = by_partner(refs[:-2]), refs[-2], refs[-1]
    for j, part in enumerate(parts):
        sum_s[j * CAP : (j + 1) * CAP, :] = part[...].astype(f32)
    out_ref[...] = sum_s[...].astype(bf16)


def prep_kernel(
    cot_ref, w_ref, wq_ref, wk_ref, wv_ref, low_ref, place_ref, attt_ref,
    gh_ref, stack_ref, k_ref, qt_ref, vt_ref, wout_ref, qsel_ref, ght_s, mcot_s,
):
    count, tokens, width = gh_ref.shape
    for i in range(0, tokens, 256):
        rows = pl.ds(i, 256)
        where = place_ref[rows, :].astype(f32)
        free = 1.0 - jnp.sum(where, axis=-1, keepdims=True)
        mcot_s[rows, :] = (cot_ref[rows, :].astype(f32) * free).astype(bf16)
        slots = jnp.transpose(where).astype(bf16)
        for h in range(count):
            stack_ref[h, width:, rows] = slots
    gh = dot_nt(mcot_s[...], w_ref[...]).astype(bf16)
    ght_s[...] = dot_nt(w_ref[...], mcot_s[...]).astype(bf16)
    k = dot_nt(low_ref[...], wk_ref[...]).astype(bf16)
    qt_ref[...] = dot_nt(wq_ref[...], low_ref[...]).astype(bf16) * bf16(width ** (-0.5))
    vt_ref[...] = dot_nt(wv_ref[...], low_ref[...]).astype(bf16)
    for h in range(count):
        cols = slice(h * width, (h + 1) * width)
        gh_ref[h] = gh[:, cols]
        k_ref[h] = k[:, cols]
        stack_ref[h, 0:width, :] = ght_s[cols, :]
    wout_ref[...] = dot(attt_ref[...], mcot_s[...])
    qsel_ref[...] = dot(qt_ref[...], place_ref[...]).astype(bf16)


def masked_back_kernel(
    gh_ref, stack_ref, k_ref, qt_ref, vt_ref, att_ref, prob_ref,
    dq_ref, dkt_ref, dvt_ref, offs_ref, psel_ref, acc_s, score_s, *, h,
):
    tokens, width = dq_ref.shape
    acc_s[...] = jnp.zeros_like(acc_s)
    cols = slice(h * width, (h + 1) * width)
    for i in range(0, tokens, 2 * BLOCK):
        rows = pl.ds(i, 2 * BLOCK)
        gh = gh_ref[h, rows, :]
        delta = jnp.sum(gh.astype(f32) * att_ref[h, rows, :].astype(f32), axis=-1, keepdims=True)
        grads = dot(gh, vt_ref[cols, :]) - delta
        for j in range(2):
            start = i + j * BLOCK
            first = tokens - BLOCK - start
            here = pl.ds(start, BLOCK)
            score = prob_ref[h, here, :].astype(f32) * grads[j * BLOCK : (j + 1) * BLOCK]
            acc_s[:, first : first + tokens] += score
            score_s[here, :] = score.astype(bf16)
    dq_ref[...] = dot(score_s[...], k_ref[h]) * (width ** (-0.5))
    dkt_ref[...] = dot(qt_ref[cols, :], score_s[...])
    both = dot(stack_ref[h], prob_ref[h])
    dvt_ref[...] = both[:width]
    psel_ref[...] = both[width:].astype(bf16)
    offs_ref[...] = diagonals(acc_s[...])


def diagonals(acc):
    span = acc.shape[1]
    rows = acc.shape[0] // 2
    while rows >= 8:
        acc = acc[:rows] + pltpu.roll(acc[rows:], span - rows, 1)
        rows //= 2
    total = acc[0:1]
    for r in range(1, 8):
        total = total + pltpu.roll(acc[r : r + 1], span - r, 1)
    return jnp.broadcast_to(pltpu.roll(total, BLOCK - 1, 1), (8, span))


def slot_back_kernel(*refs, heads):
    parts = refs[:heads]
    (up_ref, normed_ref, hidden_ref, probs_ref, router_ref, gain_ref, w_ref, att_ref,
     wout0_ref) = refs[heads : heads + 9]
    (dv_ref, comb_ref, small_ref, wout_ref, gh_ref, ght_ref, delta_ref, ret_s, wide_s
     ) = refs[heads + 9 :]
    head, shard = lax.axis_index("head"), lax.axis_index("seq")
    ret_s[...] = jnp.zeros_like(ret_s)
    for d in range(heads):
        part = parts[d][...].astype(f32)
        for j in range(part.shape[0] // CAP):
            first = pl.multiple_of((shard ^ j) * SLOT, SLOT)
            ret_s[head ^ d, pl.ds(first, CAP), :] = part[j * CAP : (j + 1) * CAP]
    back = [ret_s[k] for k in range(heads)]
    combined = jnp.concatenate(back[: heads // 2], axis=1)
    grad_buf = jnp.concatenate(back[heads // 2 :], axis=1)
    up = up_ref[...].astype(f32)
    hidden, normed, probs, gain = hidden_ref[...], normed_ref[...], probs_ref[...], gain_ref[...]
    chosen = chosen_of(probs.shape)
    gate = jnp.sum(jnp.where(chosen, probs, 0.0), axis=-1, keepdims=True)
    comb_ref[...] = gate * combined
    gate_grad = jnp.sum(up * combined, axis=-1, keepdims=True)
    marked = jnp.where(chosen, gate_grad, 0.0)
    logit_grad = probs * (marked - jnp.sum(marked * probs, axis=-1, keepdims=True))
    experts = probs.shape[1]
    grad = grad_buf + jnp.dot(
        logit_grad, router_ref[...], precision=highest, preferred_element_type=f32
    )
    inverse = lax.rsqrt(jnp.mean(hidden * hidden, axis=-1, keepdims=True) + EPS)
    scaled = grad * gain
    inner_sum = jnp.mean(scaled * hidden, axis=-1, keepdims=True)
    dv = inverse * scaled - hidden * (inverse * inverse * inverse * inner_sum)
    dv_ref[...] = dv
    small_ref[...] = jnp.zeros_like(small_ref)
    small_ref[0:1, :] = jnp.sum(grad * hidden * inverse, axis=0, keepdims=True)
    small_ref[8 : 8 + experts, :] = dot_tn(logit_grad, normed, highest)
    grad_low = (up + dv).astype(bf16)
    half = att_ref.shape[0]
    inner = w_ref.shape[0]
    att = jnp.concatenate(
        [att_ref[:, 0:inner].astype(f32), att_ref[:, inner : 2 * inner].astype(f32)], axis=0
    )
    att = widen(att, wide_s)
    wout_ref[...] = wout0_ref[...] + dot_tn(att.astype(bf16), grad_low)
    gh = dot_nt(grad_low, w_ref[...])
    gh_low = gh.astype(bf16)
    count = gh_ref.shape[0]
    each = inner // count
    ght_ref[...] = dot_nt(w_ref[...], grad_low).astype(bf16)
    for h in range(count):
        cols = slice(h * each, (h + 1) * each)
        gh_ref[h] = gh_low[:, cols]
        delta_ref[h] = jnp.sum(
            gh_low[:, cols].astype(f32) * att[:, cols], axis=-1, keepdims=True
        )


def sparse_back_kernel(
    gh_ref, ght_ref, delta_ref, vt_ref, k_ref, qsel_ref,
    place_ref, wq_ref, wk_ref, wv_ref, low_ref, gain_ref, small_ref, wout_ref, *refs, heads,
):
    per_head, refs = refs[: 4 * gh_ref.shape[0]], refs[4 * gh_ref.shape[0] :]
    psels, dq0s, dkt0s, dvt0s = (per_head[i :: 4] for i in range(4))
    chunks = refs[:5]
    (score_ref, send_ref, keep_ref, out_ref,
     dq_s, q_low, k_low, v_low, kt_s, vt_s, all_s) = refs[5:]
    head = lax.axis_index("head")
    count, rows, width = gh_ref.shape
    tokens = vt_ref.shape[1]
    inner = count * width
    for h in range(count):
        cols = slice(h * width, (h + 1) * width)
        grad = dot(gh_ref[h], vt_ref[cols, :])
        prob = psels[h][...]
        score = (prob.astype(f32) * (grad - delta_ref[h])).astype(bf16)
        score_ref[h] = score
        dq_s[:, cols] = dot(score, k_ref[h]) * (width ** (-0.5))
        dkt = dkt0s[h][...] + dot(qsel_ref[cols, :], score)
        dvt = dvt0s[h][...] + dot(ght_ref[cols, :], prob)
        kt_s[cols, :] = dkt.astype(bf16)
        vt_s[cols, :] = dvt.astype(bf16)
        k_low[:, cols] = jnp.transpose(dkt).astype(bf16)
        v_low[:, cols] = jnp.transpose(dvt).astype(bf16)
    spread = dot(place_ref[...], dq_s[...].astype(bf16))
    for h in range(count):
        cols = slice(h * width, (h + 1) * width)
        q_low[:, cols] = (spread[:, cols] + dq0s[h][...]).astype(bf16)
    part = tokens // heads
    half = part // 2
    own, to_1, to_2, rest_1, rest_2 = chunks
    to_1[part:, :] = jnp.zeros((EXTRA, to_1.shape[1]), bf16)
    places = (
        ((own, 0), (own, half)),
        ((to_1, 0), (rest_1, 0)),
        ((rest_2, 0), (to_2, 0)),
        ((to_1, half), (to_2, half)),
    )
    for d in range(heads):
        mine = pl.ds(pl.multiple_of((head ^ d) * part, part), part)
        rows_part = (
            dot(q_low[mine, :], wq_ref[...])
            + dot(k_low[mine, :], wk_ref[...])
            + dot(v_low[mine, :], wv_ref[...])
        ).astype(bf16)
        for n, (ref, first) in enumerate(places[d]):
            ref[first : first + half, :] = rows_part[n * half : (n + 1) * half]
    low = low_ref[...]
    total = None
    grads = (dot_tn(q_low[...], low), dot(kt_s[...], low), dot(vt_s[...], low))
    for i, (grad, w) in enumerate(zip(grads, (wq_ref, wk_ref, wv_ref))):
        all_s[i * inner : (i + 1) * inner, :] = grad
        term = jnp.sum(grad * w[...].astype(f32), axis=0, keepdims=True)
        total = term if total is None else total + term
    all_s[3 * inner :, :] = wout_ref[...]
    out_ref[...] = small_ref[...]
    out_ref[1:2, :] = total / gain_ref[...]
    to_1[part : part + 1, :] = (total / gain_ref[...]).astype(bf16)
    split_rows(all_s, 1, send_ref, keep_ref)


def is_upper(bit):
    return (lax.axis_index("seq") & bit) != 0


def split_rows(all_s, bit, send_ref, keep_ref):
    half = send_ref.shape[0]
    low, high = all_s[0:half, :], all_s[half : 2 * half, :]
    keep_ref[...] = jnp.where(is_upper(bit), high, low)
    send_ref[...] = jnp.where(is_upper(bit), low, high).astype(bf16)


def halve_kernel(keep_ref, got_ref, *refs, bit):
    send_ref, out_ref, all_s = refs[-3:]
    if len(refs) > 3:
        rest_1, got_1, rest_2, got_2, small_ref, next_1, next_2 = refs[:-3]
        half = rest_1.shape[0]
        for rest, got, onward in ((rest_1, got_2, next_1), (rest_2, got_1, next_2)):
            got_rest = got[half : 2 * half, :].astype(f32)
            onward[0:half, :] = (rest[...].astype(f32) + got_rest).astype(bf16)
        mine = small_ref[1:2, :].astype(bf16).astype(f32)
        next_2[half:, :] = jnp.zeros((EXTRA, next_2.shape[1]), bf16)
        next_2[half : half + 1, :] = (mine + got_1[2 * half : 2 * half + 1, :].astype(f32)).astype(bf16)
    all_s[...] = keep_ref[...] + got_ref[...].astype(f32)
    split_rows(all_s, bit, send_ref, out_ref)


def join_rows(mine_ref, got_ref, all_s, bit, count):
    mine, got = mine_ref[...].astype(f32), got_ref[...].astype(f32)
    all_s[0:count, :] = jnp.where(is_upper(bit), got[:count], mine[:count])
    all_s[count : 2 * count, :] = jnp.where(is_upper(bit), mine[:count], got[:count])
    all_s[2 * count :, :] = mine[count:] + got[count:]


def pair_kernel(mine_ref, got_ref, *refs, bit, count):
    out_ref, all_s = refs[-2:]
    if len(refs) > 2:
        got_1, got_2, next_1, next_2 = refs[:-2]
        half = next_1.shape[0]
        next_2[...] = got_1[0:half, :]
        next_1[...] = got_2[half:, :]
    join_rows(mine_ref, got_ref, all_s, bit, count)
    out_ref[...] = all_s[...].astype(bf16)


def final_kernel(mine_ref, got_ref, *refs, bit, count):
    gain1_ref, gain2_ref, table_ref, router_ref, all_s = refs[-5:]
    outs = refs[:-5]
    join_rows(mine_ref, got_ref, all_s, bit, count)
    inner = outs[0].shape[0]
    for i, out in enumerate(outs):
        out[...] = all_s[i * inner : (i + 1) * inner, :]
    small = all_s[2 * count :, :]
    gain1_ref[...] = small[1, :]
    gain2_ref[...] = small[0, :]
    heads, buckets = table_ref.shape
    table_ref[...] = small[2 : 2 + heads, :buckets]
    router_ref[...] = small[8 : 8 + router_ref.shape[0], :]


def bias_grad_kernel(
    score_ref, place_ref, buckets_ref, small_ref, *refs, bucket_count
):
    count = score_ref.shape[0]
    offs, out_ref, acc_s, sums_s = refs[:count], *refs[count:]
    tokens = place_ref.shape[0]
    offsets = buckets_ref.shape[1]
    out_ref[...] = small_ref[...]
    bucket_hot = (iota((bucket_count, offsets), 0) == buckets_ref[...]).astype(f32)

    def one_head(h, carry):
        acc_s[...] = jnp.zeros_like(acc_s)
        for i in range(0, tokens, BLOCK):
            first = tokens - BLOCK - i
            acc_s[:, first : first + tokens] += dot(place_ref[i : i + BLOCK, :], score_ref[h])
        sums_s[h] = diagonals(acc_s[...])
        return carry

    lax.fori_loop(0, count, one_head, 0)
    for h in range(count):
        sums = sums_s[h] + offs[h][...]
        out_ref[2 + h : 3 + h, :bucket_count] = dot_nt(sums[:, :offsets], bucket_hot, highest)[0:1]


def hidden_kernel(*refs, heads):
    att_parts, w_ref, x_ref, out_ref, att_s = refs[:heads], *refs[heads:]
    head = lax.axis_index("head")
    tokens = x_ref.shape[0]
    inner = att_parts[0].shape[0]
    for d in range(heads):
        mine = pl.ds(pl.multiple_of((head ^ d) * inner, inner), inner)
        att_s[mine, :] = att_parts[d][...]

    def block(i, carry):
        rows = pl.ds(pl.multiple_of(i * 256, 256), 256)
        out_ref[rows, :] = x_ref[rows, :].astype(f32) + dot_tn(att_s[:, rows], w_ref[...])
        return carry

    lax.fori_loop(0, tokens // 256, block, 0)


def output_kernel(hidden_ref, place_ref, comb_ref, out_ref):
    high, rest = split_two(comb_ref[...])

    def block(i, carry):
        rows = pl.ds(pl.multiple_of(i * 256, 256), 256)
        where = place_ref[rows, :]
        out_ref[rows, :] = hidden_ref[rows, :] + (dot(where, high) + dot(where, rest))
        return carry

    lax.fori_loop(0, hidden_ref.shape[0] // 256, block, 0)


def first_norm_kernel(
    own, got_1, got_2, last_1, last_2, next_2, small_ref,
    x_ref, cot_ref, place_ref, dv_ref, gain_ref, keep_ref, got_ref, out_ref, sum_ref,
):
    half = last_1.shape[0]
    high, rest = split_two(dv_ref[...])
    for first, near, far in ((0, got_1, last_2), (half, got_2, last_1)):
        rows = pl.ds(first, half)
        grad = own[rows, :].astype(f32) + near[0:half, :].astype(f32)
        grad = grad + far[0:half, :].astype(f32)
        x = x_ref[rows, :].astype(f32)
        inverse = lax.rsqrt(jnp.mean(x * x, axis=-1, keepdims=True) + EPS)
        scaled = grad * gain_ref[...]
        inner_sum = jnp.mean(scaled * x, axis=-1, keepdims=True)
        where = place_ref[rows, :]
        hidden_grad = cot_ref[rows, :].astype(f32) + (dot(where, high) + dot(where, rest))
        out_ref[rows, :] = (
            hidden_grad + inverse * scaled - x * (inverse * inverse * inverse * inner_sum)
        ).astype(bf16)
    count = keep_ref.shape[0]
    sum_ref[0:count, :] = (keep_ref[...] + got_ref[...].astype(f32)).astype(bf16)
    gain1 = next_2[half:, :].astype(f32)[0:1] + last_2[half:, :].astype(f32)[0:1]
    small = small_ref[...]
    sum_ref[count:, :] = jnp.where(iota(small.shape, 0) == 1, gain1, small).astype(bf16)


def spread_near_kernel(own, got_1, got_2, out_ref, token, wide_s, sems):
    head = lax.axis_index("head")
    part = own.shape[0]
    copies = []
    for d, piece in enumerate((own, got_1, got_2)):
        wide_s[d] = piece[...].astype(f32)
        mine = pl.ds(pl.multiple_of((head ^ d) * part, part), part)
        copies.append(pltpu.make_async_copy(wide_s.at[d], out_ref.at[mine], sems.at[d]))
        copies[-1].start()
    token[...] = jnp.zeros_like(token)
    for copy in copies:
        copy.wait()


def spread_far_kernel(last_1, last_2, given, out_ref, wide_s, sem):
    head = lax.axis_index("head")
    half = last_1.shape[0]
    wide_s[0:half, :] = last_2[...].astype(f32)
    wide_s[half:, :] = last_1[...].astype(f32)
    mine = pl.ds(pl.multiple_of((head ^ 3) * 2 * half, 2 * half), 2 * half)
    copy = pltpu.make_async_copy(wide_s, out_ref.at[mine], sem)
    copy.start()
    copy.wait()


def swap(x, axis, d):
    size = lax.axis_size(axis)
    return lax.ppermute(x, axis, [(i, i ^ d) for i in range(size)])


def share(x, axis):
    return [x] + [swap(x, axis, d) for d in range(1, lax.axis_size(axis))]


def trade(pieces, axis):
    return lax.all_to_all(pieces, axis, split_axis=0, concat_axis=0, tiled=True)


def swap_all(pieces, axis):
    return [pieces[0]] + [swap(pieces[d], axis, d) for d in range(1, len(pieces))]


def bits_of(axis):
    return [b for b in (1 << i for i in range(16)) if b < lax.axis_size(axis)]


def halve(send, keep, bit, after, onward=()):
    rows, width = keep.shape
    outs = []
    if onward:
        half = onward[0].shape[0]
        outs = [shape_of(half, width, bf16), shape_of(half + EXTRA, width, bf16)]
    return call(
        partial(halve_kernel, bit=bit),
        outs + [shape_of(rows // 2, width, bf16), shape_of(rows // 2, width, f32)],
        (keep, swap(send, "seq", bit // 2)) + tuple(onward),
        scratch=[pltpu.VMEM((rows, width), f32)],
        name="halve",
        after=after,
        token=True,
    )


def pair(now, small_rows, bit, after, onward=()):
    rows, width = now.shape
    count = rows - small_rows
    outs = [shape_of(onward[0].shape[0] // 2, width, bf16)] * 2 if onward else []
    return call(
        partial(pair_kernel, bit=bit, count=count),
        outs + [shape_of(rows + count, width, bf16)],
        (now, swap(now, "seq", bit)) + tuple(onward),
        scratch=[pltpu.VMEM((rows + count, width), f32)],
        name="pair",
        after=after,
        token=True,
    )


def on_device(
    layer_input, cotangent, norm1_gain, w_query, w_key, w_value, w_attn_out, bias_table,
    norm2_gain, w_router, w_expert_in, w_expert_out, expert_ids, slot_ids, buckets,
):
    tokens, width = layer_input.shape
    shards = lax.axis_size("seq")
    heads = lax.axis_size("head")
    bucket_count, count = bias_table.shape
    inner = w_query.shape[1]
    each = inner // count
    experts = w_router.shape[1]
    rows, filled = experts * SLOT, experts * CAP
    hidden_units = w_expert_in.shape[2]
    part = tokens // heads
    split = 2 * width // heads
    span = 2 * tokens
    params = pltpu.CompilerParams(vmem_limit_bytes=VMEM_LIMIT if rows <= 256 else VMEM_ALL)

    ids = expert_ids.reshape(1, tokens)
    slots = slot_ids.reshape(1, tokens)
    bucket_row = buckets.reshape(1, -1)
    wq_t, wk_t, wv_t = jnp.transpose(w_query), jnp.transpose(w_key), jnp.transpose(w_value)
    router_t, table_t = jnp.transpose(w_router), jnp.transpose(bias_table)
    w_in = w_expert_in.reshape(width, hidden_units)
    w_out = w_expert_out.reshape(hidden_units, width)

    w_mix = share(w_attn_out, "head")

    low, prob, att, att_t, att_sel = pl.pallas_call(
        attend_kernel,
        out_shape=(
            shape_of(tokens, width, bf16),
            jax.ShapeDtypeStruct((count, tokens, tokens), bf16),
            jax.ShapeDtypeStruct((count, tokens, each), bf16),
            shape_of(inner, tokens, bf16),
            shape_of(filled // 2, 2 * inner, bf16),
        ),
        in_specs=[spec(pltpu.HBM)] * 9,
        out_specs=(spec(pltpu.VMEM),) * 5,
        scratch_shapes=[
            pltpu.VMEM((count, tokens, each), bf16),
            pltpu.VMEM((inner, tokens), bf16),
            pltpu.VMEM((count, tokens, each), bf16),
            pltpu.VMEM((8, span), f32),
            pltpu.VMEM((2, BLOCK, span), f32),
            pltpu.VMEM((filled, tokens), bf16),
            pltpu.VMEM((2, 2 * BLOCK, tokens), f32),
            pltpu.VMEM((tokens, width), bf16),
            pltpu.VMEM((width,), f32),
            pltpu.VMEM((inner, width), bf16),
            pltpu.VMEM((inner, width), bf16),
            pltpu.VMEM((inner, width), bf16),
            pltpu.VMEM((count, bucket_count), f32),
            pltpu.VMEM((1, span - 1), jnp.int32),
            pltpu.VMEM((1, tokens), jnp.int32),
            pltpu.VMEM((1, tokens), jnp.int32),
            pltpu.SemaphoreType.DMA((9,)),
        ],
        compiler_params=params,
        cost_estimate=NO_COST,
        name="attend",
    )(
        *(
            pltpu.with_memory_space_constraint(a, pltpu.HBM)
            for a in (layer_input, norm1_gain, wq_t, wk_t, wv_t, table_t, bucket_row, ids, slots)
        )
    )

    (att_sel,) = call(
        pass_kernel,
        [shape_of(filled // 2, 2 * inner, bf16)],
        (att_sel,),
        name="pass",
        after=(w_mix[1],),
    )
    sel_parts = share(att_sel, "head")
    sel_in, sel_up, place, place_c, x_c, cot_c, w_full = call(
        partial(place_kernel, heads=heads),
        [
            shape_of(rows, width, bf16),
            shape_of(rows, width, bf16),
            shape_of(tokens, rows, bf16),
            shape_of(part, rows, bf16),
            shape_of(part, width, bf16),
            shape_of(part, width, bf16),
            shape_of(heads * inner, width, bf16),
        ],
        (layer_input, cotangent, ids, slots) + tuple(w_mix),
        scratch=[pltpu.VMEM((tokens, rows), f32)],
        moved=12 * 2**20,
        name="place",
        after=(att_sel,),
    )
    routed = call(
        partial(route_kernel, shards=shards, heads=heads),
        [
            shape_of(rows, width, f32),
            shape_of(rows, width, f32),
            shape_of(rows, experts, f32),
            shape_of(inner, tokens, bf16),
        ]
        + [shape_of(TALL, packed_width(width), bf16)] * shards,
        tuple(sel_parts) + (w_full, sel_in, sel_up, norm2_gain, router_t, att_t),
        scratch=[
            pltpu.VMEM((heads, filled, inner), bf16),
            pltpu.VMEM((rows, 2 * width), f32),
            pltpu.VMEM((rows, width), f32),
            pltpu.VMEM((shards * TALL, packed_width(width)), f32),
        ],
        name="route",
    )
    hidden_sel, normed_sel, probs, att_on = routed[:4]
    pay_parts = swap_all(routed[4:], "seq")
    att_parts = [att_t] + [swap(att_on, "head", d) for d in range(1, heads - 1)]

    def masked_back(h, after):
        return call(
            partial(masked_back_kernel, h=h),
            [
                shape_of(tokens, each, f32),
                shape_of(each, tokens, f32),
                shape_of(each, tokens, f32),
                shape_of(8, span, f32),
                shape_of(rows, tokens, bf16),
            ],
            (gh, stack, k_rows, q_t, v_t, att, prob),
            scratch=[pltpu.VMEM((BLOCK, span), f32), pltpu.VMEM((tokens, tokens), bf16)],
            name="masked_back",
            after=after,
            moved=11 * 2**20,
            token=True,
        )

    done = call(
        partial(expert_kernel, shards=shards, heads=heads),
        [shape_of(filled, split, bf16)] * heads
        + [
            shape_of(rows, width, bf16),
            shape_of(rows, hidden_units, bf16),
            shape_of(rows, hidden_units, bf16),
            shape_of(rows, width, bf16),
        ],
        tuple(pay_parts[d] for d in far_first(shards)) + (w_in, w_out),
        scratch=[
            pltpu.VMEM((rows, 2 * width), f32),
            pltpu.VMEM((rows, 1), f32),
            pltpu.VMEM((heads, filled, split), f32),
        ],
        name="expert",
        after=tuple(att_parts[1:]),
        token=True,
    )
    x_rows, act, pre_low, out_low, token = done[heads:]
    gh, stack, k_rows, q_t, v_t, wout0, q_sel, token = call(
        prep_kernel,
        [
            jax.ShapeDtypeStruct((count, tokens, each), bf16),
            jax.ShapeDtypeStruct((count, each + rows, tokens), bf16),
            jax.ShapeDtypeStruct((count, tokens, each), bf16),
            shape_of(inner, tokens, bf16),
            shape_of(inner, tokens, bf16),
            shape_of(inner, width, f32),
            shape_of(inner, rows, bf16),
        ],
        (cotangent, w_attn_out, wq_t, wk_t, wv_t, low, place, att_t),
        scratch=[pltpu.VMEM((inner, tokens), bf16), pltpu.VMEM((tokens, width), bf16)],
        name="prep",
        after=(token,),
        moved=8 * 2**20,
        token=True,
    )

    masked = []
    for h in range(count - 2):
        masked.append(masked_back(h, (token,)))
        token = masked[-1][-1]
    returned = call(
        partial(sum_kernel, heads=heads),
        [shape_of(inner, tokens, bf16)] + [shape_of(CAP, split, bf16)] * shards,
        [att_t] + swap_all(done[:heads], "head"),
        scratch=[pltpu.VMEM((filled, split), f32)],
        name="sum",
        after=(token,),
        token=True,
    )
    masked.append(masked_back(count - 2, (returned[-1],)))
    att_parts.append(swap(returned[0], "head", heads - 1))
    answers = swap_all(returned[1:-1], "seq")
    joined, token = call(
        join_kernel,
        [shape_of(filled, split, bf16)],
        [answers[d] for d in far_first(shards)],
        scratch=[pltpu.VMEM((filled, split), f32)],
        name="join",
        after=(masked[-1][-1], att_parts[-1]),
        token=True,
    )
    masked.append(masked_back(count - 1, (token,)))
    full_parts = share(joined, "head")

    small_rows = 8 + -(-experts // 8) * 8
    dv_sel, comb_sel, small, wout_part, gh_sel, ght_sel, delta_sel = call(
        partial(slot_back_kernel, heads=heads),
        [
            shape_of(rows, width, f32),
            shape_of(rows, width, f32),
            shape_of(small_rows, width, f32),
            shape_of(inner, width, f32),
            jax.ShapeDtypeStruct((count, rows, each), bf16),
            shape_of(inner, rows, bf16),
            jax.ShapeDtypeStruct((count, rows, 1), f32),
        ],
        tuple(full_parts)
        + (sel_up, normed_sel, hidden_sel, probs, router_t, norm2_gain)
        + (w_attn_out, att_sel, wout0),
        scratch=[pltpu.VMEM((heads, rows, split), f32), pltpu.VMEM((rows, inner), f32)],
        name="slot_back",
        after=(masked[-1][-1],),
    )

    back = call(
        partial(sparse_back_kernel, heads=heads),
        [shape_of(part, width, bf16), shape_of(part + EXTRA, width, bf16)]
        + [shape_of(part, width, bf16)]
        + [shape_of(part // 2, width, bf16)] * 2
        + [
            jax.ShapeDtypeStruct((count, rows, tokens), bf16),
            shape_of(2 * inner, width, bf16),
            shape_of(2 * inner, width, f32),
            shape_of(small_rows, width, f32),
        ],
        (gh_sel, ght_sel, delta_sel, v_t, k_rows, q_sel, place)
        + (wq_t, wk_t, wv_t, low, norm1_gain, small, wout_part)
        + tuple(a for m in masked for a in (m[4], m[0], m[1], m[2])),
        scratch=[
            pltpu.VMEM((rows, inner), f32),
            pltpu.VMEM((tokens, inner), bf16),
            pltpu.VMEM((tokens, inner), bf16),
            pltpu.VMEM((tokens, inner), bf16),
            pltpu.VMEM((inner, tokens), bf16),
            pltpu.VMEM((inner, tokens), bf16),
            pltpu.VMEM((4 * inner, width), f32),
        ],
        name="sparse_back",
    )
    score_sel, send, keep, small = back[5:]
    own, to_1, to_2, rest_1, rest_2 = back[:5]
    got_1, got_2 = swap(to_1, "head", 1), swap(to_2, "head", 2)

    bits = bits_of("seq")
    send, keep, token = halve(send, keep, bits[1], ())
    small_part = small
    small, token = call(
        partial(bias_grad_kernel, bucket_count=bucket_count),
        [shape_of(small_rows, width, f32)],
        (score_sel, place, bucket_row, small) + tuple(m[3] for m in masked),
        scratch=[pltpu.VMEM((BLOCK, span), f32), pltpu.VMEM((count, 8, span), f32)],
        name="bias_grad",
        after=(token,),
        moved=16 * 2**20,
        token=True,
    )
    next_1, next_2, send, keep, token = halve(
        send, keep, bits[2], (token,), (rest_1, got_1, rest_2, got_2, small_part)
    )
    last_1, last_2 = swap(next_1, "head", 1), swap(next_2, "head", 2)
    w_in_grad, w_out_grad, token = call(
        expert_grad_kernel,
        [
            jax.ShapeDtypeStruct(w_expert_in.shape, f32),
            jax.ShapeDtypeStruct(w_expert_out.shape, f32),
        ],
        (x_rows, pre_low, act, out_low),
        name="expert_grad",
        after=(token,),
        moved=10 * 2**20,
        token=True,
    )
    hidden, token = call(
        partial(hidden_kernel, heads=heads),
        [shape_of(tokens, width, f32)],
        tuple(att_parts) + (w_full, layer_input),
        scratch=[pltpu.VMEM((heads * inner, tokens), bf16)],
        name="hidden",
        after=(token,),
        moved=6 * 2**20,
        token=True,
    )
    for bit in bits[3:]:
        send, keep, token = halve(send, keep, bit, (token,))

    grad_part, weights, token = call(
        first_norm_kernel,
        [shape_of(part, width, bf16), shape_of(keep.shape[0] + small_rows, width, bf16)],
        (own, got_1, got_2, last_1, last_2, next_2, small)
        + (x_c, cot_c, place_c, dv_sel, norm1_gain)
        + (keep, swap(send, "seq", bits[-1])),
        name="first_norm",
        after=(token,),
        token=True,
    )
    grad_1, grad_2 = swap(grad_part, "head", 1), swap(grad_part, "head", 2)
    layer_output, token = call(
        output_kernel,
        [shape_of(tokens, width, f32)],
        (hidden, place, comb_sel),
        name="output",
        after=(token,),
        moved=10 * 2**20,
        token=True,
    )
    for bit in reversed(bits[3:]):
        weights, token = pair(weights, small_rows, bit, (token,))
    next_1, next_2, weights, token = pair(
        weights, small_rows, bits[2], (token,), (grad_1, grad_2)
    )
    grad_3 = (swap(next_1, "head", 1), swap(next_2, "head", 2))
    near, token = pl.pallas_call(
        spread_near_kernel,
        out_shape=(shape_of(tokens, width, f32), shape_of(8, 128, f32)),
        in_specs=[spec(pltpu.VMEM)] * 3,
        out_specs=(spec(pltpu.HBM), spec(pltpu.VMEM)),
        scratch_shapes=[pltpu.VMEM((3, part, width), f32), pltpu.SemaphoreType.DMA((3,))],
        compiler_params=params,
        cost_estimate=pl.CostEstimate(flops=1, bytes_accessed=5 * 2**20, transcendentals=0),
        name="spread_near",
    )(grad_part, grad_1, grad_2)
    weights, token = pair(weights, small_rows, bits[1], grad_3 + (token,))
    last = call(
        partial(final_kernel, bit=bits[0], count=2 * inner),
        [shape_of(inner, width, f32)] * 4
        + [
            jax.ShapeDtypeStruct((width,), f32),
            jax.ShapeDtypeStruct((width,), f32),
            shape_of(count, bucket_count, f32),
            shape_of(experts, width, f32),
        ],
        (weights, swap(weights, "seq", bits[0])),
        scratch=[pltpu.VMEM((4 * inner + small_rows, width), f32)],
        name="weights_out",
    )
    weight_sums = last[:4]
    gain1_sum, gain2_sum, table_sum, router_sum = last[4:]
    input_grad = pl.pallas_call(
        spread_far_kernel,
        out_shape=shape_of(tokens, width, f32),
        in_specs=[spec(pltpu.VMEM), spec(pltpu.VMEM), spec(pltpu.HBM)],
        out_specs=spec(pltpu.HBM),
        scratch_shapes=[pltpu.VMEM((part, width), f32), pltpu.SemaphoreType.DMA(())],
        input_output_aliases={2: 0},
        compiler_params=params,
        cost_estimate=NO_COST,
        name="spread_far",
    )(*grad_3, near)

    return (
        layer_output,
        input_grad,
        gain1_sum,
        jnp.transpose(weight_sums[0]),
        jnp.transpose(weight_sums[1]),
        jnp.transpose(weight_sums[2]),
        weight_sums[3],
        jnp.transpose(table_sum),
        gain2_sum,
        jnp.transpose(router_sum),
        w_in_grad,
        w_out_grad,
    )


def solution(mesh):
    return jax.shard_map(
        on_device,
        mesh=mesh,
        in_specs=(
            P("seq", None),
            P("seq", None),
            P(),
            P(None, "head"),
            P(None, "head"),
            P(None, "head"),
            P("head", None),
            P(None, "head"),
            P(),
            P(),
            P("seq", None, "head"),
            P("seq", "head", None),
            P("seq"),
            P("seq"),
            P(),
        ),
        out_specs=(
            P("seq", None),
            P("seq", None),
            P(),
            P(None, "head"),
            P(None, "head"),
            P(None, "head"),
            P("head", None),
            P(None, "head"),
            P(),
            P(),
            P("seq", None, "head"),
            P("seq", "head", None),
        ),
        check_vma=False,
    )
```

```python
from functools import partial

import jax
import jax.numpy as jnp
import numpy as np
from jax import lax
from jax.experimental import pallas as pl
from jax.experimental.pallas import tpu as pltpu
from jax.sharding import PartitionSpec as P

CAP = 20
SLOT = 24
EPS = 1e-06
BLOCK = 128
ROWS = 8
EXTRA = 16
TALL = 16
VMEM_LIMIT = 26 * 1024 * 1024
VMEM_ALL = 60 * 1024 * 1024
NO_COST = pl.CostEstimate(flops=1, bytes_accessed=1, transcendentals=0)

f32 = jnp.float32
bf16 = jnp.bfloat16
highest = lax.Precision.HIGHEST


def dot(a, b):
    return jnp.dot(a, b, preferred_element_type=f32)


def dot_nt(a, b, precision=None):
    return lax.dot_general(
        a, b, (((1,), (1,)), ((), ())), precision=precision, preferred_element_type=f32
    )


def dot_tn(a, b, precision=None):
    return lax.dot_general(
        a, b, (((0,), (0,)), ((), ())), precision=precision, preferred_element_type=f32
    )


def iota(shape, dim):
    return lax.broadcasted_iota(jnp.int32, shape, dim)


def split_two(v):
    high = v.astype(bf16)
    return high, (v - high.astype(f32)).astype(bf16)


def shape_of(rows, cols, dtype):
    return jax.ShapeDtypeStruct((rows, cols), dtype)


def spec(memory):
    return pl.BlockSpec(memory_space=memory)


def call(kernel, outs, args, scratch=(), name=None, after=(), moved=1, token=False):
    outs, args = tuple(outs), tuple(args)
    held = sum(int(np.prod(a.shape)) * np.dtype(a.dtype).itemsize for a in args + outs)
    if token:
        outs += (shape_of(8, 128, f32),)
    first_out = len(args) + len(after)

    def body(*refs):
        results = refs[first_out : first_out + len(outs)]
        if token:
            results[-1][...] = jnp.zeros((8, 128), f32)
            results = results[:-1]
        kernel(*refs[: len(args)], *results, *refs[first_out + len(outs) :])

    return pl.pallas_call(
        body,
        out_shape=outs,
        in_specs=[spec(pltpu.VMEM)] * len(args) + [spec(pl.ANY)] * len(after),
        out_specs=tuple(spec(pltpu.VMEM) for _ in outs),
        scratch_shapes=list(scratch),
        compiler_params=pltpu.CompilerParams(
            vmem_limit_bytes=VMEM_LIMIT if 2 * held < VMEM_LIMIT else VMEM_ALL
        ),
        cost_estimate=pl.CostEstimate(flops=1, bytes_accessed=moved, transcendentals=0),
        name=name,
    )(*args, *after)


def slot_rows(ids, slots, rows, each):
    cell = jnp.where(slots < CAP, ids * each + slots, -1)
    return (iota((rows, cell.shape[1]), 0) == cell).astype(f32)


def place_kernel(x_ref, cot_ref, ids_ref, slots_ref, *refs, heads):
    w_parts = refs[:heads]
    sel_in, sel_up, place, place_c, x_c, cot_c, w_ref, place_s = refs[heads:]
    head = lax.axis_index("head")
    part = x_c.shape[0]
    slot_hot = slot_rows(ids_ref[...], slots_ref[...], sel_in.shape[0], SLOT)
    place_s[...] = jnp.transpose(slot_hot)
    slot_low = slot_hot.astype(bf16)
    sel_in[...] = dot(slot_low, x_ref[...]).astype(bf16)
    sel_up[...] = dot(slot_low, cot_ref[...]).astype(bf16)
    place[...] = place_s[...].astype(bf16)
    mine = pl.ds(pl.multiple_of(head * part, part), part)
    place_c[...] = place_s[mine, :].astype(bf16)
    x_c[...] = x_ref[mine, :]
    cot_c[...] = cot_ref[mine, :]
    inner = w_parts[0].shape[0]
    for d in range(heads):
        rows = pl.ds(pl.multiple_of((head ^ d) * inner, inner), inner)
        w_ref[rows, :] = w_parts[d][...]


def attend_kernel(*refs):
    given, refs = refs[:9], refs[9:]
    low_ref, prob_ref, att_ref, attt_ref, sel_ref = refs[:5]
    q_s, kt_s, v_s, bias_s, skew_s, slot_s, score_s = refs[5:12]
    here, sems = refs[12:21], refs[21]
    x_ref, gain_ref, wq_ref, wk_ref, wv_ref, table_ref, buckets_ref, ids_ref, slots_ref = here
    copies = [
        pltpu.make_async_copy(far, near, sems.at[i])
        for i, (far, near) in enumerate(zip(given, here))
    ]
    tokens = x_ref.shape[0]
    inner = wq_ref.shape[0]
    count = q_s.shape[0]
    width = inner // count
    span = skew_s.shape[2]
    tall = 2 * BLOCK
    for copy in copies:
        copy.start()
    for copy in copies[5:]:
        copy.wait()
    slot_s[...] = slot_rows(ids_ref[...], slots_ref[...], slot_s.shape[0], CAP).astype(bf16)
    offsets = buckets_ref.shape[1]
    bucket_hot = (iota((table_ref.shape[1], offsets), 0) == buckets_ref[...]).astype(f32)
    bias_s[...] = jnp.zeros_like(bias_s)
    bias_s[:count, :offsets] = jnp.dot(
        table_ref[...], bucket_hot, precision=highest, preferred_element_type=f32
    )
    for copy in copies[:2]:
        copy.wait()
    for i in range(0, tokens, 256):
        rows = pl.ds(i, 256)
        x = x_ref[rows, :].astype(f32)
        inverse = lax.rsqrt(jnp.mean(x * x, axis=-1, keepdims=True) + EPS)
        low_ref[rows, :] = (x * inverse * gain_ref[...]).astype(bf16)
    for copy in copies[2:5]:
        copy.wait()
    low = low_ref[...]
    q = dot_nt(low, wq_ref[...]).astype(bf16) * bf16(width ** (-0.5))
    kt_s[...] = dot_nt(wk_ref[...], low).astype(bf16)
    v = dot_nt(low, wv_ref[...]).astype(bf16)
    for h in range(count):
        cols = slice(h * width, (h + 1) * width)
        q_s[h] = q[:, cols]
        v_s[h] = v[:, cols]

    blocks = tokens // tall
    half = sel_ref.shape[0]

    def lay_bias(h):
        skew_s[h % 2] = pltpu.roll(
            jnp.broadcast_to(bias_s[h : h + 1, :], skew_s.shape[1:]),
            span - (BLOCK - 1), 1, stride=1, stride_axis=0,
        )

    def scores(h, n):
        score_s[n % 2] = dot(
            q_s[h, pl.ds(n * tall, tall), :], kt_s[h * width : (h + 1) * width, :]
        )

    def weights(h, n):
        for j in range(0, tall, ROWS):
            row = n * tall + j
            first = tokens - BLOCK - row // BLOCK * BLOCK
            bias = skew_s[h % 2, j % BLOCK : j % BLOCK + ROWS, first : first + tokens]
            score = score_s[n % 2, j : j + ROWS, :] + bias
            weight = jnp.exp(score - jnp.max(score, axis=-1, keepdims=True))
            total = jnp.sum(weight, axis=-1, keepdims=True)
            prob_ref[h, pl.ds(row, ROWS), :] = (weight * (1.0 / total)).astype(bf16)

    lay_bias(0)
    scores(0, 0)
    for h in range(count):
        for n in range(blocks):
            if n + 1 < blocks:
                scores(h, n + 1)
            elif h + 1 < count:
                lay_bias(h + 1)
                scores(h + 1, 0)
            weights(h, n)
        att = dot(prob_ref[h], v_s[h])
        att_low = att.astype(bf16)
        att_ref[h] = att_low
        attt_ref[h * width : (h + 1) * width, :] = jnp.transpose(att).astype(bf16)
        picked = dot(slot_s[...], att_low).astype(bf16)
        for part in range(2):
            start = part * inner + h * width
            sel_ref[:, start : start + width] = picked[part * half : (part + 1) * half]


def pass_kernel(given, passed):
    passed[...] = given[...]


def widen(rows, wide_s):
    wide_s[...] = jnp.zeros_like(wide_s)
    for e in range(rows.shape[0] // CAP):
        wide_s[e * SLOT : e * SLOT + CAP, :] = rows[e * CAP : (e + 1) * CAP]
    return wide_s[...]


def packed_width(width):
    return 2 * width + width // 2 + 128


def short_rows(width):
    each = width // 2
    for i in range(CAP - TALL):
        for k in range(4):
            yield TALL + i, slice(k * each, (k + 1) * each), 4 * i + k


def route_kernel(*refs, shards, heads):
    att_parts, w_ref = refs[:heads], refs[heads]
    (sel_in, sel_up, gain_ref, router_ref, att_t, hidden_ref, normed_ref, probs_ref, att_on
     ) = refs[heads + 1 : heads + 10]
    pieces = refs[heads + 10 : heads + 10 + shards]
    att_s, pay_s, wide_s, pack_s = refs[heads + 10 + shards :]
    head = lax.axis_index("head")
    half = att_parts[0].shape[0]
    inner = w_ref.shape[0] // heads
    for d in range(heads):
        att_s[d, 0:half, :] = att_parts[d][:, 0:inner]
        att_s[d, half : 2 * half, :] = att_parts[d][:, inner : 2 * inner]
    mixed = None
    for k in range(heads):
        term = dot(att_s[head ^ k], w_ref[k * inner : (k + 1) * inner, :])
        mixed = term if mixed is None else mixed + term
    hidden = sel_in[...].astype(f32) + widen(mixed, wide_s)
    hidden_ref[...] = hidden
    inverse = lax.rsqrt(jnp.mean(hidden * hidden, axis=-1, keepdims=True) + EPS)
    normed = hidden * inverse * gain_ref[...]
    normed_ref[...] = normed
    logits = dot_nt(normed, router_ref[...], highest)
    logits = logits - jnp.max(logits, axis=-1, keepdims=True)
    powers = jnp.exp(logits)
    probs = powers / jnp.sum(powers, axis=-1, keepdims=True)
    probs_ref[...] = probs
    gate = jnp.sum(jnp.where(chosen_of(probs.shape), probs, 0.0), axis=-1, keepdims=True)
    high = gate.astype(bf16).astype(f32)
    lane = iota((gate.shape[0], 128), 1)
    width = normed.shape[1]
    rest = gate - high
    first_gates = jnp.where(lane == 0, high, jnp.where(lane == 1, rest, 0.0))
    last_gates = jnp.where(lane == 2, high, jnp.where(lane == 3, rest, 0.0))
    pay_s[:, :width] = normed
    pay_s[:, width:] = sel_up[...].astype(f32)
    full, side = 2 * width, 2 * width + width // 2
    for e in range(shards):
        rows, packed = e * SLOT, e * TALL
        pack_s[packed : packed + TALL, :full] = pay_s[rows : rows + TALL, :]
        for row, lanes, to in short_rows(width):
            pack_s[packed + to : packed + to + 1, full:side] = pay_s[
                rows + row : rows + row + 1, lanes
            ]
        pack_s[packed : packed + 8, side:] = (
            first_gates[rows : rows + 8] + last_gates[rows + TALL : rows + SLOT]
        )
        pack_s[packed + 8 : packed + TALL, side:] = first_gates[rows + 8 : rows + TALL]
    shard = lax.axis_index("seq")
    for j in range(shards):
        first = pl.multiple_of((shard ^ j) * TALL, TALL)
        pieces[j][...] = pack_s[pl.ds(first, TALL), :].astype(bf16)
    att_on[...] = att_t[...]


def chosen_of(shape):
    expert = iota(shape, 1) * SLOT
    slot_row = iota(shape, 0)
    return (slot_row >= expert) & (slot_row < expert + SLOT)


def far_first(count):
    near = list(range(2, count // 2)) + [d for d in (1, 0) if d < count]
    return list(range(count // 2, count)) + [d for d in near if d < count // 2]


def by_partner(refs):
    return [ref for _, ref in sorted(zip(far_first(len(refs)), refs), key=lambda t: t[0])]


def expert_kernel(*refs, shards, heads):
    parts = by_partner(refs[:shards])
    w_in, w_out = refs[shards : shards + 2]
    chunks = refs[shards + 2 : shards + 2 + heads]
    x_ref, act_ref, pre_ref, out_ref, pay_s, gate_s, both_s = refs[shards + 2 + heads :]
    head = lax.axis_index("head")
    width = x_ref.shape[1]
    full, side = 2 * width, 2 * width + width // 2
    for j in range(shards):
        rows = j * SLOT
        part = parts[j][...].astype(f32)
        pay_s[rows : rows + TALL, :] = part[:, :full]
        pay_s[rows + TALL : rows + SLOT, :] = jnp.zeros((SLOT - TALL, full), f32)
        for row, lanes, place in short_rows(width):
            pay_s[rows + row : rows + row + 1, lanes] = part[place : place + 1, full:side]
        gate_s[rows : rows + TALL, :] = part[:, side : side + 1] + part[:, side + 1 : side + 2]
        gate_s[rows + TALL : rows + SLOT, :] = (
            part[:8, side + 2 : side + 3] + part[:8, side + 3 : side + 4]
        )
    x = pay_s[:, :width].astype(bf16)
    up = pay_s[:, width:]
    gate = gate_s[...]
    out_low = (gate * up).astype(bf16)
    pre = dot(x, w_in[...])
    cdf = 0.5 * (1.0 + lax.erf(pre * (0.5**0.5)))
    act = (pre * cdf).astype(bf16)
    slope = cdf + pre * jnp.exp(-0.5 * pre * pre) * ((2.0 * np.pi) ** (-0.5))
    pre_low = (dot_nt(out_low, w_out[...]) * slope).astype(bf16)
    both = (dot(act, w_out[...]), dot_nt(pre_low, w_in[...]))
    part = both_s.shape[2]
    for k in range(heads):
        start = k % (heads // 2) * part
        for j in range(shards):
            both_s[k, j * CAP : (j + 1) * CAP, :] = both[k // (heads // 2)][
                j * SLOT : j * SLOT + CAP, start : start + part
            ]
    for d in range(heads):
        chunks[d][...] = both_s[head ^ d].astype(bf16)
    pre_ref[...] = pre_low
    out_ref[...] = out_low
    x_ref[...] = x
    act_ref[...] = act


def expert_grad_kernel(x_ref, pre_ref, act_ref, out_ref, in_grad, out_grad):
    in_grad[0] = dot_tn(x_ref[...], pre_ref[...])
    out_grad[0] = dot_tn(act_ref[...], out_ref[...])


def sum_kernel(att_ref, *refs, heads):
    parts, att_on, pieces, sum_s = refs[:heads], refs[heads], refs[heads + 1 : -1], refs[-1]
    att_on[...] = att_ref[...]
    total = parts[0][...].astype(f32)
    for d in range(1, heads):
        total = total + parts[d][...].astype(f32)
    sum_s[...] = total
    for j, piece in enumerate(pieces):
        piece[...] = sum_s[j * CAP : (j + 1) * CAP, :].astype(bf16)


def join_kernel(*refs):
    parts, out_ref, sum_s = by_partner(refs[:-2]), refs[-2], refs[-1]
    for j, part in enumerate(parts):
        sum_s[j * CAP : (j + 1) * CAP, :] = part[...].astype(f32)
    out_ref[...] = sum_s[...].astype(bf16)


def prep_kernel(
    cot_ref, w_ref, wq_ref, wk_ref, wv_ref, low_ref, place_ref, attt_ref,
    gh_ref, stack_ref, k_ref, qt_ref, vt_ref, wout_ref, qsel_ref, ght_s, mcot_s,
):
    count, tokens, width = gh_ref.shape
    for i in range(0, tokens, 256):
        rows = pl.ds(i, 256)
        where = place_ref[rows, :].astype(f32)
        free = 1.0 - jnp.sum(where, axis=-1, keepdims=True)
        mcot_s[rows, :] = (cot_ref[rows, :].astype(f32) * free).astype(bf16)
        slots = jnp.transpose(where).astype(bf16)
        for h in range(count):
            stack_ref[h, width:, rows] = slots
    gh = dot_nt(mcot_s[...], w_ref[...]).astype(bf16)
    ght_s[...] = dot_nt(w_ref[...], mcot_s[...]).astype(bf16)
    k = dot_nt(low_ref[...], wk_ref[...]).astype(bf16)
    qt_ref[...] = dot_nt(wq_ref[...], low_ref[...]).astype(bf16) * bf16(width ** (-0.5))
    vt_ref[...] = dot_nt(wv_ref[...], low_ref[...]).astype(bf16)
    for h in range(count):
        cols = slice(h * width, (h + 1) * width)
        gh_ref[h] = gh[:, cols]
        k_ref[h] = k[:, cols]
        stack_ref[h, 0:width, :] = ght_s[cols, :]
    wout_ref[...] = dot(attt_ref[...], mcot_s[...])
    qsel_ref[...] = dot(qt_ref[...], place_ref[...]).astype(bf16)


def masked_back_kernel(
    gh_ref, stack_ref, k_ref, qt_ref, vt_ref, att_ref, prob_ref,
    dq_ref, dkt_ref, dvt_ref, offs_ref, psel_ref, acc_s, score_s, *, h,
):
    tokens, width = dq_ref.shape
    acc_s[...] = jnp.zeros_like(acc_s)
    cols = slice(h * width, (h + 1) * width)
    for i in range(0, tokens, 2 * BLOCK):
        rows = pl.ds(i, 2 * BLOCK)
        gh = gh_ref[h, rows, :]
        delta = jnp.sum(gh.astype(f32) * att_ref[h, rows, :].astype(f32), axis=-1, keepdims=True)
        grads = dot(gh, vt_ref[cols, :]) - delta
        for j in range(2):
            start = i + j * BLOCK
            first = tokens - BLOCK - start
            here = pl.ds(start, BLOCK)
            score = prob_ref[h, here, :].astype(f32) * grads[j * BLOCK : (j + 1) * BLOCK]
            acc_s[:, first : first + tokens] += score
            score_s[here, :] = score.astype(bf16)
    dq_ref[...] = dot(score_s[...], k_ref[h]) * (width ** (-0.5))
    dkt_ref[...] = dot(qt_ref[cols, :], score_s[...])
    both = dot(stack_ref[h], prob_ref[h])
    dvt_ref[...] = both[:width]
    psel_ref[...] = both[width:].astype(bf16)
    offs_ref[...] = diagonals(acc_s[...])


def diagonals(acc):
    span = acc.shape[1]
    rows = acc.shape[0] // 2
    while rows >= 8:
        acc = acc[:rows] + pltpu.roll(acc[rows:], span - rows, 1)
        rows //= 2
    total = acc[0:1]
    for r in range(1, 8):
        total = total + pltpu.roll(acc[r : r + 1], span - r, 1)
    return jnp.broadcast_to(pltpu.roll(total, BLOCK - 1, 1), (8, span))


def slot_back_kernel(*refs, heads):
    parts = refs[:heads]
    (up_ref, normed_ref, hidden_ref, probs_ref, router_ref, gain_ref, w_ref, att_ref,
     wout0_ref) = refs[heads : heads + 9]
    (dv_ref, comb_ref, small_ref, wout_ref, gh_ref, ght_ref, delta_ref, ret_s, wide_s
     ) = refs[heads + 9 :]
    head, shard = lax.axis_index("head"), lax.axis_index("seq")
    ret_s[...] = jnp.zeros_like(ret_s)
    for d in range(heads):
        part = parts[d][...].astype(f32)
        for j in range(part.shape[0] // CAP):
            first = pl.multiple_of((shard ^ j) * SLOT, SLOT)
            ret_s[head ^ d, pl.ds(first, CAP), :] = part[j * CAP : (j + 1) * CAP]
    back = [ret_s[k] for k in range(heads)]
    combined = jnp.concatenate(back[: heads // 2], axis=1)
    grad_buf = jnp.concatenate(back[heads // 2 :], axis=1)
    up = up_ref[...].astype(f32)
    hidden, normed, probs, gain = hidden_ref[...], normed_ref[...], probs_ref[...], gain_ref[...]
    chosen = chosen_of(probs.shape)
    gate = jnp.sum(jnp.where(chosen, probs, 0.0), axis=-1, keepdims=True)
    comb_ref[...] = gate * combined
    gate_grad = jnp.sum(up * combined, axis=-1, keepdims=True)
    marked = jnp.where(chosen, gate_grad, 0.0)
    logit_grad = probs * (marked - jnp.sum(marked * probs, axis=-1, keepdims=True))
    experts = probs.shape[1]
    grad = grad_buf + jnp.dot(
        logit_grad, router_ref[...], precision=highest, preferred_element_type=f32
    )
    inverse = lax.rsqrt(jnp.mean(hidden * hidden, axis=-1, keepdims=True) + EPS)
    scaled = grad * gain
    inner_sum = jnp.mean(scaled * hidden, axis=-1, keepdims=True)
    dv = inverse * scaled - hidden * (inverse * inverse * inverse * inner_sum)
    dv_ref[...] = dv
    small_ref[...] = jnp.zeros_like(small_ref)
    small_ref[0:1, :] = jnp.sum(grad * hidden * inverse, axis=0, keepdims=True)
    small_ref[8 : 8 + experts, :] = dot_tn(logit_grad, normed, highest)
    grad_low = (up + dv).astype(bf16)
    half = att_ref.shape[0]
    inner = w_ref.shape[0]
    att = jnp.concatenate(
        [att_ref[:, 0:inner].astype(f32), att_ref[:, inner : 2 * inner].astype(f32)], axis=0
    )
    att = widen(att, wide_s)
    wout_ref[...] = wout0_ref[...] + dot_tn(att.astype(bf16), grad_low)
    gh = dot_nt(grad_low, w_ref[...])
    gh_low = gh.astype(bf16)
    count = gh_ref.shape[0]
    each = inner // count
    ght_ref[...] = dot_nt(w_ref[...], grad_low).astype(bf16)
    for h in range(count):
        cols = slice(h * each, (h + 1) * each)
        gh_ref[h] = gh_low[:, cols]
        delta_ref[h] = jnp.sum(
            gh_low[:, cols].astype(f32) * att[:, cols], axis=-1, keepdims=True
        )


def sparse_back_kernel(
    gh_ref, ght_ref, delta_ref, vt_ref, k_ref, qsel_ref,
    place_ref, wq_ref, wk_ref, wv_ref, low_ref, gain_ref, small_ref, wout_ref, *refs, heads,
):
    per_head, refs = refs[: 4 * gh_ref.shape[0]], refs[4 * gh_ref.shape[0] :]
    psels, dq0s, dkt0s, dvt0s = (per_head[i :: 4] for i in range(4))
    chunks = refs[:5]
    (score_ref, send_ref, keep_ref, out_ref,
     dq_s, q_low, k_low, v_low, kt_s, vt_s, all_s) = refs[5:]
    head = lax.axis_index("head")
    count, rows, width = gh_ref.shape
    tokens = vt_ref.shape[1]
    inner = count * width
    for h in range(count):
        cols = slice(h * width, (h + 1) * width)
        grad = dot(gh_ref[h], vt_ref[cols, :])
        prob = psels[h][...]
        score = (prob.astype(f32) * (grad - delta_ref[h])).astype(bf16)
        score_ref[h] = score
        dq_s[:, cols] = dot(score, k_ref[h]) * (width ** (-0.5))
        dkt = dkt0s[h][...] + dot(qsel_ref[cols, :], score)
        dvt = dvt0s[h][...] + dot(ght_ref[cols, :], prob)
        kt_s[cols, :] = dkt.astype(bf16)
        vt_s[cols, :] = dvt.astype(bf16)
        k_low[:, cols] = jnp.transpose(dkt).astype(bf16)
        v_low[:, cols] = jnp.transpose(dvt).astype(bf16)
    spread = dot(place_ref[...], dq_s[...].astype(bf16))
    for h in range(count):
        cols = slice(h * width, (h + 1) * width)
        q_low[:, cols] = (spread[:, cols] + dq0s[h][...]).astype(bf16)
    part = tokens // heads
    half = part // 2
    own, to_1, to_2, rest_1, rest_2 = chunks
    to_1[part:, :] = jnp.zeros((EXTRA, to_1.shape[1]), bf16)
    places = (
        ((own, 0), (own, half)),
        ((to_1, 0), (rest_1, 0)),
        ((rest_2, 0), (to_2, 0)),
        ((to_1, half), (to_2, half)),
    )
    for d in range(heads):
        mine = pl.ds(pl.multiple_of((head ^ d) * part, part), part)
        rows_part = (
            dot(q_low[mine, :], wq_ref[...])
            + dot(k_low[mine, :], wk_ref[...])
            + dot(v_low[mine, :], wv_ref[...])
        ).astype(bf16)
        for n, (ref, first) in enumerate(places[d]):
            ref[first : first + half, :] = rows_part[n * half : (n + 1) * half]
    low = low_ref[...]
    total = None
    grads = (dot_tn(q_low[...], low), dot(kt_s[...], low), dot(vt_s[...], low))
    for i, (grad, w) in enumerate(zip(grads, (wq_ref, wk_ref, wv_ref))):
        all_s[i * inner : (i + 1) * inner, :] = grad
        term = jnp.sum(grad * w[...].astype(f32), axis=0, keepdims=True)
        total = term if total is None else total + term
    all_s[3 * inner :, :] = wout_ref[...]
    out_ref[...] = small_ref[...]
    out_ref[1:2, :] = total / gain_ref[...]
    to_1[part : part + 1, :] = (total / gain_ref[...]).astype(bf16)
    split_rows(all_s, 1, send_ref, keep_ref)


def is_upper(bit):
    return (lax.axis_index("seq") & bit) != 0


def split_rows(all_s, bit, send_ref, keep_ref):
    half = send_ref.shape[0]
    low, high = all_s[0:half, :], all_s[half : 2 * half, :]
    keep_ref[...] = jnp.where(is_upper(bit), high, low)
    send_ref[...] = jnp.where(is_upper(bit), low, high).astype(bf16)


def halve_kernel(keep_ref, got_ref, *refs, bit):
    send_ref, out_ref, all_s = refs[-3:]
    if len(refs) > 3:
        rest_1, got_1, rest_2, got_2, small_ref, next_1, next_2 = refs[:-3]
        half = rest_1.shape[0]
        for rest, got, onward in ((rest_1, got_2, next_1), (rest_2, got_1, next_2)):
            got_rest = got[half : 2 * half, :].astype(f32)
            onward[0:half, :] = (rest[...].astype(f32) + got_rest).astype(bf16)
        mine = small_ref[1:2, :].astype(bf16).astype(f32)
        next_2[half:, :] = jnp.zeros((EXTRA, next_2.shape[1]), bf16)
        next_2[half : half + 1, :] = (mine + got_1[2 * half : 2 * half + 1, :].astype(f32)).astype(bf16)
    all_s[...] = keep_ref[...] + got_ref[...].astype(f32)
    split_rows(all_s, bit, send_ref, out_ref)


def join_rows(mine_ref, got_ref, all_s, bit, count):
    mine, got = mine_ref[...].astype(f32), got_ref[...].astype(f32)
    all_s[0:count, :] = jnp.where(is_upper(bit), got[:count], mine[:count])
    all_s[count : 2 * count, :] = jnp.where(is_upper(bit), mine[:count], got[:count])
    all_s[2 * count :, :] = mine[count:] + got[count:]


def pair_kernel(mine_ref, got_ref, *refs, bit, count):
    out_ref, all_s = refs[-2:]
    if len(refs) > 2:
        got_1, got_2, next_1, next_2 = refs[:-2]
        half = next_1.shape[0]
        next_2[...] = got_1[0:half, :]
        next_1[...] = got_2[half:, :]
    join_rows(mine_ref, got_ref, all_s, bit, count)
    out_ref[...] = all_s[...].astype(bf16)


def final_kernel(mine_ref, got_ref, *refs, bit, count):
    gain1_ref, gain2_ref, table_ref, router_ref, all_s = refs[-5:]
    outs = refs[:-5]
    join_rows(mine_ref, got_ref, all_s, bit, count)
    inner = outs[0].shape[0]
    for i, out in enumerate(outs):
        out[...] = all_s[i * inner : (i + 1) * inner, :]
    small = all_s[2 * count :, :]
    gain1_ref[...] = small[1, :]
    gain2_ref[...] = small[0, :]
    heads, buckets = table_ref.shape
    table_ref[...] = small[2 : 2 + heads, :buckets]
    router_ref[...] = small[8 : 8 + router_ref.shape[0], :]


def bias_grad_kernel(
    score_ref, place_ref, buckets_ref, small_ref, *refs, bucket_count
):
    count = score_ref.shape[0]
    offs, out_ref, acc_s, sums_s = refs[:count], *refs[count:]
    tokens = place_ref.shape[0]
    offsets = buckets_ref.shape[1]
    out_ref[...] = small_ref[...]
    bucket_hot = (iota((bucket_count, offsets), 0) == buckets_ref[...]).astype(f32)

    def one_head(h, carry):
        acc_s[...] = jnp.zeros_like(acc_s)
        for i in range(0, tokens, BLOCK):
            first = tokens - BLOCK - i
            acc_s[:, first : first + tokens] += dot(place_ref[i : i + BLOCK, :], score_ref[h])
        sums_s[h] = diagonals(acc_s[...])
        return carry

    lax.fori_loop(0, count, one_head, 0)
    for h in range(count):
        sums = sums_s[h] + offs[h][...]
        out_ref[2 + h : 3 + h, :bucket_count] = dot_nt(sums[:, :offsets], bucket_hot, highest)[0:1]


def hidden_kernel(*refs, heads):
    att_parts, w_ref, x_ref, out_ref, att_s = refs[:heads], *refs[heads:]
    head = lax.axis_index("head")
    tokens = x_ref.shape[0]
    inner = att_parts[0].shape[0]
    for d in range(heads):
        mine = pl.ds(pl.multiple_of((head ^ d) * inner, inner), inner)
        att_s[mine, :] = att_parts[d][...]

    def block(i, carry):
        rows = pl.ds(pl.multiple_of(i * 256, 256), 256)
        out_ref[rows, :] = x_ref[rows, :].astype(f32) + dot_tn(att_s[:, rows], w_ref[...])
        return carry

    lax.fori_loop(0, tokens // 256, block, 0)


def output_kernel(hidden_ref, place_ref, comb_ref, out_ref):
    high, rest = split_two(comb_ref[...])

    def block(i, carry):
        rows = pl.ds(pl.multiple_of(i * 256, 256), 256)
        where = place_ref[rows, :]
        out_ref[rows, :] = hidden_ref[rows, :] + (dot(where, high) + dot(where, rest))
        return carry

    lax.fori_loop(0, hidden_ref.shape[0] // 256, block, 0)


def first_norm_kernel(
    own, got_1, got_2, last_1, last_2, next_2, small_ref,
    x_ref, cot_ref, place_ref, dv_ref, gain_ref, keep_ref, got_ref, out_ref, sum_ref,
):
    half = last_1.shape[0]
    high, rest = split_two(dv_ref[...])
    for first, near, far in ((0, got_1, last_2), (half, got_2, last_1)):
        rows = pl.ds(first, half)
        grad = own[rows, :].astype(f32) + near[0:half, :].astype(f32)
        grad = grad + far[0:half, :].astype(f32)
        x = x_ref[rows, :].astype(f32)
        inverse = lax.rsqrt(jnp.mean(x * x, axis=-1, keepdims=True) + EPS)
        scaled = grad * gain_ref[...]
        inner_sum = jnp.mean(scaled * x, axis=-1, keepdims=True)
        where = place_ref[rows, :]
        hidden_grad = cot_ref[rows, :].astype(f32) + (dot(where, high) + dot(where, rest))
        out_ref[rows, :] = (
            hidden_grad + inverse * scaled - x * (inverse * inverse * inverse * inner_sum)
        ).astype(bf16)
    count = keep_ref.shape[0]
    sum_ref[0:count, :] = (keep_ref[...] + got_ref[...].astype(f32)).astype(bf16)
    gain1 = next_2[half:, :].astype(f32)[0:1] + last_2[half:, :].astype(f32)[0:1]
    small = small_ref[...]
    sum_ref[count:, :] = jnp.where(iota(small.shape, 0) == 1, gain1, small).astype(bf16)


def spread_near_kernel(own, got_1, got_2, out_ref, token, wide_s, sems):
    head = lax.axis_index("head")
    part = own.shape[0]
    copies = []
    for d, piece in enumerate((own, got_1, got_2)):
        wide_s[d] = piece[...].astype(f32)
        mine = pl.ds(pl.multiple_of((head ^ d) * part, part), part)
        copies.append(pltpu.make_async_copy(wide_s.at[d], out_ref.at[mine], sems.at[d]))
        copies[-1].start()
    token[...] = jnp.zeros_like(token)
    for copy in copies:
        copy.wait()


def spread_far_kernel(last_1, last_2, given, out_ref, wide_s, sem):
    head = lax.axis_index("head")
    half = last_1.shape[0]
    wide_s[0:half, :] = last_2[...].astype(f32)
    wide_s[half:, :] = last_1[...].astype(f32)
    mine = pl.ds(pl.multiple_of((head ^ 3) * 2 * half, 2 * half), 2 * half)
    copy = pltpu.make_async_copy(wide_s, out_ref.at[mine], sem)
    copy.start()
    copy.wait()


def swap(x, axis, d):
    size = lax.axis_size(axis)
    return lax.ppermute(x, axis, [(i, i ^ d) for i in range(size)])


def share(x, axis):
    return [x] + [swap(x, axis, d) for d in range(1, lax.axis_size(axis))]


def trade(pieces, axis):
    return lax.all_to_all(pieces, axis, split_axis=0, concat_axis=0, tiled=True)


def swap_all(pieces, axis):
    return [pieces[0]] + [swap(pieces[d], axis, d) for d in range(1, len(pieces))]


def bits_of(axis):
    return [b for b in (1 << i for i in range(16)) if b < lax.axis_size(axis)]


def halve(send, keep, bit, after, onward=()):
    rows, width = keep.shape
    outs = []
    if onward:
        half = onward[0].shape[0]
        outs = [shape_of(half, width, bf16), shape_of(half + EXTRA, width, bf16)]
    return call(
        partial(halve_kernel, bit=bit),
        outs + [shape_of(rows // 2, width, bf16), shape_of(rows // 2, width, f32)],
        (keep, swap(send, "seq", bit // 2)) + tuple(onward),
        scratch=[pltpu.VMEM((rows, width), f32)],
        name="halve",
        after=after,
        token=True,
    )


def pair(now, small_rows, bit, after, onward=()):
    rows, width = now.shape
    count = rows - small_rows
    outs = [shape_of(onward[0].shape[0] // 2, width, bf16)] * 2 if onward else []
    return call(
        partial(pair_kernel, bit=bit, count=count),
        outs + [shape_of(rows + count, width, bf16)],
        (now, swap(now, "seq", bit)) + tuple(onward),
        scratch=[pltpu.VMEM((rows + count, width), f32)],
        name="pair",
        after=after,
        token=True,
    )


def on_device(
    layer_input, cotangent, norm1_gain, w_query, w_key, w_value, w_attn_out, bias_table,
    norm2_gain, w_router, w_expert_in, w_expert_out, expert_ids, slot_ids, buckets,
):
    tokens, width = layer_input.shape
    shards = lax.axis_size("seq")
    heads = lax.axis_size("head")
    bucket_count, count = bias_table.shape
    inner = w_query.shape[1]
    each = inner // count
    experts = w_router.shape[1]
    rows, filled = experts * SLOT, experts * CAP
    hidden_units = w_expert_in.shape[2]
    part = tokens // heads
    split = 2 * width // heads
    span = 2 * tokens
    params = pltpu.CompilerParams(vmem_limit_bytes=VMEM_LIMIT if rows <= 256 else VMEM_ALL)

    ids = expert_ids.reshape(1, tokens)
    slots = slot_ids.reshape(1, tokens)
    bucket_row = buckets.reshape(1, -1)
    wq_t, wk_t, wv_t = jnp.transpose(w_query), jnp.transpose(w_key), jnp.transpose(w_value)
    router_t, table_t = jnp.transpose(w_router), jnp.transpose(bias_table)
    w_in = w_expert_in.reshape(width, hidden_units)
    w_out = w_expert_out.reshape(hidden_units, width)

    w_mix = share(w_attn_out, "head")

    low, prob, att, att_t, att_sel = pl.pallas_call(
        attend_kernel,
        out_shape=(
            shape_of(tokens, width, bf16),
            jax.ShapeDtypeStruct((count, tokens, tokens), bf16),
            jax.ShapeDtypeStruct((count, tokens, each), bf16),
            shape_of(inner, tokens, bf16),
            shape_of(filled // 2, 2 * inner, bf16),
        ),
        in_specs=[spec(pltpu.HBM)] * 9,
        out_specs=(spec(pltpu.VMEM),) * 5,
        scratch_shapes=[
            pltpu.VMEM((count, tokens, each), bf16),
            pltpu.VMEM((inner, tokens), bf16),
            pltpu.VMEM((count, tokens, each), bf16),
            pltpu.VMEM((8, span), f32),
            pltpu.VMEM((2, BLOCK, span), f32),
            pltpu.VMEM((filled, tokens), bf16),
            pltpu.VMEM((2, 2 * BLOCK, tokens), f32),
            pltpu.VMEM((tokens, width), bf16),
            pltpu.VMEM((width,), f32),
            pltpu.VMEM((inner, width), bf16),
            pltpu.VMEM((inner, width), bf16),
            pltpu.VMEM((inner, width), bf16),
            pltpu.VMEM((count, bucket_count), f32),
            pltpu.VMEM((1, span - 1), jnp.int32),
            pltpu.VMEM((1, tokens), jnp.int32),
            pltpu.VMEM((1, tokens), jnp.int32),
            pltpu.SemaphoreType.DMA((9,)),
        ],
        compiler_params=params,
        cost_estimate=NO_COST,
        name="attend",
    )(
        *(
            pltpu.with_memory_space_constraint(a, pltpu.HBM)
            for a in (layer_input, norm1_gain, wq_t, wk_t, wv_t, table_t, bucket_row, ids, slots)
        )
    )

    (att_sel,) = call(
        pass_kernel,
        [shape_of(filled // 2, 2 * inner, bf16)],
        (att_sel,),
        name="pass",
        after=(w_mix[1],),
    )
    sel_parts = share(att_sel, "head")
    sel_in, sel_up, place, place_c, x_c, cot_c, w_full = call(
        partial(place_kernel, heads=heads),
        [
            shape_of(rows, width, bf16),
            shape_of(rows, width, bf16),
            shape_of(tokens, rows, bf16),
            shape_of(part, rows, bf16),
            shape_of(part, width, bf16),
            shape_of(part, width, bf16),
            shape_of(heads * inner, width, bf16),
        ],
        (layer_input, cotangent, ids, slots) + tuple(w_mix),
        scratch=[pltpu.VMEM((tokens, rows), f32)],
        moved=12 * 2**20,
        name="place",
        after=(att_sel,),
    )
    routed = call(
        partial(route_kernel, shards=shards, heads=heads),
        [
            shape_of(rows, width, f32),
            shape_of(rows, width, f32),
            shape_of(rows, experts, f32),
            shape_of(inner, tokens, bf16),
        ]
        + [shape_of(TALL, packed_width(width), bf16)] * shards,
        tuple(sel_parts) + (w_full, sel_in, sel_up, norm2_gain, router_t, att_t),
        scratch=[
            pltpu.VMEM((heads, filled, inner), bf16),
            pltpu.VMEM((rows, 2 * width), f32),
            pltpu.VMEM((rows, width), f32),
            pltpu.VMEM((shards * TALL, packed_width(width)), f32),
        ],
        name="route",
    )
    hidden_sel, normed_sel, probs, att_on = routed[:4]
    pay_parts = swap_all(routed[4:], "seq")
    att_parts = [att_t] + [swap(att_on, "head", d) for d in range(1, heads - 1)]

    def masked_back(h, after):
        return call(
            partial(masked_back_kernel, h=h),
            [
                shape_of(tokens, each, f32),
                shape_of(each, tokens, f32),
                shape_of(each, tokens, f32),
                shape_of(8, span, f32),
                shape_of(rows, tokens, bf16),
            ],
            (gh, stack, k_rows, q_t, v_t, att, prob),
            scratch=[pltpu.VMEM((BLOCK, span), f32), pltpu.VMEM((tokens, tokens), bf16)],
            name="masked_back",
            after=after,
            moved=11 * 2**20,
            token=True,
        )

    done = call(
        partial(expert_kernel, shards=shards, heads=heads),
        [shape_of(filled, split, bf16)] * heads
        + [
            shape_of(rows, width, bf16),
            shape_of(rows, hidden_units, bf16),
            shape_of(rows, hidden_units, bf16),
            shape_of(rows, width, bf16),
        ],
        tuple(pay_parts[d] for d in far_first(shards)) + (w_in, w_out),
        scratch=[
            pltpu.VMEM((rows, 2 * width), f32),
            pltpu.VMEM((rows, 1), f32),
            pltpu.VMEM((heads, filled, split), f32),
        ],
        name="expert",
        after=tuple(att_parts[1:]),
        token=True,
    )
    x_rows, act, pre_low, out_low, token = done[heads:]
    gh, stack, k_rows, q_t, v_t, wout0, q_sel, token = call(
        prep_kernel,
        [
            jax.ShapeDtypeStruct((count, tokens, each), bf16),
            jax.ShapeDtypeStruct((count, each + rows, tokens), bf16),
            jax.ShapeDtypeStruct((count, tokens, each), bf16),
            shape_of(inner, tokens, bf16),
            shape_of(inner, tokens, bf16),
            shape_of(inner, width, f32),
            shape_of(inner, rows, bf16),
        ],
        (cotangent, w_attn_out, wq_t, wk_t, wv_t, low, place, att_t),
        scratch=[pltpu.VMEM((inner, tokens), bf16), pltpu.VMEM((tokens, width), bf16)],
        name="prep",
        after=(token,),
        moved=8 * 2**20,
        token=True,
    )

    masked = []
    for h in range(count - 2):
        masked.append(masked_back(h, (token,)))
        token = masked[-1][-1]
    returned = call(
        partial(sum_kernel, heads=heads),
        [shape_of(inner, tokens, bf16)] + [shape_of(CAP, split, bf16)] * shards,
        [att_t] + swap_all(done[:heads], "head"),
        scratch=[pltpu.VMEM((filled, split), f32)],
        name="sum",
        after=(token,),
        token=True,
    )
    masked.append(masked_back(count - 2, (returned[-1],)))
    att_parts.append(swap(returned[0], "head", heads - 1))
    answers = swap_all(returned[1:-1], "seq")
    joined, token = call(
        join_kernel,
        [shape_of(filled, split, bf16)],
        [answers[d] for d in far_first(shards)],
        scratch=[pltpu.VMEM((filled, split), f32)],
        name="join",
        after=(masked[-1][-1], att_parts[-1]),
        token=True,
    )
    masked.append(masked_back(count - 1, (token,)))
    full_parts = share(joined, "head")

    small_rows = 8 + -(-experts // 8) * 8
    dv_sel, comb_sel, small, wout_part, gh_sel, ght_sel, delta_sel = call(
        partial(slot_back_kernel, heads=heads),
        [
            shape_of(rows, width, f32),
            shape_of(rows, width, f32),
            shape_of(small_rows, width, f32),
            shape_of(inner, width, f32),
            jax.ShapeDtypeStruct((count, rows, each), bf16),
            shape_of(inner, rows, bf16),
            jax.ShapeDtypeStruct((count, rows, 1), f32),
        ],
        tuple(full_parts)
        + (sel_up, normed_sel, hidden_sel, probs, router_t, norm2_gain)
        + (w_attn_out, att_sel, wout0),
        scratch=[pltpu.VMEM((heads, rows, split), f32), pltpu.VMEM((rows, inner), f32)],
        name="slot_back",
        after=(masked[-1][-1],),
    )

    back = call(
        partial(sparse_back_kernel, heads=heads),
        [shape_of(part, width, bf16), shape_of(part + EXTRA, width, bf16)]
        + [shape_of(part, width, bf16)]
        + [shape_of(part // 2, width, bf16)] * 2
        + [
            jax.ShapeDtypeStruct((count, rows, tokens), bf16),
            shape_of(2 * inner, width, bf16),
            shape_of(2 * inner, width, f32),
            shape_of(small_rows, width, f32),
        ],
        (gh_sel, ght_sel, delta_sel, v_t, k_rows, q_sel, place)
        + (wq_t, wk_t, wv_t, low, norm1_gain, small, wout_part)
        + tuple(a for m in masked for a in (m[4], m[0], m[1], m[2])),
        scratch=[
            pltpu.VMEM((rows, inner), f32),
            pltpu.VMEM((tokens, inner), bf16),
            pltpu.VMEM((tokens, inner), bf16),
            pltpu.VMEM((tokens, inner), bf16),
            pltpu.VMEM((inner, tokens), bf16),
            pltpu.VMEM((inner, tokens), bf16),
            pltpu.VMEM((4 * inner, width), f32),
        ],
        name="sparse_back",
    )
    score_sel, send, keep, small = back[5:]
    own, to_1, to_2, rest_1, rest_2 = back[:5]
    got_1, got_2 = swap(to_1, "head", 1), swap(to_2, "head", 2)

    bits = bits_of("seq")
    send, keep, token = halve(send, keep, bits[1], ())
    small_part = small
    small, token = call(
        partial(bias_grad_kernel, bucket_count=bucket_count),
        [shape_of(small_rows, width, f32)],
        (score_sel, place, bucket_row, small) + tuple(m[3] for m in masked),
        scratch=[pltpu.VMEM((BLOCK, span), f32), pltpu.VMEM((count, 8, span), f32)],
        name="bias_grad",
        after=(token,),
        moved=16 * 2**20,
        token=True,
    )
    next_1, next_2, send, keep, token = halve(
        send, keep, bits[2], (token,), (rest_1, got_1, rest_2, got_2, small_part)
    )
    last_1, last_2 = swap(next_1, "head", 1), swap(next_2, "head", 2)
    w_in_grad, w_out_grad, token = call(
        expert_grad_kernel,
        [
            jax.ShapeDtypeStruct(w_expert_in.shape, f32),
            jax.ShapeDtypeStruct(w_expert_out.shape, f32),
        ],
        (x_rows, pre_low, act, out_low),
        name="expert_grad",
        after=(token,),
        moved=10 * 2**20,
        token=True,
    )
    hidden, token = call(
        partial(hidden_kernel, heads=heads),
        [shape_of(tokens, width, f32)],
        tuple(att_parts) + (w_full, layer_input),
        scratch=[pltpu.VMEM((heads * inner, tokens), bf16)],
        name="hidden",
        after=(token,),
        moved=6 * 2**20,
        token=True,
    )
    for bit in bits[3:]:
        send, keep, token = halve(send, keep, bit, (token,))

    grad_part, weights, token = call(
        first_norm_kernel,
        [shape_of(part, width, bf16), shape_of(keep.shape[0] + small_rows, width, bf16)],
        (own, got_1, got_2, last_1, last_2, next_2, small)
        + (x_c, cot_c, place_c, dv_sel, norm1_gain)
        + (keep, swap(send, "seq", bits[-1])),
        name="first_norm",
        after=(token,),
        token=True,
    )
    grad_1, grad_2 = swap(grad_part, "head", 1), swap(grad_part, "head", 2)
    layer_output, token = call(
        output_kernel,
        [shape_of(tokens, width, f32)],
        (hidden, place, comb_sel),
        name="output",
        after=(token,),
        moved=10 * 2**20,
        token=True,
    )
    for bit in reversed(bits[3:]):
        weights, token = pair(weights, small_rows, bit, (token,))
    next_1, next_2, weights, token = pair(
        weights, small_rows, bits[2], (token,), (grad_1, grad_2)
    )
    grad_3 = (swap(next_1, "head", 1), swap(next_2, "head", 2))
    near, token = pl.pallas_call(
        spread_near_kernel,
        out_shape=(shape_of(tokens, width, f32), shape_of(8, 128, f32)),
        in_specs=[spec(pltpu.VMEM)] * 3,
        out_specs=(spec(pltpu.HBM), spec(pltpu.VMEM)),
        scratch_shapes=[pltpu.VMEM((3, part, width), f32), pltpu.SemaphoreType.DMA((3,))],
        compiler_params=params,
        cost_estimate=pl.CostEstimate(flops=1, bytes_accessed=5 * 2**20, transcendentals=0),
        name="spread_near",
    )(grad_part, grad_1, grad_2)
    weights, token = pair(weights, small_rows, bits[1], grad_3 + (token,))
    last = call(
        partial(final_kernel, bit=bits[0], count=2 * inner),
        [shape_of(inner, width, f32)] * 4
        + [
            jax.ShapeDtypeStruct((width,), f32),
            jax.ShapeDtypeStruct((width,), f32),
            shape_of(count, bucket_count, f32),
            shape_of(experts, width, f32),
        ],
        (weights, swap(weights, "seq", bits[0])),
        scratch=[pltpu.VMEM((4 * inner + small_rows, width), f32)],
        name="weights_out",
    )
    weight_sums = last[:4]
    gain1_sum, gain2_sum, table_sum, router_sum = last[4:]
    input_grad = pl.pallas_call(
        spread_far_kernel,
        out_shape=shape_of(tokens, width, f32),
        in_specs=[spec(pltpu.VMEM), spec(pltpu.VMEM), spec(pltpu.HBM)],
        out_specs=spec(pltpu.HBM),
        scratch_shapes=[pltpu.VMEM((part, width), f32), pltpu.SemaphoreType.DMA(())],
        input_output_aliases={2: 0},
        compiler_params=params,
        cost_estimate=NO_COST,
        name="spread_far",
    )(*grad_3, near)

    return (
        layer_output,
        input_grad,
        gain1_sum,
        jnp.transpose(weight_sums[0]),
        jnp.transpose(weight_sums[1]),
        jnp.transpose(weight_sums[2]),
        weight_sums[3],
        jnp.transpose(table_sum),
        gain2_sum,
        jnp.transpose(router_sum),
        w_in_grad,
        w_out_grad,
    )


def solution(mesh):
    return jax.shard_map(
        on_device,
        mesh=mesh,
        in_specs=(
            P("seq", None),
            P("seq", None),
            P(),
            P(None, "head"),
            P(None, "head"),
            P(None, "head"),
            P("head", None),
            P(None, "head"),
            P(),
            P(),
            P("seq", None, "head"),
            P("seq", "head", None),
            P("seq"),
            P("seq"),
            P(),
        ),
        out_specs=(
            P("seq", None),
            P("seq", None),
            P(),
            P(None, "head"),
            P(None, "head"),
            P(None, "head"),
            P("head", None),
            P(None, "head"),
            P(),
            P(),
            P("seq", None, "head"),
            P("seq", "head", None),
        ),
        check_vma=False,
    )
```

```python
from functools import partial

import jax
import jax.numpy as jnp
import numpy as np
from jax import lax
from jax.experimental import pallas as pl
from jax.experimental.pallas import tpu as pltpu
from jax.sharding import PartitionSpec as P

CAP = 20
SLOT = 24
EPS = 1e-06
BLOCK = 128
ROWS = 16
EXTRA = 16
TALL = 16
VMEM_LIMIT = 26 * 1024 * 1024
VMEM_ALL = 60 * 1024 * 1024
NO_COST = pl.CostEstimate(flops=1, bytes_accessed=1, transcendentals=0)

f32 = jnp.float32
bf16 = jnp.bfloat16
highest = lax.Precision.HIGHEST


def dot(a, b):
    return jnp.dot(a, b, preferred_element_type=f32)


def dot_nt(a, b, precision=None):
    return lax.dot_general(
        a, b, (((1,), (1,)), ((), ())), precision=precision, preferred_element_type=f32
    )


def dot_tn(a, b, precision=None):
    return lax.dot_general(
        a, b, (((0,), (0,)), ((), ())), precision=precision, preferred_element_type=f32
    )


def iota(shape, dim):
    return lax.broadcasted_iota(jnp.int32, shape, dim)


def split_two(v):
    high = v.astype(bf16)
    return high, (v - high.astype(f32)).astype(bf16)


def shape_of(rows, cols, dtype):
    return jax.ShapeDtypeStruct((rows, cols), dtype)


def spec(memory):
    return pl.BlockSpec(memory_space=memory)


def call(kernel, outs, args, scratch=(), name=None, after=(), moved=1, token=False):
    outs, args = tuple(outs), tuple(args)
    held = sum(int(np.prod(a.shape)) * np.dtype(a.dtype).itemsize for a in args + outs)
    if token:
        outs += (shape_of(8, 128, f32),)
    first_out = len(args) + len(after)

    def body(*refs):
        results = refs[first_out : first_out + len(outs)]
        if token:
            results[-1][...] = jnp.zeros((8, 128), f32)
            results = results[:-1]
        kernel(*refs[: len(args)], *results, *refs[first_out + len(outs) :])

    return pl.pallas_call(
        body,
        out_shape=outs,
        in_specs=[spec(pltpu.VMEM)] * len(args) + [spec(pl.ANY)] * len(after),
        out_specs=tuple(spec(pltpu.VMEM) for _ in outs),
        scratch_shapes=list(scratch),
        compiler_params=pltpu.CompilerParams(
            vmem_limit_bytes=VMEM_LIMIT if 2 * held < VMEM_LIMIT else VMEM_ALL
        ),
        cost_estimate=pl.CostEstimate(flops=1, bytes_accessed=moved, transcendentals=0),
        name=name,
    )(*args, *after)


def slot_rows(ids, slots, rows, each):
    cell = jnp.where(slots < CAP, ids * each + slots, -1)
    return (iota((rows, cell.shape[1]), 0) == cell).astype(f32)


def place_kernel(x_ref, cot_ref, ids_ref, slots_ref, *refs, heads):
    w_parts = refs[:heads]
    sel_in, sel_up, place, place_c, x_c, cot_c, w_ref, place_s = refs[heads:]
    head = lax.axis_index("head")
    part = x_c.shape[0]
    slot_hot = slot_rows(ids_ref[...], slots_ref[...], sel_in.shape[0], SLOT)
    place_s[...] = jnp.transpose(slot_hot)
    slot_low = slot_hot.astype(bf16)
    sel_in[...] = dot(slot_low, x_ref[...]).astype(bf16)
    sel_up[...] = dot(slot_low, cot_ref[...]).astype(bf16)
    place[...] = place_s[...].astype(bf16)
    mine = pl.ds(pl.multiple_of(head * part, part), part)
    place_c[...] = place_s[mine, :].astype(bf16)
    x_c[...] = x_ref[mine, :]
    cot_c[...] = cot_ref[mine, :]
    inner = w_parts[0].shape[0]
    for d in range(heads):
        rows = pl.ds(pl.multiple_of((head ^ d) * inner, inner), inner)
        w_ref[rows, :] = w_parts[d][...]


def attend_kernel(*refs):
    given, refs = refs[:9], refs[9:]
    low_ref, prob_ref, att_ref, attt_ref, sel_ref = refs[:5]
    q_s, kt_s, v_s, bias_s, skew_s, slot_s, score_s = refs[5:12]
    here, sems = refs[12:21], refs[21]
    x_ref, gain_ref, wq_ref, wk_ref, wv_ref, table_ref, buckets_ref, ids_ref, slots_ref = here
    copies = [
        pltpu.make_async_copy(far, near, sems.at[i])
        for i, (far, near) in enumerate(zip(given, here))
    ]
    tokens = x_ref.shape[0]
    inner = wq_ref.shape[0]
    count = q_s.shape[0]
    width = inner // count
    span = skew_s.shape[2]
    tall = 2 * BLOCK
    for copy in copies:
        copy.start()
    for copy in copies[5:]:
        copy.wait()
    slot_s[...] = slot_rows(ids_ref[...], slots_ref[...], slot_s.shape[0], CAP).astype(bf16)
    offsets = buckets_ref.shape[1]
    bucket_hot = (iota((table_ref.shape[1], offsets), 0) == buckets_ref[...]).astype(f32)
    bias_s[...] = jnp.zeros_like(bias_s)
    bias_s[:count, :offsets] = jnp.dot(
        table_ref[...], bucket_hot, precision=highest, preferred_element_type=f32
    )
    for copy in copies[:2]:
        copy.wait()
    for i in range(0, tokens, 256):
        rows = pl.ds(i, 256)
        x = x_ref[rows, :].astype(f32)
        inverse = lax.rsqrt(jnp.mean(x * x, axis=-1, keepdims=True) + EPS)
        low_ref[rows, :] = (x * inverse * gain_ref[...]).astype(bf16)
    for copy in copies[2:5]:
        copy.wait()
    low = low_ref[...]
    q = dot_nt(low, wq_ref[...]).astype(bf16) * bf16(width ** (-0.5))
    kt_s[...] = dot_nt(wk_ref[...], low).astype(bf16)
    v = dot_nt(low, wv_ref[...]).astype(bf16)
    for h in range(count):
        cols = slice(h * width, (h + 1) * width)
        q_s[h] = q[:, cols]
        v_s[h] = v[:, cols]

    blocks = tokens // tall
    half = sel_ref.shape[0]

    def lay_bias(h):
        skew_s[h % 2] = pltpu.roll(
            jnp.broadcast_to(bias_s[h : h + 1, :], skew_s.shape[1:]),
            span - (BLOCK - 1), 1, stride=1, stride_axis=0,
        )

    def scores(h, n):
        score_s[n % 2] = dot(
            q_s[h, pl.ds(n * tall, tall), :], kt_s[h * width : (h + 1) * width, :]
        )

    def weights(h, n):
        for j in range(0, tall, ROWS):
            row = n * tall + j
            first = tokens - BLOCK - row // BLOCK * BLOCK
            bias = skew_s[h % 2, j % BLOCK : j % BLOCK + ROWS, first : first + tokens]
            score = score_s[n % 2, j : j + ROWS, :] + bias
            weight = jnp.exp(score - jnp.max(score, axis=-1, keepdims=True))
            total = jnp.sum(weight, axis=-1, keepdims=True)
            prob_ref[h, pl.ds(row, ROWS), :] = (weight * (1.0 / total)).astype(bf16)

    lay_bias(0)
    scores(0, 0)
    for h in range(count):
        for n in range(blocks):
            if n + 1 < blocks:
                scores(h, n + 1)
            elif h + 1 < count:
                lay_bias(h + 1)
                scores(h + 1, 0)
            weights(h, n)
        att = dot(prob_ref[h], v_s[h])
        att_low = att.astype(bf16)
        att_ref[h] = att_low
        attt_ref[h * width : (h + 1) * width, :] = jnp.transpose(att).astype(bf16)
        picked = dot(slot_s[...], att_low).astype(bf16)
        for part in range(2):
            start = part * inner + h * width
            sel_ref[:, start : start + width] = picked[part * half : (part + 1) * half]


def pass_kernel(given, passed):
    passed[...] = given[...]


def widen(rows, wide_s):
    wide_s[...] = jnp.zeros_like(wide_s)
    for e in range(rows.shape[0] // CAP):
        wide_s[e * SLOT : e * SLOT + CAP, :] = rows[e * CAP : (e + 1) * CAP]
    return wide_s[...]


def packed_width(width):
    return 2 * width + width // 2 + 128


def short_rows(width):
    each = width // 2
    for i in range(CAP - TALL):
        for k in range(4):
            yield TALL + i, slice(k * each, (k + 1) * each), 4 * i + k


def route_kernel(*refs, shards, heads):
    att_parts, w_ref = refs[:heads], refs[heads]
    (sel_in, sel_up, gain_ref, router_ref, att_t, hidden_ref, normed_ref, probs_ref, att_on
     ) = refs[heads + 1 : heads + 10]
    pieces = refs[heads + 10 : heads + 10 + shards]
    att_s, pay_s, wide_s, pack_s = refs[heads + 10 + shards :]
    head = lax.axis_index("head")
    half = att_parts[0].shape[0]
    inner = w_ref.shape[0] // heads
    for d in range(heads):
        att_s[d, 0:half, :] = att_parts[d][:, 0:inner]
        att_s[d, half : 2 * half, :] = att_parts[d][:, inner : 2 * inner]
    mixed = None
    for k in range(heads):
        term = dot(att_s[head ^ k], w_ref[k * inner : (k + 1) * inner, :])
        mixed = term if mixed is None else mixed + term
    hidden = sel_in[...].astype(f32) + widen(mixed, wide_s)
    hidden_ref[...] = hidden
    inverse = lax.rsqrt(jnp.mean(hidden * hidden, axis=-1, keepdims=True) + EPS)
    normed = hidden * inverse * gain_ref[...]
    normed_ref[...] = normed
    logits = dot_nt(normed, router_ref[...], highest)
    logits = logits - jnp.max(logits, axis=-1, keepdims=True)
    powers = jnp.exp(logits)
    probs = powers / jnp.sum(powers, axis=-1, keepdims=True)
    probs_ref[...] = probs
    gate = jnp.sum(jnp.where(chosen_of(probs.shape), probs, 0.0), axis=-1, keepdims=True)
    high = gate.astype(bf16).astype(f32)
    lane = iota((gate.shape[0], 128), 1)
    width = normed.shape[1]
    rest = gate - high
    first_gates = jnp.where(lane == 0, high, jnp.where(lane == 1, rest, 0.0))
    last_gates = jnp.where(lane == 2, high, jnp.where(lane == 3, rest, 0.0))
    pay_s[:, :width] = normed
    pay_s[:, width:] = sel_up[...].astype(f32)
    full, side = 2 * width, 2 * width + width // 2
    for e in range(shards):
        rows, packed = e * SLOT, e * TALL
        pack_s[packed : packed + TALL, :full] = pay_s[rows : rows + TALL, :]
        for row, lanes, to in short_rows(width):
            pack_s[packed + to : packed + to + 1, full:side] = pay_s[
                rows + row : rows + row + 1, lanes
            ]
        pack_s[packed : packed + 8, side:] = (
            first_gates[rows : rows + 8] + last_gates[rows + TALL : rows + SLOT]
        )
        pack_s[packed + 8 : packed + TALL, side:] = first_gates[rows + 8 : rows + TALL]
    shard = lax.axis_index("seq")
    for j in range(shards):
        first = pl.multiple_of((shard ^ j) * TALL, TALL)
        pieces[j][...] = pack_s[pl.ds(first, TALL), :].astype(bf16)
    att_on[...] = att_t[...]


def chosen_of(shape):
    expert = iota(shape, 1) * SLOT
    slot_row = iota(shape, 0)
    return (slot_row >= expert) & (slot_row < expert + SLOT)


def far_first(count):
    return list(range(count - 2, 1, -2)) + list(range(count - 1, 2, -2)) + [1, 0]


def by_partner(refs):
    return [ref for _, ref in sorted(zip(far_first(len(refs)), refs), key=lambda t: t[0])]


def expert_kernel(*refs, shards, heads):
    parts = by_partner(refs[:shards])
    w_in, w_out = refs[shards : shards + 2]
    chunks = refs[shards + 2 : shards + 2 + heads]
    x_ref, act_ref, pre_ref, out_ref, pay_s, gate_s, both_s = refs[shards + 2 + heads :]
    head = lax.axis_index("head")
    width = x_ref.shape[1]
    full, side = 2 * width, 2 * width + width // 2
    for j in range(shards):
        rows = j * SLOT
        part = parts[j][...].astype(f32)
        pay_s[rows : rows + TALL, :] = part[:, :full]
        pay_s[rows + TALL : rows + SLOT, :] = jnp.zeros((SLOT - TALL, full), f32)
        for row, lanes, place in short_rows(width):
            pay_s[rows + row : rows + row + 1, lanes] = part[place : place + 1, full:side]
        gate_s[rows : rows + TALL, :] = part[:, side : side + 1] + part[:, side + 1 : side + 2]
        gate_s[rows + TALL : rows + SLOT, :] = (
            part[:8, side + 2 : side + 3] + part[:8, side + 3 : side + 4]
        )
    x = pay_s[:, :width].astype(bf16)
    up = pay_s[:, width:]
    gate = gate_s[...]
    out_low = (gate * up).astype(bf16)
    pre = dot(x, w_in[...])
    cdf = 0.5 * (1.0 + lax.erf(pre * (0.5**0.5)))
    act = (pre * cdf).astype(bf16)
    slope = cdf + pre * jnp.exp(-0.5 * pre * pre) * ((2.0 * np.pi) ** (-0.5))
    pre_low = (dot_nt(out_low, w_out[...]) * slope).astype(bf16)
    both = (dot(act, w_out[...]), dot_nt(pre_low, w_in[...]))
    part = both_s.shape[2]
    for k in range(heads):
        start = k % (heads // 2) * part
        for j in range(shards):
            both_s[k, j * CAP : (j + 1) * CAP, :] = both[k // (heads // 2)][
                j * SLOT : j * SLOT + CAP, start : start + part
            ]
    for d in range(heads):
        chunks[d][...] = both_s[head ^ d].astype(bf16)
    pre_ref[...] = pre_low
    out_ref[...] = out_low
    x_ref[...] = x
    act_ref[...] = act


def expert_grad_kernel(x_ref, pre_ref, act_ref, out_ref, in_grad, out_grad):
    in_grad[0] = dot_tn(x_ref[...], pre_ref[...])
    out_grad[0] = dot_tn(act_ref[...], out_ref[...])


def sum_kernel(att_ref, *refs, heads):
    parts, att_on, pieces, sum_s = refs[:heads], refs[heads], refs[heads + 1 : -1], refs[-1]
    att_on[...] = att_ref[...]
    total = parts[0][...].astype(f32)
    for d in range(1, heads):
        total = total + parts[d][...].astype(f32)
    sum_s[...] = total
    for j, piece in enumerate(pieces):
        piece[...] = sum_s[j * CAP : (j + 1) * CAP, :].astype(bf16)


def join_kernel(*refs):
    parts, out_ref, sum_s = by_partner(refs[:-2]), refs[-2], refs[-1]
    for j, part in enumerate(parts):
        sum_s[j * CAP : (j + 1) * CAP, :] = part[...].astype(f32)
    out_ref[...] = sum_s[...].astype(bf16)


def prep_kernel(
    cot_ref, w_ref, wq_ref, wk_ref, wv_ref, low_ref, place_ref, attt_ref,
    gh_ref, stack_ref, k_ref, qt_ref, vt_ref, wout_ref, qsel_ref, ght_s, mcot_s,
):
    count, tokens, width = gh_ref.shape
    for i in range(0, tokens, 256):
        rows = pl.ds(i, 256)
        where = place_ref[rows, :].astype(f32)
        free = 1.0 - jnp.sum(where, axis=-1, keepdims=True)
        mcot_s[rows, :] = (cot_ref[rows, :].astype(f32) * free).astype(bf16)
        slots = jnp.transpose(where).astype(bf16)
        for h in range(count):
            stack_ref[h, width:, rows] = slots
    gh = dot_nt(mcot_s[...], w_ref[...]).astype(bf16)
    ght_s[...] = dot_nt(w_ref[...], mcot_s[...]).astype(bf16)
    k = dot_nt(low_ref[...], wk_ref[...]).astype(bf16)
    qt_ref[...] = dot_nt(wq_ref[...], low_ref[...]).astype(bf16) * bf16(width ** (-0.5))
    vt_ref[...] = dot_nt(wv_ref[...], low_ref[...]).astype(bf16)
    for h in range(count):
        cols = slice(h * width, (h + 1) * width)
        gh_ref[h] = gh[:, cols]
        k_ref[h] = k[:, cols]
        stack_ref[h, 0:width, :] = ght_s[cols, :]
    wout_ref[...] = dot(attt_ref[...], mcot_s[...])
    qsel_ref[...] = dot(qt_ref[...], place_ref[...]).astype(bf16)


def masked_back_kernel(
    gh_ref, stack_ref, k_ref, qt_ref, vt_ref, att_ref, prob_ref,
    dq_ref, dkt_ref, dvt_ref, offs_ref, psel_ref, acc_s, score_s, *, h,
):
    tokens, width = dq_ref.shape
    acc_s[...] = jnp.zeros_like(acc_s)
    cols = slice(h * width, (h + 1) * width)
    for i in range(0, tokens, 2 * BLOCK):
        rows = pl.ds(i, 2 * BLOCK)
        gh = gh_ref[h, rows, :]
        delta = jnp.sum(gh.astype(f32) * att_ref[h, rows, :].astype(f32), axis=-1, keepdims=True)
        grads = dot(gh, vt_ref[cols, :]) - delta
        for j in range(2):
            start = i + j * BLOCK
            first = tokens - BLOCK - start
            here = pl.ds(start, BLOCK)
            score = prob_ref[h, here, :].astype(f32) * grads[j * BLOCK : (j + 1) * BLOCK]
            acc_s[:, first : first + tokens] += score
            score_s[here, :] = score.astype(bf16)
    dq_ref[...] = dot(score_s[...], k_ref[h]) * (width ** (-0.5))
    dkt_ref[...] = dot(qt_ref[cols, :], score_s[...])
    both = dot(stack_ref[h], prob_ref[h])
    dvt_ref[...] = both[:width]
    psel_ref[...] = both[width:].astype(bf16)
    offs_ref[...] = diagonals(acc_s[...])


def diagonals(acc):
    span = acc.shape[1]
    rows = acc.shape[0] // 2
    while rows >= 8:
        acc = acc[:rows] + pltpu.roll(acc[rows:], span - rows, 1)
        rows //= 2
    total = acc[0:1]
    for r in range(1, 8):
        total = total + pltpu.roll(acc[r : r + 1], span - r, 1)
    return jnp.broadcast_to(pltpu.roll(total, BLOCK - 1, 1), (8, span))


def slot_back_kernel(*refs, heads):
    parts = refs[:heads]
    (up_ref, normed_ref, hidden_ref, probs_ref, router_ref, gain_ref, w_ref, att_ref,
     wout0_ref) = refs[heads : heads + 9]
    (dv_ref, comb_ref, small_ref, wout_ref, gh_ref, ght_ref, delta_ref, ret_s, wide_s
     ) = refs[heads + 9 :]
    head, shard = lax.axis_index("head"), lax.axis_index("seq")
    ret_s[...] = jnp.zeros_like(ret_s)
    for d in range(heads):
        part = parts[d][...].astype(f32)
        for j in range(part.shape[0] // CAP):
            first = pl.multiple_of((shard ^ j) * SLOT, SLOT)
            ret_s[head ^ d, pl.ds(first, CAP), :] = part[j * CAP : (j + 1) * CAP]
    back = [ret_s[k] for k in range(heads)]
    combined = jnp.concatenate(back[: heads // 2], axis=1)
    grad_buf = jnp.concatenate(back[heads // 2 :], axis=1)
    up = up_ref[...].astype(f32)
    hidden, normed, probs, gain = hidden_ref[...], normed_ref[...], probs_ref[...], gain_ref[...]
    chosen = chosen_of(probs.shape)
    gate = jnp.sum(jnp.where(chosen, probs, 0.0), axis=-1, keepdims=True)
    comb_ref[...] = gate * combined
    gate_grad = jnp.sum(up * combined, axis=-1, keepdims=True)
    marked = jnp.where(chosen, gate_grad, 0.0)
    logit_grad = probs * (marked - jnp.sum(marked * probs, axis=-1, keepdims=True))
    experts = probs.shape[1]
    grad = grad_buf + jnp.dot(
        logit_grad, router_ref[...], precision=highest, preferred_element_type=f32
    )
    inverse = lax.rsqrt(jnp.mean(hidden * hidden, axis=-1, keepdims=True) + EPS)
    scaled = grad * gain
    inner_sum = jnp.mean(scaled * hidden, axis=-1, keepdims=True)
    dv = inverse * scaled - hidden * (inverse * inverse * inverse * inner_sum)
    dv_ref[...] = dv
    small_ref[...] = jnp.zeros_like(small_ref)
    small_ref[0:1, :] = jnp.sum(grad * hidden * inverse, axis=0, keepdims=True)
    small_ref[8 : 8 + experts, :] = dot_tn(logit_grad, normed, highest)
    grad_low = (up + dv).astype(bf16)
    half = att_ref.shape[0]
    inner = w_ref.shape[0]
    att = jnp.concatenate(
        [att_ref[:, 0:inner].astype(f32), att_ref[:, inner : 2 * inner].astype(f32)], axis=0
    )
    att = widen(att, wide_s)
    wout_ref[...] = wout0_ref[...] + dot_tn(att.astype(bf16), grad_low)
    gh = dot_nt(grad_low, w_ref[...])
    gh_low = gh.astype(bf16)
    count = gh_ref.shape[0]
    each = inner // count
    ght_ref[...] = dot_nt(w_ref[...], grad_low).astype(bf16)
    for h in range(count):
        cols = slice(h * each, (h + 1) * each)
        gh_ref[h] = gh_low[:, cols]
        delta_ref[h] = jnp.sum(
            gh_low[:, cols].astype(f32) * att[:, cols], axis=-1, keepdims=True
        )


def sparse_back_kernel(
    gh_ref, ght_ref, delta_ref, vt_ref, k_ref, qsel_ref,
    place_ref, wq_ref, wk_ref, wv_ref, low_ref, gain_ref, small_ref, wout_ref, *refs, heads,
):
    per_head, refs = refs[: 4 * gh_ref.shape[0]], refs[4 * gh_ref.shape[0] :]
    psels, dq0s, dkt0s, dvt0s = (per_head[i :: 4] for i in range(4))
    chunks = refs[:5]
    (score_ref, send_ref, keep_ref, out_ref,
     dq_s, q_low, k_low, v_low, kt_s, vt_s, all_s) = refs[5:]
    head = lax.axis_index("head")
    count, rows, width = gh_ref.shape
    tokens = vt_ref.shape[1]
    inner = count * width
    for h in range(count):
        cols = slice(h * width, (h + 1) * width)
        grad = dot(gh_ref[h], vt_ref[cols, :])
        prob = psels[h][...]
        score = (prob.astype(f32) * (grad - delta_ref[h])).astype(bf16)
        score_ref[h] = score
        dq_s[:, cols] = dot(score, k_ref[h]) * (width ** (-0.5))
        dkt = dkt0s[h][...] + dot(qsel_ref[cols, :], score)
        dvt = dvt0s[h][...] + dot(ght_ref[cols, :], prob)
        kt_s[cols, :] = dkt.astype(bf16)
        vt_s[cols, :] = dvt.astype(bf16)
        k_low[:, cols] = jnp.transpose(dkt).astype(bf16)
        v_low[:, cols] = jnp.transpose(dvt).astype(bf16)
    spread = dot(place_ref[...], dq_s[...].astype(bf16))
    for h in range(count):
        cols = slice(h * width, (h + 1) * width)
        q_low[:, cols] = (spread[:, cols] + dq0s[h][...]).astype(bf16)
    part = tokens // heads
    half = part // 2
    own, to_1, to_2, rest_1, rest_2 = chunks
    to_1[part:, :] = jnp.zeros((EXTRA, to_1.shape[1]), bf16)
    places = (
        ((own, 0), (own, half)),
        ((to_1, 0), (rest_1, 0)),
        ((rest_2, 0), (to_2, 0)),
        ((to_1, half), (to_2, half)),
    )
    for d in range(heads):
        mine = pl.ds(pl.multiple_of((head ^ d) * part, part), part)
        rows_part = (
            dot(q_low[mine, :], wq_ref[...])
            + dot(k_low[mine, :], wk_ref[...])
            + dot(v_low[mine, :], wv_ref[...])
        ).astype(bf16)
        for n, (ref, first) in enumerate(places[d]):
            ref[first : first + half, :] = rows_part[n * half : (n + 1) * half]
    low = low_ref[...]
    total = None
    grads = (dot_tn(q_low[...], low), dot(kt_s[...], low), dot(vt_s[...], low))
    for i, (grad, w) in enumerate(zip(grads, (wq_ref, wk_ref, wv_ref))):
        all_s[i * inner : (i + 1) * inner, :] = grad
        term = jnp.sum(grad * w[...].astype(f32), axis=0, keepdims=True)
        total = term if total is None else total + term
    all_s[3 * inner :, :] = wout_ref[...]
    out_ref[...] = small_ref[...]
    out_ref[1:2, :] = total / gain_ref[...]
    to_1[part : part + 1, :] = (total / gain_ref[...]).astype(bf16)
    split_rows(all_s, 1, send_ref, keep_ref)


def is_upper(bit):
    return (lax.axis_index("seq") & bit) != 0


def split_rows(all_s, bit, send_ref, keep_ref):
    half = send_ref.shape[0]
    low, high = all_s[0:half, :], all_s[half : 2 * half, :]
    keep_ref[...] = jnp.where(is_upper(bit), high, low)
    send_ref[...] = jnp.where(is_upper(bit), low, high).astype(bf16)


def halve_kernel(keep_ref, got_ref, *refs, bit):
    send_ref, out_ref, all_s = refs[-3:]
    if len(refs) > 3:
        rest_1, got_1, rest_2, got_2, small_ref, next_1, next_2 = refs[:-3]
        half = rest_1.shape[0]
        for rest, got, onward in ((rest_1, got_2, next_1), (rest_2, got_1, next_2)):
            got_rest = got[half : 2 * half, :].astype(f32)
            onward[0:half, :] = (rest[...].astype(f32) + got_rest).astype(bf16)
        mine = small_ref[1:2, :].astype(bf16).astype(f32)
        next_2[half:, :] = jnp.zeros((EXTRA, next_2.shape[1]), bf16)
        next_2[half : half + 1, :] = (mine + got_1[2 * half : 2 * half + 1, :].astype(f32)).astype(bf16)
    all_s[...] = keep_ref[...] + got_ref[...].astype(f32)
    split_rows(all_s, bit, send_ref, out_ref)


def join_rows(mine_ref, got_ref, all_s, bit, count):
    mine, got = mine_ref[...].astype(f32), got_ref[...].astype(f32)
    all_s[0:count, :] = jnp.where(is_upper(bit), got[:count], mine[:count])
    all_s[count : 2 * count, :] = jnp.where(is_upper(bit), mine[:count], got[:count])
    all_s[2 * count :, :] = mine[count:] + got[count:]


def pair_kernel(mine_ref, got_ref, *refs, bit, count):
    out_ref, all_s = refs[-2:]
    if len(refs) > 2:
        got_1, got_2, next_1, next_2 = refs[:-2]
        half = next_1.shape[0]
        next_2[...] = got_1[0:half, :]
        next_1[...] = got_2[half:, :]
    join_rows(mine_ref, got_ref, all_s, bit, count)
    out_ref[...] = all_s[...].astype(bf16)


def final_kernel(mine_ref, got_ref, *refs, bit, count):
    gain1_ref, gain2_ref, table_ref, router_ref, all_s = refs[-5:]
    outs = refs[:-5]
    join_rows(mine_ref, got_ref, all_s, bit, count)
    inner = outs[0].shape[0]
    for i, out in enumerate(outs):
        out[...] = all_s[i * inner : (i + 1) * inner, :]
    small = all_s[2 * count :, :]
    gain1_ref[...] = small[1, :]
    gain2_ref[...] = small[0, :]
    heads, buckets = table_ref.shape
    table_ref[...] = small[2 : 2 + heads, :buckets]
    router_ref[...] = small[8 : 8 + router_ref.shape[0], :]


def bias_grad_kernel(
    score_ref, place_ref, buckets_ref, small_ref, *refs, bucket_count
):
    count = score_ref.shape[0]
    offs, out_ref, acc_s, sums_s = refs[:count], *refs[count:]
    tokens = place_ref.shape[0]
    offsets = buckets_ref.shape[1]
    out_ref[...] = small_ref[...]
    bucket_hot = (iota((bucket_count, offsets), 0) == buckets_ref[...]).astype(f32)

    def one_head(h, carry):
        acc_s[...] = jnp.zeros_like(acc_s)
        for i in range(0, tokens, BLOCK):
            first = tokens - BLOCK - i
            acc_s[:, first : first + tokens] += dot(place_ref[i : i + BLOCK, :], score_ref[h])
        sums_s[h] = diagonals(acc_s[...])
        return carry

    lax.fori_loop(0, count, one_head, 0)
    for h in range(count):
        sums = sums_s[h] + offs[h][...]
        out_ref[2 + h : 3 + h, :bucket_count] = dot_nt(sums[:, :offsets], bucket_hot, highest)[0:1]


def hidden_kernel(*refs, heads):
    att_parts, w_ref, x_ref, out_ref, att_s = refs[:heads], *refs[heads:]
    head = lax.axis_index("head")
    tokens = x_ref.shape[0]
    inner = att_parts[0].shape[0]
    for d in range(heads):
        mine = pl.ds(pl.multiple_of((head ^ d) * inner, inner), inner)
        att_s[mine, :] = att_parts[d][...]

    def block(i, carry):
        rows = pl.ds(pl.multiple_of(i * 256, 256), 256)
        out_ref[rows, :] = x_ref[rows, :].astype(f32) + dot_tn(att_s[:, rows], w_ref[...])
        return carry

    lax.fori_loop(0, tokens // 256, block, 0)


def output_kernel(hidden_ref, place_ref, comb_ref, out_ref):
    high, rest = split_two(comb_ref[...])

    def block(i, carry):
        rows = pl.ds(pl.multiple_of(i * 256, 256), 256)
        where = place_ref[rows, :]
        out_ref[rows, :] = hidden_ref[rows, :] + (dot(where, high) + dot(where, rest))
        return carry

    lax.fori_loop(0, hidden_ref.shape[0] // 256, block, 0)


def first_norm_kernel(
    own, got_1, got_2, last_1, last_2, next_2, small_ref,
    x_ref, cot_ref, place_ref, dv_ref, gain_ref, keep_ref, got_ref, out_ref, sum_ref,
):
    half = last_1.shape[0]
    high, rest = split_two(dv_ref[...])
    for first, near, far in ((0, got_1, last_2), (half, got_2, last_1)):
        rows = pl.ds(first, half)
        grad = own[rows, :].astype(f32) + near[0:half, :].astype(f32)
        grad = grad + far[0:half, :].astype(f32)
        x = x_ref[rows, :].astype(f32)
        inverse = lax.rsqrt(jnp.mean(x * x, axis=-1, keepdims=True) + EPS)
        scaled = grad * gain_ref[...]
        inner_sum = jnp.mean(scaled * x, axis=-1, keepdims=True)
        where = place_ref[rows, :]
        hidden_grad = cot_ref[rows, :].astype(f32) + (dot(where, high) + dot(where, rest))
        out_ref[rows, :] = (
            hidden_grad + inverse * scaled - x * (inverse * inverse * inverse * inner_sum)
        ).astype(bf16)
    count = keep_ref.shape[0]
    sum_ref[0:count, :] = (keep_ref[...] + got_ref[...].astype(f32)).astype(bf16)
    gain1 = next_2[half:, :].astype(f32)[0:1] + last_2[half:, :].astype(f32)[0:1]
    small = small_ref[...]
    sum_ref[count:, :] = jnp.where(iota(small.shape, 0) == 1, gain1, small).astype(bf16)


def spread_near_kernel(own, got_1, got_2, out_ref, token, wide_s, sems):
    head = lax.axis_index("head")
    part = own.shape[0]
    copies = []
    for d, piece in enumerate((own, got_1, got_2)):
        wide_s[d] = piece[...].astype(f32)
        mine = pl.ds(pl.multiple_of((head ^ d) * part, part), part)
        copies.append(pltpu.make_async_copy(wide_s.at[d], out_ref.at[mine], sems.at[d]))
        copies[-1].start()
    token[...] = jnp.zeros_like(token)
    for copy in copies:
        copy.wait()


def spread_far_kernel(last_1, last_2, given, out_ref, wide_s, sem):
    head = lax.axis_index("head")
    half = last_1.shape[0]
    wide_s[0:half, :] = last_2[...].astype(f32)
    wide_s[half:, :] = last_1[...].astype(f32)
    mine = pl.ds(pl.multiple_of((head ^ 3) * 2 * half, 2 * half), 2 * half)
    copy = pltpu.make_async_copy(wide_s, out_ref.at[mine], sem)
    copy.start()
    copy.wait()


def swap(x, axis, d):
    size = lax.axis_size(axis)
    return lax.ppermute(x, axis, [(i, i ^ d) for i in range(size)])


def share(x, axis):
    return [x] + [swap(x, axis, d) for d in range(1, lax.axis_size(axis))]


def trade(pieces, axis):
    return lax.all_to_all(pieces, axis, split_axis=0, concat_axis=0, tiled=True)


def swap_all(pieces, axis):
    return [pieces[0]] + [swap(pieces[d], axis, d) for d in range(1, len(pieces))]


def bits_of(axis):
    return [b for b in (1 << i for i in range(16)) if b < lax.axis_size(axis)]


def halve(send, keep, bit, after, onward=()):
    rows, width = keep.shape
    outs = []
    if onward:
        half = onward[0].shape[0]
        outs = [shape_of(half, width, bf16), shape_of(half + EXTRA, width, bf16)]
    return call(
        partial(halve_kernel, bit=bit),
        outs + [shape_of(rows // 2, width, bf16), shape_of(rows // 2, width, f32)],
        (keep, swap(send, "seq", bit // 2)) + tuple(onward),
        scratch=[pltpu.VMEM((rows, width), f32)],
        name="halve",
        after=after,
        token=True,
    )


def pair(now, small_rows, bit, after, onward=()):
    rows, width = now.shape
    count = rows - small_rows
    outs = [shape_of(onward[0].shape[0] // 2, width, bf16)] * 2 if onward else []
    return call(
        partial(pair_kernel, bit=bit, count=count),
        outs + [shape_of(rows + count, width, bf16)],
        (now, swap(now, "seq", bit)) + tuple(onward),
        scratch=[pltpu.VMEM((rows + count, width), f32)],
        name="pair",
        after=after,
        token=True,
    )


def on_device(
    layer_input, cotangent, norm1_gain, w_query, w_key, w_value, w_attn_out, bias_table,
    norm2_gain, w_router, w_expert_in, w_expert_out, expert_ids, slot_ids, buckets,
):
    tokens, width = layer_input.shape
    shards = lax.axis_size("seq")
    heads = lax.axis_size("head")
    bucket_count, count = bias_table.shape
    inner = w_query.shape[1]
    each = inner // count
    experts = w_router.shape[1]
    rows, filled = experts * SLOT, experts * CAP
    hidden_units = w_expert_in.shape[2]
    part = tokens // heads
    split = 2 * width // heads
    span = 2 * tokens
    params = pltpu.CompilerParams(vmem_limit_bytes=VMEM_LIMIT if rows <= 256 else VMEM_ALL)

    ids = expert_ids.reshape(1, tokens)
    slots = slot_ids.reshape(1, tokens)
    bucket_row = buckets.reshape(1, -1)
    wq_t, wk_t, wv_t = jnp.transpose(w_query), jnp.transpose(w_key), jnp.transpose(w_value)
    router_t, table_t = jnp.transpose(w_router), jnp.transpose(bias_table)
    w_in = w_expert_in.reshape(width, hidden_units)
    w_out = w_expert_out.reshape(hidden_units, width)

    w_mix = share(w_attn_out, "head")

    low, prob, att, att_t, att_sel = pl.pallas_call(
        attend_kernel,
        out_shape=(
            shape_of(tokens, width, bf16),
            jax.ShapeDtypeStruct((count, tokens, tokens), bf16),
            jax.ShapeDtypeStruct((count, tokens, each), bf16),
            shape_of(inner, tokens, bf16),
            shape_of(filled // 2, 2 * inner, bf16),
        ),
        in_specs=[spec(pltpu.HBM)] * 9,
        out_specs=(spec(pltpu.VMEM),) * 5,
        scratch_shapes=[
            pltpu.VMEM((count, tokens, each), bf16),
            pltpu.VMEM((inner, tokens), bf16),
            pltpu.VMEM((count, tokens, each), bf16),
            pltpu.VMEM((8, span), f32),
            pltpu.VMEM((2, BLOCK, span), f32),
            pltpu.VMEM((filled, tokens), bf16),
            pltpu.VMEM((2, 2 * BLOCK, tokens), f32),
            pltpu.VMEM((tokens, width), bf16),
            pltpu.VMEM((width,), f32),
            pltpu.VMEM((inner, width), bf16),
            pltpu.VMEM((inner, width), bf16),
            pltpu.VMEM((inner, width), bf16),
            pltpu.VMEM((count, bucket_count), f32),
            pltpu.VMEM((1, span - 1), jnp.int32),
            pltpu.VMEM((1, tokens), jnp.int32),
            pltpu.VMEM((1, tokens), jnp.int32),
            pltpu.SemaphoreType.DMA((9,)),
        ],
        compiler_params=params,
        cost_estimate=NO_COST,
        name="attend",
    )(
        *(
            pltpu.with_memory_space_constraint(a, pltpu.HBM)
            for a in (layer_input, norm1_gain, wq_t, wk_t, wv_t, table_t, bucket_row, ids, slots)
        )
    )

    (att_sel,) = call(
        pass_kernel,
        [shape_of(filled // 2, 2 * inner, bf16)],
        (att_sel,),
        name="pass",
        after=(w_mix[1],),
    )
    sel_parts = share(att_sel, "head")
    sel_in, sel_up, place, place_c, x_c, cot_c, w_full = call(
        partial(place_kernel, heads=heads),
        [
            shape_of(rows, width, bf16),
            shape_of(rows, width, bf16),
            shape_of(tokens, rows, bf16),
            shape_of(part, rows, bf16),
            shape_of(part, width, bf16),
            shape_of(part, width, bf16),
            shape_of(heads * inner, width, bf16),
        ],
        (layer_input, cotangent, ids, slots) + tuple(w_mix),
        scratch=[pltpu.VMEM((tokens, rows), f32)],
        moved=12 * 2**20,
        name="place",
        after=(att_sel,),
    )
    routed = call(
        partial(route_kernel, shards=shards, heads=heads),
        [
            shape_of(rows, width, f32),
            shape_of(rows, width, f32),
            shape_of(rows, experts, f32),
            shape_of(inner, tokens, bf16),
        ]
        + [shape_of(TALL, packed_width(width), bf16)] * shards,
        tuple(sel_parts) + (w_full, sel_in, sel_up, norm2_gain, router_t, att_t),
        scratch=[
            pltpu.VMEM((heads, filled, inner), bf16),
            pltpu.VMEM((rows, 2 * width), f32),
            pltpu.VMEM((rows, width), f32),
            pltpu.VMEM((shards * TALL, packed_width(width)), f32),
        ],
        name="route",
    )
    hidden_sel, normed_sel, probs, att_on = routed[:4]
    pay_parts = swap_all(routed[4:], "seq")
    att_parts = [att_t] + [swap(att_on, "head", d) for d in range(1, heads - 1)]

    def masked_back(h, after):
        return call(
            partial(masked_back_kernel, h=h),
            [
                shape_of(tokens, each, f32),
                shape_of(each, tokens, f32),
                shape_of(each, tokens, f32),
                shape_of(8, span, f32),
                shape_of(rows, tokens, bf16),
            ],
            (gh, stack, k_rows, q_t, v_t, att, prob),
            scratch=[pltpu.VMEM((BLOCK, span), f32), pltpu.VMEM((tokens, tokens), bf16)],
            name="masked_back",
            after=after,
            moved=11 * 2**20,
            token=True,
        )

    done = call(
        partial(expert_kernel, shards=shards, heads=heads),
        [shape_of(filled, split, bf16)] * heads
        + [
            shape_of(rows, width, bf16),
            shape_of(rows, hidden_units, bf16),
            shape_of(rows, hidden_units, bf16),
            shape_of(rows, width, bf16),
        ],
        tuple(pay_parts[d] for d in far_first(shards)) + (w_in, w_out),
        scratch=[
            pltpu.VMEM((rows, 2 * width), f32),
            pltpu.VMEM((rows, 1), f32),
            pltpu.VMEM((heads, filled, split), f32),
        ],
        name="expert",
        after=tuple(att_parts[1:]),
        token=True,
    )
    x_rows, act, pre_low, out_low, token = done[heads:]
    gh, stack, k_rows, q_t, v_t, wout0, q_sel, token = call(
        prep_kernel,
        [
            jax.ShapeDtypeStruct((count, tokens, each), bf16),
            jax.ShapeDtypeStruct((count, each + rows, tokens), bf16),
            jax.ShapeDtypeStruct((count, tokens, each), bf16),
            shape_of(inner, tokens, bf16),
            shape_of(inner, tokens, bf16),
            shape_of(inner, width, f32),
            shape_of(inner, rows, bf16),
        ],
        (cotangent, w_attn_out, wq_t, wk_t, wv_t, low, place, att_t),
        scratch=[pltpu.VMEM((inner, tokens), bf16), pltpu.VMEM((tokens, width), bf16)],
        name="prep",
        after=(token,),
        moved=8 * 2**20,
        token=True,
    )

    masked = []
    for h in range(count - 2):
        masked.append(masked_back(h, (token,)))
        token = masked[-1][-1]
    returned = call(
        partial(sum_kernel, heads=heads),
        [shape_of(inner, tokens, bf16)] + [shape_of(CAP, split, bf16)] * shards,
        [att_t] + swap_all(done[:heads], "head"),
        scratch=[pltpu.VMEM((filled, split), f32)],
        name="sum",
        after=(token,),
        token=True,
    )
    masked.append(masked_back(count - 2, (returned[-1],)))
    att_parts.append(swap(returned[0], "head", heads - 1))
    answers = swap_all(returned[1:-1], "seq")
    joined, token = call(
        join_kernel,
        [shape_of(filled, split, bf16)],
        [answers[d] for d in far_first(shards)],
        scratch=[pltpu.VMEM((filled, split), f32)],
        name="join",
        after=(masked[-1][-1], att_parts[-1]),
        token=True,
    )
    masked.append(masked_back(count - 1, (token,)))
    full_parts = share(joined, "head")

    small_rows = 8 + -(-experts // 8) * 8
    dv_sel, comb_sel, small, wout_part, gh_sel, ght_sel, delta_sel = call(
        partial(slot_back_kernel, heads=heads),
        [
            shape_of(rows, width, f32),
            shape_of(rows, width, f32),
            shape_of(small_rows, width, f32),
            shape_of(inner, width, f32),
            jax.ShapeDtypeStruct((count, rows, each), bf16),
            shape_of(inner, rows, bf16),
            jax.ShapeDtypeStruct((count, rows, 1), f32),
        ],
        tuple(full_parts)
        + (sel_up, normed_sel, hidden_sel, probs, router_t, norm2_gain)
        + (w_attn_out, att_sel, wout0),
        scratch=[pltpu.VMEM((heads, rows, split), f32), pltpu.VMEM((rows, inner), f32)],
        name="slot_back",
        after=(masked[-1][-1],),
    )

    back = call(
        partial(sparse_back_kernel, heads=heads),
        [shape_of(part, width, bf16), shape_of(part + EXTRA, width, bf16)]
        + [shape_of(part, width, bf16)]
        + [shape_of(part // 2, width, bf16)] * 2
        + [
            jax.ShapeDtypeStruct((count, rows, tokens), bf16),
            shape_of(2 * inner, width, bf16),
            shape_of(2 * inner, width, f32),
            shape_of(small_rows, width, f32),
        ],
        (gh_sel, ght_sel, delta_sel, v_t, k_rows, q_sel, place)
        + (wq_t, wk_t, wv_t, low, norm1_gain, small, wout_part)
        + tuple(a for m in masked for a in (m[4], m[0], m[1], m[2])),
        scratch=[
            pltpu.VMEM((rows, inner), f32),
            pltpu.VMEM((tokens, inner), bf16),
            pltpu.VMEM((tokens, inner), bf16),
            pltpu.VMEM((tokens, inner), bf16),
            pltpu.VMEM((inner, tokens), bf16),
            pltpu.VMEM((inner, tokens), bf16),
            pltpu.VMEM((4 * inner, width), f32),
        ],
        name="sparse_back",
    )
    score_sel, send, keep, small = back[5:]
    own, to_1, to_2, rest_1, rest_2 = back[:5]
    got_1, got_2 = swap(to_1, "head", 1), swap(to_2, "head", 2)

    bits = bits_of("seq")
    send, keep, token = halve(send, keep, bits[1], ())
    small_part = small
    small, token = call(
        partial(bias_grad_kernel, bucket_count=bucket_count),
        [shape_of(small_rows, width, f32)],
        (score_sel, place, bucket_row, small) + tuple(m[3] for m in masked),
        scratch=[pltpu.VMEM((BLOCK, span), f32), pltpu.VMEM((count, 8, span), f32)],
        name="bias_grad",
        after=(token,),
        moved=16 * 2**20,
        token=True,
    )
    next_1, next_2, send, keep, token = halve(
        send, keep, bits[2], (token,), (rest_1, got_1, rest_2, got_2, small_part)
    )
    last_1, last_2 = swap(next_1, "head", 1), swap(next_2, "head", 2)
    w_in_grad, w_out_grad, token = call(
        expert_grad_kernel,
        [
            jax.ShapeDtypeStruct(w_expert_in.shape, f32),
            jax.ShapeDtypeStruct(w_expert_out.shape, f32),
        ],
        (x_rows, pre_low, act, out_low),
        name="expert_grad",
        after=(token,),
        moved=10 * 2**20,
        token=True,
    )
    hidden, token = call(
        partial(hidden_kernel, heads=heads),
        [shape_of(tokens, width, f32)],
        tuple(att_parts) + (w_full, layer_input),
        scratch=[pltpu.VMEM((heads * inner, tokens), bf16)],
        name="hidden",
        after=(token,),
        moved=6 * 2**20,
        token=True,
    )
    for bit in bits[3:]:
        send, keep, token = halve(send, keep, bit, (token,))

    grad_part, weights, token = call(
        first_norm_kernel,
        [shape_of(part, width, bf16), shape_of(keep.shape[0] + small_rows, width, bf16)],
        (own, got_1, got_2, last_1, last_2, next_2, small)
        + (x_c, cot_c, place_c, dv_sel, norm1_gain)
        + (keep, swap(send, "seq", bits[-1])),
        name="first_norm",
        after=(token,),
        token=True,
    )
    grad_1, grad_2 = swap(grad_part, "head", 1), swap(grad_part, "head", 2)
    layer_output, token = call(
        output_kernel,
        [shape_of(tokens, width, f32)],
        (hidden, place, comb_sel),
        name="output",
        after=(token,),
        moved=10 * 2**20,
        token=True,
    )
    for bit in reversed(bits[3:]):
        weights, token = pair(weights, small_rows, bit, (token,))
    next_1, next_2, weights, token = pair(
        weights, small_rows, bits[2], (token,), (grad_1, grad_2)
    )
    grad_3 = (swap(next_1, "head", 1), swap(next_2, "head", 2))
    near, token = pl.pallas_call(
        spread_near_kernel,
        out_shape=(shape_of(tokens, width, f32), shape_of(8, 128, f32)),
        in_specs=[spec(pltpu.VMEM)] * 3,
        out_specs=(spec(pltpu.HBM), spec(pltpu.VMEM)),
        scratch_shapes=[pltpu.VMEM((3, part, width), f32), pltpu.SemaphoreType.DMA((3,))],
        compiler_params=params,
        cost_estimate=pl.CostEstimate(flops=1, bytes_accessed=5 * 2**20, transcendentals=0),
        name="spread_near",
    )(grad_part, grad_1, grad_2)
    weights, token = pair(weights, small_rows, bits[1], grad_3 + (token,))
    last = call(
        partial(final_kernel, bit=bits[0], count=2 * inner),
        [shape_of(inner, width, f32)] * 4
        + [
            jax.ShapeDtypeStruct((width,), f32),
            jax.ShapeDtypeStruct((width,), f32),
            shape_of(count, bucket_count, f32),
            shape_of(experts, width, f32),
        ],
        (weights, swap(weights, "seq", bits[0])),
        scratch=[pltpu.VMEM((4 * inner + small_rows, width), f32)],
        name="weights_out",
    )
    weight_sums = last[:4]
    gain1_sum, gain2_sum, table_sum, router_sum = last[4:]
    input_grad = pl.pallas_call(
        spread_far_kernel,
        out_shape=shape_of(tokens, width, f32),
        in_specs=[spec(pltpu.VMEM), spec(pltpu.VMEM), spec(pltpu.HBM)],
        out_specs=spec(pltpu.HBM),
        scratch_shapes=[pltpu.VMEM((part, width), f32), pltpu.SemaphoreType.DMA(())],
        input_output_aliases={2: 0},
        compiler_params=params,
        cost_estimate=NO_COST,
        name="spread_far",
    )(*grad_3, near)

    return (
        layer_output,
        input_grad,
        gain1_sum,
        jnp.transpose(weight_sums[0]),
        jnp.transpose(weight_sums[1]),
        jnp.transpose(weight_sums[2]),
        weight_sums[3],
        jnp.transpose(table_sum),
        gain2_sum,
        jnp.transpose(router_sum),
        w_in_grad,
        w_out_grad,
    )


def solution(mesh):
    return jax.shard_map(
        on_device,
        mesh=mesh,
        in_specs=(
            P("seq", None),
            P("seq", None),
            P(),
            P(None, "head"),
            P(None, "head"),
            P(None, "head"),
            P("head", None),
            P(None, "head"),
            P(),
            P(),
            P("seq", None, "head"),
            P("seq", "head", None),
            P("seq"),
            P("seq"),
            P(),
        ),
        out_specs=(
            P("seq", None),
            P("seq", None),
            P(),
            P(None, "head"),
            P(None, "head"),
            P(None, "head"),
            P("head", None),
            P(None, "head"),
            P(),
            P(),
            P("seq", None, "head"),
            P("seq", "head", None),
        ),
        check_vma=False,
    )
```

```python
from functools import partial

import jax
import jax.numpy as jnp
import numpy as np
from jax import lax
from jax.experimental import pallas as pl
from jax.experimental.pallas import tpu as pltpu
from jax.sharding import PartitionSpec as P

CAP = 20
SLOT = 24
EPS = 1e-06
BLOCK = 128
ROWS = 16
EXTRA = 16
TALL = 16
VMEM_LIMIT = 26 * 1024 * 1024
VMEM_ALL = 60 * 1024 * 1024
NO_COST = pl.CostEstimate(flops=1, bytes_accessed=1, transcendentals=0)

f32 = jnp.float32
bf16 = jnp.bfloat16
highest = lax.Precision.HIGHEST


def dot(a, b):
    return jnp.dot(a, b, preferred_element_type=f32)


def dot_nt(a, b, precision=None):
    return lax.dot_general(
        a, b, (((1,), (1,)), ((), ())), precision=precision, preferred_element_type=f32
    )


def dot_tn(a, b, precision=None):
    return lax.dot_general(
        a, b, (((0,), (0,)), ((), ())), precision=precision, preferred_element_type=f32
    )


def iota(shape, dim):
    return lax.broadcasted_iota(jnp.int32, shape, dim)


def split_two(v):
    high = v.astype(bf16)
    return high, (v - high.astype(f32)).astype(bf16)


def shape_of(rows, cols, dtype):
    return jax.ShapeDtypeStruct((rows, cols), dtype)


def spec(memory):
    return pl.BlockSpec(memory_space=memory)


def call(kernel, outs, args, scratch=(), name=None, after=(), moved=1, token=False):
    outs, args = tuple(outs), tuple(args)
    held = sum(int(np.prod(a.shape)) * np.dtype(a.dtype).itemsize for a in args + outs)
    if token:
        outs += (shape_of(8, 128, f32),)
    first_out = len(args) + len(after)

    def body(*refs):
        results = refs[first_out : first_out + len(outs)]
        if token:
            results[-1][...] = jnp.zeros((8, 128), f32)
            results = results[:-1]
        kernel(*refs[: len(args)], *results, *refs[first_out + len(outs) :])

    return pl.pallas_call(
        body,
        out_shape=outs,
        in_specs=[spec(pltpu.VMEM)] * len(args) + [spec(pl.ANY)] * len(after),
        out_specs=tuple(spec(pltpu.VMEM) for _ in outs),
        scratch_shapes=list(scratch),
        compiler_params=pltpu.CompilerParams(
            vmem_limit_bytes=VMEM_LIMIT if 2 * held < VMEM_LIMIT else VMEM_ALL
        ),
        cost_estimate=pl.CostEstimate(flops=1, bytes_accessed=moved, transcendentals=0),
        name=name,
    )(*args, *after)


def slot_rows(ids, slots, rows, each):
    cell = jnp.where(slots < CAP, ids * each + slots, -1)
    return (iota((rows, cell.shape[1]), 0) == cell).astype(f32)


def place_kernel(x_ref, cot_ref, ids_ref, slots_ref, *refs, heads):
    w_parts = refs[:heads]
    sel_in, sel_up, place, place_c, x_c, cot_c, w_ref, place_s = refs[heads:]
    head = lax.axis_index("head")
    part = x_c.shape[0]
    slot_hot = slot_rows(ids_ref[...], slots_ref[...], sel_in.shape[0], SLOT)
    place_s[...] = jnp.transpose(slot_hot)
    slot_low = slot_hot.astype(bf16)
    sel_in[...] = dot(slot_low, x_ref[...]).astype(bf16)
    sel_up[...] = dot(slot_low, cot_ref[...]).astype(bf16)
    place[...] = place_s[...].astype(bf16)
    mine = pl.ds(pl.multiple_of(head * part, part), part)
    place_c[...] = place_s[mine, :].astype(bf16)
    x_c[...] = x_ref[mine, :]
    cot_c[...] = cot_ref[mine, :]
    inner = w_parts[0].shape[0]
    for d in range(heads):
        rows = pl.ds(pl.multiple_of((head ^ d) * inner, inner), inner)
        w_ref[rows, :] = w_parts[d][...]


def attend_kernel(*refs):
    given, refs = refs[:9], refs[9:]
    low_ref, prob_ref, att_ref, attt_ref, sel_ref = refs[:5]
    q_s, kt_s, v_s, bias_s, skew_s, slot_s, score_s = refs[5:12]
    here, sems = refs[12:21], refs[21]
    x_ref, gain_ref, wq_ref, wk_ref, wv_ref, table_ref, buckets_ref, ids_ref, slots_ref = here
    copies = [
        pltpu.make_async_copy(far, near, sems.at[i])
        for i, (far, near) in enumerate(zip(given, here))
    ]
    tokens = x_ref.shape[0]
    inner = wq_ref.shape[0]
    count = q_s.shape[0]
    width = inner // count
    span = skew_s.shape[2]
    tall = 2 * BLOCK
    for copy in copies:
        copy.start()
    for copy in copies[5:]:
        copy.wait()
    slot_s[...] = slot_rows(ids_ref[...], slots_ref[...], slot_s.shape[0], CAP).astype(bf16)
    offsets = buckets_ref.shape[1]
    bucket_hot = (iota((table_ref.shape[1], offsets), 0) == buckets_ref[...]).astype(f32)
    bias_s[...] = jnp.zeros_like(bias_s)
    bias_s[:count, :offsets] = jnp.dot(
        table_ref[...], bucket_hot, precision=highest, preferred_element_type=f32
    )
    for copy in copies[:2]:
        copy.wait()
    for i in range(0, tokens, 256):
        rows = pl.ds(i, 256)
        x = x_ref[rows, :].astype(f32)
        inverse = lax.rsqrt(jnp.mean(x * x, axis=-1, keepdims=True) + EPS)
        low_ref[rows, :] = (x * inverse * gain_ref[...]).astype(bf16)
    for copy in copies[2:5]:
        copy.wait()
    low = low_ref[...]
    q = dot_nt(low, wq_ref[...]).astype(bf16) * bf16(width ** (-0.5))
    kt_s[...] = dot_nt(wk_ref[...], low).astype(bf16)
    v = dot_nt(low, wv_ref[...]).astype(bf16)
    for h in range(count):
        cols = slice(h * width, (h + 1) * width)
        q_s[h] = q[:, cols]
        v_s[h] = v[:, cols]

    blocks = tokens // tall
    half = sel_ref.shape[0]

    def lay_bias(h):
        skew_s[h % 2] = pltpu.roll(
            jnp.broadcast_to(bias_s[h : h + 1, :], skew_s.shape[1:]),
            span - (BLOCK - 1), 1, stride=1, stride_axis=0,
        )

    def scores(h, n):
        score_s[n % 2] = dot(
            q_s[h, pl.ds(n * tall, tall), :], kt_s[h * width : (h + 1) * width, :]
        )

    def weights(h, n):
        for j in range(0, tall, ROWS):
            row = n * tall + j
            first = tokens - BLOCK - row // BLOCK * BLOCK
            bias = skew_s[h % 2, j % BLOCK : j % BLOCK + ROWS, first : first + tokens]
            score = score_s[n % 2, j : j + ROWS, :] + bias
            weight = jnp.exp(score - jnp.max(score, axis=-1, keepdims=True))
            total = jnp.sum(weight, axis=-1, keepdims=True)
            prob_ref[h, pl.ds(row, ROWS), :] = (weight * (1.0 / total)).astype(bf16)

    lay_bias(0)
    scores(0, 0)
    for h in range(count):
        for n in range(blocks):
            if n + 1 < blocks:
                scores(h, n + 1)
            elif h + 1 < count:
                lay_bias(h + 1)
                scores(h + 1, 0)
            weights(h, n)
        att = dot(prob_ref[h], v_s[h])
        att_low = att.astype(bf16)
        att_ref[h] = att_low
        attt_ref[h * width : (h + 1) * width, :] = jnp.transpose(att).astype(bf16)
        picked = dot(slot_s[...], att_low).astype(bf16)
        for part in range(2):
            start = part * inner + h * width
            sel_ref[:, start : start + width] = picked[part * half : (part + 1) * half]


def pass_kernel(given, passed):
    passed[...] = given[...]


def widen(rows, wide_s):
    wide_s[...] = jnp.zeros_like(wide_s)
    for e in range(rows.shape[0] // CAP):
        wide_s[e * SLOT : e * SLOT + CAP, :] = rows[e * CAP : (e + 1) * CAP]
    return wide_s[...]


def packed_width(width):
    return 2 * width + width // 2 + 128


def short_rows(width):
    each = width // 2
    for i in range(CAP - TALL):
        for k in range(4):
            yield TALL + i, slice(k * each, (k + 1) * each), 4 * i + k


def route_kernel(*refs, shards, heads):
    att_parts, w_ref = refs[:heads], refs[heads]
    (sel_in, sel_up, gain_ref, router_ref, att_t, hidden_ref, normed_ref, probs_ref, att_on
     ) = refs[heads + 1 : heads + 10]
    pieces = refs[heads + 10 : heads + 10 + shards]
    att_s, pay_s, wide_s, pack_s = refs[heads + 10 + shards :]
    head = lax.axis_index("head")
    half = att_parts[0].shape[0]
    inner = w_ref.shape[0] // heads
    for d in range(heads):
        att_s[d, 0:half, :] = att_parts[d][:, 0:inner]
        att_s[d, half : 2 * half, :] = att_parts[d][:, inner : 2 * inner]
    mixed = None
    for k in range(heads):
        term = dot(att_s[head ^ k], w_ref[k * inner : (k + 1) * inner, :])
        mixed = term if mixed is None else mixed + term
    hidden = sel_in[...].astype(f32) + widen(mixed, wide_s)
    hidden_ref[...] = hidden
    inverse = lax.rsqrt(jnp.mean(hidden * hidden, axis=-1, keepdims=True) + EPS)
    normed = hidden * inverse * gain_ref[...]
    normed_ref[...] = normed
    logits = dot_nt(normed, router_ref[...], highest)
    logits = logits - jnp.max(logits, axis=-1, keepdims=True)
    powers = jnp.exp(logits)
    probs = powers / jnp.sum(powers, axis=-1, keepdims=True)
    probs_ref[...] = probs
    gate = jnp.sum(jnp.where(chosen_of(probs.shape), probs, 0.0), axis=-1, keepdims=True)
    high = gate.astype(bf16).astype(f32)
    lane = iota((gate.shape[0], 128), 1)
    width = normed.shape[1]
    rest = gate - high
    first_gates = jnp.where(lane == 0, high, jnp.where(lane == 1, rest, 0.0))
    last_gates = jnp.where(lane == 2, high, jnp.where(lane == 3, rest, 0.0))
    pay_s[:, :width] = normed
    pay_s[:, width:] = sel_up[...].astype(f32)
    full, side = 2 * width, 2 * width + width // 2
    for e in range(shards):
        rows, packed = e * SLOT, e * TALL
        pack_s[packed : packed + TALL, :full] = pay_s[rows : rows + TALL, :]
        for row, lanes, to in short_rows(width):
            pack_s[packed + to : packed + to + 1, full:side] = pay_s[
                rows + row : rows + row + 1, lanes
            ]
        pack_s[packed : packed + 8, side:] = (
            first_gates[rows : rows + 8] + last_gates[rows + TALL : rows + SLOT]
        )
        pack_s[packed + 8 : packed + TALL, side:] = first_gates[rows + 8 : rows + TALL]
    shard = lax.axis_index("seq")
    for j in range(shards):
        first = pl.multiple_of((shard ^ j) * TALL, TALL)
        pieces[j][...] = pack_s[pl.ds(first, TALL), :].astype(bf16)
    att_on[...] = att_t[...]


def chosen_of(shape):
    expert = iota(shape, 1) * SLOT
    slot_row = iota(shape, 0)
    return (slot_row >= expert) & (slot_row < expert + SLOT)


def far_first(count):
    return list(range(count - 2, 1, -2)) + list(range(count - 1, 2, -2)) + [1, 0]


def by_partner(refs):
    return [ref for _, ref in sorted(zip(far_first(len(refs)), refs), key=lambda t: t[0])]


def expert_kernel(*refs, shards, heads):
    parts = by_partner(refs[:shards])
    w_in, w_out = refs[shards : shards + 2]
    chunks = refs[shards + 2 : shards + 2 + heads]
    x_ref, act_ref, pre_ref, out_ref, pay_s, gate_s, both_s = refs[shards + 2 + heads :]
    head = lax.axis_index("head")
    width = x_ref.shape[1]
    full, side = 2 * width, 2 * width + width // 2
    for j in range(shards):
        rows = j * SLOT
        part = parts[j][...].astype(f32)
        pay_s[rows : rows + TALL, :] = part[:, :full]
        pay_s[rows + TALL : rows + SLOT, :] = jnp.zeros((SLOT - TALL, full), f32)
        for row, lanes, place in short_rows(width):
            pay_s[rows + row : rows + row + 1, lanes] = part[place : place + 1, full:side]
        gate_s[rows : rows + TALL, :] = part[:, side : side + 1] + part[:, side + 1 : side + 2]
        gate_s[rows + TALL : rows + SLOT, :] = (
            part[:8, side + 2 : side + 3] + part[:8, side + 3 : side + 4]
        )
    x = pay_s[:, :width].astype(bf16)
    up = pay_s[:, width:]
    gate = gate_s[...]
    out_low = (gate * up).astype(bf16)
    pre = dot(x, w_in[...])
    cdf = 0.5 * (1.0 + lax.erf(pre * (0.5**0.5)))
    act = (pre * cdf).astype(bf16)
    slope = cdf + pre * jnp.exp(-0.5 * pre * pre) * ((2.0 * np.pi) ** (-0.5))
    pre_low = (dot_nt(out_low, w_out[...]) * slope).astype(bf16)
    both = (dot(act, w_out[...]), dot_nt(pre_low, w_in[...]))
    part = both_s.shape[2]
    for k in range(heads):
        start = k % (heads // 2) * part
        for j in range(shards):
            both_s[k, j * CAP : (j + 1) * CAP, :] = both[k // (heads // 2)][
                j * SLOT : j * SLOT + CAP, start : start + part
            ]
    for d in range(heads):
        chunks[d][...] = both_s[head ^ d].astype(bf16)
    pre_ref[...] = pre_low
    out_ref[...] = out_low
    x_ref[...] = x
    act_ref[...] = act


def expert_grad_kernel(x_ref, pre_ref, act_ref, out_ref, in_grad, out_grad):
    in_grad[0] = dot_tn(x_ref[...], pre_ref[...])
    out_grad[0] = dot_tn(act_ref[...], out_ref[...])


def sum_kernel(att_ref, *refs, heads):
    parts, att_on, pieces, sum_s = refs[:heads], refs[heads], refs[heads + 1 : -1], refs[-1]
    att_on[...] = att_ref[...]
    total = parts[0][...].astype(f32)
    for d in range(1, heads):
        total = total + parts[d][...].astype(f32)
    sum_s[...] = total
    for j, piece in enumerate(pieces):
        piece[...] = sum_s[j * CAP : (j + 1) * CAP, :].astype(bf16)


def join_kernel(*refs):
    parts, out_ref, sum_s = by_partner(refs[:-2]), refs[-2], refs[-1]
    for j, part in enumerate(parts):
        sum_s[j * CAP : (j + 1) * CAP, :] = part[...].astype(f32)
    out_ref[...] = sum_s[...].astype(bf16)


def prep_kernel(
    cot_ref, w_ref, wq_ref, wk_ref, wv_ref, low_ref, place_ref, attt_ref,
    gh_ref, stack_ref, k_ref, qt_ref, vt_ref, wout_ref, qsel_ref, ght_s, mcot_s,
):
    count, tokens, width = gh_ref.shape
    for i in range(0, tokens, 256):
        rows = pl.ds(i, 256)
        where = place_ref[rows, :].astype(f32)
        free = 1.0 - jnp.sum(where, axis=-1, keepdims=True)
        mcot_s[rows, :] = (cot_ref[rows, :].astype(f32) * free).astype(bf16)
        slots = jnp.transpose(where).astype(bf16)
        for h in range(count):
            stack_ref[h, width:, rows] = slots
    gh = dot_nt(mcot_s[...], w_ref[...]).astype(bf16)
    ght_s[...] = dot_nt(w_ref[...], mcot_s[...]).astype(bf16)
    k = dot_nt(low_ref[...], wk_ref[...]).astype(bf16)
    qt_ref[...] = dot_nt(wq_ref[...], low_ref[...]).astype(bf16) * bf16(width ** (-0.5))
    vt_ref[...] = dot_nt(wv_ref[...], low_ref[...]).astype(bf16)
    for h in range(count):
        cols = slice(h * width, (h + 1) * width)
        gh_ref[h] = gh[:, cols]
        k_ref[h] = k[:, cols]
        stack_ref[h, 0:width, :] = ght_s[cols, :]
    wout_ref[...] = dot(attt_ref[...], mcot_s[...])
    qsel_ref[...] = dot(qt_ref[...], place_ref[...]).astype(bf16)


def masked_back_kernel(
    gh_ref, stack_ref, k_ref, qt_ref, vt_ref, att_ref, prob_ref,
    dq_ref, dkt_ref, dvt_ref, offs_ref, psel_ref, acc_s, score_s, *, h,
):
    tokens, width = dq_ref.shape
    acc_s[...] = jnp.zeros_like(acc_s)
    cols = slice(h * width, (h + 1) * width)
    for i in range(0, tokens, 2 * BLOCK):
        rows = pl.ds(i, 2 * BLOCK)
        gh = gh_ref[h, rows, :]
        delta = jnp.sum(gh.astype(f32) * att_ref[h, rows, :].astype(f32), axis=-1, keepdims=True)
        grads = dot(gh, vt_ref[cols, :]) - delta
        for j in range(2):
            start = i + j * BLOCK
            first = tokens - BLOCK - start
            here = pl.ds(start, BLOCK)
            score = prob_ref[h, here, :].astype(f32) * grads[j * BLOCK : (j + 1) * BLOCK]
            acc_s[:, first : first + tokens] += score
            score_s[here, :] = score.astype(bf16)
    dq_ref[...] = dot(score_s[...], k_ref[h]) * (width ** (-0.5))
    dkt_ref[...] = dot(qt_ref[cols, :], score_s[...])
    both = dot(stack_ref[h], prob_ref[h])
    dvt_ref[...] = both[:width]
    psel_ref[...] = both[width:].astype(bf16)
    offs_ref[...] = diagonals(acc_s[...])


def diagonals(acc):
    span = acc.shape[1]
    rows = acc.shape[0] // 2
    while rows >= 8:
        acc = acc[:rows] + pltpu.roll(acc[rows:], span - rows, 1)
        rows //= 2
    total = acc[0:1]
    for r in range(1, 8):
        total = total + pltpu.roll(acc[r : r + 1], span - r, 1)
    return jnp.broadcast_to(pltpu.roll(total, BLOCK - 1, 1), (8, span))


def slot_back_kernel(*refs, heads):
    parts = refs[:heads]
    (up_ref, normed_ref, hidden_ref, probs_ref, router_ref, gain_ref, w_ref, att_ref,
     wout0_ref) = refs[heads : heads + 9]
    (dv_ref, comb_ref, small_ref, wout_ref, gh_ref, ght_ref, delta_ref, ret_s, wide_s
     ) = refs[heads + 9 :]
    head, shard = lax.axis_index("head"), lax.axis_index("seq")
    ret_s[...] = jnp.zeros_like(ret_s)
    for d in range(heads):
        part = parts[d][...].astype(f32)
        for j in range(part.shape[0] // CAP):
            first = pl.multiple_of((shard ^ j) * SLOT, SLOT)
            ret_s[head ^ d, pl.ds(first, CAP), :] = part[j * CAP : (j + 1) * CAP]
    back = [ret_s[k] for k in range(heads)]
    combined = jnp.concatenate(back[: heads // 2], axis=1)
    grad_buf = jnp.concatenate(back[heads // 2 :], axis=1)
    up = up_ref[...].astype(f32)
    hidden, normed, probs, gain = hidden_ref[...], normed_ref[...], probs_ref[...], gain_ref[...]
    chosen = chosen_of(probs.shape)
    gate = jnp.sum(jnp.where(chosen, probs, 0.0), axis=-1, keepdims=True)
    comb_ref[...] = gate * combined
    gate_grad = jnp.sum(up * combined, axis=-1, keepdims=True)
    marked = jnp.where(chosen, gate_grad, 0.0)
    logit_grad = probs * (marked - jnp.sum(marked * probs, axis=-1, keepdims=True))
    experts = probs.shape[1]
    grad = grad_buf + jnp.dot(
        logit_grad, router_ref[...], precision=highest, preferred_element_type=f32
    )
    inverse = lax.rsqrt(jnp.mean(hidden * hidden, axis=-1, keepdims=True) + EPS)
    scaled = grad * gain
    inner_sum = jnp.mean(scaled * hidden, axis=-1, keepdims=True)
    dv = inverse * scaled - hidden * (inverse * inverse * inverse * inner_sum)
    dv_ref[...] = dv
    small_ref[...] = jnp.zeros_like(small_ref)
    small_ref[0:1, :] = jnp.sum(grad * hidden * inverse, axis=0, keepdims=True)
    small_ref[8 : 8 + experts, :] = dot_tn(logit_grad, normed, highest)
    grad_low = (up + dv).astype(bf16)
    half = att_ref.shape[0]
    inner = w_ref.shape[0]
    att = jnp.concatenate(
        [att_ref[:, 0:inner].astype(f32), att_ref[:, inner : 2 * inner].astype(f32)], axis=0
    )
    att = widen(att, wide_s)
    wout_ref[...] = wout0_ref[...] + dot_tn(att.astype(bf16), grad_low)
    gh = dot_nt(grad_low, w_ref[...])
    gh_low = gh.astype(bf16)
    count = gh_ref.shape[0]
    each = inner // count
    ght_ref[...] = dot_nt(w_ref[...], grad_low).astype(bf16)
    for h in range(count):
        cols = slice(h * each, (h + 1) * each)
        gh_ref[h] = gh_low[:, cols]
        delta_ref[h] = jnp.sum(
            gh_low[:, cols].astype(f32) * att[:, cols], axis=-1, keepdims=True
        )


def sparse_back_kernel(
    gh_ref, ght_ref, delta_ref, vt_ref, k_ref, qsel_ref,
    place_ref, wq_ref, wk_ref, wv_ref, low_ref, gain_ref, small_ref, wout_ref, *refs, heads,
):
    per_head, refs = refs[: 4 * gh_ref.shape[0]], refs[4 * gh_ref.shape[0] :]
    psels, dq0s, dkt0s, dvt0s = (per_head[i :: 4] for i in range(4))
    chunks = refs[:5]
    (score_ref, send_ref, keep_ref, out_ref,
     dq_s, q_low, k_low, v_low, kt_s, vt_s, all_s) = refs[5:]
    head = lax.axis_index("head")
    count, rows, width = gh_ref.shape
    tokens = vt_ref.shape[1]
    inner = count * width
    for h in range(count):
        cols = slice(h * width, (h + 1) * width)
        grad = dot(gh_ref[h], vt_ref[cols, :])
        prob = psels[h][...]
        score = (prob.astype(f32) * (grad - delta_ref[h])).astype(bf16)
        score_ref[h] = score
        dq_s[:, cols] = dot(score, k_ref[h]) * (width ** (-0.5))
        dkt = dkt0s[h][...] + dot(qsel_ref[cols, :], score)
        dvt = dvt0s[h][...] + dot(ght_ref[cols, :], prob)
        kt_s[cols, :] = dkt.astype(bf16)
        vt_s[cols, :] = dvt.astype(bf16)
        k_low[:, cols] = jnp.transpose(dkt).astype(bf16)
        v_low[:, cols] = jnp.transpose(dvt).astype(bf16)
    spread = dot(place_ref[...], dq_s[...].astype(bf16))
    for h in range(count):
        cols = slice(h * width, (h + 1) * width)
        q_low[:, cols] = (spread[:, cols] + dq0s[h][...]).astype(bf16)
    part = tokens // heads
    half = part // 2
    own, to_1, to_2, rest_1, rest_2 = chunks
    to_1[part:, :] = jnp.zeros((EXTRA, to_1.shape[1]), bf16)
    places = (
        ((own, 0), (own, half)),
        ((to_1, 0), (rest_1, 0)),
        ((rest_2, 0), (to_2, 0)),
        ((to_1, half), (to_2, half)),
    )
    for d in range(heads):
        mine = pl.ds(pl.multiple_of((head ^ d) * part, part), part)
        rows_part = (
            dot(q_low[mine, :], wq_ref[...])
            + dot(k_low[mine, :], wk_ref[...])
            + dot(v_low[mine, :], wv_ref[...])
        ).astype(bf16)
        for n, (ref, first) in enumerate(places[d]):
            ref[first : first + half, :] = rows_part[n * half : (n + 1) * half]
    low = low_ref[...]
    total = None
    grads = (dot_tn(q_low[...], low), dot(kt_s[...], low), dot(vt_s[...], low))
    for i, (grad, w) in enumerate(zip(grads, (wq_ref, wk_ref, wv_ref))):
        all_s[i * inner : (i + 1) * inner, :] = grad
        term = jnp.sum(grad * w[...].astype(f32), axis=0, keepdims=True)
        total = term if total is None else total + term
    all_s[3 * inner :, :] = wout_ref[...]
    out_ref[...] = small_ref[...]
    out_ref[1:2, :] = total / gain_ref[...]
    to_1[part : part + 1, :] = (total / gain_ref[...]).astype(bf16)
    split_rows(all_s, 1, send_ref, keep_ref)


def is_upper(bit):
    return (lax.axis_index("seq") & bit) != 0


def split_rows(all_s, bit, send_ref, keep_ref):
    half = send_ref.shape[0]
    low, high = all_s[0:half, :], all_s[half : 2 * half, :]
    keep_ref[...] = jnp.where(is_upper(bit), high, low)
    send_ref[...] = jnp.where(is_upper(bit), low, high).astype(bf16)


def halve_kernel(keep_ref, got_ref, *refs, bit):
    send_ref, out_ref, all_s = refs[-3:]
    if len(refs) > 3:
        rest_1, got_1, rest_2, got_2, small_ref, next_1, next_2 = refs[:-3]
        half = rest_1.shape[0]
        for rest, got, onward in ((rest_1, got_2, next_1), (rest_2, got_1, next_2)):
            got_rest = got[half : 2 * half, :].astype(f32)
            onward[0:half, :] = (rest[...].astype(f32) + got_rest).astype(bf16)
        mine = small_ref[1:2, :].astype(bf16).astype(f32)
        next_2[half:, :] = jnp.zeros((EXTRA, next_2.shape[1]), bf16)
        next_2[half : half + 1, :] = (mine + got_1[2 * half : 2 * half + 1, :].astype(f32)).astype(bf16)
    all_s[...] = keep_ref[...] + got_ref[...].astype(f32)
    split_rows(all_s, bit, send_ref, out_ref)


def join_rows(mine_ref, got_ref, all_s, bit, count):
    mine, got = mine_ref[...].astype(f32), got_ref[...].astype(f32)
    all_s[0:count, :] = jnp.where(is_upper(bit), got[:count], mine[:count])
    all_s[count : 2 * count, :] = jnp.where(is_upper(bit), mine[:count], got[:count])
    all_s[2 * count :, :] = mine[count:] + got[count:]


def pair_kernel(mine_ref, got_ref, *refs, bit, count):
    out_ref, all_s = refs[-2:]
    if len(refs) > 2:
        got_1, got_2, next_1, next_2 = refs[:-2]
        half = next_1.shape[0]
        next_2[...] = got_1[0:half, :]
        next_1[...] = got_2[half:, :]
    join_rows(mine_ref, got_ref, all_s, bit, count)
    out_ref[...] = all_s[...].astype(bf16)


def final_kernel(mine_ref, got_ref, *refs, bit, count):
    gain1_ref, gain2_ref, table_ref, router_ref, all_s = refs[-5:]
    outs = refs[:-5]
    join_rows(mine_ref, got_ref, all_s, bit, count)
    inner = outs[0].shape[0]
    for i, out in enumerate(outs):
        out[...] = all_s[i * inner : (i + 1) * inner, :]
    small = all_s[2 * count :, :]
    gain1_ref[...] = small[1, :]
    gain2_ref[...] = small[0, :]
    heads, buckets = table_ref.shape
    table_ref[...] = small[2 : 2 + heads, :buckets]
    router_ref[...] = small[8 : 8 + router_ref.shape[0], :]


def bias_grad_kernel(
    score_ref, place_ref, buckets_ref, small_ref, *refs, bucket_count
):
    count = score_ref.shape[0]
    offs, out_ref, acc_s, sums_s = refs[:count], *refs[count:]
    tokens = place_ref.shape[0]
    offsets = buckets_ref.shape[1]
    out_ref[...] = small_ref[...]
    bucket_hot = (iota((bucket_count, offsets), 0) == buckets_ref[...]).astype(f32)

    def one_head(h, carry):
        acc_s[...] = jnp.zeros_like(acc_s)
        for i in range(0, tokens, BLOCK):
            first = tokens - BLOCK - i
            acc_s[:, first : first + tokens] += dot(place_ref[i : i + BLOCK, :], score_ref[h])
        sums_s[h] = diagonals(acc_s[...])
        return carry

    lax.fori_loop(0, count, one_head, 0)
    for h in range(count):
        sums = sums_s[h] + offs[h][...]
        out_ref[2 + h : 3 + h, :bucket_count] = dot_nt(sums[:, :offsets], bucket_hot, highest)[0:1]


def hidden_kernel(*refs, heads):
    att_parts, w_ref, x_ref, out_ref, att_s = refs[:heads], *refs[heads:]
    head = lax.axis_index("head")
    tokens = x_ref.shape[0]
    inner = att_parts[0].shape[0]
    for d in range(heads):
        mine = pl.ds(pl.multiple_of((head ^ d) * inner, inner), inner)
        att_s[mine, :] = att_parts[d][...]

    def block(i, carry):
        rows = pl.ds(pl.multiple_of(i * 256, 256), 256)
        out_ref[rows, :] = x_ref[rows, :].astype(f32) + dot_tn(att_s[:, rows], w_ref[...])
        return carry

    lax.fori_loop(0, tokens // 256, block, 0)


def output_kernel(hidden_ref, place_ref, comb_ref, out_ref):
    high, rest = split_two(comb_ref[...])

    def block(i, carry):
        rows = pl.ds(pl.multiple_of(i * 256, 256), 256)
        where = place_ref[rows, :]
        out_ref[rows, :] = hidden_ref[rows, :] + (dot(where, high) + dot(where, rest))
        return carry

    lax.fori_loop(0, hidden_ref.shape[0] // 256, block, 0)


def first_norm_kernel(
    own, got_1, got_2, last_1, last_2, next_2, small_ref,
    x_ref, cot_ref, place_ref, dv_ref, gain_ref, keep_ref, got_ref, out_ref, sum_ref,
):
    half = last_1.shape[0]
    high, rest = split_two(dv_ref[...])
    for first, near, far in ((0, got_1, last_2), (half, got_2, last_1)):
        rows = pl.ds(first, half)
        grad = own[rows, :].astype(f32) + near[0:half, :].astype(f32)
        grad = grad + far[0:half, :].astype(f32)
        x = x_ref[rows, :].astype(f32)
        inverse = lax.rsqrt(jnp.mean(x * x, axis=-1, keepdims=True) + EPS)
        scaled = grad * gain_ref[...]
        inner_sum = jnp.mean(scaled * x, axis=-1, keepdims=True)
        where = place_ref[rows, :]
        hidden_grad = cot_ref[rows, :].astype(f32) + (dot(where, high) + dot(where, rest))
        out_ref[rows, :] = (
            hidden_grad + inverse * scaled - x * (inverse * inverse * inverse * inner_sum)
        ).astype(bf16)
    count = keep_ref.shape[0]
    sum_ref[0:count, :] = (keep_ref[...] + got_ref[...].astype(f32)).astype(bf16)
    gain1 = next_2[half:, :].astype(f32)[0:1] + last_2[half:, :].astype(f32)[0:1]
    small = small_ref[...]
    sum_ref[count:, :] = jnp.where(iota(small.shape, 0) == 1, gain1, small).astype(bf16)


def spread_near_kernel(own, got_1, got_2, out_ref, token, wide_s, sems):
    head = lax.axis_index("head")
    part = own.shape[0]
    copies = []
    for d, piece in enumerate((own, got_1, got_2)):
        wide_s[d] = piece[...].astype(f32)
        mine = pl.ds(pl.multiple_of((head ^ d) * part, part), part)
        copies.append(pltpu.make_async_copy(wide_s.at[d], out_ref.at[mine], sems.at[d]))
        copies[-1].start()
    token[...] = jnp.zeros_like(token)
    for copy in copies:
        copy.wait()


def spread_far_kernel(last_1, last_2, given, out_ref, wide_s, sem):
    head = lax.axis_index("head")
    half = last_1.shape[0]
    wide_s[0:half, :] = last_2[...].astype(f32)
    wide_s[half:, :] = last_1[...].astype(f32)
    mine = pl.ds(pl.multiple_of((head ^ 3) * 2 * half, 2 * half), 2 * half)
    copy = pltpu.make_async_copy(wide_s, out_ref.at[mine], sem)
    copy.start()
    copy.wait()


def swap(x, axis, d):
    size = lax.axis_size(axis)
    return lax.ppermute(x, axis, [(i, i ^ d) for i in range(size)])


def share(x, axis):
    return [x] + [swap(x, axis, d) for d in range(1, lax.axis_size(axis))]


def trade(pieces, axis):
    return lax.all_to_all(pieces, axis, split_axis=0, concat_axis=0, tiled=True)


def swap_all(pieces, axis):
    return [pieces[0]] + [swap(pieces[d], axis, d) for d in range(1, len(pieces))]


def bits_of(axis):
    return [b for b in (1 << i for i in range(16)) if b < lax.axis_size(axis)]


def halve(send, keep, bit, after, onward=()):
    rows, width = keep.shape
    outs = []
    if onward:
        half = onward[0].shape[0]
        outs = [shape_of(half, width, bf16), shape_of(half + EXTRA, width, bf16)]
    return call(
        partial(halve_kernel, bit=bit),
        outs + [shape_of(rows // 2, width, bf16), shape_of(rows // 2, width, f32)],
        (keep, swap(send, "seq", bit // 2)) + tuple(onward),
        scratch=[pltpu.VMEM((rows, width), f32)],
        name="halve",
        after=after,
        token=True,
    )


def pair(now, small_rows, bit, after, onward=()):
    rows, width = now.shape
    count = rows - small_rows
    outs = [shape_of(onward[0].shape[0] // 2, width, bf16)] * 2 if onward else []
    return call(
        partial(pair_kernel, bit=bit, count=count),
        outs + [shape_of(rows + count, width, bf16)],
        (now, swap(now, "seq", bit)) + tuple(onward),
        scratch=[pltpu.VMEM((rows + count, width), f32)],
        name="pair",
        after=after,
        token=True,
    )


def on_device(
    layer_input, cotangent, norm1_gain, w_query, w_key, w_value, w_attn_out, bias_table,
    norm2_gain, w_router, w_expert_in, w_expert_out, expert_ids, slot_ids, buckets,
):
    tokens, width = layer_input.shape
    shards = lax.axis_size("seq")
    heads = lax.axis_size("head")
    bucket_count, count = bias_table.shape
    inner = w_query.shape[1]
    each = inner // count
    experts = w_router.shape[1]
    rows, filled = experts * SLOT, experts * CAP
    hidden_units = w_expert_in.shape[2]
    part = tokens // heads
    split = 2 * width // heads
    span = 2 * tokens
    params = pltpu.CompilerParams(vmem_limit_bytes=VMEM_LIMIT if rows <= 256 else VMEM_ALL)

    ids = expert_ids.reshape(1, tokens)
    slots = slot_ids.reshape(1, tokens)
    bucket_row = buckets.reshape(1, -1)
    wq_t, wk_t, wv_t = jnp.transpose(w_query), jnp.transpose(w_key), jnp.transpose(w_value)
    router_t, table_t = jnp.transpose(w_router), jnp.transpose(bias_table)
    w_in = w_expert_in.reshape(width, hidden_units)
    w_out = w_expert_out.reshape(hidden_units, width)

    w_mix = share(w_attn_out, "head")

    low, prob, att, att_t, att_sel = pl.pallas_call(
        attend_kernel,
        out_shape=(
            shape_of(tokens, width, bf16),
            jax.ShapeDtypeStruct((count, tokens, tokens), bf16),
            jax.ShapeDtypeStruct((count, tokens, each), bf16),
            shape_of(inner, tokens, bf16),
            shape_of(filled // 2, 2 * inner, bf16),
        ),
        in_specs=[spec(pltpu.HBM)] * 9,
        out_specs=(spec(pltpu.VMEM),) * 5,
        scratch_shapes=[
            pltpu.VMEM((count, tokens, each), bf16),
            pltpu.VMEM((inner, tokens), bf16),
            pltpu.VMEM((count, tokens, each), bf16),
            pltpu.VMEM((8, span), f32),
            pltpu.VMEM((2, BLOCK, span), f32),
            pltpu.VMEM((filled, tokens), bf16),
            pltpu.VMEM((2, 2 * BLOCK, tokens), f32),
            pltpu.VMEM((tokens, width), bf16),
            pltpu.VMEM((width,), f32),
            pltpu.VMEM((inner, width), bf16),
            pltpu.VMEM((inner, width), bf16),
            pltpu.VMEM((inner, width), bf16),
            pltpu.VMEM((count, bucket_count), f32),
            pltpu.VMEM((1, span - 1), jnp.int32),
            pltpu.VMEM((1, tokens), jnp.int32),
            pltpu.VMEM((1, tokens), jnp.int32),
            pltpu.SemaphoreType.DMA((9,)),
        ],
        compiler_params=params,
        cost_estimate=NO_COST,
        name="attend",
    )(
        *(
            pltpu.with_memory_space_constraint(a, pltpu.HBM)
            for a in (layer_input, norm1_gain, wq_t, wk_t, wv_t, table_t, bucket_row, ids, slots)
        )
    )

    (att_sel,) = call(
        pass_kernel,
        [shape_of(filled // 2, 2 * inner, bf16)],
        (att_sel,),
        name="pass",
        after=(w_mix[1],),
    )
    sel_parts = share(att_sel, "head")
    sel_in, sel_up, place, place_c, x_c, cot_c, w_full = call(
        partial(place_kernel, heads=heads),
        [
            shape_of(rows, width, bf16),
            shape_of(rows, width, bf16),
            shape_of(tokens, rows, bf16),
            shape_of(part, rows, bf16),
            shape_of(part, width, bf16),
            shape_of(part, width, bf16),
            shape_of(heads * inner, width, bf16),
        ],
        (layer_input, cotangent, ids, slots) + tuple(w_mix),
        scratch=[pltpu.VMEM((tokens, rows), f32)],
        moved=12 * 2**20,
        name="place",
        after=(att_sel,),
    )
    routed = call(
        partial(route_kernel, shards=shards, heads=heads),
        [
            shape_of(rows, width, f32),
            shape_of(rows, width, f32),
            shape_of(rows, experts, f32),
            shape_of(inner, tokens, bf16),
        ]
        + [shape_of(TALL, packed_width(width), bf16)] * shards,
        tuple(sel_parts) + (w_full, sel_in, sel_up, norm2_gain, router_t, att_t),
        scratch=[
            pltpu.VMEM((heads, filled, inner), bf16),
            pltpu.VMEM((rows, 2 * width), f32),
            pltpu.VMEM((rows, width), f32),
            pltpu.VMEM((shards * TALL, packed_width(width)), f32),
        ],
        name="route",
    )
    hidden_sel, normed_sel, probs, att_on = routed[:4]
    pay_parts = swap_all(routed[4:], "seq")
    att_parts = [att_t] + [swap(att_on, "head", d) for d in range(1, heads - 1)]

    def masked_back(h, after):
        return call(
            partial(masked_back_kernel, h=h),
            [
                shape_of(tokens, each, f32),
                shape_of(each, tokens, f32),
                shape_of(each, tokens, f32),
                shape_of(8, span, f32),
                shape_of(rows, tokens, bf16),
            ],
            (gh, stack, k_rows, q_t, v_t, att, prob),
            scratch=[pltpu.VMEM((BLOCK, span), f32), pltpu.VMEM((tokens, tokens), bf16)],
            name="masked_back",
            after=after,
            moved=11 * 2**20,
            token=True,
        )

    done = call(
        partial(expert_kernel, shards=shards, heads=heads),
        [shape_of(filled, split, bf16)] * heads
        + [
            shape_of(rows, width, bf16),
            shape_of(rows, hidden_units, bf16),
            shape_of(rows, hidden_units, bf16),
            shape_of(rows, width, bf16),
        ],
        tuple(pay_parts[d] for d in far_first(shards)) + (w_in, w_out),
        scratch=[
            pltpu.VMEM((rows, 2 * width), f32),
            pltpu.VMEM((rows, 1), f32),
            pltpu.VMEM((heads, filled, split), f32),
        ],
        name="expert",
        after=tuple(att_parts[1:]),
        token=True,
    )
    x_rows, act, pre_low, out_low, token = done[heads:]
    gh, stack, k_rows, q_t, v_t, wout0, q_sel, token = call(
        prep_kernel,
        [
            jax.ShapeDtypeStruct((count, tokens, each), bf16),
            jax.ShapeDtypeStruct((count, each + rows, tokens), bf16),
            jax.ShapeDtypeStruct((count, tokens, each), bf16),
            shape_of(inner, tokens, bf16),
            shape_of(inner, tokens, bf16),
            shape_of(inner, width, f32),
            shape_of(inner, rows, bf16),
        ],
        (cotangent, w_attn_out, wq_t, wk_t, wv_t, low, place, att_t),
        scratch=[pltpu.VMEM((inner, tokens), bf16), pltpu.VMEM((tokens, width), bf16)],
        name="prep",
        after=(token,),
        moved=8 * 2**20,
        token=True,
    )

    masked = []
    for h in range(count - 2):
        masked.append(masked_back(h, (token,)))
        token = masked[-1][-1]
    returned = call(
        partial(sum_kernel, heads=heads),
        [shape_of(inner, tokens, bf16)] + [shape_of(CAP, split, bf16)] * shards,
        [att_t] + swap_all(done[:heads], "head"),
        scratch=[pltpu.VMEM((filled, split), f32)],
        name="sum",
        after=(token,),
        token=True,
    )
    att_parts.append(swap(returned[0], "head", heads - 1))
    answers = swap_all(returned[1:-1], "seq")
    joined, token = call(
        join_kernel,
        [shape_of(filled, split, bf16)],
        [answers[d] for d in far_first(shards)],
        scratch=[pltpu.VMEM((filled, split), f32)],
        name="join",
        token=True,
    )
    masked.append(masked_back(count - 2, (token, att_parts[-1])))
    masked.append(masked_back(count - 1, (masked[-1][-1],)))
    full_parts = share(joined, "head")

    small_rows = 8 + -(-experts // 8) * 8
    dv_sel, comb_sel, small, wout_part, gh_sel, ght_sel, delta_sel = call(
        partial(slot_back_kernel, heads=heads),
        [
            shape_of(rows, width, f32),
            shape_of(rows, width, f32),
            shape_of(small_rows, width, f32),
            shape_of(inner, width, f32),
            jax.ShapeDtypeStruct((count, rows, each), bf16),
            shape_of(inner, rows, bf16),
            jax.ShapeDtypeStruct((count, rows, 1), f32),
        ],
        tuple(full_parts)
        + (sel_up, normed_sel, hidden_sel, probs, router_t, norm2_gain)
        + (w_attn_out, att_sel, wout0),
        scratch=[pltpu.VMEM((heads, rows, split), f32), pltpu.VMEM((rows, inner), f32)],
        name="slot_back",
        after=(masked[-1][-1],),
    )

    back = call(
        partial(sparse_back_kernel, heads=heads),
        [shape_of(part, width, bf16), shape_of(part + EXTRA, width, bf16)]
        + [shape_of(part, width, bf16)]
        + [shape_of(part // 2, width, bf16)] * 2
        + [
            jax.ShapeDtypeStruct((count, rows, tokens), bf16),
            shape_of(2 * inner, width, bf16),
            shape_of(2 * inner, width, f32),
            shape_of(small_rows, width, f32),
        ],
        (gh_sel, ght_sel, delta_sel, v_t, k_rows, q_sel, place)
        + (wq_t, wk_t, wv_t, low, norm1_gain, small, wout_part)
        + tuple(a for m in masked for a in (m[4], m[0], m[1], m[2])),
        scratch=[
            pltpu.VMEM((rows, inner), f32),
            pltpu.VMEM((tokens, inner), bf16),
            pltpu.VMEM((tokens, inner), bf16),
            pltpu.VMEM((tokens, inner), bf16),
            pltpu.VMEM((inner, tokens), bf16),
            pltpu.VMEM((inner, tokens), bf16),
            pltpu.VMEM((4 * inner, width), f32),
        ],
        name="sparse_back",
    )
    score_sel, send, keep, small = back[5:]
    own, to_1, to_2, rest_1, rest_2 = back[:5]
    got_1, got_2 = swap(to_1, "head", 1), swap(to_2, "head", 2)

    bits = bits_of("seq")
    send, keep, token = halve(send, keep, bits[1], ())
    small_part = small
    small, token = call(
        partial(bias_grad_kernel, bucket_count=bucket_count),
        [shape_of(small_rows, width, f32)],
        (score_sel, place, bucket_row, small) + tuple(m[3] for m in masked),
        scratch=[pltpu.VMEM((BLOCK, span), f32), pltpu.VMEM((count, 8, span), f32)],
        name="bias_grad",
        after=(token,),
        moved=16 * 2**20,
        token=True,
    )
    next_1, next_2, send, keep, token = halve(
        send, keep, bits[2], (token,), (rest_1, got_1, rest_2, got_2, small_part)
    )
    last_1, last_2 = swap(next_1, "head", 1), swap(next_2, "head", 2)
    w_in_grad, w_out_grad, token = call(
        expert_grad_kernel,
        [
            jax.ShapeDtypeStruct(w_expert_in.shape, f32),
            jax.ShapeDtypeStruct(w_expert_out.shape, f32),
        ],
        (x_rows, pre_low, act, out_low),
        name="expert_grad",
        after=(token,),
        moved=10 * 2**20,
        token=True,
    )
    hidden, token = call(
        partial(hidden_kernel, heads=heads),
        [shape_of(tokens, width, f32)],
        tuple(att_parts) + (w_full, layer_input),
        scratch=[pltpu.VMEM((heads * inner, tokens), bf16)],
        name="hidden",
        after=(token,),
        moved=6 * 2**20,
        token=True,
    )
    for bit in bits[3:]:
        send, keep, token = halve(send, keep, bit, (token,))

    grad_part, weights, token = call(
        first_norm_kernel,
        [shape_of(part, width, bf16), shape_of(keep.shape[0] + small_rows, width, bf16)],
        (own, got_1, got_2, last_1, last_2, next_2, small)
        + (x_c, cot_c, place_c, dv_sel, norm1_gain)
        + (keep, swap(send, "seq", bits[-1])),
        name="first_norm",
        after=(token,),
        token=True,
    )
    grad_1, grad_2 = swap(grad_part, "head", 1), swap(grad_part, "head", 2)
    layer_output, token = call(
        output_kernel,
        [shape_of(tokens, width, f32)],
        (hidden, place, comb_sel),
        name="output",
        after=(token,),
        moved=10 * 2**20,
        token=True,
    )
    for bit in reversed(bits[3:]):
        weights, token = pair(weights, small_rows, bit, (token,))
    next_1, next_2, weights, token = pair(
        weights, small_rows, bits[2], (token,), (grad_1, grad_2)
    )
    grad_3 = (swap(next_1, "head", 1), swap(next_2, "head", 2))
    near, token = pl.pallas_call(
        spread_near_kernel,
        out_shape=(shape_of(tokens, width, f32), shape_of(8, 128, f32)),
        in_specs=[spec(pltpu.VMEM)] * 3,
        out_specs=(spec(pltpu.HBM), spec(pltpu.VMEM)),
        scratch_shapes=[pltpu.VMEM((3, part, width), f32), pltpu.SemaphoreType.DMA((3,))],
        compiler_params=params,
        cost_estimate=pl.CostEstimate(flops=1, bytes_accessed=5 * 2**20, transcendentals=0),
        name="spread_near",
    )(grad_part, grad_1, grad_2)
    weights, token = pair(weights, small_rows, bits[1], grad_3 + (token,))
    last = call(
        partial(final_kernel, bit=bits[0], count=2 * inner),
        [shape_of(inner, width, f32)] * 4
        + [
            jax.ShapeDtypeStruct((width,), f32),
            jax.ShapeDtypeStruct((width,), f32),
            shape_of(count, bucket_count, f32),
            shape_of(experts, width, f32),
        ],
        (weights, swap(weights, "seq", bits[0])),
        scratch=[pltpu.VMEM((4 * inner + small_rows, width), f32)],
        name="weights_out",
    )
    weight_sums = last[:4]
    gain1_sum, gain2_sum, table_sum, router_sum = last[4:]
    input_grad = pl.pallas_call(
        spread_far_kernel,
        out_shape=shape_of(tokens, width, f32),
        in_specs=[spec(pltpu.VMEM), spec(pltpu.VMEM), spec(pltpu.HBM)],
        out_specs=spec(pltpu.HBM),
        scratch_shapes=[pltpu.VMEM((part, width), f32), pltpu.SemaphoreType.DMA(())],
        input_output_aliases={2: 0},
        compiler_params=params,
        cost_estimate=NO_COST,
        name="spread_far",
    )(*grad_3, near)

    return (
        layer_output,
        input_grad,
        gain1_sum,
        jnp.transpose(weight_sums[0]),
        jnp.transpose(weight_sums[1]),
        jnp.transpose(weight_sums[2]),
        weight_sums[3],
        jnp.transpose(table_sum),
        gain2_sum,
        jnp.transpose(router_sum),
        w_in_grad,
        w_out_grad,
    )


def solution(mesh):
    return jax.shard_map(
        on_device,
        mesh=mesh,
        in_specs=(
            P("seq", None),
            P("seq", None),
            P(),
            P(None, "head"),
            P(None, "head"),
            P(None, "head"),
            P("head", None),
            P(None, "head"),
            P(),
            P(),
            P("seq", None, "head"),
            P("seq", "head", None),
            P("seq"),
            P("seq"),
            P(),
        ),
        out_specs=(
            P("seq", None),
            P("seq", None),
            P(),
            P(None, "head"),
            P(None, "head"),
            P(None, "head"),
            P("head", None),
            P(None, "head"),
            P(),
            P(),
            P("seq", None, "head"),
            P("seq", "head", None),
        ),
        check_vma=False,
    )
```
